32 devices in a mesh: inline: 8 (over z, x), col: 4 (over y, core).
Axes of the slice: x: 2, y: 2, z: 4, core: 2. Of those that a mesh axis runs over, the one named last changes fastest.
Arguments:
- seismic: bfloat16 [4, 16, 32, 1024], P(None, 'inline', 'col'), may hold values from -12 to 12
- validity: int32 [4, 16, 32], P(None, 'inline', 'col'), may hold values 0 or 1
- prior_weight: float32 [16, 32], P('inline', 'col'), may hold values from 0.2 to 5
- lateral_strength: float32 [3], replicated, may hold values from 0.5 to 2
- avo_coeffs: float32 [4, 3, 1024], replicated, may hold values from -4 to 4
- wavelets: float32 [4, 129], replicated, may hold values from -0.5 to 0.5
Outputs:
- solution_field: float32 [3, 16, 32, 1024], P(None, 'inline', 'col')
- residual: float32 [3, 16, 32, 1024], P(None, 'inline', 'col')
The draws below stay inside these ranges and needn't reach their ends.
All inputs are finite; a program needn't handle non-finite values. No bound on the sum of `validity` on one device may be relied on, other than what follows from the above.
Results may differ from the reference program's by a relative error of at most 0.0005.
Values sent between devices are 32-bit elements; how exact they have to be, the bound alone decides.
No kernel may reach another device: no remote copies, remote signals or barrier semaphores. Data moves between devices by JAX's collectives and lax.ppermute only.
A program may use at most 64 MiB of HBM per device.

```python
import math
import jax
import jax.numpy as jnp
from jax import lax

S = 1024
ANG = 4
COMP = 3
HW = 64
ITERS = 2
NI = 16
NC = 32


def draw_seismic(key, part):
    key = jax.random.fold_in(key, 11)
    ramp_inline = jnp.arange(NI, dtype=jnp.float32) / max(NI - 1, 1)
    ramp_column = jnp.arange(NC, dtype=jnp.float32) / max(NC - 1, 1)
    scale = jnp.exp(jnp.log(3.0) * (ramp_inline[:, None] + ramp_column[None, :])) / 3.0
    base = jax.random.truncated_normal(key, -4.0, 4.0, (ANG, NI, NC, S), jnp.float32)
    return (base * scale[None, :, :, None]).astype(jnp.bfloat16)


def place_ends(drawn, stream_key, least, high):
    shape = drawn.shape
    index_at = [jax.random.randint(jax.random.fold_in(stream_key, axis), (), 0, shape[axis]) for axis in range(len(shape))]
    drawn = drawn.at[tuple(index_at)].set(least)
    longest = shape.index(max(shape))
    index_at[longest] = (index_at[longest] + 1) % shape[longest]
    return drawn.at[tuple(index_at)].set(high)


def level_of(own_key, extent, cuts, smallest, high):
    def one(dim, blocks):
        draws = jax.random.uniform(jax.random.fold_in(jax.random.fold_in(own_key, 6), dim), (blocks,), jnp.float32, smallest / len(cuts), high / len(cuts))
        return jnp.repeat(jnp.exp(draws), extent[dim] // blocks).reshape((-1,) + (1,) * (len(extent) - dim - 1))

    loudness = one(*cuts[0])
    for cut in cuts[1:]:
        loudness = loudness * one(*cut)
    return loudness


def bell_draw(stream_key, shape, width, bound, kind=jnp.bfloat16):
    return jnp.clip(width * jax.random.normal(stream_key, shape, jnp.float32), -bound, bound).astype(kind)


def setup_inputs(seed: int = 0) -> dict:
    arg_keys = jax.random.split(jax.random.key(seed), 7)
    seismic = draw_seismic(jax.random.fold_in(arg_keys[6], 71), 0)
    validity = place_ends((jax.random.randint(arg_keys[1], (ANG, NI, NC), 0, 4) < 3).astype(jnp.int32), jax.random.fold_in(arg_keys[1], 1), 0, 1)
    prior_weight = jnp.clip(jnp.exp(math.log(5.0) - 3.218876 * jax.random.uniform(arg_keys[2], (NI, NC), jnp.float32) ** level_of(arg_keys[2], (NI, NC), ((0, 8), (1, 4)), -0.2, 0.2)), 0.2, 5.0)
    lateral_strength = jnp.clip(jnp.exp(jax.random.uniform(arg_keys[3], (COMP,), jnp.float32, math.log(0.5), math.log(2.0))), 0.5, 2.0)
    avo_coeffs = bell_draw(arg_keys[4], (ANG, COMP, S), 1.0, 4.0, jnp.float32)
    wavelets = bell_draw(arg_keys[5], (ANG, 2 * HW + 1), (2 * HW + 1) ** -0.5, 0.5, jnp.float32)
    return dict(seismic=seismic, validity=validity, prior_weight=prior_weight, lateral_strength=lateral_strength, avo_coeffs=avo_coeffs, wavelets=wavelets)


HIGH = lax.Precision.HIGHEST


def band_blocks(taps):
    half = (taps.shape[0] - 1) // 2
    rows = jnp.arange(128, dtype=jnp.int32)[:, None]
    cols = jnp.arange(128, dtype=jnp.int32)[None, :]
    lags = jnp.arange(taps.shape[0], dtype=jnp.int32)
    blocks = []
    for shift in (-1, 0, 1):
        offset = rows - cols - 128 * shift + half
        hits = (offset[:, :, None] == lags[None, None, :]).astype(taps.dtype)
        blocks.append(jnp.einsum("ijk,k->ij", hits, taps, precision=HIGH))
    return jnp.stack(blocks)


def convolve(field, blocks):
    shape = field.shape
    tiles = field.reshape(shape[:-1] + (shape[-1] // 128, 128))
    zero = jnp.zeros_like(tiles[..., :1, :])
    before = jnp.concatenate([zero, tiles[..., :-1, :]], axis=-2)
    after = jnp.concatenate([tiles[..., 1:, :], zero], axis=-2)
    result = jnp.einsum("...kj,ij->...ki", before, blocks[0], precision=HIGH)
    result = result + jnp.einsum("...kj,ij->...ki", tiles, blocks[1], precision=HIGH)
    result = result + jnp.einsum("...kj,ij->...ki", after, blocks[2], precision=HIGH)
    return result.reshape(shape)


def lateral(field):
    padded = jnp.pad(field, ((0, 0), (1, 1), (1, 1), (0, 0)))
    side = padded[:, 2:, 1:-1] + padded[:, :-2, 1:-1] + padded[:, 1:-1, 2:] + padded[:, 1:-1, :-2]
    return 4.0 * field - side


def apply_normal(field, coeffs, forward, backward, masks, prior_weight, lateral_strength):
    total = jnp.zeros_like(field)
    for angle in range(coeffs.shape[0]):
        weights = coeffs[angle][:, None, None, :]
        mixed = jnp.sum(weights * field, axis=0)
        synth = convolve(mixed, forward[angle]) * masks[angle][:, :, None]
        total = total + weights * convolve(synth, backward[angle])[None]
    prior = prior_weight[None, :, :, None] * field + lateral(field)
    return total + lateral_strength[:, None, None, None] * prior


def reference(seismic, validity, prior_weight, lateral_strength, avo_coeffs, wavelets):
    forward = [band_blocks(wavelets[a]) for a in range(wavelets.shape[0])]
    backward = [band_blocks(wavelets[a, ::-1]) for a in range(wavelets.shape[0])]
    masks = validity.astype(jnp.float32)
    right = jnp.zeros((avo_coeffs.shape[1],) + seismic.shape[1:], jnp.float32)
    for angle in range(seismic.shape[0]):
        traces = seismic[angle].astype(jnp.float32) * masks[angle][:, :, None]
        right = right + avo_coeffs[angle][:, None, None, :] * convolve(traces, backward[angle])[None]
    solution_field = jnp.zeros_like(right)
    residual, direction = right, right
    norm_now = jnp.sum(residual * residual)
    for step in range(ITERS):
        image = apply_normal(direction, avo_coeffs, forward, backward, masks, prior_weight, lateral_strength)
        alpha = norm_now / jnp.sum(direction * image)
        solution_field = solution_field + alpha * direction
        residual = residual - alpha * image
        norm_next = jnp.sum(residual * residual)
        direction = residual + (norm_next / norm_now) * direction
        norm_now = norm_next
    return solution_field, residual
```

```python
import functools

import jax
import jax.numpy as jnp
from jax import lax
from jax.experimental import pallas as pl
from jax.experimental.pallas import tpu as pltpu
from jax.sharding import PartitionSpec as P

LANES = 128
F32 = jnp.float32
BF16 = jnp.bfloat16


def split(value):
    high = value.astype(BF16)
    return high, (value - high.astype(F32)).astype(BF16)


def circulant(taps_ref, padded_ref, angle):
    line = jnp.broadcast_to(padded_ref[angle : angle + 1, :], (2 * LANES, 2 * LANES))
    return pltpu.roll(line, LANES, 1, stride=1, stride_axis=0)


def fill_taps(taps_ref, padded_ref):
    padded_ref[...] = jnp.zeros_like(padded_ref)
    padded_ref[0 : taps_ref.shape[0], 0 : taps_ref.shape[1]] = taps_ref[...]


def forward_band(circ):
    return jnp.concatenate(split(circ[:, :LANES]), axis=1)


def backward_band(circ):
    return jnp.concatenate(split(circ[LANES:, :]), axis=0)


def column(row):
    n = row.shape[1]
    same = lax.broadcasted_iota(jnp.int32, (n, n), 0) == lax.broadcasted_iota(jnp.int32, (n, n), 1)
    return jnp.sum(jnp.where(same, jnp.broadcast_to(row, (n, n)), 0.0), axis=1, keepdims=True)


def trace_columns(ref, *lead):
    rows = ref[lead].astype(F32) if lead else ref[...].astype(F32)
    return jnp.concatenate([column(rows[r : r + 1, :]) for r in range(rows.shape[0])], axis=0)


def windows(tiles):
    pairs = [jnp.concatenate(pair, axis=1) for pair in zip(tiles[:-1], tiles[1:])]
    return jnp.concatenate(pairs, axis=0)


def halves_sum(wide):
    return wide[:, :LANES] + wide[:, LANES:]


def forward(tiles, band):
    zero = jnp.zeros_like(tiles[0]).astype(BF16)
    highs, lows = zip(*[split(t) for t in tiles])
    n, size = len(tiles) + 1, tiles[0].shape[0]
    rows = [windows([zero, *part, zero]) for part in (highs, lows)]
    out = jnp.dot(jnp.concatenate(rows, axis=0), band, preferred_element_type=F32)
    out = halves_sum(out)
    out = out[: n * size] + out[n * size :]
    return [out[k * size : (k + 1) * size] for k in range(n)]


def backward(parts, band):
    n, size = len(parts[0]) - 1, parts[0][0].shape[0]
    rows = jnp.concatenate([windows(part) for part in parts], axis=0)
    out = lax.dot_general(rows, band, (((1,), (1,)), ((), ())), preferred_element_type=F32)
    out = halves_sum(out)
    total = out[: n * size]
    for p in range(1, len(parts)):
        total = total + out[p * n * size : (p + 1) * n * size]
    return [total[k * size : (k + 1) * size] for k in range(n)]


def coeff(avo_ref, angle, contrast, k):
    return avo_ref[angle, contrast : contrast + 1, pl.ds(k * LANES, LANES)]


def stack_tile(ref, contrast, k):
    rows = [ref[contrast, r, :, pl.ds(k * LANES, LANES)] for r in range(ref.shape[1])]
    return jnp.concatenate(rows, axis=0)


def store_tiles(out_ref, tiles):
    for c in range(out_ref.shape[0]):
        for k, tile in enumerate(tiles[c]):
            for r in range(out_ref.shape[1]):
                size = out_ref.shape[2]
                out_ref[c, r, :, pl.ds(k * LANES, LANES)] = tile[r * size : (r + 1) * size]


def store_edges(field_ref, top_ref, bottom_ref, left_ref, right_ref):
    contrasts, rows, traces, _ = field_ref.shape
    for c in range(contrasts):
        top_ref[c] = field_ref[c, 0]
        bottom_ref[c] = field_ref[c, rows - 1]
        for r in range(rows):
            left_ref[c * rows + r : c * rows + r + 1, :] = field_ref[c, r, 0:1, :]
            right_ref[c * rows + r : c * rows + r + 1, :] = field_ref[c, r, traces - 1 : traces, :]


def start_kernel(seis_ref, valid_ref, avo_ref, taps_ref, b_ref, top, bottom, left, right, padded):
    angles, rows, traces, samples = seis_ref.shape
    contrasts, n = avo_ref.shape[1], samples // LANES
    fill_taps(taps_ref, padded)
    lane = lax.broadcasted_iota(jnp.int32, (rows * traces, LANES), 1)
    total = [[None] * n for _ in range(contrasts)]
    for a in range(angles):
        mask = trace_columns(valid_ref, a)
        data = jnp.concatenate([seis_ref[a, r].astype(F32) for r in range(rows)], axis=0) * mask
        turned = [
            pltpu.roll(data[:, k * LANES : (k + 1) * LANES], LANES // 2, 1) for k in range(n)
        ]
        zero = jnp.zeros_like(turned[0])
        shifted = [
            jnp.where(lane < LANES // 2, before, here).astype(BF16)
            for before, here in zip([zero, *turned], [*turned, zero])
        ]
        band = backward_band(circulant(taps_ref, padded, a))
        result = backward([shifted], band)
        for c in range(contrasts):
            for k in range(n):
                term = coeff(avo_ref, a, c, k) * result[k]
                total[c][k] = term if a == 0 else total[c][k] + term
    store_tiles(b_ref, total)
    store_edges(b_ref, top, bottom, left, right)


def normal_kernel(field_ref, valid_ref, avo_ref, taps_ref, out_ref, padded):
    contrasts, rows, traces, samples = field_ref.shape
    angles, n = avo_ref.shape[0], samples // LANES
    fill_taps(taps_ref, padded)
    lane = lax.broadcasted_iota(jnp.int32, (rows * traces, LANES), 1)
    total = [[None] * n for _ in range(contrasts)]
    for a in range(angles):
        mask = trace_columns(valid_ref, a)
        circ = circulant(taps_ref, padded, a)
        mixed = []
        for k in range(n):
            parts = [coeff(avo_ref, a, c, k) * stack_tile(field_ref, c, k) for c in range(contrasts)]
            mixed.append(functools.reduce(jnp.add, parts))
        synth = [tile * mask for tile in forward(mixed, forward_band(circ))]
        synth[0] = jnp.where(lane < LANES // 2, 0.0, synth[0])
        synth[n] = jnp.where(lane < LANES // 2, synth[n], 0.0)
        result = backward(list(zip(*[split(t) for t in synth])), backward_band(circ))
        for c in range(contrasts):
            for k in range(n):
                term = coeff(avo_ref, a, c, k) * result[k]
                total[c][k] = term if a == 0 else total[c][k] + term
    store_tiles(out_ref, total)


def add_prior(field_ref, data_ref, prior_ref, strength_ref, above, below, left, right, out_ref):
    contrasts, rows, traces, samples = field_ref.shape
    place = lax.broadcasted_iota(jnp.int32, (traces, samples), 0)
    weights = [column(prior_ref[r : r + 1, :]) + 4.0 for r in range(rows)]
    for c in range(contrasts):
        for r in range(rows):
            here = field_ref[c, r]
            edge = c * rows + r
            west = jnp.where(place == 0, left[edge : edge + 1, :], pltpu.roll(here, 1, 0))
            east = jnp.where(
                place == traces - 1, right[edge : edge + 1, :], pltpu.roll(here, traces - 1, 0)
            )
            north = above[c] if r == 0 else field_ref[c, r - 1]
            south = below[c] if r == rows - 1 else field_ref[c, r + 1]
            prior = weights[r] * here - ((south + north) + (east + west))
            out_ref[c, r] = data_ref[c, r] + strength_ref[c] * prior


def first_image_kernel(
    field, data, prior, strength, above, below, left, right, out, o_top, o_bottom, o_left, o_right
):
    add_prior(field, data, prior, strength, above, below, left, right, out)
    store_edges(out, o_top, o_bottom, o_left, o_right)


def second_image_kernel(
    field, data, prior, strength, above, below, left, right, b_ref, out, gram_ref
):
    add_prior(field, data, prior, strength, above, below, left, right, out)
    contrasts, rows, traces, samples = field.shape
    pairs = ((b_ref, b_ref), (b_ref, field), (field, field), (field, out))
    gram_ref[...] = jnp.zeros_like(gram_ref)
    for q, (one, two) in enumerate(pairs):
        total = jnp.zeros((traces, LANES), F32)
        for c in range(contrasts):
            for r in range(rows):
                product = one[c, r] * two[c, r]
                tiles = [product[:, k : k + LANES] for k in range(0, samples, LANES)]
                total = total + functools.reduce(jnp.add, tiles)
        total = jnp.sum(jnp.sum(total, axis=0, keepdims=True), axis=1, keepdims=True)
        gram_ref[q : q + 1, :] = jnp.broadcast_to(total, (1, LANES))


def finish_kernel(gram_ref, b_ref, one_ref, two_ref, solution_ref, residual_ref):
    g00, g01, g11, g12 = (gram_ref[q : q + 1, 0:1] for q in range(4))
    first = g00 / g01
    ratio = first * g11 / g01
    second = (ratio - 1.0) * g01 / (first * g12 - ratio * g11)
    near = first + second * ratio
    far = first * second
    for c in range(b_ref.shape[0]):
        for r in range(b_ref.shape[1]):
            b, one, two = b_ref[c, r], one_ref[c, r], two_ref[c, r]
            solution_ref[c, r] = near * b - far * one
            residual_ref[c, r] = b - near * one + far * two


VMEM = pl.BlockSpec(memory_space=pltpu.VMEM)
SMEM = pl.BlockSpec(memory_space=pltpu.SMEM)


def call(kernel, outs, ins, flops, scratch=(), scalars=()):
    moved = sum(x.size * x.dtype.itemsize for x in (*ins, *outs))
    return pl.pallas_call(
        kernel,
        out_shape=outs,
        in_specs=[SMEM if i in scalars else VMEM for i in range(len(ins))],
        out_specs=jax.tree.map(lambda _: VMEM, outs),
        scratch_shapes=list(scratch),
        compiler_params=pltpu.CompilerParams(vmem_limit_bytes=24 * 1024 * 1024),
        cost_estimate=pl.CostEstimate(flops=flops, bytes_accessed=moved, transcendentals=0),
        name=kernel.__name__,
    )(*ins)


def exchange(edges):
    top, bottom, left, right = edges
    moved = []
    for axis, first, last in (("inline", top, bottom), ("col", left, right)):
        size = lax.axis_size(axis)
        ahead = [(i, i + 1) for i in range(size - 1)]
        back = [(j, i) for i, j in ahead]
        moved.append(lax.ppermute(last, axis, ahead))
        moved.append(lax.ppermute(first, axis, back))
    return moved


def shards(seismic, validity, prior_weight, lateral_strength, avo_coeffs, wavelets):
    angles, rows, traces, samples = seismic.shape
    contrasts = avo_coeffs.shape[1]
    field = jax.ShapeDtypeStruct((contrasts, rows, traces, samples), F32)
    row = jax.ShapeDtypeStruct((contrasts, traces, samples), F32)
    side = jax.ShapeDtypeStruct((contrasts * rows, samples), F32)
    edges = (row, row, side, side)
    taps = [pltpu.VMEM((8, 2 * LANES), F32)]
    work = 2 * angles * rows * traces * samples * 256 * 4

    b, *sent = call(
        start_kernel,
        (field, *edges),
        (seismic, validity, avo_coeffs, wavelets),
        work,
        taps,
    )
    around = exchange(sent)
    (data,) = call(normal_kernel, (field,), (b, validity, avo_coeffs, wavelets), 2 * work, taps)
    one, *sent = call(
        first_image_kernel,
        (field, *edges),
        (b, data, prior_weight, lateral_strength, *around),
        20 * field.size,
        scalars=(3,),
    )
    around = exchange(sent)
    (data,) = call(normal_kernel, (field,), (one, validity, avo_coeffs, wavelets), 2 * work, taps)
    two, gram = call(
        second_image_kernel,
        (field, jax.ShapeDtypeStruct((8, LANES), F32)),
        (one, data, prior_weight, lateral_strength, *around, b),
        30 * field.size,
        scalars=(3,),
    )
    gram = lax.psum(gram, ("inline", "col"))
    return tuple(call(finish_kernel, (field, field), (gram, b, one, two), 8 * field.size))


def solution(mesh):
    placed = (
        P(None, "inline", "col", None),
        P(None, "inline", "col"),
        P("inline", "col"),
        P(),
        P(),
        P(),
    )
    return jax.shard_map(
        shards,
        mesh=mesh,
        in_specs=placed,
        out_specs=(P(None, "inline", "col", None), P(None, "inline", "col", None)),
        check_vma=False,
    )
```

```python
import functools

import jax
import jax.numpy as jnp
from jax import lax
from jax.experimental import pallas as pl
from jax.experimental.pallas import tpu as pltpu
from jax.sharding import PartitionSpec as P

LANES = 128
F32 = jnp.float32
BF16 = jnp.bfloat16


def split(value):
    high = value.astype(BF16)
    return high, (value - high.astype(F32)).astype(BF16)


def circulant(taps_ref, padded_ref, angle):
    line = jnp.broadcast_to(padded_ref[angle : angle + 1, :], (2 * LANES, 2 * LANES))
    return pltpu.roll(line, LANES, 1, stride=1, stride_axis=0)


def fill_taps(taps_ref, padded_ref):
    padded_ref[...] = jnp.zeros_like(padded_ref)
    padded_ref[0 : taps_ref.shape[0], 0 : taps_ref.shape[1]] = taps_ref[...]


def forward_band(circ):
    return jnp.concatenate(split(circ[:, :LANES]), axis=1)


def backward_band(circ):
    return jnp.concatenate(split(circ[LANES:, :]), axis=0)


def column(row):
    n = row.shape[1]
    same = lax.broadcasted_iota(jnp.int32, (n, n), 0) == lax.broadcasted_iota(jnp.int32, (n, n), 1)
    return jnp.sum(jnp.where(same, jnp.broadcast_to(row, (n, n)), 0.0), axis=1, keepdims=True)


def trace_columns(ref, *lead):
    rows = ref[lead].astype(F32) if lead else ref[...].astype(F32)
    return jnp.concatenate([column(rows[r : r + 1, :]) for r in range(rows.shape[0])], axis=0)


def windows(tiles):
    pairs = [jnp.concatenate(pair, axis=1) for pair in zip(tiles[:-1], tiles[1:])]
    return jnp.concatenate(pairs, axis=0)


def halves_sum(wide):
    return wide[:, :LANES] + wide[:, LANES:]


def forward(tiles, band):
    zero = jnp.zeros_like(tiles[0]).astype(BF16)
    highs, lows = zip(*[split(t) for t in tiles])
    n, size = len(tiles) + 1, tiles[0].shape[0]
    rows = [windows([zero, *part, zero]) for part in (highs, lows)]
    out = jnp.dot(jnp.concatenate(rows, axis=0), band, preferred_element_type=F32)
    out = halves_sum(out)
    out = out[: n * size] + out[n * size :]
    return [out[k * size : (k + 1) * size] for k in range(n)]


def backward(parts, band):
    n, size = len(parts[0]) - 1, parts[0][0].shape[0]
    rows = jnp.concatenate([windows(part) for part in parts], axis=0)
    out = lax.dot_general(rows, band, (((1,), (1,)), ((), ())), preferred_element_type=F32)
    out = halves_sum(out)
    total = out[: n * size]
    for p in range(1, len(parts)):
        total = total + out[p * n * size : (p + 1) * n * size]
    return [total[k * size : (k + 1) * size] for k in range(n)]


def coeff(avo_ref, angle, contrast, k):
    return avo_ref[angle, contrast : contrast + 1, pl.ds(k * LANES, LANES)]


def stack_tile(ref, contrast, k):
    rows = [ref[contrast, r, :, pl.ds(k * LANES, LANES)] for r in range(ref.shape[1])]
    return jnp.concatenate(rows, axis=0)


def store_tiles(out_ref, tiles):
    for c in range(out_ref.shape[0]):
        for k, tile in enumerate(tiles[c]):
            for r in range(out_ref.shape[1]):
                size = out_ref.shape[2]
                out_ref[c, r, :, pl.ds(k * LANES, LANES)] = tile[r * size : (r + 1) * size]


def store_edges(field_ref, top_ref, bottom_ref, left_ref, right_ref):
    contrasts, rows, traces, _ = field_ref.shape
    for c in range(contrasts):
        top_ref[c] = field_ref[c, 0]
        bottom_ref[c] = field_ref[c, rows - 1]
        for r in range(rows):
            left_ref[c * rows + r : c * rows + r + 1, :] = field_ref[c, r, 0:1, :]
            right_ref[c * rows + r : c * rows + r + 1, :] = field_ref[c, r, traces - 1 : traces, :]


def start_kernel(seis_ref, valid_ref, avo_ref, taps_ref, b_ref, top, bottom, left, right, padded):
    angles, rows, traces, samples = seis_ref.shape
    contrasts, n = avo_ref.shape[1], samples // LANES
    fill_taps(taps_ref, padded)
    lane = lax.broadcasted_iota(jnp.int32, (rows * traces, LANES), 1)
    total = [[None] * n for _ in range(contrasts)]
    for a in range(angles):
        mask = trace_columns(valid_ref, a)
        data = jnp.concatenate([seis_ref[a, r].astype(F32) for r in range(rows)], axis=0) * mask
        turned = [
            pltpu.roll(data[:, k * LANES : (k + 1) * LANES], LANES // 2, 1) for k in range(n)
        ]
        zero = jnp.zeros_like(turned[0])
        shifted = [
            jnp.where(lane < LANES // 2, before, here).astype(BF16)
            for before, here in zip([zero, *turned], [*turned, zero])
        ]
        band = backward_band(circulant(taps_ref, padded, a))
        result = backward([shifted], band)
        for c in range(contrasts):
            for k in range(n):
                term = coeff(avo_ref, a, c, k) * result[k]
                total[c][k] = term if a == 0 else total[c][k] + term
    store_tiles(b_ref, total)
    store_edges(b_ref, top, bottom, left, right)


def normal_kernel(field_ref, valid_ref, avo_ref, taps_ref, out_ref, padded):
    contrasts, rows, traces, samples = field_ref.shape
    angles, n = avo_ref.shape[0], samples // LANES
    fill_taps(taps_ref, padded)
    lane = lax.broadcasted_iota(jnp.int32, (rows * traces, LANES), 1)
    total = [[None] * n for _ in range(contrasts)]
    for a in range(angles):
        mask = trace_columns(valid_ref, a)
        circ = circulant(taps_ref, padded, a)
        mixed = []
        for k in range(n):
            parts = [coeff(avo_ref, a, c, k) * stack_tile(field_ref, c, k) for c in range(contrasts)]
            mixed.append(functools.reduce(jnp.add, parts))
        synth = [tile * mask for tile in forward(mixed, forward_band(circ))]
        synth[0] = jnp.where(lane < LANES // 2, 0.0, synth[0])
        synth[n] = jnp.where(lane < LANES // 2, synth[n], 0.0)
        result = backward(list(zip(*[split(t) for t in synth])), backward_band(circ))
        for c in range(contrasts):
            for k in range(n):
                term = coeff(avo_ref, a, c, k) * result[k]
                total[c][k] = term if a == 0 else total[c][k] + term
    store_tiles(out_ref, total)


def add_prior(field_ref, data_ref, prior_ref, strength_ref, above, below, left, right, out_ref):
    contrasts, rows, traces, samples = field_ref.shape
    place = lax.broadcasted_iota(jnp.int32, (traces, samples), 0)
    weights = [column(prior_ref[r : r + 1, :]) + 4.0 for r in range(rows)]
    for c in range(contrasts):
        for r in range(rows):
            here = field_ref[c, r]
            edge = c * rows + r
            west = jnp.where(place == 0, left[edge : edge + 1, :], pltpu.roll(here, 1, 0))
            east = jnp.where(
                place == traces - 1, right[edge : edge + 1, :], pltpu.roll(here, traces - 1, 0)
            )
            north = above[c] if r == 0 else field_ref[c, r - 1]
            south = below[c] if r == rows - 1 else field_ref[c, r + 1]
            prior = weights[r] * here - ((south + north) + (east + west))
            out_ref[c, r] = data_ref[c, r] + strength_ref[c] * prior


def first_image_kernel(
    field, data, prior, strength, above, below, left, right, out, o_top, o_bottom, o_left, o_right
):
    add_prior(field, data, prior, strength, above, below, left, right, out)
    store_edges(out, o_top, o_bottom, o_left, o_right)


def second_image_kernel(
    field, data, prior, strength, above, below, left, right, b_ref, out, gram_ref
):
    add_prior(field, data, prior, strength, above, below, left, right, out)
    contrasts, rows, traces, samples = field.shape
    pairs = ((b_ref, b_ref), (b_ref, field), (field, field), (field, out))
    gram_ref[...] = jnp.zeros_like(gram_ref)
    for q, (one, two) in enumerate(pairs):
        total = jnp.zeros((traces, LANES), F32)
        for c in range(contrasts):
            for r in range(rows):
                product = one[c, r] * two[c, r]
                tiles = [product[:, k : k + LANES] for k in range(0, samples, LANES)]
                total = total + functools.reduce(jnp.add, tiles)
        total = jnp.sum(jnp.sum(total, axis=0, keepdims=True), axis=1, keepdims=True)
        gram_ref[:, q, :] = jnp.broadcast_to(total, (gram_ref.shape[0], LANES))


def finish_kernel(gram_ref, b_ref, one_ref, two_ref, solution_ref, residual_ref):
    sums = jnp.sum(gram_ref[...], axis=0)
    g00, g01, g11, g12 = (sums[q : q + 1, 0:1] for q in range(4))
    first = g00 / g01
    ratio = first * g11 / g01
    second = (ratio - 1.0) * g01 / (first * g12 - ratio * g11)
    near = first + second * ratio
    far = first * second
    for c in range(b_ref.shape[0]):
        for r in range(b_ref.shape[1]):
            b, one, two = b_ref[c, r], one_ref[c, r], two_ref[c, r]
            solution_ref[c, r] = near * b - far * one
            residual_ref[c, r] = b - near * one + far * two


VMEM = pl.BlockSpec(memory_space=pltpu.VMEM)
SMEM = pl.BlockSpec(memory_space=pltpu.SMEM)


def call(kernel, outs, ins, flops, scratch=(), scalars=()):
    moved = sum(x.size * x.dtype.itemsize for x in (*ins, *outs))
    return pl.pallas_call(
        kernel,
        out_shape=outs,
        in_specs=[SMEM if i in scalars else VMEM for i in range(len(ins))],
        out_specs=jax.tree.map(lambda _: VMEM, outs),
        scratch_shapes=list(scratch),
        compiler_params=pltpu.CompilerParams(vmem_limit_bytes=24 * 1024 * 1024),
        cost_estimate=pl.CostEstimate(flops=flops, bytes_accessed=moved, transcendentals=0),
        name=kernel.__name__,
    )(*ins)


def exchange(edges):
    top, bottom, left, right = edges
    moved = []
    for axis, first, last in (("inline", top, bottom), ("col", left, right)):
        size = lax.axis_size(axis)
        ahead = [(i, i + 1) for i in range(size - 1)]
        back = [(j, i) for i, j in ahead]
        moved.append(lax.ppermute(last, axis, ahead))
        moved.append(lax.ppermute(first, axis, back))
    return moved


def shards(seismic, validity, prior_weight, lateral_strength, avo_coeffs, wavelets):
    angles, rows, traces, samples = seismic.shape
    contrasts = avo_coeffs.shape[1]
    axes = ("inline", "col")
    field = jax.ShapeDtypeStruct((contrasts, rows, traces, samples), F32)
    row = jax.ShapeDtypeStruct((contrasts, traces, samples), F32)
    side = jax.ShapeDtypeStruct((contrasts * rows, samples), F32)
    edges = (row, row, side, side)
    taps = [pltpu.VMEM((8, 2 * LANES), F32)]
    work = 2 * angles * rows * traces * samples * 256 * 4

    b, *sent = call(
        start_kernel,
        (field, *edges),
        (seismic, validity, avo_coeffs, wavelets),
        work,
        taps,
    )
    around = exchange(sent)
    (data,) = call(normal_kernel, (field,), (b, validity, avo_coeffs, wavelets), 2 * work, taps)
    one, *sent = call(
        first_image_kernel,
        (field, *edges),
        (b, data, prior_weight, lateral_strength, *around),
        20 * field.size,
        scalars=(3,),
    )
    around = exchange(sent)
    (data,) = call(normal_kernel, (field,), (one, validity, avo_coeffs, wavelets), 2 * work, taps)
    two, gram = call(
        second_image_kernel,
        (field, jax.ShapeDtypeStruct((lax.axis_size(axes), 8, LANES), F32)),
        (one, data, prior_weight, lateral_strength, *around, b),
        30 * field.size,
        scalars=(3,),
    )
    gram = lax.all_to_all(gram, axes, 0, 0)
    return tuple(call(finish_kernel, (field, field), (gram, b, one, two), 8 * field.size))


def solution(mesh):
    placed = (
        P(None, "inline", "col", None),
        P(None, "inline", "col"),
        P("inline", "col"),
        P(),
        P(),
        P(),
    )
    return jax.shard_map(
        shards,
        mesh=mesh,
        in_specs=placed,
        out_specs=(P(None, "inline", "col", None), P(None, "inline", "col", None)),
        check_vma=False,
    )
```

```python
import functools

import jax
import jax.numpy as jnp
from jax import lax
from jax.experimental import pallas as pl
from jax.experimental.pallas import tpu as pltpu
from jax.sharding import PartitionSpec as P

LANES = 128
F32 = jnp.float32
BF16 = jnp.bfloat16


def split(value):
    high = value.astype(BF16)
    return high, (value - high.astype(F32)).astype(BF16)


def circulant(taps_ref, padded_ref, angle):
    line = jnp.broadcast_to(padded_ref[angle : angle + 1, :], (2 * LANES, 2 * LANES))
    return pltpu.roll(line, LANES, 1, stride=1, stride_axis=0)


def fill_taps(taps_ref, padded_ref):
    padded_ref[...] = jnp.zeros_like(padded_ref)
    padded_ref[0 : taps_ref.shape[0], 0 : taps_ref.shape[1]] = taps_ref[...]


def forward_band(circ):
    return jnp.concatenate(split(circ[:, :LANES]), axis=1)


def backward_band(circ):
    return jnp.concatenate(split(circ[LANES:, :]), axis=0)


def column(row):
    n = row.shape[1]
    same = lax.broadcasted_iota(jnp.int32, (n, n), 0) == lax.broadcasted_iota(jnp.int32, (n, n), 1)
    return jnp.sum(jnp.where(same, jnp.broadcast_to(row, (n, n)), 0.0), axis=1, keepdims=True)


def trace_columns(ref, *lead):
    rows = ref[lead].astype(F32) if lead else ref[...].astype(F32)
    return jnp.concatenate([column(rows[r : r + 1, :]) for r in range(rows.shape[0])], axis=0)


def windows(tiles):
    pairs = [jnp.concatenate(pair, axis=1) for pair in zip(tiles[:-1], tiles[1:])]
    return jnp.concatenate(pairs, axis=0)


def halves_sum(wide):
    return wide[:, :LANES] + wide[:, LANES:]


def forward(tiles, band):
    zero = jnp.zeros_like(tiles[0]).astype(BF16)
    highs, lows = zip(*[split(t) for t in tiles])
    n, size = len(tiles) + 1, tiles[0].shape[0]
    rows = [windows([zero, *part, zero]) for part in (highs, lows)]
    out = jnp.dot(jnp.concatenate(rows, axis=0), band, preferred_element_type=F32)
    out = halves_sum(out)
    out = out[: n * size] + out[n * size :]
    return [out[k * size : (k + 1) * size] for k in range(n)]


def backward(parts, band):
    n, size = len(parts[0]) - 1, parts[0][0].shape[0]
    rows = jnp.concatenate([windows(part) for part in parts], axis=0)
    out = lax.dot_general(rows, band, (((1,), (1,)), ((), ())), preferred_element_type=F32)
    out = halves_sum(out)
    total = out[: n * size]
    for p in range(1, len(parts)):
        total = total + out[p * n * size : (p + 1) * n * size]
    return [total[k * size : (k + 1) * size] for k in range(n)]


def coeff(avo_ref, angle, contrast, k):
    return avo_ref[contrast, angle : angle + 1, pl.ds(k * LANES, LANES)]


def stack_tile(ref, contrast, k):
    rows = [ref[contrast, r, :, pl.ds(k * LANES, LANES)] for r in range(ref.shape[1])]
    return jnp.concatenate(rows, axis=0)


def store_tiles(out_ref, tiles):
    for c in range(out_ref.shape[0]):
        for k, tile in enumerate(tiles[c]):
            for r in range(out_ref.shape[1]):
                size = out_ref.shape[2]
                out_ref[c, r, :, pl.ds(k * LANES, LANES)] = tile[r * size : (r + 1) * size]


def store_edges(field_ref, top_ref, bottom_ref, left_ref, right_ref):
    contrasts, rows, traces, _ = field_ref.shape
    for c in range(contrasts):
        top_ref[c] = field_ref[c, 0]
        bottom_ref[c] = field_ref[c, rows - 1]
        for r in range(rows):
            left_ref[c * rows + r : c * rows + r + 1, :] = field_ref[c, r, 0:1, :]
            right_ref[c * rows + r : c * rows + r + 1, :] = field_ref[c, r, traces - 1 : traces, :]


def start_kernel(seis_ref, valid_ref, avo_ref, taps_ref, b_ref, top, bottom, left, right, padded):
    angles, rows, traces, samples = seis_ref.shape
    contrasts, n = avo_ref.shape[0], samples // LANES
    fill_taps(taps_ref, padded)
    lane = lax.broadcasted_iota(jnp.int32, (rows * traces, LANES), 1)
    total = [[None] * n for _ in range(contrasts)]
    for a in range(angles):
        mask = trace_columns(valid_ref, a)
        data = jnp.concatenate([seis_ref[a, r].astype(F32) for r in range(rows)], axis=0) * mask
        turned = [
            pltpu.roll(data[:, k * LANES : (k + 1) * LANES], LANES // 2, 1) for k in range(n)
        ]
        zero = jnp.zeros_like(turned[0])
        shifted = [
            jnp.where(lane < LANES // 2, before, here).astype(BF16)
            for before, here in zip([zero, *turned], [*turned, zero])
        ]
        band = backward_band(circulant(taps_ref, padded, a))
        result = backward([shifted], band)
        for c in range(contrasts):
            for k in range(n):
                term = coeff(avo_ref, a, c, k) * result[k]
                total[c][k] = term if a == 0 else total[c][k] + term
    store_tiles(b_ref, total)
    store_edges(b_ref, top, bottom, left, right)


def normal_kernel(field_ref, valid_ref, avo_ref, taps_ref, out_ref, padded):
    contrasts, rows, traces, samples = field_ref.shape
    angles, n = avo_ref.shape[1], samples // LANES
    fill_taps(taps_ref, padded)
    lane = lax.broadcasted_iota(jnp.int32, (rows * traces, LANES), 1)
    total = [[None] * n for _ in range(contrasts)]
    for a in range(angles):
        mask = trace_columns(valid_ref, a)
        circ = circulant(taps_ref, padded, a)
        mixed = []
        for k in range(n):
            parts = [coeff(avo_ref, a, c, k) * stack_tile(field_ref, c, k) for c in range(contrasts)]
            mixed.append(functools.reduce(jnp.add, parts))
        synth = [tile * mask for tile in forward(mixed, forward_band(circ))]
        synth[0] = jnp.where(lane < LANES // 2, 0.0, synth[0])
        synth[n] = jnp.where(lane < LANES // 2, synth[n], 0.0)
        result = backward(list(zip(*[split(t) for t in synth])), backward_band(circ))
        for c in range(contrasts):
            for k in range(n):
                term = coeff(avo_ref, a, c, k) * result[k]
                total[c][k] = term if a == 0 else total[c][k] + term
    store_tiles(out_ref, total)


def add_prior(field_ref, data_ref, prior_ref, strength_ref, above, below, left, right, out_ref):
    contrasts, rows, traces, samples = field_ref.shape
    place = lax.broadcasted_iota(jnp.int32, (traces, samples), 0)
    weights = [column(prior_ref[r : r + 1, :]) + 4.0 for r in range(rows)]
    for c in range(contrasts):
        for r in range(rows):
            here = field_ref[c, r]
            edge = c * rows + r
            west = jnp.where(place == 0, left[edge : edge + 1, :], pltpu.roll(here, 1, 0))
            east = jnp.where(
                place == traces - 1, right[edge : edge + 1, :], pltpu.roll(here, traces - 1, 0)
            )
            north = above[c] if r == 0 else field_ref[c, r - 1]
            south = below[c] if r == rows - 1 else field_ref[c, r + 1]
            prior = weights[r] * here - ((south + north) + (east + west))
            out_ref[c, r] = data_ref[c, r] + strength_ref[c] * prior


def first_image_kernel(
    field, data, prior, strength, above, below, left, right, out, o_top, o_bottom, o_left, o_right
):
    add_prior(field, data, prior, strength, above, below, left, right, out)
    store_edges(out, o_top, o_bottom, o_left, o_right)


def second_image_kernel(
    field, data, prior, strength, above, below, left, right, b_ref, out, gram_ref
):
    add_prior(field, data, prior, strength, above, below, left, right, out)
    contrasts, rows, traces, samples = field.shape
    pairs = ((b_ref, b_ref), (b_ref, field), (field, field), (field, out))
    gram_ref[...] = jnp.zeros_like(gram_ref)
    for q, (one, two) in enumerate(pairs):
        total = jnp.zeros((traces, LANES), F32)
        for c in range(contrasts):
            for r in range(rows):
                product = one[c, r] * two[c, r]
                tiles = [product[:, k : k + LANES] for k in range(0, samples, LANES)]
                total = total + functools.reduce(jnp.add, tiles)
        total = jnp.sum(jnp.sum(total, axis=0, keepdims=True), axis=1, keepdims=True)
        gram_ref[:, q, :] = jnp.broadcast_to(total, (gram_ref.shape[0], LANES))


def spread_kernel(parts_ref, out_ref):
    out_ref[...] = jnp.broadcast_to(jnp.sum(parts_ref[...], axis=0, keepdims=True), out_ref.shape)


def finish_kernel(gram_ref, b_ref, one_ref, two_ref, solution_ref, residual_ref):
    sums = jnp.sum(gram_ref[...], axis=0)
    g00, g01, g11, g12 = (sums[q : q + 1, 0:1] for q in range(4))
    first = g00 / g01
    ratio = first * g11 / g01
    second = (ratio - 1.0) * g01 / (first * g12 - ratio * g11)
    near = first + second * ratio
    far = first * second
    for c in range(b_ref.shape[0]):
        for r in range(b_ref.shape[1]):
            b, one, two = b_ref[c, r], one_ref[c, r], two_ref[c, r]
            solution_ref[c, r] = near * b - far * one
            residual_ref[c, r] = b - near * one + far * two


VMEM = pl.BlockSpec(memory_space=pltpu.VMEM)
SMEM = pl.BlockSpec(memory_space=pltpu.SMEM)


def call(kernel, outs, ins, flops, scratch=(), scalars=()):
    moved = sum(x.size * x.dtype.itemsize for x in (*ins, *outs))
    return pl.pallas_call(
        kernel,
        out_shape=outs,
        in_specs=[SMEM if i in scalars else VMEM for i in range(len(ins))],
        out_specs=jax.tree.map(lambda _: VMEM, outs),
        scratch_shapes=list(scratch),
        compiler_params=pltpu.CompilerParams(vmem_limit_bytes=24 * 1024 * 1024),
        cost_estimate=pl.CostEstimate(flops=flops, bytes_accessed=moved, transcendentals=0),
        name=kernel.__name__,
    )(*ins)


def exchange(edges):
    top, bottom, left, right = edges
    moved = []
    for axis, first, last in (("inline", top, bottom), ("col", left, right)):
        size = lax.axis_size(axis)
        ahead = [(i, i + 1) for i in range(size - 1)]
        back = [(j, i) for i, j in ahead]
        moved.append(lax.ppermute(last, axis, ahead))
        moved.append(lax.ppermute(first, axis, back))
    return moved


def shards(seismic, validity, prior_weight, lateral_strength, avo_coeffs, wavelets):
    angles, rows, traces, samples = seismic.shape
    contrasts = avo_coeffs.shape[1]
    avo_coeffs = jnp.swapaxes(avo_coeffs, 0, 1)
    inline, col = lax.axis_size("inline"), lax.axis_size("col")
    field = jax.ShapeDtypeStruct((contrasts, rows, traces, samples), F32)
    row = jax.ShapeDtypeStruct((contrasts, traces, samples), F32)
    side = jax.ShapeDtypeStruct((contrasts * rows, samples), F32)
    edges = (row, row, side, side)
    taps = [pltpu.VMEM((8, 2 * LANES), F32)]
    work = 2 * angles * rows * traces * samples * 256 * 4

    b, *sent = call(
        start_kernel,
        (field, *edges),
        (seismic, validity, avo_coeffs, wavelets),
        work,
        taps,
    )
    around = exchange(sent)
    (data,) = call(normal_kernel, (field,), (b, validity, avo_coeffs, wavelets), 2 * work, taps)
    one, *sent = call(
        first_image_kernel,
        (field, *edges),
        (b, data, prior_weight, lateral_strength, *around),
        20 * field.size,
        scalars=(3,),
    )
    around = exchange(sent)
    (data,) = call(normal_kernel, (field,), (one, validity, avo_coeffs, wavelets), 2 * work, taps)
    two, gram = call(
        second_image_kernel,
        (field, jax.ShapeDtypeStruct((col, 8, LANES), F32)),
        (one, data, prior_weight, lateral_strength, *around, b),
        30 * field.size,
        scalars=(3,),
    )
    gram = lax.all_to_all(gram, "col", 0, 0)
    (gram,) = call(spread_kernel, (jax.ShapeDtypeStruct((inline, 8, LANES), F32),), (gram,), 8)
    gram = lax.all_to_all(gram, "inline", 0, 0)
    return tuple(call(finish_kernel, (field, field), (gram, b, one, two), 8 * field.size))


def solution(mesh):
    placed = (
        P(None, "inline", "col", None),
        P(None, "inline", "col"),
        P("inline", "col"),
        P(),
        P(),
        P(),
    )
    return jax.shard_map(
        shards,
        mesh=mesh,
        in_specs=placed,
        out_specs=(P(None, "inline", "col", None), P(None, "inline", "col", None)),
        check_vma=False,
    )
```

```python
import functools

import jax
import jax.numpy as jnp
from jax import lax
from jax.experimental import pallas as pl
from jax.experimental.pallas import tpu as pltpu
from jax.sharding import PartitionSpec as P

LANES = 128
F32 = jnp.float32
BF16 = jnp.bfloat16


def split(value):
    high = value.astype(BF16)
    return high, (value - high.astype(F32)).astype(BF16)


def circulant(padded_ref, angle):
    line = jnp.broadcast_to(padded_ref[angle : angle + 1, :], (2 * LANES, 2 * LANES))
    return pltpu.roll(line, LANES, 1, stride=1, stride_axis=0)


def fill_taps(taps_ref, padded_ref):
    padded_ref[...] = jnp.zeros_like(padded_ref)
    padded_ref[0 : taps_ref.shape[0], 0 : taps_ref.shape[1]] = taps_ref[...]


def forward_band(circ):
    return jnp.concatenate(split(circ[:, :LANES]), axis=1)


def backward_band(circ):
    return jnp.concatenate(split(circ[LANES:, :]), axis=0)


def column(row):
    n = row.shape[1]
    same = lax.broadcasted_iota(jnp.int32, (n, n), 0) == lax.broadcasted_iota(jnp.int32, (n, n), 1)
    return jnp.sum(jnp.where(same, jnp.broadcast_to(row, (n, n)), 0.0), axis=1, keepdims=True)


def trace_columns(ref, *lead):
    rows = ref[lead].astype(F32)
    return jnp.concatenate([column(rows[r : r + 1, :]) for r in range(rows.shape[0])], axis=0)


def windows(tiles):
    pairs = [jnp.concatenate(pair, axis=1) for pair in zip(tiles[:-1], tiles[1:])]
    return jnp.concatenate(pairs, axis=0)


def halves_sum(wide):
    return wide[:, :LANES] + wide[:, LANES:]


def forward(tiles, band):
    zero = jnp.zeros_like(tiles[0]).astype(BF16)
    highs, lows = zip(*[split(t) for t in tiles])
    n, size = len(tiles) + 1, tiles[0].shape[0]
    rows = [windows([zero, *part, zero]) for part in (highs, lows)]
    out = jnp.dot(jnp.concatenate(rows, axis=0), band, preferred_element_type=F32)
    out = halves_sum(out)
    out = out[: n * size] + out[n * size :]
    return [out[k * size : (k + 1) * size] for k in range(n)]


def backward(parts, band):
    n, size = len(parts[0]) - 1, parts[0][0].shape[0]
    rows = jnp.concatenate([windows(part) for part in parts], axis=0)
    out = lax.dot_general(rows, band, (((1,), (1,)), ((), ())), preferred_element_type=F32)
    out = halves_sum(out)
    total = out[: n * size]
    for p in range(1, len(parts)):
        total = total + out[p * n * size : (p + 1) * n * size]
    return [total[k * size : (k + 1) * size] for k in range(n)]


def coeff(avo_ref, angle, contrast, k):
    return avo_ref[contrast, angle : angle + 1, pl.ds(k * LANES, LANES)]


def add_terms(total, avo_ref, angle, result):
    for c, line in enumerate(total):
        for k, tile in enumerate(result):
            term = coeff(avo_ref, angle, c, k) * tile
            line[k] = term if angle == 0 else line[k] + term


def store_tiles(out_ref, tiles):
    size = out_ref.shape[2]
    for c in range(out_ref.shape[0]):
        for k, tile in enumerate(tiles[c]):
            for r in range(out_ref.shape[1]):
                out_ref[c, r, :, pl.ds(k * LANES, LANES)] = tile[r * size : (r + 1) * size]


def right_side(seis_ref, masks, avo_ref, circs):
    angles, rows, _, samples = seis_ref.shape
    n = samples // LANES
    total = [[None] * n for _ in range(avo_ref.shape[0])]
    for a in range(angles):
        data = jnp.concatenate([seis_ref[a, r].astype(F32) for r in range(rows)], axis=0)
        data = data * masks[a]
        turned = [
            pltpu.roll(data[:, k * LANES : (k + 1) * LANES], LANES // 2, 1) for k in range(n)
        ]
        zero = jnp.zeros_like(turned[0])
        left_half = lax.broadcasted_iota(jnp.int32, zero.shape, 1) < LANES // 2
        shifted = [
            jnp.where(left_half, before, here).astype(BF16)
            for before, here in zip([zero, *turned], [*turned, zero])
        ]
        add_terms(total, avo_ref, a, backward([shifted], backward_band(circs[a])))
    return total


def normal(field, masks, avo_ref, circs):
    contrasts, n = len(field), len(field[0])
    total = [[None] * n for _ in range(contrasts)]
    for a, circ in enumerate(circs):
        mixed = []
        for k in range(n):
            parts = [coeff(avo_ref, a, c, k) * field[c][k] for c in range(contrasts)]
            mixed.append(functools.reduce(jnp.add, parts))
        synth = [tile * masks[a] for tile in forward(mixed, forward_band(circ))]
        left_half = lax.broadcasted_iota(jnp.int32, synth[0].shape, 1) < LANES // 2
        synth[0] = jnp.where(left_half, 0.0, synth[0])
        synth[n] = jnp.where(left_half, synth[n], 0.0)
        result = backward(list(zip(*[split(t) for t in synth])), backward_band(circ))
        add_terms(total, avo_ref, a, result)
    return total


def lateral(here, north, south, west, east):
    traces = here.shape[0]
    place = lax.broadcasted_iota(jnp.int32, here.shape, 0)
    from_west = jnp.where(place == 0, 0.0 if west is None else west, pltpu.roll(here, 1, 0))
    from_east = jnp.where(
        place == traces - 1, 0.0 if east is None else east, pltpu.roll(here, traces - 1, 0)
    )
    around = from_west + from_east
    for other in (north, south):
        around = around if other is None else around + other
    return around


def copy_in(pairs, sems):
    copies = [pltpu.make_async_copy(a, b, sems.at[i]) for i, (a, b) in enumerate(pairs)]
    for copy in copies:
        copy.start()
    return copies


def start_kernel(
    seis_hbm, valid_hbm, avo_hbm, taps_hbm, prior_hbm, strength_ref,
    b_ref, p_ref, top_ref, bottom_ref,
    seis_ref, valid_ref, avo_ref, taps_ref, prior_ref, padded, sems,
):
    copies = copy_in(
        (
            (taps_hbm, taps_ref),
            (valid_hbm, valid_ref),
            (prior_hbm, prior_ref),
            (avo_hbm, avo_ref),
            (seis_hbm, seis_ref),
        ),
        sems,
    )
    for copy in copies[:3]:
        copy.wait()
    fill_taps(taps_ref, padded)
    contrasts, angles, samples = avo_ref.shape
    rows = seis_ref.shape[1]
    circs = [circulant(padded, a) for a in range(angles)]
    masks = [trace_columns(valid_ref, a) for a in range(angles)]
    for copy in copies[3:]:
        copy.wait()
    b = right_side(seis_ref, masks, avo_ref, circs)
    store_tiles(b_ref, b)
    store_tiles(p_ref, normal(b, masks, avo_ref, circs))
    weights = [column(prior_ref[r : r + 1, :]) + 4.0 for r in range(rows)]
    for c in range(contrasts):
        for r in range(rows):
            here = b_ref[c, r]
            north = b_ref[c, r - 1] if r else None
            south = b_ref[c, r + 1] if r < rows - 1 else None
            around = lateral(here, north, south, None, None)
            p_ref[c, r] = p_ref[c, r] + strength_ref[c] * (weights[r] * here - around)
        for out_ref, r in ((top_ref, 0), (bottom_ref, rows - 1)):
            out_ref[0, c] = b_ref[c, r]
            out_ref[1, c] = p_ref[c, r]


def inside(axis):
    place = lax.axis_index(axis)
    last = lax.axis_size(axis) - 1
    return (place > 0).astype(F32), (place < last).astype(F32)


def rows_kernel(b_ref, p_ref, above_ref, below_ref, strength_ref, v_ref, left_ref, right_ref):
    contrasts, rows, traces, _ = b_ref.shape
    has_above, has_below = inside("inline")
    for c in range(contrasts):
        strength = strength_ref[c]
        own = [p_ref[c, r] for r in range(rows)]
        own[0] = own[0] - strength * above_ref[0, c]
        own[-1] = own[-1] - strength * below_ref[0, c]
        over = has_above * (above_ref[1, c] - strength * b_ref[c, 0])
        under = has_below * (below_ref[1, c] - strength * b_ref[c, rows - 1])
        for r, line in enumerate([over, *own, under]):
            v_ref[c, r] = line
        lines = [above_ref[0, c], *[b_ref[c, r] for r in range(rows)], below_ref[0, c], *own]
        base = c * len(lines)
        for e, line in enumerate(lines):
            left_ref[base + e : base + e + 1, :] = line[0:1, :]
            right_ref[base + e : base + e + 1, :] = line[traces - 1 : traces, :]


def image_kernel(
    b_ref, v_ref, left_ref, right_ref, valid_ref, avo_ref, taps_ref, prior_ref, strength_ref,
    one_ref, two_ref, gram_ref, padded,
):
    contrasts, rows, traces, samples = b_ref.shape
    angles, n = avo_ref.shape[1], samples // LANES
    has_left, has_right = inside("col")
    place = lax.broadcasted_iota(jnp.int32, (traces, samples), 0)
    first, last = place == 0, place == traces - 1
    ext = rows + 2
    whole = []
    for c in range(contrasts):
        base = c * (ext + rows)
        lines = []
        for r in range(ext):
            edge = base + r
            missing = jnp.where(
                first,
                left_ref[edge : edge + 1, :],
                jnp.where(last, right_ref[edge : edge + 1, :], 0.0),
            )
            lines.append(v_ref[c, r] - strength_ref[c] * missing)
        whole.append(lines)
        for r in range(rows):
            one_ref[c, r] = lines[r + 1]
    fill_taps(taps_ref, padded)
    circs = [circulant(padded, a) for a in range(angles)]
    masks = [trace_columns(valid_ref, a) for a in range(angles)]
    field = [
        [
            jnp.concatenate([one_ref[c, r, :, pl.ds(k * LANES, LANES)] for r in range(rows)], axis=0)
            for k in range(n)
        ]
        for c in range(contrasts)
    ]
    store_tiles(two_ref, normal(field, masks, avo_ref, circs))
    weights = [column(prior_ref[r : r + 1, :]) + 4.0 for r in range(rows)]
    sums = [jnp.zeros((traces, LANES), F32) for _ in range(4)]
    for c in range(contrasts):
        strength = strength_ref[c]
        for r in range(rows):
            here = whole[c][r + 1]
            edge = c * (ext + rows) + ext + r
            b = b_ref[c, r]
            west = has_left * (left_ref[edge : edge + 1, :] - strength * b[0:1, :])
            east = has_right * (
                right_ref[edge : edge + 1, :] - strength * b[traces - 1 : traces, :]
            )
            around = lateral(here, whole[c][r], whole[c][r + 2], west, east)
            two = two_ref[c, r] + strength * (weights[r] * here - around)
            two_ref[c, r] = two
            for q, product in enumerate((b * b, b * here, here * here, here * two)):
                tiles = [product[:, k : k + LANES] for k in range(0, samples, LANES)]
                sums[q] = sums[q] + functools.reduce(jnp.add, tiles)
    lane = lax.broadcasted_iota(jnp.int32, (1, LANES), 1)
    packed = jnp.zeros((1, LANES), F32)
    for q, total in enumerate(sums):
        total = jnp.sum(jnp.sum(total, axis=0, keepdims=True), axis=1, keepdims=True)
        packed = jnp.where(lane == q, total, packed)
    gram_ref[...] = jnp.broadcast_to(packed[None], gram_ref.shape)


def finish_kernel(gram_ref, b_ref, one_ref, two_ref, solution_ref, residual_ref):
    sums = jnp.sum(gram_ref[...], axis=0)
    g00, g01, g11, g12 = (sums[:, q : q + 1] for q in range(4))
    first = g00 / g01
    ratio = first * g11 / g01
    second = (ratio - 1.0) * g01 / (first * g12 - ratio * g11)
    near = first + second * ratio
    far = first * second
    for c in range(b_ref.shape[0]):
        for r in range(b_ref.shape[1]):
            b, one, two = b_ref[c, r], one_ref[c, r], two_ref[c, r]
            solution_ref[c, r] = near * b - far * one
            residual_ref[c, r] = b - near * one + far * two


VMEM = pl.BlockSpec(memory_space=pltpu.VMEM)
SMEM = pl.BlockSpec(memory_space=pltpu.SMEM)
HBM = pl.BlockSpec(memory_space=pltpu.HBM)


def call(kernel, outs, ins, flops, scratch=(), places=None):
    moved = sum(x.size * x.dtype.itemsize for x in (*ins, *outs))
    return pl.pallas_call(
        kernel,
        out_shape=outs,
        in_specs=[VMEM] * len(ins) if places is None else places,
        out_specs=jax.tree.map(lambda _: VMEM, outs),
        scratch_shapes=list(scratch),
        compiler_params=pltpu.CompilerParams(vmem_limit_bytes=24 * 1024 * 1024),
        cost_estimate=pl.CostEstimate(flops=flops, bytes_accessed=moved, transcendentals=0),
        name=kernel.__name__,
    )(*ins)


def exchange(axis, first, last):
    size = lax.axis_size(axis)
    ahead = [(i, i + 1) for i in range(size - 1)]
    back = [(j, i) for i, j in ahead]
    return lax.ppermute(last, axis, ahead), lax.ppermute(first, axis, back)


def shards(seismic, validity, prior_weight, lateral_strength, avo_coeffs, wavelets):
    angles, rows, traces, samples = seismic.shape
    contrasts = avo_coeffs.shape[1]
    avo_coeffs = jnp.swapaxes(avo_coeffs, 0, 1)
    shape = lambda *dims: jax.ShapeDtypeStruct(dims, F32)
    field = shape(contrasts, rows, traces, samples)
    row = shape(2, contrasts, traces, samples)
    side = shape(contrasts * (2 * rows + 2), samples)
    padded = pltpu.VMEM((8, 2 * LANES), F32)
    work = 2 * angles * rows * traces * samples * 256 * 4
    placed = (seismic, validity, avo_coeffs, wavelets, prior_weight)

    b, part, top, bottom = call(
        start_kernel,
        (field, field, row, row),
        (*placed, lateral_strength),
        3 * work,
        [*[pltpu.VMEM(x.shape, x.dtype) for x in placed], padded, pltpu.SemaphoreType.DMA((5,))],
        [HBM] * 5 + [SMEM],
    )
    above, below = exchange("inline", top, bottom)
    ext, left, right = call(
        rows_kernel,
        (shape(contrasts, rows + 2, traces, samples), side, side),
        (b, part, above, below, lateral_strength),
        4 * field.size,
        places=[VMEM] * 4 + [SMEM],
    )
    left, right = exchange("col", left, right)
    axes = ("inline", "col")
    one, two, gram = call(
        image_kernel,
        (field, field, shape(lax.axis_size(axes), 1, LANES)),
        (b, ext, left, right, validity, avo_coeffs, wavelets, prior_weight, lateral_strength),
        2 * work,
        [padded],
        [VMEM] * 8 + [SMEM],
    )
    gram = lax.all_to_all(gram, axes, 0, 0)
    return tuple(call(finish_kernel, (field, field), (gram, b, one, two), 8 * field.size))


def solution(mesh):
    placed = (
        P(None, "inline", "col", None),
        P(None, "inline", "col"),
        P("inline", "col"),
        P(),
        P(),
        P(),
    )
    return jax.shard_map(
        shards,
        mesh=mesh,
        in_specs=placed,
        out_specs=(P(None, "inline", "col", None), P(None, "inline", "col", None)),
        check_vma=False,
    )
```

```python
import functools

import jax
import jax.numpy as jnp
from jax import lax
from jax.experimental import pallas as pl
from jax.experimental.pallas import tpu as pltpu
from jax.sharding import PartitionSpec as P

LANES = 128
F32 = jnp.float32
BF16 = jnp.bfloat16


def split(value):
    high = value.astype(BF16)
    return high, (value - high.astype(F32)).astype(BF16)


def circulant(padded_ref, angle):
    line = jnp.broadcast_to(padded_ref[angle : angle + 1, :], (2 * LANES, 2 * LANES))
    return pltpu.roll(line, LANES, 1, stride=1, stride_axis=0)


def fill_taps(taps_ref, padded_ref):
    padded_ref[...] = jnp.zeros_like(padded_ref)
    padded_ref[0 : taps_ref.shape[0], 0 : taps_ref.shape[1]] = taps_ref[...]


def forward_band(circ):
    return jnp.concatenate(split(circ[:, :LANES]), axis=1)


def backward_band(circ):
    return jnp.concatenate(split(circ[LANES:, :]), axis=0)


def column(row):
    n = row.shape[1]
    same = lax.broadcasted_iota(jnp.int32, (n, n), 0) == lax.broadcasted_iota(jnp.int32, (n, n), 1)
    return jnp.sum(jnp.where(same, jnp.broadcast_to(row, (n, n)), 0.0), axis=1, keepdims=True)


def trace_columns(ref, *lead):
    rows = ref[lead].astype(F32)
    return jnp.concatenate([column(rows[r : r + 1, :]) for r in range(rows.shape[0])], axis=0)


def windows(tiles):
    pairs = [jnp.concatenate(pair, axis=1) for pair in zip(tiles[:-1], tiles[1:])]
    return jnp.concatenate(pairs, axis=0)


def halves_sum(wide):
    return wide[:, :LANES] + wide[:, LANES:]


def forward(tiles, band):
    zero = jnp.zeros_like(tiles[0]).astype(BF16)
    highs, lows = zip(*[split(t) for t in tiles])
    n, size = len(tiles) + 1, tiles[0].shape[0]
    rows = [windows([zero, *part, zero]) for part in (highs, lows)]
    out = jnp.dot(jnp.concatenate(rows, axis=0), band, preferred_element_type=F32)
    out = halves_sum(out)
    out = out[: n * size] + out[n * size :]
    return [out[k * size : (k + 1) * size] for k in range(n)]


def backward(parts, band):
    n, size = len(parts[0]) - 1, parts[0][0].shape[0]
    rows = jnp.concatenate([windows(part) for part in parts], axis=0)
    out = lax.dot_general(rows, band, (((1,), (1,)), ((), ())), preferred_element_type=F32)
    out = halves_sum(out)
    total = out[: n * size]
    for p in range(1, len(parts)):
        total = total + out[p * n * size : (p + 1) * n * size]
    return [total[k * size : (k + 1) * size] for k in range(n)]


def coeff(avo_ref, angle, contrast, k):
    return avo_ref[contrast, angle : angle + 1, pl.ds(k * LANES, LANES)]


def add_terms(total, avo_ref, angle, result):
    for c, line in enumerate(total):
        for k, tile in enumerate(result):
            term = coeff(avo_ref, angle, c, k) * tile
            line[k] = term if angle == 0 else line[k] + term


def store_tiles(out_ref, tiles):
    size = out_ref.shape[2]
    for c in range(out_ref.shape[0]):
        for k, tile in enumerate(tiles[c]):
            for r in range(out_ref.shape[1]):
                out_ref[c, r, :, pl.ds(k * LANES, LANES)] = tile[r * size : (r + 1) * size]


def right_side(seis_ref, masks, avo_ref, circs):
    angles, rows, _, samples = seis_ref.shape
    n = samples // LANES
    total = [[None] * n for _ in range(avo_ref.shape[0])]
    for a in range(angles):
        data = jnp.concatenate([seis_ref[a, r].astype(F32) for r in range(rows)], axis=0)
        data = data * masks[a]
        turned = [
            pltpu.roll(data[:, k * LANES : (k + 1) * LANES], LANES // 2, 1) for k in range(n)
        ]
        zero = jnp.zeros_like(turned[0])
        left_half = lax.broadcasted_iota(jnp.int32, zero.shape, 1) < LANES // 2
        shifted = [
            jnp.where(left_half, before, here).astype(BF16)
            for before, here in zip([zero, *turned], [*turned, zero])
        ]
        add_terms(total, avo_ref, a, backward([shifted], backward_band(circs[a])))
    return total


def normal(field, masks, avo_ref, circs):
    contrasts, n = len(field), len(field[0])
    total = [[None] * n for _ in range(contrasts)]
    for a, circ in enumerate(circs):
        mixed = []
        for k in range(n):
            parts = [coeff(avo_ref, a, c, k) * field[c][k] for c in range(contrasts)]
            mixed.append(functools.reduce(jnp.add, parts))
        synth = [tile * masks[a] for tile in forward(mixed, forward_band(circ))]
        left_half = lax.broadcasted_iota(jnp.int32, synth[0].shape, 1) < LANES // 2
        synth[0] = jnp.where(left_half, 0.0, synth[0])
        synth[n] = jnp.where(left_half, synth[n], 0.0)
        result = backward(list(zip(*[split(t) for t in synth])), backward_band(circ))
        add_terms(total, avo_ref, a, result)
    return total


def lateral(here, north, south, west, east):
    traces = here.shape[0]
    place = lax.broadcasted_iota(jnp.int32, here.shape, 0)
    from_west = jnp.where(place == 0, 0.0 if west is None else west, pltpu.roll(here, 1, 0))
    from_east = jnp.where(
        place == traces - 1, 0.0 if east is None else east, pltpu.roll(here, traces - 1, 0)
    )
    around = from_west + from_east
    for other in (north, south):
        around = around if other is None else around + other
    return around


def copy_in(pairs, sems):
    copies = [pltpu.make_async_copy(a, b, sems.at[i]) for i, (a, b) in enumerate(pairs)]
    for copy in copies:
        copy.start()
    return copies


def start_kernel(
    seis_hbm, valid_hbm, avo_hbm, taps_hbm, prior_hbm, strength_hbm,
    b_ref, p_ref, top_b_ref, top_p_ref, bottom_ref, strength_ref,
    seis_ref, valid_ref, avo_ref, taps_ref, prior_ref, padded, sems,
):
    copies = copy_in(
        (
            (taps_hbm, taps_ref),
            (valid_hbm, valid_ref),
            (prior_hbm, prior_ref),
            (strength_hbm, strength_ref),
            (avo_hbm, avo_ref),
            (seis_hbm, seis_ref),
        ),
        sems,
    )
    for copy in copies[:4]:
        copy.wait()
    fill_taps(taps_ref, padded)
    contrasts, angles, samples = avo_ref.shape
    rows = seis_ref.shape[1]
    circs = [circulant(padded, a) for a in range(angles)]
    masks = [trace_columns(valid_ref, a) for a in range(angles)]
    for copy in copies[4:]:
        copy.wait()
    b = right_side(seis_ref, masks, avo_ref, circs)
    store_tiles(b_ref, b)
    store_tiles(p_ref, normal(b, masks, avo_ref, circs))
    weights = [column(prior_ref[r : r + 1, :]) + 4.0 for r in range(rows)]
    for c in range(contrasts):
        strength = strength_ref[:, c : c + 1]
        for r in range(rows):
            here = b_ref[c, r]
            north = b_ref[c, r - 1] if r else None
            south = b_ref[c, r + 1] if r < rows - 1 else None
            around = lateral(here, north, south, None, None)
            p_ref[c, r] = p_ref[c, r] + strength * (weights[r] * here - around)
        top_b_ref[c] = b_ref[c, 0]
        top_p_ref[c] = p_ref[c, 0]
        bottom_ref[0, c] = b_ref[c, rows - 1]
        bottom_ref[1, c] = p_ref[c, rows - 1]


def inside(axis):
    place = lax.axis_index(axis)
    last = lax.axis_size(axis) - 1
    return (place > 0).astype(F32), (place < last).astype(F32)


def starts_pair():
    return lax.axis_index("col") % 2 == 0


def rows_kernel(b_ref, p_ref, above_ref, below_ref, strength_ref, v_ref, pair_ref, other_ref):
    contrasts, rows, traces, _ = b_ref.shape
    has_above, _ = inside("inline")
    first_of_pair = starts_pair()
    for c in range(contrasts):
        strength = strength_ref[:, c : c + 1]
        own = [p_ref[c, r] for r in range(rows)]
        own[0] = own[0] - strength * above_ref[0, c]
        own[-1] = own[-1] - strength * below_ref[c]
        over = has_above * (above_ref[1, c] - strength * b_ref[c, 0])
        for r, line in enumerate([over, *own]):
            v_ref[c, r] = line
        lines = [above_ref[0, c], *[b_ref[c, r] for r in range(rows)], below_ref[c], *own]
        base = c * len(lines)
        for e, line in enumerate(lines):
            left, right = line[0:1, :], line[traces - 1 : traces, :]
            pair_ref[base + e : base + e + 1, :] = jnp.where(first_of_pair, right, left)
            other_ref[base + e : base + e + 1, :] = jnp.where(first_of_pair, left, right)


def image_kernel(
    b_ref, v_ref, under_ref, other_ref, pair_ref,
    valid_ref, avo_ref, taps_ref, prior_ref, strength_ref,
    one_ref, two_ref, gram_ref, padded,
):
    contrasts, rows, traces, samples = b_ref.shape
    angles, n = avo_ref.shape[1], samples // LANES
    has_left, has_right = inside("col")
    _, has_below = inside("inline")
    first_of_pair = starts_pair()
    left = jnp.where(first_of_pair, other_ref[...], pair_ref[...])
    right = jnp.where(first_of_pair, pair_ref[...], other_ref[...])
    place = lax.broadcasted_iota(jnp.int32, (traces, samples), 0)
    first, last = place == 0, place == traces - 1
    ext = rows + 2
    whole = []
    for c in range(contrasts):
        base = c * (ext + rows)
        lines = []
        for r in range(ext):
            edge = base + r
            missing = jnp.where(
                first,
                left[edge : edge + 1, :],
                jnp.where(last, right[edge : edge + 1, :], 0.0),
            )
            if r < ext - 1:
                line = v_ref[c, r]
            else:
                line = has_below * (under_ref[c] - strength_ref[:, c : c + 1] * b_ref[c, rows - 1])
            lines.append(line - strength_ref[:, c : c + 1] * missing)
        whole.append(lines)
        for r in range(rows):
            one_ref[c, r] = lines[r + 1]
    fill_taps(taps_ref, padded)
    circs = [circulant(padded, a) for a in range(angles)]
    masks = [trace_columns(valid_ref, a) for a in range(angles)]
    field = [
        [
            jnp.concatenate([one_ref[c, r, :, pl.ds(k * LANES, LANES)] for r in range(rows)], axis=0)
            for k in range(n)
        ]
        for c in range(contrasts)
    ]
    store_tiles(two_ref, normal(field, masks, avo_ref, circs))
    weights = [column(prior_ref[r : r + 1, :]) + 4.0 for r in range(rows)]
    sums = [jnp.zeros((traces, LANES), F32) for _ in range(4)]
    for c in range(contrasts):
        strength = strength_ref[:, c : c + 1]
        for r in range(rows):
            here = whole[c][r + 1]
            edge = c * (ext + rows) + ext + r
            b = b_ref[c, r]
            west = has_left * (left[edge : edge + 1, :] - strength * b[0:1, :])
            east = has_right * (
                right[edge : edge + 1, :] - strength * b[traces - 1 : traces, :]
            )
            around = lateral(here, whole[c][r], whole[c][r + 2], west, east)
            two = two_ref[c, r] + strength * (weights[r] * here - around)
            two_ref[c, r] = two
            for q, product in enumerate((b * b, b * here, here * here, here * two)):
                tiles = [product[:, k : k + LANES] for k in range(0, samples, LANES)]
                sums[q] = sums[q] + functools.reduce(jnp.add, tiles)
    lane = lax.broadcasted_iota(jnp.int32, (1, LANES), 1)
    packed = jnp.zeros((1, LANES), F32)
    for q, total in enumerate(sums):
        total = jnp.sum(jnp.sum(total, axis=0, keepdims=True), axis=1, keepdims=True)
        packed = jnp.where(lane == q, total, packed)
    gram_ref[...] = jnp.broadcast_to(packed[None], gram_ref.shape)


def finish_kernel(gram_ref, b_ref, one_ref, two_ref, solution_ref, residual_ref):
    sums = jnp.sum(gram_ref[...], axis=0)
    g00, g01, g11, g12 = (sums[:, q : q + 1] for q in range(4))
    first = g00 / g01
    ratio = first * g11 / g01
    second = (ratio - 1.0) * g01 / (first * g12 - ratio * g11)
    near = first + second * ratio
    far = first * second
    for c in range(b_ref.shape[0]):
        for r in range(b_ref.shape[1]):
            b, one, two = b_ref[c, r], one_ref[c, r], two_ref[c, r]
            solution_ref[c, r] = near * b - far * one
            residual_ref[c, r] = b - near * one + far * two


VMEM = pl.BlockSpec(memory_space=pltpu.VMEM)
HBM = pl.BlockSpec(memory_space=pltpu.HBM)


def call(kernel, outs, ins, flops, scratch=(), places=None):
    moved = sum(x.size * x.dtype.itemsize for x in (*ins, *outs))
    return pl.pallas_call(
        kernel,
        out_shape=outs,
        in_specs=[VMEM] * len(ins) if places is None else places,
        out_specs=jax.tree.map(lambda _: VMEM, outs),
        scratch_shapes=list(scratch),
        compiler_params=pltpu.CompilerParams(vmem_limit_bytes=24 * 1024 * 1024),
        cost_estimate=pl.CostEstimate(flops=flops, bytes_accessed=moved, transcendentals=0),
        name=kernel.__name__,
    )(*ins)


def shift(axis, value, step):
    size = lax.axis_size(axis)
    return lax.ppermute(value, axis, [(i, i + step) for i in range(size) if 0 <= i + step < size])


def swap(axis, value, first):
    starts = range(first, lax.axis_size(axis) - 1, 2)
    return lax.ppermute(value, axis, [(i + d, i + 1 - d) for i in starts for d in (0, 1)])


def shards(seismic, validity, prior_weight, lateral_strength, avo_coeffs, wavelets):
    angles, rows, traces, samples = seismic.shape
    contrasts = avo_coeffs.shape[1]
    avo_coeffs = jnp.swapaxes(avo_coeffs, 0, 1)
    shape = lambda *dims: jax.ShapeDtypeStruct(dims, F32)
    field = shape(contrasts, rows, traces, samples)
    row = shape(contrasts, traces, samples)
    side = shape(contrasts * (2 * rows + 2), samples)
    padded = pltpu.VMEM((8, 2 * LANES), F32)
    work = 2 * angles * rows * traces * samples * 256 * 4

    placed = (
        seismic, validity, avo_coeffs, wavelets, prior_weight, lateral_strength.reshape(1, -1)
    )
    b, part, top_b, top_p, bottom, strength = call(
        start_kernel,
        (field, field, row, row, shape(2, *row.shape), shape(1, contrasts)),
        [pltpu.with_memory_space_constraint(x, pltpu.HBM) for x in placed],
        3 * work,
        [*[pltpu.VMEM(x.shape, x.dtype) for x in placed[:-1]], padded, pltpu.SemaphoreType.DMA((6,))],
        [HBM] * 6,
    )
    above = shift("inline", bottom, 1)
    below = shift("inline", top_b, -1)
    under = shift("inline", top_p, -1)
    ext, pair, other = call(
        rows_kernel,
        (shape(contrasts, rows + 1, traces, samples), side, side),
        (b, part, above, below, strength),
        4 * field.size,
    )
    other = swap("col", other, 1)
    pair = swap("col", pair, 0)
    axes = ("inline", "col")
    one, two, gram = call(
        image_kernel,
        (field, field, shape(lax.axis_size(axes), 1, LANES)),
        (
            b, ext, under, other, pair,
            validity, avo_coeffs, wavelets, prior_weight, strength,
        ),
        2 * work,
        [padded],
    )
    gram = lax.all_to_all(gram, axes, 0, 0)
    return tuple(call(finish_kernel, (field, field), (gram, b, one, two), 8 * field.size))


def solution(mesh):
    placed = (
        P(None, "inline", "col", None),
        P(None, "inline", "col"),
        P("inline", "col"),
        P(),
        P(),
        P(),
    )
    return jax.shard_map(
        shards,
        mesh=mesh,
        in_specs=placed,
        out_specs=(P(None, "inline", "col", None), P(None, "inline", "col", None)),
        check_vma=False,
    )
```

```python
import functools

import jax
import jax.numpy as jnp
from jax import lax
from jax.experimental import pallas as pl
from jax.experimental.pallas import tpu as pltpu
from jax.sharding import PartitionSpec as P

LANES = 128
F32 = jnp.float32
BF16 = jnp.bfloat16


def split(value):
    high = value.astype(BF16)
    return high, (value - high.astype(F32)).astype(BF16)


def circulant(padded_ref, angle):
    line = jnp.broadcast_to(padded_ref[angle : angle + 1, :], (2 * LANES, 2 * LANES))
    return pltpu.roll(line, LANES, 1, stride=1, stride_axis=0)


def fill_taps(taps_ref, padded_ref):
    padded_ref[...] = jnp.zeros_like(padded_ref)
    padded_ref[0 : taps_ref.shape[0], 0 : taps_ref.shape[1]] = taps_ref[...]


def forward_band(circ):
    return jnp.concatenate(split(circ[:, :LANES]), axis=1)


def backward_band(circ):
    return jnp.concatenate(split(circ[LANES:, :]), axis=0)


def column(row):
    n = row.shape[1]
    same = lax.broadcasted_iota(jnp.int32, (n, n), 0) == lax.broadcasted_iota(jnp.int32, (n, n), 1)
    return jnp.sum(jnp.where(same, jnp.broadcast_to(row, (n, n)), 0.0), axis=1, keepdims=True)


def trace_columns(ref, *lead):
    rows = ref[lead].astype(F32)
    return jnp.concatenate([column(rows[r : r + 1, :]) for r in range(rows.shape[0])], axis=0)


def windows(tiles):
    pairs = [jnp.concatenate(pair, axis=1) for pair in zip(tiles[:-1], tiles[1:])]
    return jnp.concatenate(pairs, axis=0)


def halves_sum(wide):
    return wide[:, :LANES] + wide[:, LANES:]


def forward(tiles, band):
    zero = jnp.zeros_like(tiles[0]).astype(BF16)
    highs, lows = zip(*[split(t) for t in tiles])
    n, size = len(tiles) + 1, tiles[0].shape[0]
    rows = [windows([zero, *part, zero]) for part in (highs, lows)]
    out = jnp.dot(jnp.concatenate(rows, axis=0), band, preferred_element_type=F32)
    out = halves_sum(out)
    out = out[: n * size] + out[n * size :]
    return [out[k * size : (k + 1) * size] for k in range(n)]


def backward(parts, band):
    n, size = len(parts[0]) - 1, parts[0][0].shape[0]
    rows = jnp.concatenate([windows(part) for part in parts], axis=0)
    out = lax.dot_general(rows, band, (((1,), (1,)), ((), ())), preferred_element_type=F32)
    out = halves_sum(out)
    total = out[: n * size]
    for p in range(1, len(parts)):
        total = total + out[p * n * size : (p + 1) * n * size]
    return [total[k * size : (k + 1) * size] for k in range(n)]


def coeff(avo_ref, angle, contrast, k):
    return avo_ref[contrast, angle : angle + 1, pl.ds(k * LANES, LANES)]


def add_terms(total, avo_ref, angle, result):
    for c, line in enumerate(total):
        for k, tile in enumerate(result):
            term = coeff(avo_ref, angle, c, k) * tile
            line[k] = term if angle == 0 else line[k] + term


def store_tiles(out_ref, tiles):
    size = out_ref.shape[2]
    for c in range(out_ref.shape[0]):
        for k, tile in enumerate(tiles[c]):
            for r in range(out_ref.shape[1]):
                out_ref[c, r, :, pl.ds(k * LANES, LANES)] = tile[r * size : (r + 1) * size]


def right_side(seis_ref, masks, avo_ref, circs):
    angles, rows, _, samples = seis_ref.shape
    n = samples // LANES
    total = [[None] * n for _ in range(avo_ref.shape[0])]
    for a in range(angles):
        data = jnp.concatenate([seis_ref[a, r].astype(F32) for r in range(rows)], axis=0)
        data = data * masks[a]
        turned = [
            pltpu.roll(data[:, k * LANES : (k + 1) * LANES], LANES // 2, 1) for k in range(n)
        ]
        zero = jnp.zeros_like(turned[0])
        left_half = lax.broadcasted_iota(jnp.int32, zero.shape, 1) < LANES // 2
        shifted = [
            jnp.where(left_half, before, here).astype(BF16)
            for before, here in zip([zero, *turned], [*turned, zero])
        ]
        add_terms(total, avo_ref, a, backward([shifted], backward_band(circs[a])))
    return total


def normal(field, masks, avo_ref, circs):
    contrasts, n = len(field), len(field[0])
    total = [[None] * n for _ in range(contrasts)]
    for a, circ in enumerate(circs):
        mixed = []
        for k in range(n):
            parts = [coeff(avo_ref, a, c, k) * field[c][k] for c in range(contrasts)]
            mixed.append(functools.reduce(jnp.add, parts))
        synth = [tile * masks[a] for tile in forward(mixed, forward_band(circ))]
        left_half = lax.broadcasted_iota(jnp.int32, synth[0].shape, 1) < LANES // 2
        synth[0] = jnp.where(left_half, 0.0, synth[0])
        synth[n] = jnp.where(left_half, synth[n], 0.0)
        result = backward(list(zip(*[split(t) for t in synth])), backward_band(circ))
        add_terms(total, avo_ref, a, result)
    return total


def lateral(here, north, south, west, east):
    traces = here.shape[0]
    place = lax.broadcasted_iota(jnp.int32, here.shape, 0)
    from_west = jnp.where(place == 0, 0.0 if west is None else west, pltpu.roll(here, 1, 0))
    from_east = jnp.where(
        place == traces - 1, 0.0 if east is None else east, pltpu.roll(here, traces - 1, 0)
    )
    around = from_west + from_east
    for other in (north, south):
        around = around if other is None else around + other
    return around


def copy_in(pairs, sems):
    copies = [pltpu.make_async_copy(a, b, sems.at[i]) for i, (a, b) in enumerate(pairs)]
    for copy in copies:
        copy.start()
    return copies


def start_kernel(
    seis_hbm, valid_hbm, avo_hbm, taps_hbm, prior_hbm, strength_hbm,
    b_ref, p_ref, top_b_ref, top_p_ref, bottom_ref, strength_ref,
    seis_ref, valid_ref, avo_ref, taps_ref, prior_ref, padded, sems,
):
    copies = copy_in(
        (
            (taps_hbm, taps_ref),
            (valid_hbm, valid_ref),
            (prior_hbm, prior_ref),
            (strength_hbm, strength_ref),
            (avo_hbm, avo_ref),
            (seis_hbm, seis_ref),
        ),
        sems,
    )
    for copy in copies[:4]:
        copy.wait()
    fill_taps(taps_ref, padded)
    contrasts, angles, samples = avo_ref.shape
    rows = seis_ref.shape[1]
    circs = [circulant(padded, a) for a in range(angles)]
    masks = [trace_columns(valid_ref, a) for a in range(angles)]
    for copy in copies[4:]:
        copy.wait()
    b = right_side(seis_ref, masks, avo_ref, circs)
    store_tiles(b_ref, b)
    store_tiles(p_ref, normal(b, masks, avo_ref, circs))
    weights = [column(prior_ref[r : r + 1, :]) + 4.0 for r in range(rows)]
    for c in range(contrasts):
        strength = strength_ref[:, c : c + 1]
        for r in range(rows):
            here = b_ref[c, r]
            north = b_ref[c, r - 1] if r else None
            south = b_ref[c, r + 1] if r < rows - 1 else None
            around = lateral(here, north, south, None, None)
            p_ref[c, r] = p_ref[c, r] + strength * (weights[r] * here - around)
        top_b_ref[c] = b_ref[c, 0]
        top_p_ref[c] = p_ref[c, 0]
        bottom_ref[0, c] = b_ref[c, rows - 1]
        bottom_ref[1, c] = p_ref[c, rows - 1]


def inside(axis):
    place = lax.axis_index(axis)
    last = lax.axis_size(axis) - 1
    return (place > 0).astype(F32), (place < last).astype(F32)


def starts_pair():
    return lax.axis_index("col") % 2 == 0


def rows_kernel(b_ref, p_ref, above_ref, below_ref, strength_ref, v_ref, pair_ref, other_ref):
    contrasts, rows, traces, _ = b_ref.shape
    has_above, _ = inside("inline")
    first_of_pair = starts_pair()
    for c in range(contrasts):
        strength = strength_ref[:, c : c + 1]
        own = [p_ref[c, r] for r in range(rows)]
        own[0] = own[0] - strength * above_ref[0, c]
        own[-1] = own[-1] - strength * below_ref[c]
        over = has_above * (above_ref[1, c] - strength * b_ref[c, 0])
        for r, line in enumerate([over, *own]):
            v_ref[c, r] = line
        lines = [above_ref[0, c], *[b_ref[c, r] for r in range(rows)], below_ref[c], *own]
        base = c * len(lines)
        for e, line in enumerate(lines):
            left, right = line[0:1, :], line[traces - 1 : traces, :]
            pair_ref[base + e : base + e + 1, :] = jnp.where(first_of_pair, right, left)
            other_ref[base + e : base + e + 1, :] = jnp.where(first_of_pair, left, right)


def image_kernel(
    b_ref, v_ref, under_ref, other_ref, pair_ref,
    valid_ref, avo_ref, taps_ref, prior_ref, strength_ref,
    one_ref, two_ref, gram_ref, padded,
):
    contrasts, rows, traces, samples = b_ref.shape
    angles, n = avo_ref.shape[1], samples // LANES
    has_left, has_right = inside("col")
    _, has_below = inside("inline")
    first_of_pair = starts_pair()
    left = jnp.where(first_of_pair, other_ref[...], pair_ref[...])
    right = jnp.where(first_of_pair, pair_ref[...], other_ref[...])
    place = lax.broadcasted_iota(jnp.int32, (traces, samples), 0)
    first, last = place == 0, place == traces - 1
    ext = rows + 2
    whole = []
    for c in range(contrasts):
        base = c * (ext + rows)
        lines = []
        for r in range(ext):
            edge = base + r
            missing = jnp.where(
                first,
                left[edge : edge + 1, :],
                jnp.where(last, right[edge : edge + 1, :], 0.0),
            )
            if r < ext - 1:
                line = v_ref[c, r]
            else:
                line = has_below * (under_ref[c] - strength_ref[:, c : c + 1] * b_ref[c, rows - 1])
            lines.append(line - strength_ref[:, c : c + 1] * missing)
        whole.append(lines)
        for r in range(rows):
            one_ref[c, r] = lines[r + 1]
    fill_taps(taps_ref, padded)
    circs = [circulant(padded, a) for a in range(angles)]
    masks = [trace_columns(valid_ref, a) for a in range(angles)]
    field = [
        [
            jnp.concatenate([one_ref[c, r, :, pl.ds(k * LANES, LANES)] for r in range(rows)], axis=0)
            for k in range(n)
        ]
        for c in range(contrasts)
    ]
    store_tiles(two_ref, normal(field, masks, avo_ref, circs))
    weights = [column(prior_ref[r : r + 1, :]) + 4.0 for r in range(rows)]
    sums = [jnp.zeros((traces, LANES), F32) for _ in range(4)]
    for c in range(contrasts):
        strength = strength_ref[:, c : c + 1]
        for r in range(rows):
            here = whole[c][r + 1]
            edge = c * (ext + rows) + ext + r
            b = b_ref[c, r]
            west = has_left * (left[edge : edge + 1, :] - strength * b[0:1, :])
            east = has_right * (
                right[edge : edge + 1, :] - strength * b[traces - 1 : traces, :]
            )
            around = lateral(here, whole[c][r], whole[c][r + 2], west, east)
            two = two_ref[c, r] + strength * (weights[r] * here - around)
            two_ref[c, r] = two
            for q, product in enumerate((b * b, b * here, here * here, here * two)):
                tiles = [product[:, k : k + LANES] for k in range(0, samples, LANES)]
                sums[q] = sums[q] + functools.reduce(jnp.add, tiles)
    lane = lax.broadcasted_iota(jnp.int32, (1, LANES), 1)
    packed = jnp.zeros((1, LANES), F32)
    for q, total in enumerate(sums):
        total = jnp.sum(jnp.sum(total, axis=0, keepdims=True), axis=1, keepdims=True)
        packed = jnp.where(lane == q, total, packed)
    gram_ref[...] = packed


def finish_kernel(gram_ref, b_ref, one_ref, two_ref, solution_ref, residual_ref):
    sums = jnp.sum(gram_ref[...], axis=0)
    g00, g01, g11, g12 = (sums[:, q : q + 1] for q in range(4))
    first = g00 / g01
    ratio = first * g11 / g01
    second = (ratio - 1.0) * g01 / (first * g12 - ratio * g11)
    near = first + second * ratio
    far = first * second
    for c in range(b_ref.shape[0]):
        for r in range(b_ref.shape[1]):
            b, one, two = b_ref[c, r], one_ref[c, r], two_ref[c, r]
            solution_ref[c, r] = near * b - far * one
            residual_ref[c, r] = b - near * one + far * two


VMEM = pl.BlockSpec(memory_space=pltpu.VMEM)
HBM = pl.BlockSpec(memory_space=pltpu.HBM)


def call(kernel, outs, ins, flops, scratch=(), places=None):
    moved = sum(x.size * x.dtype.itemsize for x in (*ins, *outs))
    return pl.pallas_call(
        kernel,
        out_shape=outs,
        in_specs=[VMEM] * len(ins) if places is None else places,
        out_specs=jax.tree.map(lambda _: VMEM, outs),
        scratch_shapes=list(scratch),
        compiler_params=pltpu.CompilerParams(vmem_limit_bytes=24 * 1024 * 1024),
        cost_estimate=pl.CostEstimate(flops=flops, bytes_accessed=moved, transcendentals=0),
        name=kernel.__name__,
    )(*ins)


def shift(axis, value, step):
    size = lax.axis_size(axis)
    return lax.ppermute(value, axis, [(i, i + step) for i in range(size) if 0 <= i + step < size])


def swap(axis, value, first):
    starts = range(first, lax.axis_size(axis) - 1, 2)
    return lax.ppermute(value, axis, [(i + d, i + 1 - d) for i in starts for d in (0, 1)])


def shards(seismic, validity, prior_weight, lateral_strength, avo_coeffs, wavelets):
    angles, rows, traces, samples = seismic.shape
    contrasts = avo_coeffs.shape[1]
    avo_coeffs = jnp.swapaxes(avo_coeffs, 0, 1)
    shape = lambda *dims: jax.ShapeDtypeStruct(dims, F32)
    field = shape(contrasts, rows, traces, samples)
    row = shape(contrasts, traces, samples)
    side = shape(contrasts * (2 * rows + 2), samples)
    padded = pltpu.VMEM((8, 2 * LANES), F32)
    work = 2 * angles * rows * traces * samples * 256 * 4

    placed = (
        seismic, validity, avo_coeffs, wavelets, prior_weight, lateral_strength.reshape(1, -1)
    )
    b, part, top_b, top_p, bottom, strength = call(
        start_kernel,
        (field, field, row, row, shape(2, *row.shape), shape(1, contrasts)),
        [pltpu.with_memory_space_constraint(x, pltpu.HBM) for x in placed],
        3 * work,
        [*[pltpu.VMEM(x.shape, x.dtype) for x in placed[:-1]], padded, pltpu.SemaphoreType.DMA((6,))],
        [HBM] * 6,
    )
    above = shift("inline", bottom, 1)
    below = shift("inline", top_b, -1)
    under = shift("inline", top_p, -1)
    ext, pair, other = call(
        rows_kernel,
        (shape(contrasts, rows + 1, traces, samples), side, side),
        (b, part, above, below, strength),
        4 * field.size,
    )
    other = swap("col", other, 1)
    pair = swap("col", pair, 0)
    axes = ("inline", "col")
    one, two, gram = call(
        image_kernel,
        (field, field, shape(1, LANES)),
        (
            b, ext, under, other, pair,
            validity, avo_coeffs, wavelets, prior_weight, strength,
        ),
        2 * work,
        [padded],
    )
    gram = lax.all_gather(gram, axes)
    return tuple(call(finish_kernel, (field, field), (gram, b, one, two), 8 * field.size))


def solution(mesh):
    placed = (
        P(None, "inline", "col", None),
        P(None, "inline", "col"),
        P("inline", "col"),
        P(),
        P(),
        P(),
    )
    return jax.shard_map(
        shards,
        mesh=mesh,
        in_specs=placed,
        out_specs=(P(None, "inline", "col", None), P(None, "inline", "col", None)),
        check_vma=False,
    )
```

```python
import functools

import jax
import jax.numpy as jnp
from jax import lax
from jax.experimental import pallas as pl
from jax.experimental.pallas import tpu as pltpu
from jax.sharding import PartitionSpec as P

LANES = 128
F32 = jnp.float32
BF16 = jnp.bfloat16


def split(value):
    high = value.astype(BF16)
    return high, (value - high.astype(F32)).astype(BF16)


def circulant(padded_ref, angle):
    line = jnp.broadcast_to(padded_ref[angle : angle + 1, :], (2 * LANES, 2 * LANES))
    return pltpu.roll(line, LANES, 1, stride=1, stride_axis=0)


def fill_taps(taps_ref, padded_ref):
    padded_ref[...] = jnp.zeros_like(padded_ref)
    padded_ref[0 : taps_ref.shape[0], 0 : taps_ref.shape[1]] = taps_ref[...]


def forward_band(circ):
    return jnp.concatenate(split(circ[:, :LANES]), axis=1)


def backward_band(circ):
    return jnp.concatenate(split(circ[LANES:, :]), axis=0)


def column(row):
    n = row.shape[1]
    same = lax.broadcasted_iota(jnp.int32, (n, n), 0) == lax.broadcasted_iota(jnp.int32, (n, n), 1)
    return jnp.sum(jnp.where(same, jnp.broadcast_to(row, (n, n)), 0.0), axis=1, keepdims=True)


def trace_columns(ref, *lead):
    rows = ref[lead].astype(F32)
    return jnp.concatenate([column(rows[r : r + 1, :]) for r in range(rows.shape[0])], axis=0)


def windows(tiles):
    pairs = [jnp.concatenate(pair, axis=1) for pair in zip(tiles[:-1], tiles[1:])]
    return jnp.concatenate(pairs, axis=0)


def halves_sum(wide):
    return wide[:, :LANES] + wide[:, LANES:]


def forward(tiles, band):
    zero = jnp.zeros_like(tiles[0]).astype(BF16)
    highs, lows = zip(*[split(t) for t in tiles])
    n, size = len(tiles) + 1, tiles[0].shape[0]
    rows = [windows([zero, *part, zero]) for part in (highs, lows)]
    out = jnp.dot(jnp.concatenate(rows, axis=0), band, preferred_element_type=F32)
    out = halves_sum(out)
    out = out[: n * size] + out[n * size :]
    return [out[k * size : (k + 1) * size] for k in range(n)]


def backward(parts, band):
    n, size = len(parts[0]) - 1, parts[0][0].shape[0]
    rows = jnp.concatenate([windows(part) for part in parts], axis=0)
    out = lax.dot_general(rows, band, (((1,), (1,)), ((), ())), preferred_element_type=F32)
    out = halves_sum(out)
    total = out[: n * size]
    for p in range(1, len(parts)):
        total = total + out[p * n * size : (p + 1) * n * size]
    return [total[k * size : (k + 1) * size] for k in range(n)]


def coeff(avo_ref, angle, contrast, k):
    return avo_ref[contrast, angle : angle + 1, pl.ds(k * LANES, LANES)]


def add_terms(total, avo_ref, angle, result):
    for c, line in enumerate(total):
        for k, tile in enumerate(result):
            term = coeff(avo_ref, angle, c, k) * tile
            line[k] = term if angle == 0 else line[k] + term


def store_tiles(out_ref, tiles):
    size = out_ref.shape[2]
    for c in range(out_ref.shape[0]):
        for k, tile in enumerate(tiles[c]):
            for r in range(out_ref.shape[1]):
                out_ref[c, r, :, pl.ds(k * LANES, LANES)] = tile[r * size : (r + 1) * size]


def right_side(seis_ref, masks, avo_ref, circs):
    angles, rows, _, samples = seis_ref.shape
    n = samples // LANES
    total = [[None] * n for _ in range(avo_ref.shape[0])]
    for a in range(angles):
        data = jnp.concatenate([seis_ref[a, r].astype(F32) for r in range(rows)], axis=0)
        data = data * masks[a]
        turned = [
            pltpu.roll(data[:, k * LANES : (k + 1) * LANES], LANES // 2, 1) for k in range(n)
        ]
        zero = jnp.zeros_like(turned[0])
        left_half = lax.broadcasted_iota(jnp.int32, zero.shape, 1) < LANES // 2
        shifted = [
            jnp.where(left_half, before, here).astype(BF16)
            for before, here in zip([zero, *turned], [*turned, zero])
        ]
        add_terms(total, avo_ref, a, backward([shifted], backward_band(circs[a])))
    return total


def normal(field, masks, avo_ref, circs):
    contrasts, n = len(field), len(field[0])
    total = [[None] * n for _ in range(contrasts)]
    for a, circ in enumerate(circs):
        mixed = []
        for k in range(n):
            parts = [coeff(avo_ref, a, c, k) * field[c][k] for c in range(contrasts)]
            mixed.append(functools.reduce(jnp.add, parts))
        synth = [tile * masks[a] for tile in forward(mixed, forward_band(circ))]
        left_half = lax.broadcasted_iota(jnp.int32, synth[0].shape, 1) < LANES // 2
        synth[0] = jnp.where(left_half, 0.0, synth[0])
        synth[n] = jnp.where(left_half, synth[n], 0.0)
        result = backward(list(zip(*[split(t) for t in synth])), backward_band(circ))
        add_terms(total, avo_ref, a, result)
    return total


def lateral(here, north, south, west, east):
    traces = here.shape[0]
    place = lax.broadcasted_iota(jnp.int32, here.shape, 0)
    from_west = jnp.where(place == 0, 0.0 if west is None else west, pltpu.roll(here, 1, 0))
    from_east = jnp.where(
        place == traces - 1, 0.0 if east is None else east, pltpu.roll(here, traces - 1, 0)
    )
    around = from_west + from_east
    for other in (north, south):
        around = around if other is None else around + other
    return around


def copy_in(pairs, sems):
    copies = [pltpu.make_async_copy(a, b, sems.at[i]) for i, (a, b) in enumerate(pairs)]
    for copy in copies:
        copy.start()
    return copies


def start_kernel(
    seis_hbm, valid_hbm, avo_hbm, taps_hbm,
    b_ref, pair_ref, other_ref,
    seis_ref, valid_ref, avo_ref, taps_ref, padded, sems,
):
    copies = copy_in(
        (
            (taps_hbm, taps_ref),
            (valid_hbm, valid_ref),
            (avo_hbm, avo_ref),
            (seis_hbm, seis_ref),
        ),
        sems,
    )
    for copy in copies[:2]:
        copy.wait()
    fill_taps(taps_ref, padded)
    contrasts, angles, _ = avo_ref.shape
    rows = seis_ref.shape[1]
    circs = [circulant(padded, a) for a in range(angles)]
    masks = [trace_columns(valid_ref, a) for a in range(angles)]
    for copy in copies[2:]:
        copy.wait()
    store_tiles(b_ref, right_side(seis_ref, masks, avo_ref, circs))
    first = starts_pair("inline")
    for c in range(contrasts):
        top, bottom = b_ref[c, 0], b_ref[c, rows - 1]
        pair_ref[c] = jnp.where(first, bottom, top)
        other_ref[c] = jnp.where(first, top, bottom)


def part_kernel(
    b_ref, valid_ref, avo_ref, taps_ref, prior_ref, strength_ref, p_ref, top_ref, bottom_ref, padded
):
    contrasts, rows = b_ref.shape[:2]
    fill_taps(taps_ref, padded)
    angles = avo_ref.shape[1]
    circs = [circulant(padded, a) for a in range(angles)]
    masks = [trace_columns(valid_ref, a) for a in range(angles)]
    store_tiles(p_ref, normal(stack_tiles(b_ref), masks, avo_ref, circs))
    weights = [column(prior_ref[r : r + 1, :]) + 4.0 for r in range(rows)]
    for c in range(contrasts):
        strength = strength_ref[:, c : c + 1]
        for r in range(rows):
            here = b_ref[c, r]
            north = b_ref[c, r - 1] if r else None
            south = b_ref[c, r + 1] if r < rows - 1 else None
            around = lateral(here, north, south, None, None)
            p_ref[c, r] = p_ref[c, r] + strength * (weights[r] * here - around)
        top_ref[c] = p_ref[c, 0]
        bottom_ref[c] = p_ref[c, rows - 1]


def stack_tiles(ref):
    contrasts, rows, _, samples = ref.shape
    return [
        [
            jnp.concatenate([ref[c, r, :, pl.ds(k, LANES)] for r in range(rows)], axis=0)
            for k in range(0, samples, LANES)
        ]
        for c in range(contrasts)
    ]


def inside(axis):
    place = lax.axis_index(axis)
    last = lax.axis_size(axis) - 1
    return (place > 0).astype(F32), (place < last).astype(F32)


def starts_pair(axis):
    return lax.axis_index(axis) % 2 == 0


def rows_kernel(b_ref, p_ref, next_ref, mate_ref, strength_ref, v_ref, pair_ref, other_ref):
    contrasts, rows, traces, _ = b_ref.shape
    first_row, first_col = starts_pair("inline"), starts_pair("col")
    for c in range(contrasts):
        strength = strength_ref[:, c : c + 1]
        above = jnp.where(first_row, next_ref[c], mate_ref[c])
        below = jnp.where(first_row, mate_ref[c], next_ref[c])
        own = [p_ref[c, r] for r in range(rows)]
        own[0] = own[0] - strength * above
        own[-1] = own[-1] - strength * below
        for r, line in enumerate(own):
            v_ref[c, r] = line
        lines = [above, *[b_ref[c, r] for r in range(rows)], below, *own]
        base = c * len(lines)
        for e, line in enumerate(lines):
            left, right = line[0:1, :], line[traces - 1 : traces, :]
            pair_ref[base + e : base + e + 1, :] = jnp.where(first_col, right, left)
            other_ref[base + e : base + e + 1, :] = jnp.where(first_col, left, right)


def image_kernel(
    b_ref, v_ref, over_ref, other_ref, pair_ref,
    valid_ref, avo_ref, taps_ref, prior_ref, strength_ref,
    one_ref, two_ref, gram_ref, padded,
):
    contrasts, rows, traces, samples = b_ref.shape
    angles = avo_ref.shape[1]
    has_left, has_right = inside("col")
    has_above, has_below = inside("inline")
    first_col = starts_pair("col")
    left = jnp.where(first_col, other_ref[...], pair_ref[...])
    right = jnp.where(first_col, pair_ref[...], other_ref[...])
    place = lax.broadcasted_iota(jnp.int32, (traces, samples), 0)
    ext = rows + 2
    stride = ext + rows

    def beside(c, r):
        edge = c * stride + r
        west, east = left[edge : edge + 1, :], right[edge : edge + 1, :]
        return jnp.where(place == 0, west, jnp.where(place == traces - 1, east, 0.0))

    for c in range(contrasts):
        strength = strength_ref[:, c : c + 1]
        for r in range(rows):
            one_ref[c, r] = v_ref[c, r] - strength * beside(c, r + 1)
    fill_taps(taps_ref, padded)
    circs = [circulant(padded, a) for a in range(angles)]
    masks = [trace_columns(valid_ref, a) for a in range(angles)]
    store_tiles(two_ref, normal(stack_tiles(one_ref), masks, avo_ref, circs))
    weights = [column(prior_ref[r : r + 1, :]) + 4.0 for r in range(rows)]
    sums = [jnp.zeros((traces, LANES), F32) for _ in range(4)]
    for c in range(contrasts):
        strength = strength_ref[:, c : c + 1]
        over = over_ref[c] - strength * (has_above * b_ref[c, 0] + beside(c, 0))
        under = -strength * (has_below * b_ref[c, rows - 1] + beside(c, ext - 1))
        for r in range(rows):
            here, b = one_ref[c, r], b_ref[c, r]
            edge = c * stride + ext + r
            west = has_left * (left[edge : edge + 1, :] - strength * b[0:1, :])
            east = has_right * (
                right[edge : edge + 1, :] - strength * b[traces - 1 : traces, :]
            )
            north = one_ref[c, r - 1] if r else over
            south = one_ref[c, r + 1] if r < rows - 1 else None
            around = lateral(here, north, south, west, east)
            two = two_ref[c, r] + strength * (weights[r] * here - around)
            twice = two if r else two - strength * over
            two_ref[c, r] = two if r < rows - 1 else two - strength * under
            for q, product in enumerate((b * b, b * here, here * here, here * twice)):
                tiles = [product[:, k : k + LANES] for k in range(0, samples, LANES)]
                sums[q] = sums[q] + functools.reduce(jnp.add, tiles)
    lane = lax.broadcasted_iota(jnp.int32, (1, LANES), 1)
    packed = jnp.zeros((1, LANES), F32)
    for q, total in enumerate(sums):
        total = jnp.sum(jnp.sum(total, axis=0, keepdims=True), axis=1, keepdims=True)
        packed = jnp.where(lane == q, total, packed)
    gram_ref[...] = jnp.broadcast_to(packed[None], gram_ref.shape)


def finish_kernel(
    gram_ref, b_ref, one_ref, two_ref, under_ref, strength_ref, solution_ref, residual_ref
):
    sums = jnp.sum(gram_ref[...], axis=0)
    g00, g01, g11, g12 = (sums[:, q : q + 1] for q in range(4))
    first = g00 / g01
    ratio = first * g11 / g01
    second = (ratio - 1.0) * g01 / (first * g12 - ratio * g11)
    near = first + second * ratio
    far = first * second
    rows = b_ref.shape[1]
    for c in range(b_ref.shape[0]):
        for r in range(rows):
            b, one, two = b_ref[c, r], one_ref[c, r], two_ref[c, r]
            if r == rows - 1:
                two = two - strength_ref[:, c : c + 1] * under_ref[c]
            solution_ref[c, r] = near * b - far * one
            residual_ref[c, r] = b - near * one + far * two


VMEM = pl.BlockSpec(memory_space=pltpu.VMEM)
HBM = pl.BlockSpec(memory_space=pltpu.HBM)


def call(kernel, outs, ins, flops, scratch=(), places=None):
    moved = sum(x.size * x.dtype.itemsize for x in (*ins, *outs))
    return pl.pallas_call(
        kernel,
        out_shape=outs,
        in_specs=[VMEM] * len(ins) if places is None else places,
        out_specs=jax.tree.map(lambda _: VMEM, outs),
        scratch_shapes=list(scratch),
        compiler_params=pltpu.CompilerParams(vmem_limit_bytes=24 * 1024 * 1024),
        cost_estimate=pl.CostEstimate(flops=flops, bytes_accessed=moved, transcendentals=0),
        name=kernel.__name__,
    )(*ins)


def shift(axis, value, step):
    size = lax.axis_size(axis)
    return lax.ppermute(value, axis, [(i, i + step) for i in range(size) if 0 <= i + step < size])


def swap(axis, value, first):
    starts = range(first, lax.axis_size(axis) - 1, 2)
    return lax.ppermute(value, axis, [(i + d, i + 1 - d) for i in starts for d in (0, 1)])


def shards(seismic, validity, prior_weight, lateral_strength, avo_coeffs, wavelets):
    angles, rows, traces, samples = seismic.shape
    contrasts = avo_coeffs.shape[1]
    avo_coeffs = jnp.swapaxes(avo_coeffs, 0, 1)
    strength = lateral_strength.reshape(1, -1)
    shape = lambda *dims: jax.ShapeDtypeStruct(dims, F32)
    field = shape(contrasts, rows, traces, samples)
    row = shape(contrasts, traces, samples)
    side = shape(contrasts * (2 * rows + 2), samples)
    padded = pltpu.VMEM((8, 2 * LANES), F32)
    work = 2 * angles * rows * traces * samples * 256 * 4

    placed = (seismic, validity, avo_coeffs, wavelets)
    b, pair, other = call(
        start_kernel,
        (field, row, row),
        [pltpu.with_memory_space_constraint(x, pltpu.HBM) for x in placed],
        work,
        [*[pltpu.VMEM(x.shape, x.dtype) for x in placed], padded, pltpu.SemaphoreType.DMA((4,))],
        [HBM] * 4,
    )
    other = swap("inline", other, 1)
    pair = swap("inline", pair, 0)
    part, top, bottom = call(
        part_kernel,
        (field, row, row),
        (b, validity, avo_coeffs, wavelets, prior_weight, strength),
        2 * work,
        [padded],
    )
    over = shift("inline", bottom, 1)
    image, pair, other = call(
        rows_kernel,
        (field, side, side),
        (b, part, other, pair, strength),
        4 * field.size,
    )
    other = swap("col", other, 1)
    pair = swap("col", pair, 0)
    top, image = lax.optimization_barrier((top, image))
    under = shift("inline", top, -1)
    axes = ("inline", "col")
    one, two, gram = call(
        image_kernel,
        (field, field, shape(lax.axis_size(axes), 1, LANES)),
        (
            b, image, over, other, pair,
            validity, avo_coeffs, wavelets, prior_weight, strength,
        ),
        2 * work,
        [padded],
    )
    gram = lax.all_to_all(gram, axes, 0, 0)
    last = (gram, b, one, two, under, strength)
    return tuple(call(finish_kernel, (field, field), last, 8 * field.size))


def solution(mesh):
    placed = (
        P(None, "inline", "col", None),
        P(None, "inline", "col"),
        P("inline", "col"),
        P(),
        P(),
        P(),
    )
    return jax.shard_map(
        shards,
        mesh=mesh,
        in_specs=placed,
        out_specs=(P(None, "inline", "col", None), P(None, "inline", "col", None)),
        check_vma=False,
    )
```

```python
import functools

import jax
import jax.numpy as jnp
from jax import lax
from jax.experimental import pallas as pl
from jax.experimental.pallas import tpu as pltpu
from jax.sharding import PartitionSpec as P

LANES = 128
F32 = jnp.float32
BF16 = jnp.bfloat16


def split(value):
    high = value.astype(BF16)
    return high, (value - high.astype(F32)).astype(BF16)


def circulant(padded_ref, angle):
    line = jnp.broadcast_to(padded_ref[angle : angle + 1, :], (2 * LANES, 2 * LANES))
    return pltpu.roll(line, LANES, 1, stride=1, stride_axis=0)


def fill_taps(taps_ref, padded_ref):
    padded_ref[...] = jnp.zeros_like(padded_ref)
    padded_ref[0 : taps_ref.shape[0], 0 : taps_ref.shape[1]] = taps_ref[...]


def forward_band(circ):
    return jnp.concatenate(split(circ[:, :LANES]), axis=1)


def backward_band(circ):
    return jnp.concatenate(split(circ[LANES:, :]), axis=0)


def column(row):
    n = row.shape[1]
    same = lax.broadcasted_iota(jnp.int32, (n, n), 0) == lax.broadcasted_iota(jnp.int32, (n, n), 1)
    return jnp.sum(jnp.where(same, jnp.broadcast_to(row, (n, n)), 0.0), axis=1, keepdims=True)


def trace_columns(ref, *lead):
    rows = ref[lead].astype(F32)
    return jnp.concatenate([column(rows[r : r + 1, :]) for r in range(rows.shape[0])], axis=0)


def windows(tiles):
    pairs = [jnp.concatenate(pair, axis=1) for pair in zip(tiles[:-1], tiles[1:])]
    return jnp.concatenate(pairs, axis=0)


def halves_sum(wide):
    return wide[:, :LANES] + wide[:, LANES:]


def forward(tiles, band):
    zero = jnp.zeros_like(tiles[0]).astype(BF16)
    highs, lows = zip(*[split(t) for t in tiles])
    n, size = len(tiles) + 1, tiles[0].shape[0]
    rows = [windows([zero, *part, zero]) for part in (highs, lows)]
    out = jnp.dot(jnp.concatenate(rows, axis=0), band, preferred_element_type=F32)
    out = halves_sum(out)
    out = out[: n * size] + out[n * size :]
    return [out[k * size : (k + 1) * size] for k in range(n)]


def backward(parts, band):
    n, size = len(parts[0]) - 1, parts[0][0].shape[0]
    rows = jnp.concatenate([windows(part) for part in parts], axis=0)
    out = lax.dot_general(rows, band, (((1,), (1,)), ((), ())), preferred_element_type=F32)
    out = halves_sum(out)
    total = out[: n * size]
    for p in range(1, len(parts)):
        total = total + out[p * n * size : (p + 1) * n * size]
    return [total[k * size : (k + 1) * size] for k in range(n)]


def coeff(avo_ref, angle, contrast, k):
    return avo_ref[contrast, angle : angle + 1, pl.ds(k * LANES, LANES)]


def add_terms(total, avo_ref, angle, result):
    for c, line in enumerate(total):
        for k, tile in enumerate(result):
            term = coeff(avo_ref, angle, c, k) * tile
            line[k] = term if angle == 0 else line[k] + term


def store_tiles(out_ref, tiles):
    size = out_ref.shape[2]
    for c in range(out_ref.shape[0]):
        for k, tile in enumerate(tiles[c]):
            for r in range(out_ref.shape[1]):
                out_ref[c, r, :, pl.ds(k * LANES, LANES)] = tile[r * size : (r + 1) * size]


def right_side(seis_ref, masks, avo_ref, circs):
    angles, rows, _, samples = seis_ref.shape
    n = samples // LANES
    total = [[None] * n for _ in range(avo_ref.shape[0])]
    for a in range(angles):
        data = jnp.concatenate([seis_ref[a, r].astype(F32) for r in range(rows)], axis=0)
        data = data * masks[a]
        turned = [
            pltpu.roll(data[:, k * LANES : (k + 1) * LANES], LANES // 2, 1) for k in range(n)
        ]
        zero = jnp.zeros_like(turned[0])
        left_half = lax.broadcasted_iota(jnp.int32, zero.shape, 1) < LANES // 2
        shifted = [
            jnp.where(left_half, before, here).astype(BF16)
            for before, here in zip([zero, *turned], [*turned, zero])
        ]
        add_terms(total, avo_ref, a, backward([shifted], backward_band(circs[a])))
    return total


def normal(field, masks, avo_ref, circs):
    contrasts, n = len(field), len(field[0])
    total = [[None] * n for _ in range(contrasts)]
    for a, circ in enumerate(circs):
        mixed = []
        for k in range(n):
            parts = [coeff(avo_ref, a, c, k) * field[c][k] for c in range(contrasts)]
            mixed.append(functools.reduce(jnp.add, parts))
        synth = [tile * masks[a] for tile in forward(mixed, forward_band(circ))]
        left_half = lax.broadcasted_iota(jnp.int32, synth[0].shape, 1) < LANES // 2
        synth[0] = jnp.where(left_half, 0.0, synth[0])
        synth[n] = jnp.where(left_half, synth[n], 0.0)
        result = backward(list(zip(*[split(t) for t in synth])), backward_band(circ))
        add_terms(total, avo_ref, a, result)
    return total


def lateral(here, north, south, west, east):
    traces = here.shape[0]
    place = lax.broadcasted_iota(jnp.int32, here.shape, 0)
    from_west = jnp.where(place == 0, 0.0 if west is None else west, pltpu.roll(here, 1, 0))
    from_east = jnp.where(
        place == traces - 1, 0.0 if east is None else east, pltpu.roll(here, traces - 1, 0)
    )
    around = from_west + from_east
    for other in (north, south):
        around = around if other is None else around + other
    return around


def copy_in(pairs, sems):
    copies = [pltpu.make_async_copy(a, b, sems.at[i]) for i, (a, b) in enumerate(pairs)]
    for copy in copies:
        copy.start()
    return copies


def start_kernel(
    seis_hbm, valid_hbm, avo_hbm, taps_hbm, prior_hbm, strength_hbm,
    b_ref, pair_ref, other_ref, valid_ref, avo_ref, taps_ref, prior_ref, strength_ref,
    seis_ref, padded, sems,
):
    copies = copy_in(
        (
            (taps_hbm, taps_ref),
            (valid_hbm, valid_ref),
            (avo_hbm, avo_ref),
            (seis_hbm, seis_ref),
            (prior_hbm, prior_ref),
            (strength_hbm, strength_ref),
        ),
        sems,
    )
    for copy in copies[:2]:
        copy.wait()
    fill_taps(taps_ref, padded)
    contrasts, angles, _ = avo_ref.shape
    rows = seis_ref.shape[1]
    circs = [circulant(padded, a) for a in range(angles)]
    masks = [trace_columns(valid_ref, a) for a in range(angles)]
    for copy in copies[2:]:
        copy.wait()
    store_tiles(b_ref, right_side(seis_ref, masks, avo_ref, circs))
    first = starts_pair("inline")
    for c in range(contrasts):
        top, bottom = b_ref[c, 0], b_ref[c, rows - 1]
        pair_ref[c] = jnp.where(first, bottom, top)
        other_ref[c] = jnp.where(first, top, bottom)


def part_kernel(
    b_ref, valid_ref, avo_ref, taps_ref, prior_ref, strength_ref, p_ref, top_ref, bottom_ref, padded
):
    contrasts, rows = b_ref.shape[:2]
    fill_taps(taps_ref, padded)
    angles = avo_ref.shape[1]
    circs = [circulant(padded, a) for a in range(angles)]
    masks = [trace_columns(valid_ref, a) for a in range(angles)]
    store_tiles(p_ref, normal(stack_tiles(b_ref), masks, avo_ref, circs))
    weights = [column(prior_ref[r : r + 1, :]) + 4.0 for r in range(rows)]
    for c in range(contrasts):
        strength = strength_ref[:, c : c + 1]
        for r in range(rows):
            here = b_ref[c, r]
            north = b_ref[c, r - 1] if r else None
            south = b_ref[c, r + 1] if r < rows - 1 else None
            around = lateral(here, north, south, None, None)
            p_ref[c, r] = p_ref[c, r] + strength * (weights[r] * here - around)
        top_ref[c] = p_ref[c, 0]
        bottom_ref[c] = p_ref[c, rows - 1]


def stack_tiles(ref):
    contrasts, rows, _, samples = ref.shape
    return [
        [
            jnp.concatenate([ref[c, r, :, pl.ds(k, LANES)] for r in range(rows)], axis=0)
            for k in range(0, samples, LANES)
        ]
        for c in range(contrasts)
    ]


def inside(axis):
    place = lax.axis_index(axis)
    last = lax.axis_size(axis) - 1
    return (place > 0).astype(F32), (place < last).astype(F32)


def starts_pair(axis):
    return lax.axis_index(axis) % 2 == 0


def rows_kernel(b_ref, p_ref, next_ref, mate_ref, strength_ref, v_ref, pair_ref, other_ref):
    contrasts, rows, traces, _ = b_ref.shape
    first_row, first_col = starts_pair("inline"), starts_pair("col")
    for c in range(contrasts):
        strength = strength_ref[:, c : c + 1]
        above = jnp.where(first_row, next_ref[c], mate_ref[c])
        below = jnp.where(first_row, mate_ref[c], next_ref[c])
        own = [p_ref[c, r] for r in range(rows)]
        own[0] = own[0] - strength * above
        own[-1] = own[-1] - strength * below
        for r, line in enumerate(own):
            v_ref[c, r] = line
        lines = [above, *[b_ref[c, r] for r in range(rows)], below, *own]
        base = c * len(lines)
        for e, line in enumerate(lines):
            left, right = line[0:1, :], line[traces - 1 : traces, :]
            pair_ref[base + e : base + e + 1, :] = jnp.where(first_col, right, left)
            other_ref[base + e : base + e + 1, :] = jnp.where(first_col, left, right)


def image_kernel(
    b_ref, v_ref, over_ref, other_ref, pair_ref,
    valid_ref, avo_ref, taps_ref, prior_ref, strength_ref,
    one_ref, two_ref, gram_ref, padded,
):
    contrasts, rows, traces, samples = b_ref.shape
    angles = avo_ref.shape[1]
    has_left, has_right = inside("col")
    has_above, has_below = inside("inline")
    first_col = starts_pair("col")
    left = jnp.where(first_col, other_ref[...], pair_ref[...])
    right = jnp.where(first_col, pair_ref[...], other_ref[...])
    place = lax.broadcasted_iota(jnp.int32, (traces, samples), 0)
    ext = rows + 2
    stride = ext + rows

    def beside(c, r):
        edge = c * stride + r
        west, east = left[edge : edge + 1, :], right[edge : edge + 1, :]
        return jnp.where(place == 0, west, jnp.where(place == traces - 1, east, 0.0))

    for c in range(contrasts):
        strength = strength_ref[:, c : c + 1]
        for r in range(rows):
            one_ref[c, r] = v_ref[c, r] - strength * beside(c, r + 1)
    fill_taps(taps_ref, padded)
    circs = [circulant(padded, a) for a in range(angles)]
    masks = [trace_columns(valid_ref, a) for a in range(angles)]
    store_tiles(two_ref, normal(stack_tiles(one_ref), masks, avo_ref, circs))
    weights = [column(prior_ref[r : r + 1, :]) + 4.0 for r in range(rows)]
    sums = [jnp.zeros((traces, LANES), F32) for _ in range(4)]
    for c in range(contrasts):
        strength = strength_ref[:, c : c + 1]
        over = over_ref[c] - strength * (has_above * b_ref[c, 0] + beside(c, 0))
        under = -strength * (has_below * b_ref[c, rows - 1] + beside(c, ext - 1))
        for r in range(rows):
            here, b = one_ref[c, r], b_ref[c, r]
            edge = c * stride + ext + r
            west = has_left * (left[edge : edge + 1, :] - strength * b[0:1, :])
            east = has_right * (
                right[edge : edge + 1, :] - strength * b[traces - 1 : traces, :]
            )
            north = one_ref[c, r - 1] if r else over
            south = one_ref[c, r + 1] if r < rows - 1 else None
            around = lateral(here, north, south, west, east)
            two = two_ref[c, r] + strength * (weights[r] * here - around)
            twice = two if r else two - strength * over
            two_ref[c, r] = two if r < rows - 1 else two - strength * under
            for q, product in enumerate((b * b, b * here, here * here, here * twice)):
                tiles = [product[:, k : k + LANES] for k in range(0, samples, LANES)]
                sums[q] = sums[q] + functools.reduce(jnp.add, tiles)
    lane = lax.broadcasted_iota(jnp.int32, (1, LANES), 1)
    packed = jnp.zeros((1, LANES), F32)
    for q, total in enumerate(sums):
        total = jnp.sum(jnp.sum(total, axis=0, keepdims=True), axis=1, keepdims=True)
        packed = jnp.where(lane == q, total, packed)
    gram_ref[...] = jnp.broadcast_to(packed[None], gram_ref.shape)


def finish_kernel(
    gram_ref, b_ref, one_ref, two_ref, under_ref, strength_ref,
    solution_hbm, residual_hbm,
    solution_ref, residual_ref, sems,
):
    sums = jnp.sum(gram_ref[...], axis=0)
    g00, g01, g11, g12 = (sums[:, q : q + 1] for q in range(4))
    first = g00 / g01
    ratio = first * g11 / g01
    second = (ratio - 1.0) * g01 / (first * g12 - ratio * g11)
    near = first + second * ratio
    far = first * second
    rows = b_ref.shape[1]
    copies = []
    for c in range(b_ref.shape[0]):
        for r in range(rows):
            b, one, two = b_ref[c, r], one_ref[c, r], two_ref[c, r]
            if r == rows - 1:
                two = two - strength_ref[:, c : c + 1] * under_ref[c]
            solution_ref[c, r] = near * b - far * one
            residual_ref[c, r] = b - near * one + far * two
        for here, there in ((solution_ref, solution_hbm), (residual_ref, residual_hbm)):
            copies.append(pltpu.make_async_copy(here.at[c], there.at[c], sems.at[len(copies)]))
            copies[-1].start()
    for copy in copies:
        copy.wait()


VMEM = pl.BlockSpec(memory_space=pltpu.VMEM)
HBM = pl.BlockSpec(memory_space=pltpu.HBM)


def call(kernel, outs, ins, flops, scratch=(), places=None, to=VMEM):
    moved = sum(x.size * x.dtype.itemsize for x in (*ins, *outs))
    return pl.pallas_call(
        kernel,
        out_shape=outs,
        in_specs=[VMEM] * len(ins) if places is None else places,
        out_specs=jax.tree.map(lambda _: to, outs),
        scratch_shapes=list(scratch),
        compiler_params=pltpu.CompilerParams(vmem_limit_bytes=24 * 1024 * 1024),
        cost_estimate=pl.CostEstimate(flops=flops, bytes_accessed=moved, transcendentals=0),
        name=kernel.__name__,
    )(*ins)


def shift(axis, value, step):
    size = lax.axis_size(axis)
    return lax.ppermute(value, axis, [(i, i + step) for i in range(size) if 0 <= i + step < size])


def swap(axis, value, first):
    starts = range(first, lax.axis_size(axis) - 1, 2)
    return lax.ppermute(value, axis, [(i + d, i + 1 - d) for i in starts for d in (0, 1)])


def shards(seismic, validity, prior_weight, lateral_strength, avo_coeffs, wavelets):
    angles, rows, traces, samples = seismic.shape
    contrasts = avo_coeffs.shape[1]
    avo_coeffs = jnp.swapaxes(avo_coeffs, 0, 1)
    shape = lambda *dims: jax.ShapeDtypeStruct(dims, F32)
    field = shape(contrasts, rows, traces, samples)
    row = shape(contrasts, traces, samples)
    side = shape(contrasts * (2 * rows + 2), samples)
    padded = pltpu.VMEM((8, 2 * LANES), F32)
    work = 2 * angles * rows * traces * samples * 256 * 4

    given = (seismic, validity, avo_coeffs, wavelets, prior_weight, lateral_strength.reshape(1, -1))
    b, pair, other, *kept = call(
        start_kernel,
        (field, row, row, *[jax.ShapeDtypeStruct(x.shape, x.dtype) for x in given[1:]]),
        [pltpu.with_memory_space_constraint(x, pltpu.HBM) for x in given],
        work,
        [pltpu.VMEM(seismic.shape, seismic.dtype), padded, pltpu.SemaphoreType.DMA((6,))],
        [HBM] * 6,
    )
    strength = kept[-1]
    other = swap("inline", other, 1)
    pair = swap("inline", pair, 0)
    part, top, bottom = call(
        part_kernel,
        (field, row, row),
        (b, *kept),
        2 * work,
        [padded],
    )
    over = shift("inline", bottom, 1)
    image, pair, other = call(
        rows_kernel,
        (field, side, side),
        (b, part, other, pair, strength),
        4 * field.size,
    )
    other = swap("col", other, 1)
    pair = swap("col", pair, 0)
    top, image = lax.optimization_barrier((top, image))
    under = shift("inline", top, -1)
    axes = ("inline", "col")
    one, two, gram = call(
        image_kernel,
        (field, field, shape(lax.axis_size(axes), 1, LANES)),
        (b, image, over, other, pair, *kept),
        2 * work,
        [padded],
    )
    gram, under = lax.optimization_barrier((gram, under))
    gram = lax.all_to_all(gram, axes, 0, 0)
    return tuple(
        call(
            finish_kernel,
            (field, field),
            (gram, b, one, two, under, strength),
            8 * field.size,
            [*[pltpu.VMEM(field.shape, F32)] * 2, pltpu.SemaphoreType.DMA((2 * contrasts,))],
            to=HBM,
        )
    )


def solution(mesh):
    placed = (
        P(None, "inline", "col", None),
        P(None, "inline", "col"),
        P("inline", "col"),
        P(),
        P(),
        P(),
    )
    return jax.shard_map(
        shards,
        mesh=mesh,
        in_specs=placed,
        out_specs=(P(None, "inline", "col", None), P(None, "inline", "col", None)),
        check_vma=False,
    )
```

```python
import functools

import jax
import jax.numpy as jnp
from jax import lax
from jax.experimental import pallas as pl
from jax.experimental.pallas import tpu as pltpu
from jax.sharding import PartitionSpec as P

LANES = 128
F32 = jnp.float32
BF16 = jnp.bfloat16


def split(value):
    high = value.astype(BF16)
    return high, (value - high.astype(F32)).astype(BF16)


def circulant(padded_ref, angle):
    line = jnp.broadcast_to(padded_ref[angle : angle + 1, :], (2 * LANES, 2 * LANES))
    return pltpu.roll(line, LANES, 1, stride=1, stride_axis=0)


def fill_taps(taps_ref, padded_ref):
    padded_ref[...] = jnp.zeros_like(padded_ref)
    padded_ref[0 : taps_ref.shape[0], 0 : taps_ref.shape[1]] = taps_ref[...]


def forward_band(circ):
    return jnp.concatenate(split(circ[:, :LANES]), axis=1)


def backward_band(circ):
    return jnp.concatenate(split(circ[LANES:, :]), axis=0)


def column(row):
    n = row.shape[1]
    same = lax.broadcasted_iota(jnp.int32, (n, n), 0) == lax.broadcasted_iota(jnp.int32, (n, n), 1)
    return jnp.sum(jnp.where(same, jnp.broadcast_to(row, (n, n)), 0.0), axis=1, keepdims=True)


def trace_columns(ref, *lead):
    rows = ref[lead].astype(F32)
    return jnp.concatenate([column(rows[r : r + 1, :]) for r in range(rows.shape[0])], axis=0)


def windows(tiles):
    pairs = [jnp.concatenate(pair, axis=1) for pair in zip(tiles[:-1], tiles[1:])]
    return jnp.concatenate(pairs, axis=0)


def halves_sum(wide):
    return wide[:, :LANES] + wide[:, LANES:]


def forward(tiles, band):
    zero = jnp.zeros_like(tiles[0]).astype(BF16)
    highs, lows = zip(*[split(t) for t in tiles])
    n, size = len(tiles) + 1, tiles[0].shape[0]
    rows = [windows([zero, *part, zero]) for part in (highs, lows)]
    out = jnp.dot(jnp.concatenate(rows, axis=0), band, preferred_element_type=F32)
    out = halves_sum(out)
    out = out[: n * size] + out[n * size :]
    return [out[k * size : (k + 1) * size] for k in range(n)]


def backward(parts, band):
    n, size = len(parts[0]) - 1, parts[0][0].shape[0]
    rows = jnp.concatenate([windows(part) for part in parts], axis=0)
    out = lax.dot_general(rows, band, (((1,), (1,)), ((), ())), preferred_element_type=F32)
    out = halves_sum(out)
    total = out[: n * size]
    for p in range(1, len(parts)):
        total = total + out[p * n * size : (p + 1) * n * size]
    return [total[k * size : (k + 1) * size] for k in range(n)]


def coeff(avo_ref, angle, contrast, k):
    return avo_ref[contrast, angle : angle + 1, pl.ds(k * LANES, LANES)]


def add_terms(total, avo_ref, angle, result):
    for c, line in enumerate(total):
        for k, tile in enumerate(result):
            term = coeff(avo_ref, angle, c, k) * tile
            line[k] = term if angle == 0 else line[k] + term


def store_tiles(out_ref, tiles):
    size = out_ref.shape[2]
    for c in range(out_ref.shape[0]):
        for k, tile in enumerate(tiles[c]):
            for r in range(out_ref.shape[1]):
                out_ref[c, r, :, pl.ds(k * LANES, LANES)] = tile[r * size : (r + 1) * size]


def right_side(seis_ref, masks, avo_ref, circs):
    angles, rows, _, samples = seis_ref.shape
    n = samples // LANES
    total = [[None] * n for _ in range(avo_ref.shape[0])]
    for a in range(angles):
        data = jnp.concatenate([seis_ref[a, r].astype(F32) for r in range(rows)], axis=0)
        data = data * masks[a]
        turned = [
            pltpu.roll(data[:, k * LANES : (k + 1) * LANES], LANES // 2, 1) for k in range(n)
        ]
        zero = jnp.zeros_like(turned[0])
        left_half = lax.broadcasted_iota(jnp.int32, zero.shape, 1) < LANES // 2
        shifted = [
            jnp.where(left_half, before, here).astype(BF16)
            for before, here in zip([zero, *turned], [*turned, zero])
        ]
        add_terms(total, avo_ref, a, backward([shifted], backward_band(circs[a])))
    return total


def normal(field, masks, avo_ref, circs):
    contrasts, n = len(field), len(field[0])
    total = [[None] * n for _ in range(contrasts)]
    for a, circ in enumerate(circs):
        mixed = []
        for k in range(n):
            parts = [coeff(avo_ref, a, c, k) * field[c][k] for c in range(contrasts)]
            mixed.append(functools.reduce(jnp.add, parts))
        synth = [tile * masks[a] for tile in forward(mixed, forward_band(circ))]
        left_half = lax.broadcasted_iota(jnp.int32, synth[0].shape, 1) < LANES // 2
        synth[0] = jnp.where(left_half, 0.0, synth[0])
        synth[n] = jnp.where(left_half, synth[n], 0.0)
        result = backward(list(zip(*[split(t) for t in synth])), backward_band(circ))
        add_terms(total, avo_ref, a, result)
    return total


def lateral(here, north, south, west, east):
    traces = here.shape[0]
    place = lax.broadcasted_iota(jnp.int32, here.shape, 0)
    from_west = jnp.where(place == 0, 0.0 if west is None else west, pltpu.roll(here, 1, 0))
    from_east = jnp.where(
        place == traces - 1, 0.0 if east is None else east, pltpu.roll(here, traces - 1, 0)
    )
    around = from_west + from_east
    for other in (north, south):
        around = around if other is None else around + other
    return around


def copy_in(pairs, sems):
    copies = [pltpu.make_async_copy(a, b, sems.at[i]) for i, (a, b) in enumerate(pairs)]
    for copy in copies:
        copy.start()
    return copies


def start_kernel(
    seis_hbm, valid_hbm, avo_hbm, taps_hbm, prior_hbm, strength_hbm,
    b_ref, mate_ref, next_ref, valid_ref, avo_ref, taps_ref, prior_ref, strength_ref,
    seis_ref, padded, sems,
):
    copies = copy_in(
        (
            (taps_hbm, taps_ref),
            (valid_hbm, valid_ref),
            (avo_hbm, avo_ref),
            (seis_hbm, seis_ref),
            (prior_hbm, prior_ref),
            (strength_hbm, strength_ref),
        ),
        sems,
    )
    for copy in copies[:2]:
        copy.wait()
    fill_taps(taps_ref, padded)
    angles = avo_ref.shape[1]
    circs = [circulant(padded, a) for a in range(angles)]
    masks = [trace_columns(valid_ref, a) for a in range(angles)]
    for copy in copies[2:]:
        copy.wait()
    store_tiles(b_ref, right_side(seis_ref, masks, avo_ref, circs))
    send_rows(b_ref, mate_ref, next_ref)


def send_rows(field_ref, mate_ref, next_ref):
    first = starts_pair("inline")
    for c in range(field_ref.shape[0]):
        top, bottom = field_ref[c, 0], field_ref[c, field_ref.shape[1] - 1]
        mate_ref[c] = jnp.where(first, bottom, top)
        next_ref[c] = jnp.where(first, top, bottom)


def halo_rows(mate_ref, next_ref, c):
    first = starts_pair("inline")
    mate, other = mate_ref[c], next_ref[c]
    return jnp.where(first, other, mate), jnp.where(first, mate, other)


def part_kernel(
    b_ref, valid_ref, avo_ref, taps_ref, prior_ref, strength_ref, p_ref, mate_ref, next_ref, padded
):
    contrasts, rows = b_ref.shape[:2]
    fill_taps(taps_ref, padded)
    angles = avo_ref.shape[1]
    circs = [circulant(padded, a) for a in range(angles)]
    masks = [trace_columns(valid_ref, a) for a in range(angles)]
    store_tiles(p_ref, normal(stack_tiles(b_ref), masks, avo_ref, circs))
    weights = [column(prior_ref[r : r + 1, :]) + 4.0 for r in range(rows)]
    for c in range(contrasts):
        strength = strength_ref[:, c : c + 1]
        for r in range(rows):
            here = b_ref[c, r]
            north = b_ref[c, r - 1] if r else None
            south = b_ref[c, r + 1] if r < rows - 1 else None
            around = lateral(here, north, south, None, None)
            p_ref[c, r] = p_ref[c, r] + strength * (weights[r] * here - around)
    send_rows(p_ref, mate_ref, next_ref)


def stack_tiles(ref):
    contrasts, rows, _, samples = ref.shape
    return [
        [
            jnp.concatenate([ref[c, r, :, pl.ds(k, LANES)] for r in range(rows)], axis=0)
            for k in range(0, samples, LANES)
        ]
        for c in range(contrasts)
    ]


def inside(axis):
    place = lax.axis_index(axis)
    last = lax.axis_size(axis) - 1
    return (place > 0).astype(F32), (place < last).astype(F32)


def starts_pair(axis):
    return lax.axis_index(axis) % 2 == 0


def rows_kernel(b_ref, p_ref, next_ref, mate_ref, strength_ref, v_ref, pair_ref, other_ref):
    contrasts, rows, traces, _ = b_ref.shape
    first_col = starts_pair("col")
    for c in range(contrasts):
        strength = strength_ref[:, c : c + 1]
        above, below = halo_rows(mate_ref, next_ref, c)
        own = [p_ref[c, r] for r in range(rows)]
        own[0] = own[0] - strength * above
        own[-1] = own[-1] - strength * below
        for r, line in enumerate(own):
            v_ref[c, r] = line
        lines = [above, *[b_ref[c, r] for r in range(rows)], below, *own]
        base = c * len(lines)
        for e, line in enumerate(lines):
            left, right = line[0:1, :], line[traces - 1 : traces, :]
            pair_ref[base + e : base + e + 1, :] = jnp.where(first_col, right, left)
            other_ref[base + e : base + e + 1, :] = jnp.where(first_col, left, right)


def image_kernel(
    b_ref, v_ref, next_ref, mate_ref, other_ref, pair_ref,
    valid_ref, avo_ref, taps_ref, prior_ref, strength_ref,
    one_ref, two_ref, gram_ref, padded,
):
    contrasts, rows, traces, samples = b_ref.shape
    angles = avo_ref.shape[1]
    has_left, has_right = inside("col")
    has_above, has_below = inside("inline")
    first_col = starts_pair("col")
    left = jnp.where(first_col, other_ref[...], pair_ref[...])
    right = jnp.where(first_col, pair_ref[...], other_ref[...])
    place = lax.broadcasted_iota(jnp.int32, (traces, samples), 0)
    ext = rows + 2
    stride = ext + rows

    def beside(c, r):
        edge = c * stride + r
        west, east = left[edge : edge + 1, :], right[edge : edge + 1, :]
        return jnp.where(place == 0, west, jnp.where(place == traces - 1, east, 0.0))

    for c in range(contrasts):
        strength = strength_ref[:, c : c + 1]
        for r in range(rows):
            one_ref[c, r] = v_ref[c, r] - strength * beside(c, r + 1)
    fill_taps(taps_ref, padded)
    circs = [circulant(padded, a) for a in range(angles)]
    masks = [trace_columns(valid_ref, a) for a in range(angles)]
    store_tiles(two_ref, normal(stack_tiles(one_ref), masks, avo_ref, circs))
    weights = [column(prior_ref[r : r + 1, :]) + 4.0 for r in range(rows)]
    sums = [jnp.zeros((traces, LANES), F32) for _ in range(4)]
    for c in range(contrasts):
        strength = strength_ref[:, c : c + 1]
        over, under = halo_rows(mate_ref, next_ref, c)
        over = over - strength * (has_above * b_ref[c, 0] + beside(c, 0))
        under = under - strength * (has_below * b_ref[c, rows - 1] + beside(c, ext - 1))
        for r in range(rows):
            here, b = one_ref[c, r], b_ref[c, r]
            edge = c * stride + ext + r
            west = has_left * (left[edge : edge + 1, :] - strength * b[0:1, :])
            east = has_right * (
                right[edge : edge + 1, :] - strength * b[traces - 1 : traces, :]
            )
            north = one_ref[c, r - 1] if r else over
            south = one_ref[c, r + 1] if r < rows - 1 else under
            around = lateral(here, north, south, west, east)
            two = two_ref[c, r] + strength * (weights[r] * here - around)
            two_ref[c, r] = two
            for q, product in enumerate((b * b, b * here, here * here, here * two)):
                tiles = [product[:, k : k + LANES] for k in range(0, samples, LANES)]
                sums[q] = sums[q] + functools.reduce(jnp.add, tiles)
    lane = lax.broadcasted_iota(jnp.int32, (1, LANES), 1)
    packed = jnp.zeros((1, LANES), F32)
    for q, total in enumerate(sums):
        total = jnp.sum(jnp.sum(total, axis=0, keepdims=True), axis=1, keepdims=True)
        packed = jnp.where(lane == q, total, packed)
    gram_ref[...] = jnp.broadcast_to(packed[None], gram_ref.shape)


def finish_kernel(gram_ref, b_ref, one_ref, two_ref, solution_ref, residual_ref):
    sums = jnp.sum(gram_ref[...], axis=0)
    g00, g01, g11, g12 = (sums[:, q : q + 1] for q in range(4))
    first = g00 / g01
    ratio = first * g11 / g01
    second = (ratio - 1.0) * g01 / (first * g12 - ratio * g11)
    near = first + second * ratio
    far = first * second
    for c in range(b_ref.shape[0]):
        for r in range(b_ref.shape[1]):
            b, one, two = b_ref[c, r], one_ref[c, r], two_ref[c, r]
            solution_ref[c, r] = near * b - far * one
            residual_ref[c, r] = b - near * one + far * two


VMEM = pl.BlockSpec(memory_space=pltpu.VMEM)
HBM = pl.BlockSpec(memory_space=pltpu.HBM)


def call(kernel, outs, ins, flops, scratch=(), places=None):
    moved = sum(x.size * x.dtype.itemsize for x in (*ins, *outs))
    return pl.pallas_call(
        kernel,
        out_shape=outs,
        in_specs=[VMEM] * len(ins) if places is None else places,
        out_specs=jax.tree.map(lambda _: VMEM, outs),
        scratch_shapes=list(scratch),
        compiler_params=pltpu.CompilerParams(vmem_limit_bytes=24 * 1024 * 1024),
        cost_estimate=pl.CostEstimate(flops=flops, bytes_accessed=moved, transcendentals=0),
        name=kernel.__name__,
    )(*ins)


def swap(axis, value, first):
    starts = range(first, lax.axis_size(axis) - 1, 2)
    return lax.ppermute(value, axis, [(i + d, i + 1 - d) for i in starts for d in (0, 1)])


def shards(seismic, validity, prior_weight, lateral_strength, avo_coeffs, wavelets):
    angles, rows, traces, samples = seismic.shape
    contrasts = avo_coeffs.shape[1]
    avo_coeffs = jnp.swapaxes(avo_coeffs, 0, 1)
    shape = lambda *dims: jax.ShapeDtypeStruct(dims, F32)
    field = shape(contrasts, rows, traces, samples)
    row = shape(contrasts, traces, samples)
    side = shape(contrasts * (2 * rows + 2), samples)
    padded = pltpu.VMEM((8, 2 * LANES), F32)
    work = 2 * angles * rows * traces * samples * 256 * 4

    given = (seismic, validity, avo_coeffs, wavelets, prior_weight, lateral_strength.reshape(1, -1))
    b, mate, other, *kept = call(
        start_kernel,
        (field, row, row, *[jax.ShapeDtypeStruct(x.shape, x.dtype) for x in given[1:]]),
        [pltpu.with_memory_space_constraint(x, pltpu.HBM) for x in given],
        work,
        [pltpu.VMEM(seismic.shape, seismic.dtype), padded, pltpu.SemaphoreType.DMA((6,))],
        [HBM] * 6,
    )
    other = swap("inline", other, 1)
    mate = swap("inline", mate, 0)
    part, part_mate, part_other = call(
        part_kernel, (field, row, row), (b, *kept), 2 * work, [padded]
    )
    part_other = swap("inline", part_other, 1)
    part_mate = swap("inline", part_mate, 0)
    image, col_pair, col_other = call(
        rows_kernel, (field, side, side), (b, part, other, mate, kept[-1]), 4 * field.size
    )
    col_other = swap("col", col_other, 1)
    col_pair = swap("col", col_pair, 0)
    axes = ("inline", "col")
    one, two, gram = call(
        image_kernel,
        (field, field, shape(lax.axis_size(axes), 1, LANES)),
        (b, image, part_other, part_mate, col_other, col_pair, *kept),
        2 * work,
        [padded],
    )
    gram = lax.all_to_all(gram, axes, 0, 0)
    return tuple(call(finish_kernel, (field, field), (gram, b, one, two), 8 * field.size))


def solution(mesh):
    placed = (
        P(None, "inline", "col", None),
        P(None, "inline", "col"),
        P("inline", "col"),
        P(),
        P(),
        P(),
    )
    return jax.shard_map(
        shards,
        mesh=mesh,
        in_specs=placed,
        out_specs=(P(None, "inline", "col", None), P(None, "inline", "col", None)),
        check_vma=False,
    )
```

```python
import functools

import jax
import jax.numpy as jnp
from jax import lax
from jax.experimental import pallas as pl
from jax.experimental.pallas import tpu as pltpu
from jax.sharding import PartitionSpec as P

LANES = 128
F32 = jnp.float32
BF16 = jnp.bfloat16


def split(value):
    high = value.astype(BF16)
    return high, (value - high.astype(F32)).astype(BF16)


def circulant(padded_ref, angle):
    line = jnp.broadcast_to(padded_ref[angle : angle + 1, :], (2 * LANES, 2 * LANES))
    return pltpu.roll(line, LANES, 1, stride=1, stride_axis=0)


def fill_taps(taps_ref, padded_ref):
    padded_ref[...] = jnp.zeros_like(padded_ref)
    padded_ref[0 : taps_ref.shape[0], 0 : taps_ref.shape[1]] = taps_ref[...]


def forward_band(circ):
    return jnp.concatenate(split(circ[:, :LANES]), axis=1)


def backward_band(circ):
    return jnp.concatenate(split(circ[LANES:, :]), axis=0)


def column(row):
    n = row.shape[1]
    same = lax.broadcasted_iota(jnp.int32, (n, n), 0) == lax.broadcasted_iota(jnp.int32, (n, n), 1)
    return jnp.sum(jnp.where(same, jnp.broadcast_to(row, (n, n)), 0.0), axis=1, keepdims=True)


def trace_columns(ref, *lead):
    rows = ref[lead].astype(F32)
    return jnp.concatenate([column(rows[r : r + 1, :]) for r in range(rows.shape[0])], axis=0)


def windows(tiles):
    pairs = [jnp.concatenate(pair, axis=1) for pair in zip(tiles[:-1], tiles[1:])]
    return jnp.concatenate(pairs, axis=0)


def halves_sum(wide):
    return wide[:, :LANES] + wide[:, LANES:]


def forward(tiles, band):
    zero = jnp.zeros_like(tiles[0]).astype(BF16)
    highs, lows = zip(*[split(t) for t in tiles])
    n, size = len(tiles) + 1, tiles[0].shape[0]
    rows = [windows([zero, *part, zero]) for part in (highs, lows)]
    out = jnp.dot(jnp.concatenate(rows, axis=0), band, preferred_element_type=F32)
    out = halves_sum(out)
    out = out[: n * size] + out[n * size :]
    return [out[k * size : (k + 1) * size] for k in range(n)]


def backward(parts, band):
    n, size = len(parts[0]) - 1, parts[0][0].shape[0]
    rows = jnp.concatenate([windows(part) for part in parts], axis=0)
    out = lax.dot_general(rows, band, (((1,), (1,)), ((), ())), preferred_element_type=F32)
    out = halves_sum(out)
    total = out[: n * size]
    for p in range(1, len(parts)):
        total = total + out[p * n * size : (p + 1) * n * size]
    return [total[k * size : (k + 1) * size] for k in range(n)]


def coeff(avo_ref, angle, contrast, k):
    return avo_ref[contrast, angle : angle + 1, pl.ds(k * LANES, LANES)]


def add_terms(total, avo_ref, angle, result):
    for c, line in enumerate(total):
        for k, tile in enumerate(result):
            term = coeff(avo_ref, angle, c, k) * tile
            line[k] = term if angle == 0 else line[k] + term


def store_tiles(out_ref, tiles):
    size = out_ref.shape[2]
    for c in range(out_ref.shape[0]):
        for k, tile in enumerate(tiles[c]):
            for r in range(out_ref.shape[1]):
                out_ref[c, r, :, pl.ds(k * LANES, LANES)] = tile[r * size : (r + 1) * size]


def right_side(seis_ref, masks, avo_ref, circs):
    angles, rows, _, samples = seis_ref.shape
    n = samples // LANES
    total = [[None] * n for _ in range(avo_ref.shape[0])]
    for a in range(angles):
        data = jnp.concatenate([seis_ref[a, r].astype(F32) for r in range(rows)], axis=0)
        data = data * masks[a]
        turned = [
            pltpu.roll(data[:, k * LANES : (k + 1) * LANES], LANES // 2, 1) for k in range(n)
        ]
        zero = jnp.zeros_like(turned[0])
        left_half = lax.broadcasted_iota(jnp.int32, zero.shape, 1) < LANES // 2
        shifted = [
            jnp.where(left_half, before, here).astype(BF16)
            for before, here in zip([zero, *turned], [*turned, zero])
        ]
        add_terms(total, avo_ref, a, backward([shifted], backward_band(circs[a])))
    return total


def normal(field, masks, avo_ref, circs):
    contrasts, n = len(field), len(field[0])
    total = [[None] * n for _ in range(contrasts)]
    for a, circ in enumerate(circs):
        mixed = []
        for k in range(n):
            parts = [coeff(avo_ref, a, c, k) * field[c][k] for c in range(contrasts)]
            mixed.append(functools.reduce(jnp.add, parts))
        synth = [tile * masks[a] for tile in forward(mixed, forward_band(circ))]
        left_half = lax.broadcasted_iota(jnp.int32, synth[0].shape, 1) < LANES // 2
        synth[0] = jnp.where(left_half, 0.0, synth[0])
        synth[n] = jnp.where(left_half, synth[n], 0.0)
        result = backward(list(zip(*[split(t) for t in synth])), backward_band(circ))
        add_terms(total, avo_ref, a, result)
    return total


def lateral(here, north, south, west, east):
    traces = here.shape[0]
    place = lax.broadcasted_iota(jnp.int32, here.shape, 0)
    from_west = jnp.where(place == 0, 0.0 if west is None else west, pltpu.roll(here, 1, 0))
    from_east = jnp.where(
        place == traces - 1, 0.0 if east is None else east, pltpu.roll(here, traces - 1, 0)
    )
    around = from_west + from_east
    for other in (north, south):
        around = around if other is None else around + other
    return around


def copy_in(pairs, sems):
    copies = [pltpu.make_async_copy(a, b, sems.at[i]) for i, (a, b) in enumerate(pairs)]
    for copy in copies:
        copy.start()
    return copies


def start_kernel(
    seis_hbm, valid_hbm, avo_hbm, taps_hbm, prior_hbm, strength_hbm,
    b_ref, near_ref, far_ref, valid_ref, avo_ref, taps_ref, prior_ref, strength_ref,
    seis_ref, padded, sems,
):
    copies = copy_in(
        (
            (taps_hbm, taps_ref),
            (valid_hbm, valid_ref),
            (avo_hbm, avo_ref),
            (seis_hbm, seis_ref),
            (prior_hbm, prior_ref),
            (strength_hbm, strength_ref),
        ),
        sems,
    )
    for copy in copies[:2]:
        copy.wait()
    fill_taps(taps_ref, padded)
    angles = avo_ref.shape[1]
    circs = [circulant(padded, a) for a in range(angles)]
    masks = [trace_columns(valid_ref, a) for a in range(angles)]
    for copy in copies[2:]:
        copy.wait()
    store_tiles(b_ref, right_side(seis_ref, masks, avo_ref, circs))
    contrasts, rows, traces, samples = b_ref.shape
    n = samples // LANES
    first = starts_pair("inline")
    lane = lax.broadcasted_iota(jnp.int32, (traces, LANES), 1)
    notes = []
    for r in (0, rows - 1):
        note = jnp.where(lane == angles, column(prior_ref[r : r + 1, :]), 0.0)
        for a in range(angles):
            note = jnp.where(lane == a, masks[a][r * traces : (r + 1) * traces], note)
        notes.append(note)
    edges = [
        [*[b_ref[c, r, :, pl.ds(k * LANES, LANES)] for c in range(contrasts) for k in range(n)], note]
        for r, note in zip((0, rows - 1), notes)
    ]
    for e, (top, bottom) in enumerate(zip(*edges)):
        near_ref[e] = jnp.where(first, bottom, top)
        far_ref[e] = jnp.where(first, top, bottom)


def either_side(pair_ref, next_ref, *where):
    first = starts_pair("inline")
    pair, other = pair_ref[where], next_ref[where]
    return jnp.where(first, other, pair), jnp.where(first, pair, other)


def part_kernel(
    b_ref, valid_ref, avo_ref, taps_ref, prior_ref, strength_ref, p_ref, padded
):
    contrasts, rows = b_ref.shape[:2]
    fill_taps(taps_ref, padded)
    angles = avo_ref.shape[1]
    circs = [circulant(padded, a) for a in range(angles)]
    masks = [trace_columns(valid_ref, a) for a in range(angles)]
    store_tiles(p_ref, normal(stack_tiles(b_ref), masks, avo_ref, circs))
    weights = [column(prior_ref[r : r + 1, :]) + 4.0 for r in range(rows)]
    for c in range(contrasts):
        strength = strength_ref[:, c : c + 1]
        for r in range(rows):
            here = b_ref[c, r]
            north = b_ref[c, r - 1] if r else None
            south = b_ref[c, r + 1] if r < rows - 1 else None
            around = lateral(here, north, south, None, None)
            p_ref[c, r] = p_ref[c, r] + strength * (weights[r] * here - around)


def halo_kernel(
    b_ref, near_ref, far_ref, near_next_ref, far_next_ref, avo_ref, taps_ref, strength_ref,
    out_ref, padded,
):
    contrasts, rows, traces, samples = b_ref.shape
    angles, n = avo_ref.shape[1], samples // LANES
    has = inside("inline")
    fill_taps(taps_ref, padded)
    circs = [circulant(padded, a) for a in range(angles)]
    notes = either_side(near_ref, near_next_ref, contrasts * n)
    masks = [
        jnp.concatenate([note[:, a : a + 1] for note in notes], axis=0) for a in range(angles)
    ]
    field = [
        [
            jnp.concatenate(either_side(near_ref, near_next_ref, c * n + k), axis=0)
            for k in range(n)
        ]
        for c in range(contrasts)
    ]
    total = normal(field, masks, avo_ref, circs)
    for c in range(contrasts):
        strength = strength_ref[:, c : c + 1]
        for side, own in ((0, 0), (1, rows - 1)):
            weight = notes[side][:, angles : angles + 1] + 4.0
            lines = slice(side * traces, (side + 1) * traces)
            here = jnp.concatenate([tile[lines] for tile in field[c]], axis=1)
            beyond = jnp.concatenate(
                [either_side(far_ref, far_next_ref, c * n + k)[side] for k in range(n)], axis=1
            )
            around = lateral(here, beyond, has[side] * b_ref[c, own], None, None)
            data = jnp.concatenate([tile[lines] for tile in total[c]], axis=1)
            out_ref[side, c] = data + strength * (weight * here - around)


def stack_tiles(ref):
    contrasts, rows, _, samples = ref.shape
    return [
        [
            jnp.concatenate([ref[c, r, :, pl.ds(k, LANES)] for r in range(rows)], axis=0)
            for k in range(0, samples, LANES)
        ]
        for c in range(contrasts)
    ]


def inside(axis):
    place = lax.axis_index(axis)
    last = lax.axis_size(axis) - 1
    return (place > 0).astype(F32), (place < last).astype(F32)


def starts_pair(axis):
    return lax.axis_index(axis) % 2 == 0


def rows_kernel(b_ref, p_ref, near_ref, near_next_ref, strength_ref, v_ref, pair_ref, other_ref):
    contrasts, rows, traces, samples = b_ref.shape
    first_col = starts_pair("col")
    n = samples // LANES
    for c in range(contrasts):
        strength = strength_ref[:, c : c + 1]
        tiles = [either_side(near_ref, near_next_ref, c * n + k) for k in range(n)]
        above, below = (jnp.concatenate(side, axis=1) for side in zip(*tiles))
        own = [p_ref[c, r] for r in range(rows)]
        own[0] = own[0] - strength * above
        own[-1] = own[-1] - strength * below
        for r, line in enumerate(own):
            v_ref[c, r] = line
        lines = [above, *[b_ref[c, r] for r in range(rows)], below, *own]
        base = c * len(lines)
        for e, line in enumerate(lines):
            left, right = line[0:1, :], line[traces - 1 : traces, :]
            pair_ref[base + e : base + e + 1, :] = jnp.where(first_col, right, left)
            other_ref[base + e : base + e + 1, :] = jnp.where(first_col, left, right)


def image_kernel(
    b_ref, v_ref, halo_ref, other_ref, pair_ref,
    valid_ref, avo_ref, taps_ref, prior_ref, strength_ref,
    one_ref, two_ref, gram_ref, padded,
):
    contrasts, rows, traces, samples = b_ref.shape
    angles = avo_ref.shape[1]
    has_left, has_right = inside("col")
    first_col = starts_pair("col")
    left = jnp.where(first_col, other_ref[...], pair_ref[...])
    right = jnp.where(first_col, pair_ref[...], other_ref[...])
    place = lax.broadcasted_iota(jnp.int32, (traces, samples), 0)
    ext = rows + 2
    stride = ext + rows

    def beside(c, r):
        edge = c * stride + r
        west, east = left[edge : edge + 1, :], right[edge : edge + 1, :]
        return jnp.where(place == 0, west, jnp.where(place == traces - 1, east, 0.0))

    for c in range(contrasts):
        strength = strength_ref[:, c : c + 1]
        for r in range(rows):
            one_ref[c, r] = v_ref[c, r] - strength * beside(c, r + 1)
    fill_taps(taps_ref, padded)
    circs = [circulant(padded, a) for a in range(angles)]
    masks = [trace_columns(valid_ref, a) for a in range(angles)]
    store_tiles(two_ref, normal(stack_tiles(one_ref), masks, avo_ref, circs))
    weights = [column(prior_ref[r : r + 1, :]) + 4.0 for r in range(rows)]
    sums = [jnp.zeros((traces, LANES), F32) for _ in range(4)]
    for c in range(contrasts):
        strength = strength_ref[:, c : c + 1]
        over = halo_ref[0, c] - strength * beside(c, 0)
        under = halo_ref[1, c] - strength * beside(c, ext - 1)
        for r in range(rows):
            here, b = one_ref[c, r], b_ref[c, r]
            edge = c * stride + ext + r
            west = has_left * (left[edge : edge + 1, :] - strength * b[0:1, :])
            east = has_right * (
                right[edge : edge + 1, :] - strength * b[traces - 1 : traces, :]
            )
            north = one_ref[c, r - 1] if r else over
            south = one_ref[c, r + 1] if r < rows - 1 else under
            around = lateral(here, north, south, west, east)
            two = two_ref[c, r] + strength * (weights[r] * here - around)
            two_ref[c, r] = two
            for q, product in enumerate((b * b, b * here, here * here, here * two)):
                tiles = [product[:, k : k + LANES] for k in range(0, samples, LANES)]
                sums[q] = sums[q] + functools.reduce(jnp.add, tiles)
    lane = lax.broadcasted_iota(jnp.int32, (1, LANES), 1)
    packed = jnp.zeros((1, LANES), F32)
    for q, total in enumerate(sums):
        total = jnp.sum(jnp.sum(total, axis=0, keepdims=True), axis=1, keepdims=True)
        packed = jnp.where(lane == q, total, packed)
    gram_ref[...] = jnp.broadcast_to(packed[None], gram_ref.shape)


def finish_kernel(gram_ref, b_ref, one_ref, two_ref, solution_ref, residual_ref):
    sums = jnp.sum(gram_ref[...], axis=0)
    g00, g01, g11, g12 = (sums[:, q : q + 1] for q in range(4))
    first = g00 / g01
    ratio = first * g11 / g01
    second = (ratio - 1.0) * g01 / (first * g12 - ratio * g11)
    near = first + second * ratio
    far = first * second
    for c in range(b_ref.shape[0]):
        for r in range(b_ref.shape[1]):
            b, one, two = b_ref[c, r], one_ref[c, r], two_ref[c, r]
            solution_ref[c, r] = near * b - far * one
            residual_ref[c, r] = b - near * one + far * two


VMEM = pl.BlockSpec(memory_space=pltpu.VMEM)
HBM = pl.BlockSpec(memory_space=pltpu.HBM)


def call(kernel, outs, ins, flops, scratch=(), places=None):
    moved = sum(x.size * x.dtype.itemsize for x in (*ins, *outs))
    return pl.pallas_call(
        kernel,
        out_shape=outs,
        in_specs=[VMEM] * len(ins) if places is None else places,
        out_specs=jax.tree.map(lambda _: VMEM, outs),
        scratch_shapes=list(scratch),
        compiler_params=pltpu.CompilerParams(vmem_limit_bytes=24 * 1024 * 1024),
        cost_estimate=pl.CostEstimate(flops=flops, bytes_accessed=moved, transcendentals=0),
        name=kernel.__name__,
    )(*ins)


def swap(axis, value, first):
    starts = range(first, lax.axis_size(axis) - 1, 2)
    return lax.ppermute(value, axis, [(i + d, i + 1 - d) for i in starts for d in (0, 1)])


def hand_on(axis, value):
    size = lax.axis_size(axis)
    steps = [(i, i + 2 - 4 * (i % 2)) for i in range(size)]
    return lax.ppermute(value, axis, [(i, j) for i, j in steps if 0 <= j < size])


def shards(seismic, validity, prior_weight, lateral_strength, avo_coeffs, wavelets):
    angles, rows, traces, samples = seismic.shape
    contrasts = avo_coeffs.shape[1]
    avo_coeffs = jnp.swapaxes(avo_coeffs, 0, 1)
    shape = lambda *dims: jax.ShapeDtypeStruct(dims, F32)
    field = shape(contrasts, rows, traces, samples)
    side = shape(contrasts * (2 * rows + 2), samples)
    padded = pltpu.VMEM((8, 2 * LANES), F32)
    work = 2 * angles * rows * traces * samples * 256 * 4

    given = (seismic, validity, avo_coeffs, wavelets, prior_weight, lateral_strength.reshape(1, -1))
    edge = shape(contrasts * samples // LANES + 1, traces, LANES)
    b, near, far, *kept = call(
        start_kernel,
        (field, edge, edge, *[jax.ShapeDtypeStruct(x.shape, x.dtype) for x in given[1:]]),
        [pltpu.with_memory_space_constraint(x, pltpu.HBM) for x in given],
        work,
        [pltpu.VMEM(seismic.shape, seismic.dtype), padded, pltpu.SemaphoreType.DMA((6,))],
        [HBM] * 6,
    )
    avo, taps, strength = kept[1], kept[2], kept[-1]
    far = swap("inline", far, 0)
    near = swap("inline", near, 0)
    near_next = hand_on("inline", far)
    far_next = hand_on("inline", near)
    (part,) = call(part_kernel, (field,), (b, *kept), 2 * work, [padded])
    image, col_pair, col_other = call(
        rows_kernel, (field, side, side), (b, part, near, near_next, strength), 4 * field.size
    )
    col_other = swap("col", col_other, 1)
    col_pair = swap("col", col_pair, 0)
    (halo,) = call(
        halo_kernel,
        (shape(2, contrasts, traces, samples),),
        (b, near, far, near_next, far_next, avo, taps, strength),
        2 * work,
        [padded],
    )
    axes = ("inline", "col")
    one, two, gram = call(
        image_kernel,
        (field, field, shape(lax.axis_size(axes), 1, LANES)),
        (b, image, halo, col_other, col_pair, *kept),
        2 * work,
        [padded],
    )
    gram = lax.all_to_all(gram, axes, 0, 0)
    return tuple(call(finish_kernel, (field, field), (gram, b, one, two), 8 * field.size))


def solution(mesh):
    placed = (
        P(None, "inline", "col", None),
        P(None, "inline", "col"),
        P("inline", "col"),
        P(),
        P(),
        P(),
    )
    return jax.shard_map(
        shards,
        mesh=mesh,
        in_specs=placed,
        out_specs=(P(None, "inline", "col", None), P(None, "inline", "col", None)),
        check_vma=False,
    )
```

```python
import functools

import jax
import jax.numpy as jnp
from jax import lax
from jax.experimental import pallas as pl
from jax.experimental.pallas import tpu as pltpu
from jax.sharding import PartitionSpec as P

LANES = 128
F32 = jnp.float32
BF16 = jnp.bfloat16


def split(value):
    high = value.astype(BF16)
    return high, (value - high.astype(F32)).astype(BF16)


def circulant(padded_ref, angle):
    line = jnp.broadcast_to(padded_ref[angle : angle + 1, :], (2 * LANES, 2 * LANES))
    return pltpu.roll(line, LANES, 1, stride=1, stride_axis=0)


def fill_taps(taps_ref, padded_ref):
    padded_ref[...] = jnp.zeros_like(padded_ref)
    padded_ref[0 : taps_ref.shape[0], 0 : taps_ref.shape[1]] = taps_ref[...]


def forward_band(circ):
    return jnp.concatenate(split(circ[:, :LANES]), axis=1)


def backward_band(circ):
    return jnp.concatenate(split(circ[LANES:, :]), axis=0)


def column(row):
    n = row.shape[1]
    same = lax.broadcasted_iota(jnp.int32, (n, n), 0) == lax.broadcasted_iota(jnp.int32, (n, n), 1)
    return jnp.sum(jnp.where(same, jnp.broadcast_to(row, (n, n)), 0.0), axis=1, keepdims=True)


def trace_columns(ref, *lead):
    rows = ref[lead].astype(F32)
    return jnp.concatenate([column(rows[r : r + 1, :]) for r in range(rows.shape[0])], axis=0)


def windows(tiles):
    pairs = [jnp.concatenate(pair, axis=1) for pair in zip(tiles[:-1], tiles[1:])]
    return jnp.concatenate(pairs, axis=0)


def halves_sum(wide):
    return wide[:, :LANES] + wide[:, LANES:]


def forward(tiles, band):
    zero = jnp.zeros_like(tiles[0]).astype(BF16)
    highs, lows = zip(*[split(t) for t in tiles])
    n, size = len(tiles) + 1, tiles[0].shape[0]
    rows = [windows([zero, *part, zero]) for part in (highs, lows)]
    out = jnp.dot(jnp.concatenate(rows, axis=0), band, preferred_element_type=F32)
    out = halves_sum(out)
    out = out[: n * size] + out[n * size :]
    return [out[k * size : (k + 1) * size] for k in range(n)]


def backward(parts, band):
    n, size = len(parts[0]) - 1, parts[0][0].shape[0]
    rows = jnp.concatenate([windows(part) for part in parts], axis=0)
    out = lax.dot_general(rows, band, (((1,), (1,)), ((), ())), preferred_element_type=F32)
    out = halves_sum(out)
    total = out[: n * size]
    for p in range(1, len(parts)):
        total = total + out[p * n * size : (p + 1) * n * size]
    return [total[k * size : (k + 1) * size] for k in range(n)]


def coeff(avo_ref, angle, contrast, k):
    return avo_ref[contrast, angle : angle + 1, pl.ds(k * LANES, LANES)]


def add_terms(total, avo_ref, angle, result):
    for c, line in enumerate(total):
        for k, tile in enumerate(result):
            term = coeff(avo_ref, angle, c, k) * tile
            line[k] = term if angle == 0 else line[k] + term


def store_tiles(out_ref, tiles):
    size = out_ref.shape[2]
    for c in range(out_ref.shape[0]):
        for k, tile in enumerate(tiles[c]):
            for r in range(out_ref.shape[1]):
                out_ref[c, r, :, pl.ds(k * LANES, LANES)] = tile[r * size : (r + 1) * size]


def right_side(seis_ref, masks, avo_ref, circs):
    angles, rows, _, samples = seis_ref.shape
    n = samples // LANES
    total = [[None] * n for _ in range(avo_ref.shape[0])]
    for a in range(angles):
        data = jnp.concatenate([seis_ref[a, r].astype(F32) for r in range(rows)], axis=0)
        data = data * masks[a]
        turned = [
            pltpu.roll(data[:, k * LANES : (k + 1) * LANES], LANES // 2, 1) for k in range(n)
        ]
        zero = jnp.zeros_like(turned[0])
        left_half = lax.broadcasted_iota(jnp.int32, zero.shape, 1) < LANES // 2
        shifted = [
            jnp.where(left_half, before, here).astype(BF16)
            for before, here in zip([zero, *turned], [*turned, zero])
        ]
        add_terms(total, avo_ref, a, backward([shifted], backward_band(circs[a])))
    return total


def normal(field, masks, avo_ref, circs):
    contrasts, n = len(field), len(field[0])
    total = [[None] * n for _ in range(contrasts)]
    for a, circ in enumerate(circs):
        mixed = []
        for k in range(n):
            parts = [coeff(avo_ref, a, c, k) * field[c][k] for c in range(contrasts)]
            mixed.append(functools.reduce(jnp.add, parts))
        synth = [tile * masks[a] for tile in forward(mixed, forward_band(circ))]
        left_half = lax.broadcasted_iota(jnp.int32, synth[0].shape, 1) < LANES // 2
        synth[0] = jnp.where(left_half, 0.0, synth[0])
        synth[n] = jnp.where(left_half, synth[n], 0.0)
        result = backward(list(zip(*[split(t) for t in synth])), backward_band(circ))
        add_terms(total, avo_ref, a, result)
    return total


def lateral(here, north, south, west, east):
    traces = here.shape[0]
    place = lax.broadcasted_iota(jnp.int32, here.shape, 0)
    from_west = jnp.where(place == 0, 0.0 if west is None else west, pltpu.roll(here, 1, 0))
    from_east = jnp.where(
        place == traces - 1, 0.0 if east is None else east, pltpu.roll(here, traces - 1, 0)
    )
    around = from_west + from_east
    for other in (north, south):
        around = around if other is None else around + other
    return around


def copy_in(pairs, sems):
    copies = [pltpu.make_async_copy(a, b, sems.at[i]) for i, (a, b) in enumerate(pairs)]
    for copy in copies:
        copy.start()
    return copies


def start_kernel(
    seis_hbm, valid_hbm, avo_hbm, taps_hbm, prior_hbm, strength_hbm,
    b_ref, mate_ref, next_ref, valid_ref, avo_ref, taps_ref, prior_ref, strength_ref,
    seis_ref, padded, sems,
):
    copies = copy_in(
        (
            (taps_hbm, taps_ref),
            (valid_hbm, valid_ref),
            (avo_hbm, avo_ref),
            (seis_hbm, seis_ref),
            (prior_hbm, prior_ref),
            (strength_hbm, strength_ref),
        ),
        sems,
    )
    for copy in copies[:2]:
        copy.wait()
    fill_taps(taps_ref, padded)
    angles = avo_ref.shape[1]
    circs = [circulant(padded, a) for a in range(angles)]
    masks = [trace_columns(valid_ref, a) for a in range(angles)]
    for copy in copies[2:]:
        copy.wait()
    store_tiles(b_ref, right_side(seis_ref, masks, avo_ref, circs))
    send_rows(b_ref, mate_ref, next_ref)


def send_rows(field_ref, mate_ref, next_ref):
    first = starts_pair("inline")
    for c in range(field_ref.shape[0]):
        top, bottom = field_ref[c, 0], field_ref[c, field_ref.shape[1] - 1]
        mate_ref[c] = jnp.where(first, bottom, top)
        next_ref[c] = jnp.where(first, top, bottom)


def halo_rows(mate_ref, next_ref, c):
    first = starts_pair("inline")
    mate, other = mate_ref[c], next_ref[c]
    return jnp.where(first, other, mate), jnp.where(first, mate, other)


def part_kernel(
    b_ref, valid_ref, avo_ref, taps_ref, prior_ref, strength_ref, p_ref, mate_ref, next_ref, padded
):
    contrasts, rows = b_ref.shape[:2]
    fill_taps(taps_ref, padded)
    angles = avo_ref.shape[1]
    circs = [circulant(padded, a) for a in range(angles)]
    masks = [trace_columns(valid_ref, a) for a in range(angles)]
    store_tiles(p_ref, normal(stack_tiles(b_ref), masks, avo_ref, circs))
    weights = [column(prior_ref[r : r + 1, :]) + 4.0 for r in range(rows)]
    for c in range(contrasts):
        strength = strength_ref[:, c : c + 1]
        for r in range(rows):
            here = b_ref[c, r]
            north = b_ref[c, r - 1] if r else None
            south = b_ref[c, r + 1] if r < rows - 1 else None
            around = lateral(here, north, south, None, None)
            p_ref[c, r] = p_ref[c, r] + strength * (weights[r] * here - around)
    send_rows(p_ref, mate_ref, next_ref)


def stack_tiles(ref):
    contrasts, rows, _, samples = ref.shape
    return [
        [
            jnp.concatenate([ref[c, r, :, pl.ds(k, LANES)] for r in range(rows)], axis=0)
            for k in range(0, samples, LANES)
        ]
        for c in range(contrasts)
    ]


def inside(axis):
    place = lax.axis_index(axis)
    last = lax.axis_size(axis) - 1
    return (place > 0).astype(F32), (place < last).astype(F32)


def starts_pair(axis):
    return lax.axis_index(axis) % 2 == 0


def rows_kernel(b_ref, p_ref, mate_ref, next_ref, strength_ref, v_ref, pair_ref, other_ref):
    contrasts, rows, traces, _ = b_ref.shape
    first_col = starts_pair("col")
    for c in range(contrasts):
        strength = strength_ref[:, c : c + 1]
        above, below = halo_rows(mate_ref, next_ref, c)
        own = [p_ref[c, r] for r in range(rows)]
        own[0] = own[0] - strength * above
        own[-1] = own[-1] - strength * below
        for r, line in enumerate(own):
            v_ref[c, r] = line
        lines = [above, *[b_ref[c, r] for r in range(rows)], below, *own]
        base = c * len(lines)
        for e, line in enumerate(lines):
            left, right = line[0:1, :], line[traces - 1 : traces, :]
            pair_ref[base + e : base + e + 1, :] = jnp.where(first_col, right, left)
            other_ref[base + e : base + e + 1, :] = jnp.where(first_col, left, right)


def image_kernel(
    b_ref, v_ref, next_ref, mate_ref, other_ref, pair_ref,
    valid_ref, avo_ref, taps_ref, prior_ref, strength_ref,
    one_ref, two_ref, gram_ref, padded,
):
    contrasts, rows, traces, samples = b_ref.shape
    angles = avo_ref.shape[1]
    has_left, has_right = inside("col")
    has_above, has_below = inside("inline")
    first_col = starts_pair("col")
    left = jnp.where(first_col, other_ref[...], pair_ref[...])
    right = jnp.where(first_col, pair_ref[...], other_ref[...])
    place = lax.broadcasted_iota(jnp.int32, (traces, samples), 0)
    ext = rows + 2
    stride = ext + rows

    def beside(c, r):
        edge = c * stride + r
        west, east = left[edge : edge + 1, :], right[edge : edge + 1, :]
        return jnp.where(place == 0, west, jnp.where(place == traces - 1, east, 0.0))

    for c in range(contrasts):
        strength = strength_ref[:, c : c + 1]
        for r in range(rows):
            one_ref[c, r] = v_ref[c, r] - strength * beside(c, r + 1)
    fill_taps(taps_ref, padded)
    circs = [circulant(padded, a) for a in range(angles)]
    masks = [trace_columns(valid_ref, a) for a in range(angles)]
    store_tiles(two_ref, normal(stack_tiles(one_ref), masks, avo_ref, circs))
    weights = [column(prior_ref[r : r + 1, :]) + 4.0 for r in range(rows)]
    sums = [jnp.zeros((traces, LANES), F32) for _ in range(4)]
    for c in range(contrasts):
        strength = strength_ref[:, c : c + 1]
        over, under = halo_rows(mate_ref, next_ref, c)
        over = over - strength * (has_above * b_ref[c, 0] + beside(c, 0))
        under = under - strength * (has_below * b_ref[c, rows - 1] + beside(c, ext - 1))
        for r in range(rows):
            here, b = one_ref[c, r], b_ref[c, r]
            edge = c * stride + ext + r
            west = has_left * (left[edge : edge + 1, :] - strength * b[0:1, :])
            east = has_right * (
                right[edge : edge + 1, :] - strength * b[traces - 1 : traces, :]
            )
            north = one_ref[c, r - 1] if r else over
            south = one_ref[c, r + 1] if r < rows - 1 else under
            around = lateral(here, north, south, west, east)
            two = two_ref[c, r] + strength * (weights[r] * here - around)
            two_ref[c, r] = two
            for q, product in enumerate((b * b, b * here, here * here, here * two)):
                tiles = [product[:, k : k + LANES] for k in range(0, samples, LANES)]
                sums[q] = sums[q] + functools.reduce(jnp.add, tiles)
    lane = lax.broadcasted_iota(jnp.int32, (1, LANES), 1)
    packed = jnp.zeros((1, LANES), F32)
    for q, total in enumerate(sums):
        total = jnp.sum(jnp.sum(total, axis=0, keepdims=True), axis=1, keepdims=True)
        packed = jnp.where(lane == q, total, packed)
    gram_ref[...] = jnp.broadcast_to(packed[None], gram_ref.shape)


def finish_kernel(gram_ref, b_ref, one_ref, two_ref, solution_ref, residual_ref):
    sums = jnp.sum(gram_ref[...], axis=0)
    g00, g01, g11, g12 = (sums[:, q : q + 1] for q in range(4))
    first = g00 / g01
    ratio = first * g11 / g01
    second = (ratio - 1.0) * g01 / (first * g12 - ratio * g11)
    near = first + second * ratio
    far = first * second
    for c in range(b_ref.shape[0]):
        for r in range(b_ref.shape[1]):
            b, one, two = b_ref[c, r], one_ref[c, r], two_ref[c, r]
            solution_ref[c, r] = near * b - far * one
            residual_ref[c, r] = b - near * one + far * two


VMEM = pl.BlockSpec(memory_space=pltpu.VMEM)
HBM = pl.BlockSpec(memory_space=pltpu.HBM)


def call(kernel, outs, ins, flops, scratch=(), places=None):
    moved = sum(x.size * x.dtype.itemsize for x in (*ins, *outs))
    return pl.pallas_call(
        kernel,
        out_shape=outs,
        in_specs=[VMEM] * len(ins) if places is None else places,
        out_specs=jax.tree.map(lambda _: VMEM, outs),
        scratch_shapes=list(scratch),
        compiler_params=pltpu.CompilerParams(vmem_limit_bytes=24 * 1024 * 1024),
        cost_estimate=pl.CostEstimate(flops=flops, bytes_accessed=moved, transcendentals=0),
        name=kernel.__name__,
    )(*ins)


def swap(axis, value, first):
    starts = range(first, lax.axis_size(axis) - 1, 2)
    return lax.ppermute(value, axis, [(i + d, i + 1 - d) for i in starts for d in (0, 1)])


def shards(seismic, validity, prior_weight, lateral_strength, avo_coeffs, wavelets):
    angles, rows, traces, samples = seismic.shape
    contrasts = avo_coeffs.shape[1]
    avo_coeffs = jnp.swapaxes(avo_coeffs, 0, 1)
    shape = lambda *dims: jax.ShapeDtypeStruct(dims, F32)
    field = shape(contrasts, rows, traces, samples)
    row = shape(contrasts, traces, samples)
    side = shape(contrasts * (2 * rows + 2), samples)
    padded = pltpu.VMEM((8, 2 * LANES), F32)
    work = 2 * angles * rows * traces * samples * 256 * 4

    given = (seismic, validity, avo_coeffs, wavelets, prior_weight, lateral_strength.reshape(1, -1))
    b, mate, other, *kept = call(
        start_kernel,
        (field, row, row, *[jax.ShapeDtypeStruct(x.shape, x.dtype) for x in given[1:]]),
        [pltpu.with_memory_space_constraint(x, pltpu.HBM) for x in given],
        work,
        [pltpu.VMEM(seismic.shape, seismic.dtype), padded, pltpu.SemaphoreType.DMA((6,))],
        [HBM] * 6,
    )
    mate = swap("inline", mate, 0)
    other = swap("inline", other, 1)
    part, part_mate, part_other = call(
        part_kernel, (field, row, row), (b, *kept), 2 * work, [padded]
    )
    part_other = swap("inline", part_other, 1)
    part_mate = swap("inline", part_mate, 0)
    image, col_pair, col_other = call(
        rows_kernel, (field, side, side), (b, part, mate, other, kept[-1]), 4 * field.size
    )
    col_other = swap("col", col_other, 1)
    col_pair = swap("col", col_pair, 0)
    axes = ("inline", "col")
    one, two, gram = call(
        image_kernel,
        (field, field, shape(lax.axis_size(axes), 1, LANES)),
        (b, image, part_other, part_mate, col_other, col_pair, *kept),
        2 * work,
        [padded],
    )
    gram = lax.all_to_all(gram, axes, 0, 0)
    return tuple(call(finish_kernel, (field, field), (gram, b, one, two), 8 * field.size))


def solution(mesh):
    placed = (
        P(None, "inline", "col", None),
        P(None, "inline", "col"),
        P("inline", "col"),
        P(),
        P(),
        P(),
    )
    return jax.shard_map(
        shards,
        mesh=mesh,
        in_specs=placed,
        out_specs=(P(None, "inline", "col", None), P(None, "inline", "col", None)),
        check_vma=False,
    )
```

```python
import functools

import jax
import jax.numpy as jnp
from jax import lax
from jax.experimental import pallas as pl
from jax.experimental.pallas import tpu as pltpu
from jax.sharding import PartitionSpec as P

LANES = 128
F32 = jnp.float32
BF16 = jnp.bfloat16


def split(value):
    high = value.astype(BF16)
    return high, (value - high.astype(F32)).astype(BF16)


def circulant(padded_ref, angle):
    line = jnp.broadcast_to(padded_ref[angle : angle + 1, :], (2 * LANES, 2 * LANES))
    return pltpu.roll(line, LANES, 1, stride=1, stride_axis=0)


def fill_taps(taps_ref, padded_ref):
    padded_ref[...] = jnp.zeros_like(padded_ref)
    padded_ref[0 : taps_ref.shape[0], 0 : taps_ref.shape[1]] = taps_ref[...]


def forward_band(circ):
    return jnp.concatenate(split(circ[:, :LANES]), axis=1)


def backward_band(circ):
    return jnp.concatenate(split(circ[LANES:, :]), axis=0)


def column(row):
    n = row.shape[1]
    same = lax.broadcasted_iota(jnp.int32, (n, n), 0) == lax.broadcasted_iota(jnp.int32, (n, n), 1)
    return jnp.sum(jnp.where(same, jnp.broadcast_to(row, (n, n)), 0.0), axis=1, keepdims=True)


def trace_columns(ref, *lead):
    rows = ref[lead].astype(F32)
    return jnp.concatenate([column(rows[r : r + 1, :]) for r in range(rows.shape[0])], axis=0)


def windows(tiles):
    pairs = [jnp.concatenate(pair, axis=1) for pair in zip(tiles[:-1], tiles[1:])]
    return jnp.concatenate(pairs, axis=0)


def halves_sum(wide):
    return wide[:, :LANES] + wide[:, LANES:]


def forward(tiles, band):
    zero = jnp.zeros_like(tiles[0]).astype(BF16)
    highs, lows = zip(*[split(t) for t in tiles])
    n, size = len(tiles) + 1, tiles[0].shape[0]
    rows = [windows([zero, *part, zero]) for part in (highs, lows)]
    out = jnp.dot(jnp.concatenate(rows, axis=0), band, preferred_element_type=F32)
    out = halves_sum(out)
    out = out[: n * size] + out[n * size :]
    return [out[k * size : (k + 1) * size] for k in range(n)]


def backward(parts, band):
    n, size = len(parts[0]) - 1, parts[0][0].shape[0]
    rows = jnp.concatenate([windows(part) for part in parts], axis=0)
    out = lax.dot_general(rows, band, (((1,), (1,)), ((), ())), preferred_element_type=F32)
    out = halves_sum(out)
    total = out[: n * size]
    for p in range(1, len(parts)):
        total = total + out[p * n * size : (p + 1) * n * size]
    return [total[k * size : (k + 1) * size] for k in range(n)]


def coeff(avo_ref, angle, contrast, k):
    return avo_ref[contrast, angle : angle + 1, pl.ds(k * LANES, LANES)]


def add_terms(total, avo_ref, angle, result):
    for c, line in enumerate(total):
        for k, tile in enumerate(result):
            term = coeff(avo_ref, angle, c, k) * tile
            line[k] = term if angle == 0 else line[k] + term


def store_tiles(out_ref, tiles):
    size = out_ref.shape[2]
    for c in range(out_ref.shape[0]):
        for k, tile in enumerate(tiles[c]):
            for r in range(out_ref.shape[1]):
                out_ref[c, r, :, pl.ds(k * LANES, LANES)] = tile[r * size : (r + 1) * size]


def right_side(seis_ref, masks, avo_ref, circs):
    angles, rows, _, samples = seis_ref.shape
    n = samples // LANES
    total = [[None] * n for _ in range(avo_ref.shape[0])]
    for a in range(angles):
        data = jnp.concatenate([seis_ref[a, r].astype(F32) for r in range(rows)], axis=0)
        data = data * masks[a]
        turned = [
            pltpu.roll(data[:, k * LANES : (k + 1) * LANES], LANES // 2, 1) for k in range(n)
        ]
        zero = jnp.zeros_like(turned[0])
        left_half = lax.broadcasted_iota(jnp.int32, zero.shape, 1) < LANES // 2
        shifted = [
            jnp.where(left_half, before, here).astype(BF16)
            for before, here in zip([zero, *turned], [*turned, zero])
        ]
        add_terms(total, avo_ref, a, backward([shifted], backward_band(circs[a])))
    return total


def normal(field, masks, avo_ref, circs):
    contrasts, n = len(field), len(field[0])
    total = [[None] * n for _ in range(contrasts)]
    for a, circ in enumerate(circs):
        mixed = []
        for k in range(n):
            parts = [coeff(avo_ref, a, c, k) * field[c][k] for c in range(contrasts)]
            mixed.append(functools.reduce(jnp.add, parts))
        synth = [tile * masks[a] for tile in forward(mixed, forward_band(circ))]
        left_half = lax.broadcasted_iota(jnp.int32, synth[0].shape, 1) < LANES // 2
        synth[0] = jnp.where(left_half, 0.0, synth[0])
        synth[n] = jnp.where(left_half, synth[n], 0.0)
        result = backward(list(zip(*[split(t) for t in synth])), backward_band(circ))
        add_terms(total, avo_ref, a, result)
    return total


def lateral(here, north, south, west, east):
    traces = here.shape[0]
    place = lax.broadcasted_iota(jnp.int32, here.shape, 0)
    from_west = jnp.where(place == 0, 0.0 if west is None else west, pltpu.roll(here, 1, 0))
    from_east = jnp.where(
        place == traces - 1, 0.0 if east is None else east, pltpu.roll(here, traces - 1, 0)
    )
    around = from_west + from_east
    for other in (north, south):
        around = around if other is None else around + other
    return around


def copy_in(pairs, sems):
    copies = [pltpu.make_async_copy(a, b, sems.at[i]) for i, (a, b) in enumerate(pairs)]
    for copy in copies:
        copy.start()
    return copies


def start_kernel(
    seis_hbm, valid_hbm, avo_hbm, taps_hbm, prior_hbm, strength_hbm,
    b_ref, mate_ref, next_ref, valid_ref, avo_ref, taps_ref, prior_ref, strength_ref,
    seis_ref, padded, sems,
):
    copies = copy_in(
        (
            (taps_hbm, taps_ref),
            (valid_hbm, valid_ref),
            (avo_hbm, avo_ref),
            (seis_hbm, seis_ref),
            (prior_hbm, prior_ref),
            (strength_hbm, strength_ref),
        ),
        sems,
    )
    for copy in copies[:2]:
        copy.wait()
    fill_taps(taps_ref, padded)
    angles = avo_ref.shape[1]
    circs = [circulant(padded, a) for a in range(angles)]
    masks = [trace_columns(valid_ref, a) for a in range(angles)]
    for copy in copies[2:]:
        copy.wait()
    store_tiles(b_ref, right_side(seis_ref, masks, avo_ref, circs))
    send_rows(b_ref, mate_ref, next_ref)


def send_rows(field_ref, mate_ref, next_ref):
    first = starts_pair("inline")
    for c in range(field_ref.shape[0]):
        top, bottom = field_ref[c, 0], field_ref[c, field_ref.shape[1] - 1]
        mate_ref[c] = jnp.where(first, bottom, top)
        next_ref[c] = jnp.where(first, top, bottom)


def halo_rows(mate_ref, next_ref, c):
    first = starts_pair("inline")
    mate, other = mate_ref[c], next_ref[c]
    return jnp.where(first, other, mate), jnp.where(first, mate, other)


def part_kernel(
    b_ref, valid_ref, avo_ref, taps_ref, prior_ref, strength_ref, p_ref, mate_ref, next_ref, padded
):
    contrasts, rows = b_ref.shape[:2]
    fill_taps(taps_ref, padded)
    angles = avo_ref.shape[1]
    circs = [circulant(padded, a) for a in range(angles)]
    masks = [trace_columns(valid_ref, a) for a in range(angles)]
    store_tiles(p_ref, normal(stack_tiles(b_ref), masks, avo_ref, circs))
    weights = [column(prior_ref[r : r + 1, :]) + 4.0 for r in range(rows)]
    for c in range(contrasts):
        strength = strength_ref[:, c : c + 1]
        for r in range(rows):
            here = b_ref[c, r]
            north = b_ref[c, r - 1] if r else None
            south = b_ref[c, r + 1] if r < rows - 1 else None
            around = lateral(here, north, south, None, None)
            p_ref[c, r] = p_ref[c, r] + strength * (weights[r] * here - around)
    send_rows(p_ref, mate_ref, next_ref)


def stack_tiles(ref):
    contrasts, rows, _, samples = ref.shape
    return [
        [
            jnp.concatenate([ref[c, r, :, pl.ds(k, LANES)] for r in range(rows)], axis=0)
            for k in range(0, samples, LANES)
        ]
        for c in range(contrasts)
    ]


def inside(axis):
    place = lax.axis_index(axis)
    last = lax.axis_size(axis) - 1
    return (place > 0).astype(F32), (place < last).astype(F32)


def starts_pair(axis):
    return lax.axis_index(axis) % 2 == 0


def rows_kernel(b_ref, p_ref, mate_ref, next_ref, strength_ref, v_ref, pair_ref, other_ref):
    contrasts, rows, traces, _ = b_ref.shape
    first_col = starts_pair("col")
    for c in range(contrasts):
        strength = strength_ref[:, c : c + 1]
        above, below = halo_rows(mate_ref, next_ref, c)
        own = [p_ref[c, r] for r in range(rows)]
        own[0] = own[0] - strength * above
        own[-1] = own[-1] - strength * below
        for r, line in enumerate(own):
            v_ref[c, r] = line
        lines = [above, *[b_ref[c, r] for r in range(rows)], below, *own]
        base = c * len(lines)
        for e, line in enumerate(lines):
            left, right = line[0:1, :], line[traces - 1 : traces, :]
            pair_ref[base + e : base + e + 1, :] = jnp.where(first_col, right, left)
            other_ref[base + e : base + e + 1, :] = jnp.where(first_col, left, right)


def image_kernel(
    b_ref, v_ref, next_ref, mate_ref, other_ref, pair_ref,
    valid_ref, avo_ref, taps_ref, prior_ref, strength_ref,
    one_ref, two_ref, gram_ref, padded,
):
    contrasts, rows, traces, samples = b_ref.shape
    angles = avo_ref.shape[1]
    has_left, has_right = inside("col")
    has_above, has_below = inside("inline")
    first_col = starts_pair("col")
    left = jnp.where(first_col, other_ref[...], pair_ref[...])
    right = jnp.where(first_col, pair_ref[...], other_ref[...])
    place = lax.broadcasted_iota(jnp.int32, (traces, samples), 0)
    ext = rows + 2
    stride = ext + rows

    def beside(c, r):
        edge = c * stride + r
        west, east = left[edge : edge + 1, :], right[edge : edge + 1, :]
        return jnp.where(place == 0, west, jnp.where(place == traces - 1, east, 0.0))

    for c in range(contrasts):
        strength = strength_ref[:, c : c + 1]
        for r in range(rows):
            one_ref[c, r] = v_ref[c, r] - strength * beside(c, r + 1)
    fill_taps(taps_ref, padded)
    circs = [circulant(padded, a) for a in range(angles)]
    masks = [trace_columns(valid_ref, a) for a in range(angles)]
    store_tiles(two_ref, normal(stack_tiles(one_ref), masks, avo_ref, circs))
    weights = [column(prior_ref[r : r + 1, :]) + 4.0 for r in range(rows)]
    sums = [jnp.zeros((traces, LANES), F32) for _ in range(4)]
    for c in range(contrasts):
        strength = strength_ref[:, c : c + 1]
        over, under = halo_rows(mate_ref, next_ref, c)
        over = over - strength * (has_above * b_ref[c, 0] + beside(c, 0))
        under = under - strength * (has_below * b_ref[c, rows - 1] + beside(c, ext - 1))
        for r in range(rows):
            here, b = one_ref[c, r], b_ref[c, r]
            edge = c * stride + ext + r
            west = has_left * (left[edge : edge + 1, :] - strength * b[0:1, :])
            east = has_right * (
                right[edge : edge + 1, :] - strength * b[traces - 1 : traces, :]
            )
            north = one_ref[c, r - 1] if r else over
            south = one_ref[c, r + 1] if r < rows - 1 else under
            around = lateral(here, north, south, west, east)
            two = two_ref[c, r] + strength * (weights[r] * here - around)
            two_ref[c, r] = two
            for q, product in enumerate((b * b, b * here, here * here, here * two)):
                tiles = [product[:, k : k + LANES] for k in range(0, samples, LANES)]
                sums[q] = sums[q] + functools.reduce(jnp.add, tiles)
    lane = lax.broadcasted_iota(jnp.int32, (1, LANES), 1)
    packed = jnp.zeros((1, LANES), F32)
    for q, total in enumerate(sums):
        total = jnp.sum(jnp.sum(total, axis=0, keepdims=True), axis=1, keepdims=True)
        packed = jnp.where(lane == q, total, packed)
    gram_ref[...] = jnp.broadcast_to(packed[None], gram_ref.shape)


def finish_kernel(gram_ref, b_ref, one_ref, two_ref, solution_ref, residual_ref):
    sums = jnp.sum(gram_ref[...], axis=0)
    g00, g01, g11, g12 = (sums[:, q : q + 1] for q in range(4))
    first = g00 / g01
    ratio = first * g11 / g01
    second = (ratio - 1.0) * g01 / (first * g12 - ratio * g11)
    near = first + second * ratio
    far = first * second
    for c in range(b_ref.shape[0]):
        for r in range(b_ref.shape[1]):
            b, one, two = b_ref[c, r], one_ref[c, r], two_ref[c, r]
            solution_ref[c, r] = near * b - far * one
            residual_ref[c, r] = b - near * one + far * two


VMEM = pl.BlockSpec(memory_space=pltpu.VMEM)
HBM = pl.BlockSpec(memory_space=pltpu.HBM)


def call(kernel, outs, ins, flops, scratch=(), places=None):
    moved = sum(x.size * x.dtype.itemsize for x in (*ins, *outs))
    return pl.pallas_call(
        kernel,
        out_shape=outs,
        in_specs=[VMEM] * len(ins) if places is None else places,
        out_specs=jax.tree.map(lambda _: VMEM, outs),
        scratch_shapes=list(scratch),
        compiler_params=pltpu.CompilerParams(vmem_limit_bytes=24 * 1024 * 1024),
        cost_estimate=pl.CostEstimate(flops=flops, bytes_accessed=moved, transcendentals=0),
        name=kernel.__name__,
    )(*ins)


def swap(axis, value, first):
    starts = range(first, lax.axis_size(axis) - 1, 2)
    return lax.ppermute(value, axis, [(i + d, i + 1 - d) for i in starts for d in (0, 1)])


def shards(seismic, validity, prior_weight, lateral_strength, avo_coeffs, wavelets):
    angles, rows, traces, samples = seismic.shape
    contrasts = avo_coeffs.shape[1]
    avo_coeffs = jnp.swapaxes(avo_coeffs, 0, 1)
    shape = lambda *dims: jax.ShapeDtypeStruct(dims, F32)
    field = shape(contrasts, rows, traces, samples)
    row = shape(contrasts, traces, samples)
    side = shape(contrasts * (2 * rows + 2), samples)
    padded = pltpu.VMEM((8, 2 * LANES), F32)
    work = 2 * angles * rows * traces * samples * 256 * 4

    given = (seismic, validity, avo_coeffs, wavelets, prior_weight, lateral_strength.reshape(1, -1))
    b, mate, other, *kept = call(
        start_kernel,
        (field, row, row, *[jax.ShapeDtypeStruct(x.shape, x.dtype) for x in given[1:]]),
        [pltpu.with_memory_space_constraint(x, pltpu.HBM) for x in given],
        work,
        [pltpu.VMEM(seismic.shape, seismic.dtype), padded, pltpu.SemaphoreType.DMA((6,))],
        [HBM] * 6,
    )
    mate = swap("inline", mate, 0)
    other = swap("inline", other, 1)
    part, part_mate, part_other = call(
        part_kernel, (field, row, row), (b, *kept), 2 * work, [padded]
    )
    part_other = swap("inline", part_other, 1)
    part_mate = swap("inline", part_mate, 0)
    image, col_pair, col_other = call(
        rows_kernel, (field, side, side), (b, part, mate, other, kept[-1]), 4 * field.size
    )
    col_other = swap("col", col_other, 1)
    col_pair = swap("col", col_pair, 0)
    axes = ("inline", "col")
    one, two, gram = call(
        image_kernel,
        (field, field, shape(lax.axis_size(axes), 1, LANES)),
        (b, image, part_other, part_mate, col_other, col_pair, *kept),
        2 * work,
        [padded],
    )
    group = list(range(lax.axis_size(axes)))[::-1]
    gram = lax.all_to_all(gram, axes, 0, 0, axis_index_groups=[group])
    return tuple(call(finish_kernel, (field, field), (gram, b, one, two), 8 * field.size))


def solution(mesh):
    placed = (
        P(None, "inline", "col", None),
        P(None, "inline", "col"),
        P("inline", "col"),
        P(),
        P(),
        P(),
    )
    return jax.shard_map(
        shards,
        mesh=mesh,
        in_specs=placed,
        out_specs=(P(None, "inline", "col", None), P(None, "inline", "col", None)),
        check_vma=False,
    )
```

```python
import functools

import jax
import jax.numpy as jnp
from jax import lax
from jax.experimental import pallas as pl
from jax.experimental.pallas import tpu as pltpu
from jax.sharding import PartitionSpec as P

LANES = 128
F32 = jnp.float32
BF16 = jnp.bfloat16


def split(value):
    high = value.astype(BF16)
    return high, (value - high.astype(F32)).astype(BF16)


def circulant(padded_ref, angle):
    line = jnp.broadcast_to(padded_ref[angle : angle + 1, :], (2 * LANES, 2 * LANES))
    return pltpu.roll(line, LANES, 1, stride=1, stride_axis=0)


def fill_taps(taps_ref, padded_ref):
    padded_ref[...] = jnp.zeros_like(padded_ref)
    padded_ref[0 : taps_ref.shape[0], 0 : taps_ref.shape[1]] = taps_ref[...]


def forward_band(circ):
    return jnp.concatenate(split(circ[:, :LANES]), axis=1)


def backward_band(circ):
    return jnp.concatenate(split(circ[LANES:, :]), axis=0)


def column(row):
    n = row.shape[1]
    same = lax.broadcasted_iota(jnp.int32, (n, n), 0) == lax.broadcasted_iota(jnp.int32, (n, n), 1)
    return jnp.sum(jnp.where(same, jnp.broadcast_to(row, (n, n)), 0.0), axis=1, keepdims=True)


def trace_columns(ref, *lead):
    rows = ref[lead].astype(F32)
    return jnp.concatenate([column(rows[r : r + 1, :]) for r in range(rows.shape[0])], axis=0)


def windows(tiles):
    pairs = [jnp.concatenate(pair, axis=1) for pair in zip(tiles[:-1], tiles[1:])]
    return jnp.concatenate(pairs, axis=0)


def halves_sum(wide):
    return wide[:, :LANES] + wide[:, LANES:]


def forward(tiles, band):
    zero = jnp.zeros_like(tiles[0]).astype(BF16)
    highs, lows = zip(*[split(t) for t in tiles])
    n, size = len(tiles) + 1, tiles[0].shape[0]
    rows = [windows([zero, *part, zero]) for part in (highs, lows)]
    out = jnp.dot(jnp.concatenate(rows, axis=0), band, preferred_element_type=F32)
    out = halves_sum(out)
    out = out[: n * size] + out[n * size :]
    return [out[k * size : (k + 1) * size] for k in range(n)]


def backward(parts, band):
    n, size = len(parts[0]) - 1, parts[0][0].shape[0]
    rows = jnp.concatenate([windows(part) for part in parts], axis=0)
    out = lax.dot_general(rows, band, (((1,), (1,)), ((), ())), preferred_element_type=F32)
    out = halves_sum(out)
    total = out[: n * size]
    for p in range(1, len(parts)):
        total = total + out[p * n * size : (p + 1) * n * size]
    return [total[k * size : (k + 1) * size] for k in range(n)]


def coeff(avo_ref, angle, contrast, k):
    return avo_ref[contrast, angle : angle + 1, pl.ds(k * LANES, LANES)]


def add_terms(total, avo_ref, angle, result):
    for c, line in enumerate(total):
        for k, tile in enumerate(result):
            term = coeff(avo_ref, angle, c, k) * tile
            line[k] = term if angle == 0 else line[k] + term


def store_tiles(out_ref, tiles):
    size = out_ref.shape[2]
    for c in range(out_ref.shape[0]):
        for k, tile in enumerate(tiles[c]):
            for r in range(out_ref.shape[1]):
                out_ref[c, r, :, pl.ds(k * LANES, LANES)] = tile[r * size : (r + 1) * size]


def right_side(seis_ref, masks, avo_ref, circs):
    angles, rows, _, samples = seis_ref.shape
    n = samples // LANES
    total = [[None] * n for _ in range(avo_ref.shape[0])]
    for a in range(angles):
        data = jnp.concatenate([seis_ref[a, r].astype(F32) for r in range(rows)], axis=0)
        data = data * masks[a]
        turned = [
            pltpu.roll(data[:, k * LANES : (k + 1) * LANES], LANES // 2, 1) for k in range(n)
        ]
        zero = jnp.zeros_like(turned[0])
        left_half = lax.broadcasted_iota(jnp.int32, zero.shape, 1) < LANES // 2
        shifted = [
            jnp.where(left_half, before, here).astype(BF16)
            for before, here in zip([zero, *turned], [*turned, zero])
        ]
        add_terms(total, avo_ref, a, backward([shifted], backward_band(circs[a])))
    return total


def normal(field, masks, avo_ref, circs):
    contrasts, n = len(field), len(field[0])
    total = [[None] * n for _ in range(contrasts)]
    for a, circ in enumerate(circs):
        mixed = []
        for k in range(n):
            parts = [coeff(avo_ref, a, c, k) * field[c][k] for c in range(contrasts)]
            mixed.append(functools.reduce(jnp.add, parts))
        synth = [tile * masks[a] for tile in forward(mixed, forward_band(circ))]
        left_half = lax.broadcasted_iota(jnp.int32, synth[0].shape, 1) < LANES // 2
        synth[0] = jnp.where(left_half, 0.0, synth[0])
        synth[n] = jnp.where(left_half, synth[n], 0.0)
        result = backward(list(zip(*[split(t) for t in synth])), backward_band(circ))
        add_terms(total, avo_ref, a, result)
    return total


def lateral(here, north, south, west, east):
    traces = here.shape[0]
    place = lax.broadcasted_iota(jnp.int32, here.shape, 0)
    from_west = jnp.where(place == 0, 0.0 if west is None else west, pltpu.roll(here, 1, 0))
    from_east = jnp.where(
        place == traces - 1, 0.0 if east is None else east, pltpu.roll(here, traces - 1, 0)
    )
    around = from_west + from_east
    for other in (north, south):
        around = around if other is None else around + other
    return around


def copy_in(pairs, sems):
    copies = [pltpu.make_async_copy(a, b, sems.at[i]) for i, (a, b) in enumerate(pairs)]
    for copy in copies:
        copy.start()
    return copies


def start_kernel(
    seis_hbm, valid_hbm, avo_hbm, taps_hbm, prior_hbm, strength_hbm,
    b_ref, near_ref, far_ref, valid_ref, avo_ref, taps_ref, prior_ref, strength_ref,
    seis_ref, padded, sems,
):
    copies = copy_in(
        (
            (taps_hbm, taps_ref),
            (valid_hbm, valid_ref),
            (avo_hbm, avo_ref),
            (seis_hbm, seis_ref),
            (prior_hbm, prior_ref),
            (strength_hbm, strength_ref),
        ),
        sems,
    )
    for copy in copies[:2]:
        copy.wait()
    fill_taps(taps_ref, padded)
    angles = avo_ref.shape[1]
    circs = [circulant(padded, a) for a in range(angles)]
    masks = [trace_columns(valid_ref, a) for a in range(angles)]
    for copy in copies[2:]:
        copy.wait()
    store_tiles(b_ref, right_side(seis_ref, masks, avo_ref, circs))
    contrasts, rows, traces, samples = b_ref.shape
    n = samples // LANES
    first = starts_pair("inline")
    lane = lax.broadcasted_iota(jnp.int32, (traces, LANES), 1)
    notes = []
    for r in (0, rows - 1):
        note = jnp.where(lane == angles, column(prior_ref[r : r + 1, :]), 0.0)
        for a in range(angles):
            note = jnp.where(lane == a, masks[a][r * traces : (r + 1) * traces], note)
        notes.append(note)
    edges = [
        [*[b_ref[c, r, :, pl.ds(k * LANES, LANES)] for c in range(contrasts) for k in range(n)], note]
        for r, note in zip((0, rows - 1), notes)
    ]
    for e, (top, bottom) in enumerate(zip(*edges)):
        near_ref[e] = jnp.where(first, bottom, top)
        far_ref[e] = jnp.where(first, top, bottom)


def either_side(pair_ref, next_ref, *where):
    first = starts_pair("inline")
    pair, other = pair_ref[where], next_ref[where]
    return jnp.where(first, other, pair), jnp.where(first, pair, other)


def part_kernel(
    b_ref, valid_ref, avo_ref, taps_ref, prior_ref, strength_ref, p_ref, padded
):
    contrasts, rows = b_ref.shape[:2]
    fill_taps(taps_ref, padded)
    angles = avo_ref.shape[1]
    circs = [circulant(padded, a) for a in range(angles)]
    masks = [trace_columns(valid_ref, a) for a in range(angles)]
    store_tiles(p_ref, normal(stack_tiles(b_ref), masks, avo_ref, circs))
    weights = [column(prior_ref[r : r + 1, :]) + 4.0 for r in range(rows)]
    for c in range(contrasts):
        strength = strength_ref[:, c : c + 1]
        for r in range(rows):
            here = b_ref[c, r]
            north = b_ref[c, r - 1] if r else None
            south = b_ref[c, r + 1] if r < rows - 1 else None
            around = lateral(here, north, south, None, None)
            p_ref[c, r] = p_ref[c, r] + strength * (weights[r] * here - around)


def halo_kernel(
    b_ref, near_ref, near_next_ref, far_next_ref, far_ref, avo_ref, taps_ref, strength_ref,
    out_ref, padded,
):
    contrasts, rows, traces, samples = b_ref.shape
    angles, n = avo_ref.shape[1], samples // LANES
    has = inside("inline")
    fill_taps(taps_ref, padded)
    circs = [circulant(padded, a) for a in range(angles)]
    notes = either_side(near_ref, near_next_ref, contrasts * n)
    masks = [
        jnp.concatenate([note[:, a : a + 1] for note in notes], axis=0) for a in range(angles)
    ]
    field = [
        [
            jnp.concatenate(either_side(near_ref, near_next_ref, c * n + k), axis=0)
            for k in range(n)
        ]
        for c in range(contrasts)
    ]
    total = normal(field, masks, avo_ref, circs)
    for c in range(contrasts):
        strength = strength_ref[:, c : c + 1]
        for side, own in ((0, 0), (1, rows - 1)):
            weight = notes[side][:, angles : angles + 1] + 4.0
            lines = slice(side * traces, (side + 1) * traces)
            here = jnp.concatenate([tile[lines] for tile in field[c]], axis=1)
            beyond = jnp.concatenate(
                [either_side(far_ref, far_next_ref, c * n + k)[side] for k in range(n)], axis=1
            )
            around = lateral(here, beyond, has[side] * b_ref[c, own], None, None)
            data = jnp.concatenate([tile[lines] for tile in total[c]], axis=1)
            out_ref[side, c] = data + strength * (weight * here - around)


def stack_tiles(ref):
    contrasts, rows, _, samples = ref.shape
    return [
        [
            jnp.concatenate([ref[c, r, :, pl.ds(k, LANES)] for r in range(rows)], axis=0)
            for k in range(0, samples, LANES)
        ]
        for c in range(contrasts)
    ]


def inside(axis):
    place = lax.axis_index(axis)
    last = lax.axis_size(axis) - 1
    return (place > 0).astype(F32), (place < last).astype(F32)


def starts_pair(axis):
    return lax.axis_index(axis) % 2 == 0


def rows_kernel(b_ref, p_ref, near_ref, near_next_ref, strength_ref, v_ref, pair_ref, other_ref):
    contrasts, rows, traces, samples = b_ref.shape
    first_col = starts_pair("col")
    n = samples // LANES
    for c in range(contrasts):
        strength = strength_ref[:, c : c + 1]
        tiles = [either_side(near_ref, near_next_ref, c * n + k) for k in range(n)]
        above, below = (jnp.concatenate(side, axis=1) for side in zip(*tiles))
        own = [p_ref[c, r] for r in range(rows)]
        own[0] = own[0] - strength * above
        own[-1] = own[-1] - strength * below
        for r, line in enumerate(own):
            v_ref[c, r] = line
        lines = [above, *[b_ref[c, r] for r in range(rows)], below, *own]
        base = c * len(lines)
        for e, line in enumerate(lines):
            left, right = line[0:1, :], line[traces - 1 : traces, :]
            pair_ref[base + e : base + e + 1, :] = jnp.where(first_col, right, left)
            other_ref[base + e : base + e + 1, :] = jnp.where(first_col, left, right)


def image_kernel(
    b_ref, v_ref, halo_ref, other_ref, pair_ref,
    valid_ref, avo_ref, taps_ref, prior_ref, strength_ref,
    one_ref, two_ref, gram_ref, padded,
):
    contrasts, rows, traces, samples = b_ref.shape
    angles = avo_ref.shape[1]
    has_left, has_right = inside("col")
    first_col = starts_pair("col")
    left = jnp.where(first_col, other_ref[...], pair_ref[...])
    right = jnp.where(first_col, pair_ref[...], other_ref[...])
    place = lax.broadcasted_iota(jnp.int32, (traces, samples), 0)
    ext = rows + 2
    stride = ext + rows

    def beside(c, r):
        edge = c * stride + r
        west, east = left[edge : edge + 1, :], right[edge : edge + 1, :]
        return jnp.where(place == 0, west, jnp.where(place == traces - 1, east, 0.0))

    for c in range(contrasts):
        strength = strength_ref[:, c : c + 1]
        for r in range(rows):
            one_ref[c, r] = v_ref[c, r] - strength * beside(c, r + 1)
    fill_taps(taps_ref, padded)
    circs = [circulant(padded, a) for a in range(angles)]
    masks = [trace_columns(valid_ref, a) for a in range(angles)]
    store_tiles(two_ref, normal(stack_tiles(one_ref), masks, avo_ref, circs))
    weights = [column(prior_ref[r : r + 1, :]) + 4.0 for r in range(rows)]
    sums = [jnp.zeros((traces, LANES), F32) for _ in range(4)]
    for c in range(contrasts):
        strength = strength_ref[:, c : c + 1]
        over = halo_ref[0, c] - strength * beside(c, 0)
        under = halo_ref[1, c] - strength * beside(c, ext - 1)
        for r in range(rows):
            here, b = one_ref[c, r], b_ref[c, r]
            edge = c * stride + ext + r
            west = has_left * (left[edge : edge + 1, :] - strength * b[0:1, :])
            east = has_right * (
                right[edge : edge + 1, :] - strength * b[traces - 1 : traces, :]
            )
            north = one_ref[c, r - 1] if r else over
            south = one_ref[c, r + 1] if r < rows - 1 else under
            around = lateral(here, north, south, west, east)
            two = two_ref[c, r] + strength * (weights[r] * here - around)
            two_ref[c, r] = two
            for q, product in enumerate((b * b, b * here, here * here, here * two)):
                tiles = [product[:, k : k + LANES] for k in range(0, samples, LANES)]
                sums[q] = sums[q] + functools.reduce(jnp.add, tiles)
    lane = lax.broadcasted_iota(jnp.int32, (1, LANES), 1)
    packed = jnp.zeros((1, LANES), F32)
    for q, total in enumerate(sums):
        total = jnp.sum(jnp.sum(total, axis=0, keepdims=True), axis=1, keepdims=True)
        packed = jnp.where(lane == q, total, packed)
    gram_ref[...] = jnp.broadcast_to(packed[None], gram_ref.shape)


def finish_kernel(gram_ref, b_ref, one_ref, two_ref, solution_ref, residual_ref):
    sums = jnp.sum(gram_ref[...], axis=0)
    g00, g01, g11, g12 = (sums[:, q : q + 1] for q in range(4))
    first = g00 / g01
    ratio = first * g11 / g01
    second = (ratio - 1.0) * g01 / (first * g12 - ratio * g11)
    near = first + second * ratio
    far = first * second
    for c in range(b_ref.shape[0]):
        for r in range(b_ref.shape[1]):
            b, one, two = b_ref[c, r], one_ref[c, r], two_ref[c, r]
            solution_ref[c, r] = near * b - far * one
            residual_ref[c, r] = b - near * one + far * two


VMEM = pl.BlockSpec(memory_space=pltpu.VMEM)
HBM = pl.BlockSpec(memory_space=pltpu.HBM)


def call(kernel, outs, ins, flops, scratch=(), places=None):
    moved = sum(x.size * x.dtype.itemsize for x in (*ins, *outs))
    return pl.pallas_call(
        kernel,
        out_shape=outs,
        in_specs=[VMEM] * len(ins) if places is None else places,
        out_specs=jax.tree.map(lambda _: VMEM, outs),
        scratch_shapes=list(scratch),
        compiler_params=pltpu.CompilerParams(vmem_limit_bytes=24 * 1024 * 1024),
        cost_estimate=pl.CostEstimate(flops=flops, bytes_accessed=moved, transcendentals=0),
        name=kernel.__name__,
    )(*ins)


def swap(axis, value, first):
    starts = range(first, lax.axis_size(axis) - 1, 2)
    return lax.ppermute(value, axis, [(i + d, i + 1 - d) for i in starts for d in (0, 1)])


def hand_on(axis, value):
    size = lax.axis_size(axis)
    steps = [(i, i + 2 - 4 * (i % 2)) for i in range(size)]
    return lax.ppermute(value, axis, [(i, j) for i, j in steps if 0 <= j < size])


def shards(seismic, validity, prior_weight, lateral_strength, avo_coeffs, wavelets):
    angles, rows, traces, samples = seismic.shape
    contrasts = avo_coeffs.shape[1]
    avo_coeffs = jnp.swapaxes(avo_coeffs, 0, 1)
    shape = lambda *dims: jax.ShapeDtypeStruct(dims, F32)
    field = shape(contrasts, rows, traces, samples)
    side = shape(contrasts * (2 * rows + 2), samples)
    padded = pltpu.VMEM((8, 2 * LANES), F32)
    work = 2 * angles * rows * traces * samples * 256 * 4

    given = (seismic, validity, avo_coeffs, wavelets, prior_weight, lateral_strength.reshape(1, -1))
    edge = shape(contrasts * samples // LANES + 1, traces, LANES)
    b, near, far, *kept = call(
        start_kernel,
        (field, edge, edge, *[jax.ShapeDtypeStruct(x.shape, x.dtype) for x in given[1:]]),
        [pltpu.with_memory_space_constraint(x, pltpu.HBM) for x in given],
        work,
        [pltpu.VMEM(seismic.shape, seismic.dtype), padded, pltpu.SemaphoreType.DMA((6,))],
        [HBM] * 6,
    )
    avo, taps, strength = kept[1], kept[2], kept[-1]
    near = swap("inline", near, 0)
    near_next = swap("inline", far, 1)
    far_next = hand_on("inline", near)
    far = swap("inline", far, 0)
    (part,) = call(part_kernel, (field,), (b, *kept), 2 * work, [padded])
    image, col_pair, col_other = call(
        rows_kernel, (field, side, side), (b, part, near, near_next, strength), 4 * field.size
    )
    col_other = swap("col", col_other, 1)
    col_pair = swap("col", col_pair, 0)
    (halo,) = call(
        halo_kernel,
        (shape(2, contrasts, traces, samples),),
        (b, near, near_next, far_next, far, avo, taps, strength),
        2 * work,
        [padded],
    )
    axes = ("inline", "col")
    one, two, gram = call(
        image_kernel,
        (field, field, shape(lax.axis_size(axes), 1, LANES)),
        (b, image, halo, col_other, col_pair, *kept),
        2 * work,
        [padded],
    )
    gram = lax.all_to_all(gram, axes, 0, 0)
    return tuple(call(finish_kernel, (field, field), (gram, b, one, two), 8 * field.size))


def solution(mesh):
    placed = (
        P(None, "inline", "col", None),
        P(None, "inline", "col"),
        P("inline", "col"),
        P(),
        P(),
        P(),
    )
    return jax.shard_map(
        shards,
        mesh=mesh,
        in_specs=placed,
        out_specs=(P(None, "inline", "col", None), P(None, "inline", "col", None)),
        check_vma=False,
    )
```

```python
import functools

import jax
import jax.numpy as jnp
from jax import lax
from jax.experimental import pallas as pl
from jax.experimental.pallas import tpu as pltpu
from jax.sharding import PartitionSpec as P

LANES = 128
F32 = jnp.float32
BF16 = jnp.bfloat16


def split(value):
    high = value.astype(BF16)
    return high, (value - high.astype(F32)).astype(BF16)


def circulant(padded_ref, angle):
    line = jnp.broadcast_to(padded_ref[angle : angle + 1, :], (2 * LANES, 2 * LANES))
    return pltpu.roll(line, LANES, 1, stride=1, stride_axis=0)


def fill_taps(taps_ref, padded_ref):
    padded_ref[...] = jnp.zeros_like(padded_ref)
    padded_ref[0 : taps_ref.shape[0], 0 : taps_ref.shape[1]] = taps_ref[...]


def forward_band(circ):
    return jnp.concatenate(split(circ[:, :LANES]), axis=1)


def backward_band(circ):
    return jnp.concatenate(split(circ[LANES:, :]), axis=0)


def column(row):
    n = row.shape[1]
    same = lax.broadcasted_iota(jnp.int32, (n, n), 0) == lax.broadcasted_iota(jnp.int32, (n, n), 1)
    return jnp.sum(jnp.where(same, jnp.broadcast_to(row, (n, n)), 0.0), axis=1, keepdims=True)


def trace_columns(ref, *lead):
    rows = ref[lead].astype(F32)
    return jnp.concatenate([column(rows[r : r + 1, :]) for r in range(rows.shape[0])], axis=0)


def windows(tiles):
    pairs = [jnp.concatenate(pair, axis=1) for pair in zip(tiles[:-1], tiles[1:])]
    return jnp.concatenate(pairs, axis=0)


def halves_sum(wide):
    return wide[:, :LANES] + wide[:, LANES:]


def forward(tiles, band):
    zero = jnp.zeros_like(tiles[0]).astype(BF16)
    highs, lows = zip(*[split(t) for t in tiles])
    n, size = len(tiles) + 1, tiles[0].shape[0]
    rows = [windows([zero, *part, zero]) for part in (highs, lows)]
    out = jnp.dot(jnp.concatenate(rows, axis=0), band, preferred_element_type=F32)
    out = halves_sum(out)
    out = out[: n * size] + out[n * size :]
    return [out[k * size : (k + 1) * size] for k in range(n)]


def backward(parts, band):
    n, size = len(parts[0]) - 1, parts[0][0].shape[0]
    rows = jnp.concatenate([windows(part) for part in parts], axis=0)
    out = lax.dot_general(rows, band, (((1,), (1,)), ((), ())), preferred_element_type=F32)
    out = halves_sum(out)
    total = out[: n * size]
    for p in range(1, len(parts)):
        total = total + out[p * n * size : (p + 1) * n * size]
    return [total[k * size : (k + 1) * size] for k in range(n)]


def coeff(avo_ref, angle, contrast, k):
    return avo_ref[contrast, angle : angle + 1, pl.ds(k * LANES, LANES)]


def add_terms(total, avo_ref, angle, result):
    for c, line in enumerate(total):
        for k, tile in enumerate(result):
            term = coeff(avo_ref, angle, c, k) * tile
            line[k] = term if angle == 0 else line[k] + term


def store_tiles(out_ref, tiles):
    size = out_ref.shape[2]
    for c in range(out_ref.shape[0]):
        for k, tile in enumerate(tiles[c]):
            for r in range(out_ref.shape[1]):
                out_ref[c, r, :, pl.ds(k * LANES, LANES)] = tile[r * size : (r + 1) * size]


def right_side(seis_ref, masks, avo_ref, circs):
    angles, rows, _, samples = seis_ref.shape
    n = samples // LANES
    total = [[None] * n for _ in range(avo_ref.shape[0])]
    for a in range(angles):
        data = jnp.concatenate([seis_ref[a, r].astype(F32) for r in range(rows)], axis=0)
        data = data * masks[a]
        turned = [
            pltpu.roll(data[:, k * LANES : (k + 1) * LANES], LANES // 2, 1) for k in range(n)
        ]
        zero = jnp.zeros_like(turned[0])
        left_half = lax.broadcasted_iota(jnp.int32, zero.shape, 1) < LANES // 2
        shifted = [
            jnp.where(left_half, before, here).astype(BF16)
            for before, here in zip([zero, *turned], [*turned, zero])
        ]
        add_terms(total, avo_ref, a, backward([shifted], backward_band(circs[a])))
    return total


def normal(field, masks, avo_ref, circs):
    contrasts, n = len(field), len(field[0])
    total = [[None] * n for _ in range(contrasts)]
    for a, circ in enumerate(circs):
        mixed = []
        for k in range(n):
            parts = [coeff(avo_ref, a, c, k) * field[c][k] for c in range(contrasts)]
            mixed.append(functools.reduce(jnp.add, parts))
        synth = [tile * masks[a] for tile in forward(mixed, forward_band(circ))]
        left_half = lax.broadcasted_iota(jnp.int32, synth[0].shape, 1) < LANES // 2
        synth[0] = jnp.where(left_half, 0.0, synth[0])
        synth[n] = jnp.where(left_half, synth[n], 0.0)
        result = backward(list(zip(*[split(t) for t in synth])), backward_band(circ))
        add_terms(total, avo_ref, a, result)
    return total


def lateral(here, north, south, west, east):
    traces = here.shape[0]
    place = lax.broadcasted_iota(jnp.int32, here.shape, 0)
    from_west = jnp.where(place == 0, 0.0 if west is None else west, pltpu.roll(here, 1, 0))
    from_east = jnp.where(
        place == traces - 1, 0.0 if east is None else east, pltpu.roll(here, traces - 1, 0)
    )
    around = from_west + from_east
    for other in (north, south):
        around = around if other is None else around + other
    return around


def copy_in(pairs, sems):
    copies = [pltpu.make_async_copy(a, b, sems.at[i]) for i, (a, b) in enumerate(pairs)]
    for copy in copies:
        copy.start()
    return copies


def start_kernel(
    seis_hbm, valid_hbm, avo_hbm, taps_hbm, prior_hbm, strength_hbm,
    b_ref, near_ref, far_ref, valid_ref, avo_ref, taps_ref, prior_ref, strength_ref,
    seis_ref, padded, sems,
):
    copies = copy_in(
        (
            (taps_hbm, taps_ref),
            (valid_hbm, valid_ref),
            (avo_hbm, avo_ref),
            (seis_hbm, seis_ref),
            (prior_hbm, prior_ref),
            (strength_hbm, strength_ref),
        ),
        sems,
    )
    for copy in copies[:2]:
        copy.wait()
    fill_taps(taps_ref, padded)
    angles = avo_ref.shape[1]
    circs = [circulant(padded, a) for a in range(angles)]
    masks = [trace_columns(valid_ref, a) for a in range(angles)]
    for copy in copies[2:]:
        copy.wait()
    store_tiles(b_ref, right_side(seis_ref, masks, avo_ref, circs))
    contrasts, rows, traces, samples = b_ref.shape
    n = samples // LANES
    first = starts_pair("inline")
    lane = lax.broadcasted_iota(jnp.int32, (traces, LANES), 1)
    notes = []
    for r in (0, rows - 1):
        note = jnp.where(lane == angles, column(prior_ref[r : r + 1, :]), 0.0)
        for a in range(angles):
            note = jnp.where(lane == a, masks[a][r * traces : (r + 1) * traces], note)
        notes.append(note)
    edges = [
        [*[b_ref[c, r, :, pl.ds(k * LANES, LANES)] for c in range(contrasts) for k in range(n)], note]
        for r, note in zip((0, rows - 1), notes)
    ]
    for e, (top, bottom) in enumerate(zip(*edges)):
        near_ref[e] = jnp.where(first, bottom, top)
        far_ref[e] = jnp.where(first, top, bottom)


def either_side(pair_ref, next_ref, *where):
    first = starts_pair("inline")
    pair, other = pair_ref[where], next_ref[where]
    return jnp.where(first, other, pair), jnp.where(first, pair, other)


def halo_kernel(
    b_ref, near_ref, near_next_ref, far_next_ref, far_ref, avo_ref, taps_ref, strength_ref,
    out_ref, padded,
):
    contrasts, rows, traces, samples = b_ref.shape
    angles, n = avo_ref.shape[1], samples // LANES
    has = inside("inline")
    fill_taps(taps_ref, padded)
    circs = [circulant(padded, a) for a in range(angles)]
    notes = either_side(near_ref, near_next_ref, contrasts * n)
    masks = [
        jnp.concatenate([note[:, a : a + 1] for note in notes], axis=0) for a in range(angles)
    ]
    field = [
        [
            jnp.concatenate(either_side(near_ref, near_next_ref, c * n + k), axis=0)
            for k in range(n)
        ]
        for c in range(contrasts)
    ]
    total = normal(field, masks, avo_ref, circs)
    for c in range(contrasts):
        strength = strength_ref[:, c : c + 1]
        for side, own in ((0, 0), (1, rows - 1)):
            weight = notes[side][:, angles : angles + 1] + 4.0
            lines = slice(side * traces, (side + 1) * traces)
            here = jnp.concatenate([tile[lines] for tile in field[c]], axis=1)
            beyond = jnp.concatenate(
                [either_side(far_ref, far_next_ref, c * n + k)[side] for k in range(n)], axis=1
            )
            around = lateral(here, beyond, has[side] * b_ref[c, own], None, None)
            data = jnp.concatenate([tile[lines] for tile in total[c]], axis=1)
            out_ref[side, c] = data + strength * (weight * here - around)


def stack_tiles(ref):
    contrasts, rows, _, samples = ref.shape
    return [
        [
            jnp.concatenate([ref[c, r, :, pl.ds(k, LANES)] for r in range(rows)], axis=0)
            for k in range(0, samples, LANES)
        ]
        for c in range(contrasts)
    ]


def inside(axis):
    place = lax.axis_index(axis)
    last = lax.axis_size(axis) - 1
    return (place > 0).astype(F32), (place < last).astype(F32)


def starts_pair(axis):
    return lax.axis_index(axis) % 2 == 0


def row_pair(near_ref, next_ref, c, n):
    tiles = [either_side(near_ref, next_ref, c * n + k) for k in range(n)]
    return [jnp.concatenate(side, axis=1) for side in zip(*tiles)]


def column_kernel(b_ref, near_ref, near_next_ref, valid_ref, prior_ref, pair_ref, other_ref):
    contrasts, rows, traces, samples = b_ref.shape
    angles = valid_ref.shape[0]
    first_col = starts_pair("col")
    lines = []
    for c in range(contrasts):
        above, below = row_pair(near_ref, near_next_ref, c, samples // LANES)
        own = [b_ref[c, r] for r in range(rows)]
        lines += [(line[0:1], line[traces - 1 :]) for line in (above, *own, below)]
        lines += [(line[1:2], line[traces - 2 : traces - 1]) for line in own]
    for e, (left, right) in enumerate(lines):
        place = (slice(e % rows, e % rows + 1), pl.ds(e // rows * samples, samples))
        pair_ref[place] = jnp.where(first_col, right, left)
        other_ref[place] = jnp.where(first_col, left, right)
    lane = lax.broadcasted_iota(jnp.int32, (1, LANES), 1)
    for r in range(rows):
        notes = []
        for t in (0, traces - 1):
            note = jnp.where(lane == angles, prior_ref[r : r + 1, t : t + 1], 0.0)
            for a in range(angles):
                note = jnp.where(lane == a, valid_ref[a, r : r + 1, t : t + 1].astype(F32), note)
            notes.append(note)
        left, right = notes
        place = (slice(r, r + 1), pl.ds(len(lines) // rows * samples, LANES))
        pair_ref[place] = jnp.where(first_col, right, left)
        other_ref[place] = jnp.where(first_col, left, right)


def inner_kernel(
    b_ref, near_ref, near_next_ref, valid_ref, avo_ref, taps_ref, prior_ref, strength_ref,
    v_ref, data_ref, padded,
):
    contrasts, rows, _, samples = b_ref.shape
    fill_taps(taps_ref, padded)
    angles = avo_ref.shape[1]
    circs = [circulant(padded, a) for a in range(angles)]
    masks = [trace_columns(valid_ref, a) for a in range(angles)]
    store_tiles(v_ref, normal(stack_tiles(b_ref), masks, avo_ref, circs))
    weights = [column(prior_ref[r : r + 1, :]) + 4.0 for r in range(rows)]
    for c in range(contrasts):
        strength = strength_ref[:, c : c + 1]
        above, below = row_pair(near_ref, near_next_ref, c, samples // LANES)
        for r in range(rows):
            here = b_ref[c, r]
            north = b_ref[c, r - 1] if r else above
            south = b_ref[c, r + 1] if r < rows - 1 else below
            around = lateral(here, north, south, None, None)
            v_ref[c, r] = v_ref[c, r] + strength * (weights[r] * here - around)
    store_tiles(data_ref, normal(stack_tiles(v_ref), masks, avo_ref, circs))


def image_kernel(
    b_ref, v_ref, data_ref, halo_ref, other_ref, pair_ref,
    valid_ref, avo_ref, taps_ref, prior_ref, strength_ref,
    one_ref, two_ref, gram_ref, padded,
):
    contrasts, rows, traces, samples = b_ref.shape
    angles, n = avo_ref.shape[1], samples // LANES
    has_left, has_right = inside("col")
    first_col = starts_pair("col")
    left = jnp.where(first_col, other_ref[...], pair_ref[...])
    right = jnp.where(first_col, pair_ref[...], other_ref[...])
    place = lax.broadcasted_iota(jnp.int32, (traces, samples), 0)
    ext = rows + 2

    def trace(side, c, i):
        e = c * (ext + rows) + i
        return side[e % rows : e % rows + 1, e // rows * samples : (e // rows + 1) * samples]

    def note(side, r, i):
        at = contrasts * (ext + rows) // rows * samples + i
        return side[r : r + 1, at : at + 1]

    def beside(c, i):
        west, east = trace(left, c, i), trace(right, c, i)
        return jnp.where(place == 0, west, jnp.where(place == traces - 1, east, 0.0))

    def spread(values):
        total = values[-1]
        for t in range(traces - 2, -1, -1):
            total = jnp.where(place[:, : values[0].shape[1]] == t, values[t], total)
        return total

    fill_taps(taps_ref, padded)
    circs = [circulant(padded, a) for a in range(angles)]
    masks = []
    for a in range(angles):
        own = [
            [valid_ref[a, r : r + 1, t : t + 1].astype(F32) for r in range(rows)]
            for t in (0, traces - 1)
        ]
        west, east = ([note(side, r, a) for r in range(rows)] for side in (left, right))
        masks.append(spread([*own[0], *west, *east[::-1], *own[1][::-1]]))
    tile = []
    for c in range(contrasts):
        strength = strength_ref[:, c : c + 1]
        west, east = ([trace(side, c, r + 1) for r in range(rows)] for side in (left, right))
        less = [-strength * line for line in west], [-strength * line for line in east]
        whole = spread([*less[0], *west, *east[::-1], *less[1][::-1]])
        tile.append([whole[:, k * LANES : (k + 1) * LANES] for k in range(n)])
    edge = [jnp.concatenate(line, axis=1) for line in normal(tile, masks, avo_ref, circs)]

    weights = [column(prior_ref[r : r + 1, :]) + 4.0 for r in range(rows)]
    sums = [jnp.zeros((traces, LANES), F32) for _ in range(4)]
    for c in range(contrasts):
        strength = strength_ref[:, c : c + 1]
        lines = [halo_ref[0, c], *[v_ref[c, r] for r in range(rows)], halo_ref[1, c]]
        lines = [line - strength * beside(c, i) for i, line in enumerate(lines)]
        for r in range(rows):
            here, b = lines[r + 1], b_ref[c, r]
            beyond = []
            for side, has, t, u in (
                (left, has_left, 0, rows + r),
                (right, has_right, traces - 1, traces - rows - 1 - r),
            ):
                weight = note(side, r, angles) + 4.0
                around = trace(side, c, r) + trace(side, c, r + 2) + trace(side, c, ext + r)
                around = around + has * b[t : t + 1]
                prior = strength * (weight * trace(side, c, r + 1) - around)
                beyond.append(edge[c][u : u + 1] + prior)
            around = lateral(here, lines[r], lines[r + 2], *beyond)
            first, last = edge[c][r : r + 1], edge[c][traces - 1 - r : traces - r]
            mend = jnp.where(place == 0, first, jnp.where(place == traces - 1, last, 0.0))
            two = data_ref[c, r] + mend + strength * (weights[r] * here - around)
            one_ref[c, r] = here
            two_ref[c, r] = two
            for q, product in enumerate((b * b, b * here, here * here, here * two)):
                tiles = [product[:, k : k + LANES] for k in range(0, samples, LANES)]
                sums[q] = sums[q] + functools.reduce(jnp.add, tiles)
    lane = lax.broadcasted_iota(jnp.int32, (1, LANES), 1)
    packed = jnp.zeros((1, LANES), F32)
    for q, total in enumerate(sums):
        total = jnp.sum(jnp.sum(total, axis=0, keepdims=True), axis=1, keepdims=True)
        packed = jnp.where(lane == q, total, packed)
    gram_ref[...] = jnp.broadcast_to(packed[None], gram_ref.shape)


def finish_kernel(gram_ref, b_ref, one_ref, two_ref, solution_ref, residual_ref):
    sums = jnp.sum(gram_ref[...], axis=0)
    g00, g01, g11, g12 = (sums[:, q : q + 1] for q in range(4))
    first = g00 / g01
    ratio = first * g11 / g01
    second = (ratio - 1.0) * g01 / (first * g12 - ratio * g11)
    near = first + second * ratio
    far = first * second
    for c in range(b_ref.shape[0]):
        for r in range(b_ref.shape[1]):
            b, one, two = b_ref[c, r], one_ref[c, r], two_ref[c, r]
            solution_ref[c, r] = near * b - far * one
            residual_ref[c, r] = b - near * one + far * two


VMEM = pl.BlockSpec(memory_space=pltpu.VMEM)
HBM = pl.BlockSpec(memory_space=pltpu.HBM)


def call(kernel, outs, ins, flops, scratch=(), places=None):
    moved = sum(x.size * x.dtype.itemsize for x in (*ins, *outs))
    return pl.pallas_call(
        kernel,
        out_shape=outs,
        in_specs=[VMEM] * len(ins) if places is None else places,
        out_specs=jax.tree.map(lambda _: VMEM, outs),
        scratch_shapes=list(scratch),
        compiler_params=pltpu.CompilerParams(vmem_limit_bytes=24 * 1024 * 1024),
        cost_estimate=pl.CostEstimate(flops=flops, bytes_accessed=moved, transcendentals=0),
        name=kernel.__name__,
    )(*ins)


def swap(axis, value, first):
    starts = range(first, lax.axis_size(axis) - 1, 2)
    return lax.ppermute(value, axis, [(i + d, i + 1 - d) for i in starts for d in (0, 1)])


def hand_on(axis, value):
    size = lax.axis_size(axis)
    steps = [(i, i + 2 - 4 * (i % 2)) for i in range(size)]
    return lax.ppermute(value, axis, [(i, j) for i, j in steps if 0 <= j < size])


def shards(seismic, validity, prior_weight, lateral_strength, avo_coeffs, wavelets):
    angles, rows, traces, samples = seismic.shape
    contrasts = avo_coeffs.shape[1]
    avo_coeffs = jnp.swapaxes(avo_coeffs, 0, 1)
    shape = lambda *dims: jax.ShapeDtypeStruct(dims, F32)
    field = shape(contrasts, rows, traces, samples)
    side = shape(rows, contrasts * (2 * rows + 2) // rows * samples + LANES)
    padded = pltpu.VMEM((8, 2 * LANES), F32)
    work = 2 * angles * rows * traces * samples * 256 * 4

    given = (seismic, validity, avo_coeffs, wavelets, prior_weight, lateral_strength.reshape(1, -1))
    edge = shape(contrasts * samples // LANES + 1, traces, LANES)
    b, near, far, *kept = call(
        start_kernel,
        (field, edge, edge, *[jax.ShapeDtypeStruct(x.shape, x.dtype) for x in given[1:]]),
        [pltpu.with_memory_space_constraint(x, pltpu.HBM) for x in given],
        work,
        [pltpu.VMEM(seismic.shape, seismic.dtype), padded, pltpu.SemaphoreType.DMA((6,))],
        [HBM] * 6,
    )
    avo, taps, strength = kept[1], kept[2], kept[-1]
    near = swap("inline", near, 0)
    near_next = swap("inline", far, 1)
    far_next = hand_on("inline", near)
    far = swap("inline", far, 0)
    col_pair, col_other = call(
        column_kernel, (side, side), (b, near, near_next, kept[0], kept[3]), 2 * field.size
    )
    col_other = swap("col", col_other, 1)
    col_pair = swap("col", col_pair, 0)
    image, data = call(
        inner_kernel, (field, field), (b, near, near_next, *kept), 4 * work, [padded]
    )
    (halo,) = call(
        halo_kernel,
        (shape(2, contrasts, traces, samples),),
        (b, near, near_next, far_next, far, avo, taps, strength),
        2 * work,
        [padded],
    )
    axes = ("inline", "col")
    one, two, gram = call(
        image_kernel,
        (field, field, shape(lax.axis_size(axes), 1, LANES)),
        (b, image, data, halo, col_other, col_pair, *kept),
        2 * work,
        [padded],
    )
    gram = lax.all_to_all(gram, axes, 0, 0)
    return tuple(call(finish_kernel, (field, field), (gram, b, one, two), 8 * field.size))


def solution(mesh):
    placed = (
        P(None, "inline", "col", None),
        P(None, "inline", "col"),
        P("inline", "col"),
        P(),
        P(),
        P(),
    )
    return jax.shard_map(
        shards,
        mesh=mesh,
        in_specs=placed,
        out_specs=(P(None, "inline", "col", None), P(None, "inline", "col", None)),
        check_vma=False,
    )
```

```python
import functools

import jax
import jax.numpy as jnp
from jax import lax
from jax.experimental import pallas as pl
from jax.experimental.pallas import tpu as pltpu
from jax.sharding import PartitionSpec as P

LANES = 128
F32 = jnp.float32
BF16 = jnp.bfloat16


def split(value):
    high = value.astype(BF16)
    return high, (value - high.astype(F32)).astype(BF16)


def circulant(padded_ref, angle):
    line = jnp.broadcast_to(padded_ref[angle : angle + 1, :], (2 * LANES, 2 * LANES))
    return pltpu.roll(line, LANES, 1, stride=1, stride_axis=0)


def fill_taps(taps_ref, padded_ref):
    padded_ref[...] = jnp.zeros_like(padded_ref)
    padded_ref[0 : taps_ref.shape[0], 0 : taps_ref.shape[1]] = taps_ref[...]


def forward_band(circ):
    return jnp.concatenate(split(circ[:, :LANES]), axis=1)


def backward_band(circ):
    return jnp.concatenate(split(circ[LANES:, :]), axis=0)


def column(row):
    n = row.shape[1]
    same = lax.broadcasted_iota(jnp.int32, (n, n), 0) == lax.broadcasted_iota(jnp.int32, (n, n), 1)
    return jnp.sum(jnp.where(same, jnp.broadcast_to(row, (n, n)), 0.0), axis=1, keepdims=True)


def trace_columns(ref, *lead):
    rows = ref[lead].astype(F32)
    return jnp.concatenate([column(rows[r : r + 1, :]) for r in range(rows.shape[0])], axis=0)


def windows(tiles):
    pairs = [jnp.concatenate(pair, axis=1) for pair in zip(tiles[:-1], tiles[1:])]
    return jnp.concatenate(pairs, axis=0)


def halves_sum(wide):
    return wide[:, :LANES] + wide[:, LANES:]


def forward(tiles, band):
    zero = jnp.zeros_like(tiles[0]).astype(BF16)
    highs, lows = zip(*[split(t) for t in tiles])
    n, size = len(tiles) + 1, tiles[0].shape[0]
    rows = [windows([zero, *part, zero]) for part in (highs, lows)]
    out = jnp.dot(jnp.concatenate(rows, axis=0), band, preferred_element_type=F32)
    out = halves_sum(out)
    out = out[: n * size] + out[n * size :]
    return [out[k * size : (k + 1) * size] for k in range(n)]


def backward(parts, band):
    n, size = len(parts[0]) - 1, parts[0][0].shape[0]
    rows = jnp.concatenate([windows(part) for part in parts], axis=0)
    out = lax.dot_general(rows, band, (((1,), (1,)), ((), ())), preferred_element_type=F32)
    out = halves_sum(out)
    total = out[: n * size]
    for p in range(1, len(parts)):
        total = total + out[p * n * size : (p + 1) * n * size]
    return [total[k * size : (k + 1) * size] for k in range(n)]


def coeff(avo_ref, angle, contrast, k):
    return avo_ref[contrast, angle : angle + 1, pl.ds(k * LANES, LANES)]


def add_terms(total, avo_ref, angle, result):
    for c, line in enumerate(total):
        for k, tile in enumerate(result):
            term = coeff(avo_ref, angle, c, k) * tile
            line[k] = term if angle == 0 else line[k] + term


def store_tiles(out_ref, tiles):
    size = out_ref.shape[2]
    for c in range(out_ref.shape[0]):
        for k, tile in enumerate(tiles[c]):
            for r in range(out_ref.shape[1]):
                out_ref[c, r, :, pl.ds(k * LANES, LANES)] = tile[r * size : (r + 1) * size]


def right_side(seis_ref, masks, avo_ref, circs):
    angles, rows, _, samples = seis_ref.shape
    n = samples // LANES
    total = [[None] * n for _ in range(avo_ref.shape[0])]
    for a in range(angles):
        data = jnp.concatenate([seis_ref[a, r].astype(F32) for r in range(rows)], axis=0)
        data = data * masks[a]
        turned = [
            pltpu.roll(data[:, k * LANES : (k + 1) * LANES], LANES // 2, 1) for k in range(n)
        ]
        zero = jnp.zeros_like(turned[0])
        left_half = lax.broadcasted_iota(jnp.int32, zero.shape, 1) < LANES // 2
        shifted = [
            jnp.where(left_half, before, here).astype(BF16)
            for before, here in zip([zero, *turned], [*turned, zero])
        ]
        add_terms(total, avo_ref, a, backward([shifted], backward_band(circs[a])))
    return total


def normal(field, masks, avo_ref, bands):
    contrasts, n = len(field), len(field[0])
    total = [[None] * n for _ in range(contrasts)]
    for a, (ahead, back) in enumerate(bands):
        mixed = []
        for k in range(n):
            parts = [coeff(avo_ref, a, c, k) * field[c][k] for c in range(contrasts)]
            mixed.append(functools.reduce(jnp.add, parts))
        synth = [tile * masks[a] for tile in forward(mixed, ahead)]
        left_half = lax.broadcasted_iota(jnp.int32, synth[0].shape, 1) < LANES // 2
        synth[0] = jnp.where(left_half, 0.0, synth[0])
        synth[n] = jnp.where(left_half, synth[n], 0.0)
        result = backward(list(zip(*[split(t) for t in synth])), back)
        add_terms(total, avo_ref, a, result)
    return total


def lateral(here, north, south, west, east):
    traces = here.shape[0]
    place = lax.broadcasted_iota(jnp.int32, here.shape, 0)
    from_west = jnp.where(place == 0, 0.0 if west is None else west, pltpu.roll(here, 1, 0))
    from_east = jnp.where(
        place == traces - 1, 0.0 if east is None else east, pltpu.roll(here, traces - 1, 0)
    )
    around = from_west + from_east
    for other in (north, south):
        around = around if other is None else around + other
    return around


def copy_in(pairs, sems):
    copies = [pltpu.make_async_copy(a, b, sems.at[i]) for i, (a, b) in enumerate(pairs)]
    for copy in copies:
        copy.start()
    return copies


def start_kernel(
    seis_hbm, valid_hbm, avo_hbm, taps_hbm, prior_hbm, strength_hbm,
    b_ref, near_ref, far_ref, valid_ref, avo_ref, taps_ref, prior_ref, strength_ref,
    seis_ref, padded, sems,
):
    copies = copy_in(
        (
            (taps_hbm, taps_ref),
            (valid_hbm, valid_ref),
            (avo_hbm, avo_ref),
            (seis_hbm, seis_ref),
            (prior_hbm, prior_ref),
            (strength_hbm, strength_ref),
        ),
        sems,
    )
    for copy in copies[:2]:
        copy.wait()
    fill_taps(taps_ref, padded)
    angles = avo_ref.shape[1]
    circs = [circulant(padded, a) for a in range(angles)]
    masks = [trace_columns(valid_ref, a) for a in range(angles)]
    for copy in copies[2:]:
        copy.wait()
    store_tiles(b_ref, right_side(seis_ref, masks, avo_ref, circs))
    contrasts, rows, traces, samples = b_ref.shape
    n = samples // LANES
    first = starts_pair("inline")
    lane = lax.broadcasted_iota(jnp.int32, (traces, LANES), 1)
    notes = []
    for r in (0, rows - 1):
        note = jnp.where(lane == angles, column(prior_ref[r : r + 1, :]), 0.0)
        for a in range(angles):
            note = jnp.where(lane == a, masks[a][r * traces : (r + 1) * traces], note)
        notes.append(note)
    edges = [
        [*[b_ref[c, r, :, pl.ds(k * LANES, LANES)] for c in range(contrasts) for k in range(n)], note]
        for r, note in zip((0, rows - 1), notes)
    ]
    for e, (top, bottom) in enumerate(zip(*edges)):
        near_ref[e] = jnp.where(first, bottom, top)
        far_ref[e] = jnp.where(first, top, bottom)


def either_side(pair_ref, next_ref, *where):
    first = starts_pair("inline")
    pair, other = pair_ref[where], next_ref[where]
    return jnp.where(first, other, pair), jnp.where(first, pair, other)


def stack_tiles(ref):
    contrasts, rows, _, samples = ref.shape
    return [
        [
            jnp.concatenate([ref[c, r, :, pl.ds(k, LANES)] for r in range(rows)], axis=0)
            for k in range(0, samples, LANES)
        ]
        for c in range(contrasts)
    ]


def inside(axis):
    place = lax.axis_index(axis)
    last = lax.axis_size(axis) - 1
    return (place > 0).astype(F32), (place < last).astype(F32)


def starts_pair(axis):
    return lax.axis_index(axis) % 2 == 0


def row_pair(near_ref, next_ref, c, n):
    tiles = [either_side(near_ref, next_ref, c * n + k) for k in range(n)]
    return [jnp.concatenate(side, axis=1) for side in zip(*tiles)]


def column_kernel(b_ref, near_ref, near_next_ref, valid_ref, prior_ref, pair_ref, other_ref):
    contrasts, rows, traces, samples = b_ref.shape
    angles = valid_ref.shape[0]
    first_col = starts_pair("col")
    lines = []
    for c in range(contrasts):
        above, below = row_pair(near_ref, near_next_ref, c, samples // LANES)
        own = [b_ref[c, r] for r in range(rows)]
        lines += [(line[0:1], line[traces - 1 :]) for line in (above, *own, below)]
        lines += [(line[1:2], line[traces - 2 : traces - 1]) for line in own]
    for e, (left, right) in enumerate(lines):
        place = (slice(e % rows, e % rows + 1), pl.ds(e // rows * samples, samples))
        pair_ref[place] = jnp.where(first_col, right, left)
        other_ref[place] = jnp.where(first_col, left, right)
    lane = lax.broadcasted_iota(jnp.int32, (1, LANES), 1)
    for r in range(rows):
        notes = []
        for t in (0, traces - 1):
            note = jnp.where(lane == angles, prior_ref[r : r + 1, t : t + 1], 0.0)
            for a in range(angles):
                note = jnp.where(lane == a, valid_ref[a, r : r + 1, t : t + 1].astype(F32), note)
            notes.append(note)
        left, right = notes
        place = (slice(r, r + 1), pl.ds(len(lines) // rows * samples, LANES))
        pair_ref[place] = jnp.where(first_col, right, left)
        other_ref[place] = jnp.where(first_col, left, right)


def inner_kernel(
    b_ref, near_ref, near_next_ref, valid_ref, avo_ref, taps_ref, prior_ref, strength_ref,
    v_ref, data_ref, halo_ref, ahead_ref, back_ref, padded,
):
    contrasts, rows, traces, samples = b_ref.shape
    angles, n = avo_ref.shape[1], samples // LANES
    fill_taps(taps_ref, padded)
    bands = []
    for a in range(angles):
        circ = circulant(padded, a)
        bands.append((forward_band(circ), backward_band(circ)))
        ahead_ref[a], back_ref[a] = bands[a]
    masks = [trace_columns(valid_ref, a) for a in range(angles)]
    weights = [column(prior_ref[r : r + 1, :]) + 4.0 for r in range(rows)]
    above, below = either_side(near_ref, near_next_ref, contrasts * n)
    wide = [
        jnp.concatenate([above[:, a : a + 1], mask, below[:, a : a + 1]], axis=0)
        for a, mask in enumerate(masks)
    ]
    weights = [above[:, angles : angles + 1] + 4.0, *weights, below[:, angles : angles + 1] + 4.0]
    field = []
    for c, line in enumerate(stack_tiles(b_ref)):
        ends = [either_side(near_ref, near_next_ref, c * n + k) for k in range(n)]
        field.append(
            [jnp.concatenate([up, own, low], axis=0) for (up, low), own in zip(ends, line)]
        )
    total = normal(field, wide, avo_ref, bands)
    has_above, has_below = inside("inline")
    for c in range(contrasts):
        strength = strength_ref[:, c : c + 1]
        whole, data = jnp.concatenate(field[c], axis=1), jnp.concatenate(total[c], axis=1)
        lines = [whole[r * traces : (r + 1) * traces] for r in range(rows + 2)]
        for r, here in enumerate(lines):
            north = lines[r - 1] if r else None
            south = lines[r + 1] if r < rows + 1 else None
            if r == 0:
                south = has_above * south
            if r == rows + 1:
                north = has_below * north
            around = lateral(here, north, south, None, None)
            image = data[r * traces : (r + 1) * traces] + strength * (weights[r] * here - around)
            if 0 < r <= rows:
                v_ref[c, r - 1] = image
            else:
                halo_ref[min(r, 1), c] = image
    store_tiles(data_ref, normal(stack_tiles(v_ref), masks, avo_ref, bands))


def image_kernel(
    b_ref, v_ref, data_ref, halo_ref, far_next_ref, far_ref, other_ref, pair_ref,
    valid_ref, avo_ref, prior_ref, strength_ref, ahead_ref, back_ref,
    one_ref, two_ref, gram_ref,
):
    contrasts, rows, traces, samples = b_ref.shape
    angles, n = avo_ref.shape[1], samples // LANES
    has_left, has_right = inside("col")
    first_col = starts_pair("col")
    left = jnp.where(first_col, other_ref[...], pair_ref[...])
    right = jnp.where(first_col, pair_ref[...], other_ref[...])
    place = lax.broadcasted_iota(jnp.int32, (traces, samples), 0)
    ext = rows + 2

    def trace(side, c, i):
        e = c * (ext + rows) + i
        return side[e % rows : e % rows + 1, e // rows * samples : (e // rows + 1) * samples]

    def note(side, r, i):
        at = contrasts * (ext + rows) // rows * samples + i
        return side[r : r + 1, at : at + 1]

    def beside(c, i):
        west, east = trace(left, c, i), trace(right, c, i)
        return jnp.where(place == 0, west, jnp.where(place == traces - 1, east, 0.0))

    def spread(values):
        total = values[-1]
        for t in range(traces - 2, -1, -1):
            total = jnp.where(place[:, : values[0].shape[1]] == t, values[t], total)
        return total

    bands = [(ahead_ref[a], back_ref[a]) for a in range(angles)]
    masks = []
    for a in range(angles):
        own = [
            [valid_ref[a, r : r + 1, t : t + 1].astype(F32) for r in range(rows)]
            for t in (0, traces - 1)
        ]
        west, east = ([note(side, r, a) for r in range(rows)] for side in (left, right))
        masks.append(spread([*own[0], *west, *east[::-1], *own[1][::-1]]))
    tile = []
    for c in range(contrasts):
        strength = strength_ref[:, c : c + 1]
        west, east = ([trace(side, c, r + 1) for r in range(rows)] for side in (left, right))
        less = [-strength * line for line in west], [-strength * line for line in east]
        whole = spread([*less[0], *west, *east[::-1], *less[1][::-1]])
        tile.append([whole[:, k * LANES : (k + 1) * LANES] for k in range(n)])
    edge = [jnp.concatenate(line, axis=1) for line in normal(tile, masks, avo_ref, bands)]

    weights = [column(prior_ref[r : r + 1, :]) + 4.0 for r in range(rows)]
    sums = [jnp.zeros((traces, LANES), F32) for _ in range(4)]
    for c in range(contrasts):
        strength = strength_ref[:, c : c + 1]
        beyond = row_pair(far_ref, far_next_ref, c, n)
        over, under = (halo_ref[i, c] - strength * beyond[i] for i in (0, 1))
        lines = [over, *[v_ref[c, r] for r in range(rows)], under]
        lines = [line - strength * beside(c, i) for i, line in enumerate(lines)]
        for r in range(rows):
            here, b = lines[r + 1], b_ref[c, r]
            beyond = []
            for side, has, t, u in (
                (left, has_left, 0, rows + r),
                (right, has_right, traces - 1, traces - rows - 1 - r),
            ):
                weight = note(side, r, angles) + 4.0
                around = trace(side, c, r) + trace(side, c, r + 2) + trace(side, c, ext + r)
                around = around + has * b[t : t + 1]
                prior = strength * (weight * trace(side, c, r + 1) - around)
                beyond.append(edge[c][u : u + 1] + prior)
            around = lateral(here, lines[r], lines[r + 2], *beyond)
            first, last = edge[c][r : r + 1], edge[c][traces - 1 - r : traces - r]
            mend = jnp.where(place == 0, first, jnp.where(place == traces - 1, last, 0.0))
            two = data_ref[c, r] + mend + strength * (weights[r] * here - around)
            one_ref[c, r] = here
            two_ref[c, r] = two
            for q, product in enumerate((b * b, b * here, here * here, here * two)):
                tiles = [product[:, k : k + LANES] for k in range(0, samples, LANES)]
                sums[q] = sums[q] + functools.reduce(jnp.add, tiles)
    lane = lax.broadcasted_iota(jnp.int32, (1, LANES), 1)
    packed = jnp.zeros((1, LANES), F32)
    for q, total in enumerate(sums):
        total = jnp.sum(jnp.sum(total, axis=0, keepdims=True), axis=1, keepdims=True)
        packed = jnp.where(lane == q, total, packed)
    gram_ref[...] = jnp.broadcast_to(packed[None], gram_ref.shape)


def finish_kernel(gram_ref, b_ref, one_ref, two_ref, solution_ref, residual_ref):
    sums = jnp.sum(gram_ref[...], axis=0)
    g00, g01, g11, g12 = (sums[:, q : q + 1] for q in range(4))
    first = g00 / g01
    ratio = first * g11 / g01
    second = (ratio - 1.0) * g01 / (first * g12 - ratio * g11)
    near = first + second * ratio
    far = first * second
    for c in range(b_ref.shape[0]):
        for r in range(b_ref.shape[1]):
            b, one, two = b_ref[c, r], one_ref[c, r], two_ref[c, r]
            solution_ref[c, r] = near * b - far * one
            residual_ref[c, r] = b - near * one + far * two


VMEM = pl.BlockSpec(memory_space=pltpu.VMEM)
HBM = pl.BlockSpec(memory_space=pltpu.HBM)


def call(kernel, outs, ins, flops, scratch=(), places=None):
    moved = sum(x.size * x.dtype.itemsize for x in (*ins, *outs))
    return pl.pallas_call(
        kernel,
        out_shape=outs,
        in_specs=[VMEM] * len(ins) if places is None else places,
        out_specs=jax.tree.map(lambda _: VMEM, outs),
        scratch_shapes=list(scratch),
        compiler_params=pltpu.CompilerParams(vmem_limit_bytes=24 * 1024 * 1024),
        cost_estimate=pl.CostEstimate(flops=flops, bytes_accessed=moved, transcendentals=0),
        name=kernel.__name__,
    )(*ins)


def swap(axis, value, first):
    starts = range(first, lax.axis_size(axis) - 1, 2)
    return lax.ppermute(value, axis, [(i + d, i + 1 - d) for i in starts for d in (0, 1)])


def hand_on(axis, value):
    size = lax.axis_size(axis)
    steps = [(i, i + 2 - 4 * (i % 2)) for i in range(size)]
    return lax.ppermute(value, axis, [(i, j) for i, j in steps if 0 <= j < size])


def shards(seismic, validity, prior_weight, lateral_strength, avo_coeffs, wavelets):
    angles, rows, traces, samples = seismic.shape
    contrasts = avo_coeffs.shape[1]
    avo_coeffs = jnp.swapaxes(avo_coeffs, 0, 1)
    shape = lambda *dims: jax.ShapeDtypeStruct(dims, F32)
    field = shape(contrasts, rows, traces, samples)
    side = shape(rows, contrasts * (2 * rows + 2) // rows * samples + LANES)
    padded = pltpu.VMEM((8, 2 * LANES), F32)
    work = 2 * angles * rows * traces * samples * 256 * 4

    given = (seismic, validity, avo_coeffs, wavelets, prior_weight, lateral_strength.reshape(1, -1))
    edge = shape(contrasts * samples // LANES + 1, traces, LANES)
    b, near, far, *kept = call(
        start_kernel,
        (field, edge, edge, *[jax.ShapeDtypeStruct(x.shape, x.dtype) for x in given[1:]]),
        [pltpu.with_memory_space_constraint(x, pltpu.HBM) for x in given],
        work,
        [pltpu.VMEM(seismic.shape, seismic.dtype), padded, pltpu.SemaphoreType.DMA((6,))],
        [HBM] * 6,
    )
    near = swap("inline", near, 0)
    near_next = swap("inline", far, 1)
    far_next = hand_on("inline", near)
    far = swap("inline", far, 0)
    col_pair, col_other = call(
        column_kernel, (side, side), (b, near, near_next, kept[0], kept[3]), 2 * field.size
    )
    col_other = swap("col", col_other, 1)
    col_pair = swap("col", col_pair, 0)
    band = jax.ShapeDtypeStruct((angles, 2 * LANES, 2 * LANES), BF16)
    image, data, halo, ahead, back = call(
        inner_kernel,
        (field, field, shape(2, contrasts, traces, samples), band, band),
        (b, near, near_next, *kept),
        6 * work,
        [padded],
    )
    axes = ("inline", "col")
    one, two, gram = call(
        image_kernel,
        (field, field, shape(lax.axis_size(axes), 1, LANES)),
        (
            b, image, data, halo, far_next, far, col_other, col_pair,
            kept[0], kept[1], kept[3], kept[4], ahead, back,
        ),
        work,
    )
    gram = lax.all_to_all(gram, axes, 0, 0)
    return tuple(call(finish_kernel, (field, field), (gram, b, one, two), 8 * field.size))


def solution(mesh):
    placed = (
        P(None, "inline", "col", None),
        P(None, "inline", "col"),
        P("inline", "col"),
        P(),
        P(),
        P(),
    )
    return jax.shard_map(
        shards,
        mesh=mesh,
        in_specs=placed,
        out_specs=(P(None, "inline", "col", None), P(None, "inline", "col", None)),
        check_vma=False,
    )
```

```python
import functools

import jax
import jax.numpy as jnp
from jax import lax
from jax.experimental import pallas as pl
from jax.experimental.pallas import tpu as pltpu
from jax.sharding import PartitionSpec as P

LANES = 128
F32 = jnp.float32
BF16 = jnp.bfloat16


def split(value):
    high = value.astype(BF16)
    return high, (value - high.astype(F32)).astype(BF16)


def band(taps_ref, angle):
    line = jnp.broadcast_to(taps_ref[angle : angle + 1, :], (2 * LANES, 2 * LANES))
    rolled = pltpu.roll(line, LANES, 1, stride=1, stride_axis=0)
    return jnp.concatenate(split(rolled[:, :LANES]), axis=1)


def fill_taps(taps_ref, padded_ref, turned_ref):
    padded_ref[...] = jnp.zeros_like(padded_ref)
    padded_ref[0 : taps_ref.shape[0], 0 : taps_ref.shape[1]] = taps_ref[...]
    rest, parts = padded_ref[...], []
    for _ in range(3):
        parts.append(rest.astype(BF16).astype(F32))
        rest = rest - parts[-1]
    size = 2 * LANES
    rows = lax.broadcasted_iota(jnp.int32, (size, size), 0)
    cols = lax.broadcasted_iota(jnp.int32, (size, size), 1)
    flip = jnp.where(rows + cols == taps_ref.shape[1] - 1, 1.0, 0.0).astype(BF16)
    lines = jnp.concatenate(parts, axis=0).astype(BF16)
    turned = jnp.dot(lines, flip, preferred_element_type=F32)
    n = padded_ref.shape[0]
    turned_ref[...] = turned[:n] + turned[n : 2 * n] + turned[2 * n :]


def column(row):
    n = row.shape[1]
    same = lax.broadcasted_iota(jnp.int32, (n, n), 0) == lax.broadcasted_iota(jnp.int32, (n, n), 1)
    return jnp.sum(jnp.where(same, jnp.broadcast_to(row, (n, n)), 0.0), axis=1, keepdims=True)


def trace_columns(ref, *lead):
    rows = ref[lead].astype(F32)
    return jnp.concatenate([column(rows[r : r + 1, :]) for r in range(rows.shape[0])], axis=0)


def windows(tiles):
    pairs = [jnp.concatenate(pair, axis=1) for pair in zip(tiles[:-1], tiles[1:])]
    return jnp.concatenate(pairs, axis=0)


def halves_sum(wide):
    return wide[:, :LANES] + wide[:, LANES:]


def forward(tiles, band):
    zero = jnp.zeros_like(tiles[0]).astype(BF16)
    highs, lows = zip(*[split(t) for t in tiles])
    n, size = len(tiles) + 1, tiles[0].shape[0]
    rows = [windows([zero, *part, zero]) for part in (highs, lows)]
    out = jnp.dot(jnp.concatenate(rows, axis=0), band, preferred_element_type=F32)
    out = halves_sum(out)
    out = out[: n * size] + out[n * size :]
    return [out[k * size : (k + 1) * size] for k in range(n)]


def backward(parts, band):
    n, size = len(parts[0]) - 1, parts[0][0].shape[0]
    rows = jnp.concatenate([windows(part) for part in parts], axis=0)
    out = jnp.dot(rows, band, preferred_element_type=F32)
    out = halves_sum(out)
    total = out[: n * size]
    for p in range(1, len(parts)):
        total = total + out[p * n * size : (p + 1) * n * size]
    return [total[k * size : (k + 1) * size] for k in range(n)]


def coeff(avo_ref, angle, contrast, k):
    return avo_ref[contrast, angle : angle + 1, pl.ds(k * LANES, LANES)]


def add_terms(total, avo_ref, angle, result):
    for c, line in enumerate(total):
        for k, tile in enumerate(result):
            term = coeff(avo_ref, angle, c, k) * tile
            line[k] = term if angle == 0 else line[k] + term


def store_tiles(out_ref, tiles):
    size = out_ref.shape[2]
    for c in range(out_ref.shape[0]):
        for k, tile in enumerate(tiles[c]):
            for r in range(out_ref.shape[1]):
                out_ref[c, r, :, pl.ds(k * LANES, LANES)] = tile[r * size : (r + 1) * size]


def right_side(seis_ref, masks, avo_ref, turned_ref):
    angles, rows, _, samples = seis_ref.shape
    n = samples // LANES
    total = [[None] * n for _ in range(avo_ref.shape[0])]
    for a in range(angles):
        data = jnp.concatenate([seis_ref[a, r].astype(F32) for r in range(rows)], axis=0)
        data = data * masks[a]
        turned = [
            pltpu.roll(data[:, k * LANES : (k + 1) * LANES], LANES // 2, 1) for k in range(n)
        ]
        zero = jnp.zeros_like(turned[0])
        left_half = lax.broadcasted_iota(jnp.int32, zero.shape, 1) < LANES // 2
        shifted = [
            jnp.where(left_half, before, here).astype(BF16)
            for before, here in zip([zero, *turned], [*turned, zero])
        ]
        add_terms(total, avo_ref, a, backward([shifted], band(turned_ref, a)))
    return total


def normal(field, masks, avo_ref, bands):
    contrasts, n = len(field), len(field[0])
    total = [[None] * n for _ in range(contrasts)]
    for a, (ahead, back) in enumerate(bands):
        mixed = []
        for k in range(n):
            parts = [coeff(avo_ref, a, c, k) * field[c][k] for c in range(contrasts)]
            mixed.append(functools.reduce(jnp.add, parts))
        synth = [tile * masks[a] for tile in forward(mixed, ahead)]
        left_half = lax.broadcasted_iota(jnp.int32, synth[0].shape, 1) < LANES // 2
        synth[0] = jnp.where(left_half, 0.0, synth[0])
        synth[n] = jnp.where(left_half, synth[n], 0.0)
        result = backward(list(zip(*[split(t) for t in synth])), back)
        add_terms(total, avo_ref, a, result)
    return total


def lateral(here, north, south, west, east):
    traces = here.shape[0]
    place = lax.broadcasted_iota(jnp.int32, here.shape, 0)
    from_west = jnp.where(place == 0, 0.0 if west is None else west, pltpu.roll(here, 1, 0))
    from_east = jnp.where(
        place == traces - 1, 0.0 if east is None else east, pltpu.roll(here, traces - 1, 0)
    )
    around = from_west + from_east
    for other in (north, south):
        around = around if other is None else around + other
    return around


def copy_in(pairs, sems):
    copies = [pltpu.make_async_copy(a, b, sems.at[i]) for i, (a, b) in enumerate(pairs)]
    for copy in copies:
        copy.start()
    return copies


def start_kernel(
    seis_hbm, valid_hbm, avo_hbm, taps_hbm, prior_hbm, strength_hbm,
    b_ref, near_ref, far_ref, padded_ref, turned_ref, valid_ref, avo_ref, prior_ref, strength_ref,
    seis_ref, taps_ref, sems,
):
    copies = copy_in(
        (
            (taps_hbm, taps_ref),
            (valid_hbm, valid_ref),
            (avo_hbm, avo_ref),
            (seis_hbm, seis_ref),
            (prior_hbm, prior_ref),
            (strength_hbm, strength_ref),
        ),
        sems,
    )
    for copy in copies[:2]:
        copy.wait()
    fill_taps(taps_ref, padded_ref, turned_ref)
    angles = avo_ref.shape[1]
    masks = [trace_columns(valid_ref, a) for a in range(angles)]
    for copy in copies[2:]:
        copy.wait()
    store_tiles(b_ref, right_side(seis_ref, masks, avo_ref, turned_ref))
    contrasts, rows, traces, samples = b_ref.shape
    n = samples // LANES
    first = starts_pair("inline")
    lane = lax.broadcasted_iota(jnp.int32, (traces, LANES), 1)
    notes = []
    for r in (0, rows - 1):
        note = jnp.where(lane == angles, column(prior_ref[r : r + 1, :]), 0.0)
        for a in range(angles):
            note = jnp.where(lane == a, masks[a][r * traces : (r + 1) * traces], note)
        notes.append(note)
    edges = [
        [*[b_ref[c, r, :, pl.ds(k * LANES, LANES)] for c in range(contrasts) for k in range(n)], note]
        for r, note in zip((0, rows - 1), notes)
    ]
    for e, (top, bottom) in enumerate(zip(*edges)):
        near_ref[e] = jnp.where(first, bottom, top)
        far_ref[e] = jnp.where(first, top, bottom)


def either_side(pair_ref, next_ref, *where):
    first = starts_pair("inline")
    pair, other = pair_ref[where], next_ref[where]
    return jnp.where(first, other, pair), jnp.where(first, pair, other)


def stack_tiles(ref):
    contrasts, rows, _, samples = ref.shape
    return [
        [
            jnp.concatenate([ref[c, r, :, pl.ds(k, LANES)] for r in range(rows)], axis=0)
            for k in range(0, samples, LANES)
        ]
        for c in range(contrasts)
    ]


def inside(axis):
    place = lax.axis_index(axis)
    last = lax.axis_size(axis) - 1
    return (place > 0).astype(F32), (place < last).astype(F32)


def starts_pair(axis):
    return lax.axis_index(axis) % 2 == 0


def row_pair(near_ref, next_ref, c, n):
    tiles = [either_side(near_ref, next_ref, c * n + k) for k in range(n)]
    return [jnp.concatenate(side, axis=1) for side in zip(*tiles)]


def column_kernel(b_ref, near_ref, near_next_ref, valid_ref, prior_ref, pair_ref, other_ref):
    contrasts, rows, traces, samples = b_ref.shape
    angles = valid_ref.shape[0]
    first_col = starts_pair("col")
    lines = []
    for c in range(contrasts):
        above, below = row_pair(near_ref, near_next_ref, c, samples // LANES)
        own = [b_ref[c, r] for r in range(rows)]
        lines += [(line[0:1], line[traces - 1 :]) for line in (above, *own, below)]
        lines += [(line[1:2], line[traces - 2 : traces - 1]) for line in own]
    for e, (left, right) in enumerate(lines):
        place = (slice(e % rows, e % rows + 1), pl.ds(e // rows * samples, samples))
        pair_ref[place] = jnp.where(first_col, right, left)
        other_ref[place] = jnp.where(first_col, left, right)
    lane = lax.broadcasted_iota(jnp.int32, (1, LANES), 1)
    for r in range(rows):
        notes = []
        for t in (0, traces - 1):
            note = jnp.where(lane == angles, prior_ref[r : r + 1, t : t + 1], 0.0)
            for a in range(angles):
                note = jnp.where(lane == a, valid_ref[a, r : r + 1, t : t + 1].astype(F32), note)
            notes.append(note)
        left, right = notes
        place = (slice(r, r + 1), pl.ds(len(lines) // rows * samples, LANES))
        pair_ref[place] = jnp.where(first_col, right, left)
        other_ref[place] = jnp.where(first_col, left, right)


def inner_kernel(
    b_ref, near_ref, near_next_ref, padded_ref, turned_ref, valid_ref, avo_ref, prior_ref,
    strength_ref, v_ref, data_ref, halo_ref, ahead_ref, back_ref,
):
    contrasts, rows, traces, samples = b_ref.shape
    angles, n = avo_ref.shape[1], samples // LANES
    bands = []
    for a in range(angles):
        bands.append((band(padded_ref, a), band(turned_ref, a)))
        ahead_ref[a], back_ref[a] = bands[a]
    masks = [trace_columns(valid_ref, a) for a in range(angles)]
    weights = [column(prior_ref[r : r + 1, :]) + 4.0 for r in range(rows)]
    above, below = either_side(near_ref, near_next_ref, contrasts * n)
    wide = [
        jnp.concatenate([above[:, a : a + 1], mask, below[:, a : a + 1]], axis=0)
        for a, mask in enumerate(masks)
    ]
    weights = [above[:, angles : angles + 1] + 4.0, *weights, below[:, angles : angles + 1] + 4.0]
    field = []
    for c, line in enumerate(stack_tiles(b_ref)):
        ends = [either_side(near_ref, near_next_ref, c * n + k) for k in range(n)]
        field.append(
            [jnp.concatenate([up, own, low], axis=0) for (up, low), own in zip(ends, line)]
        )
    total = normal(field, wide, avo_ref, bands)
    has_above, has_below = inside("inline")
    for c in range(contrasts):
        strength = strength_ref[:, c : c + 1]
        whole, data = jnp.concatenate(field[c], axis=1), jnp.concatenate(total[c], axis=1)
        lines = [whole[r * traces : (r + 1) * traces] for r in range(rows + 2)]
        for r, here in enumerate(lines):
            north = lines[r - 1] if r else None
            south = lines[r + 1] if r < rows + 1 else None
            if r == 0:
                south = has_above * south
            if r == rows + 1:
                north = has_below * north
            around = lateral(here, north, south, None, None)
            image = data[r * traces : (r + 1) * traces] + strength * (weights[r] * here - around)
            if 0 < r <= rows:
                v_ref[c, r - 1] = image
            else:
                halo_ref[min(r, 1), c] = image
    store_tiles(data_ref, normal(stack_tiles(v_ref), masks, avo_ref, bands))


def image_kernel(
    b_ref, v_ref, data_ref, halo_ref, far_next_ref, far_ref, other_ref, pair_ref,
    valid_ref, avo_ref, prior_ref, strength_ref, ahead_ref, back_ref,
    one_ref, two_ref, gram_ref,
):
    contrasts, rows, traces, samples = b_ref.shape
    angles, n = avo_ref.shape[1], samples // LANES
    has_left, has_right = inside("col")
    first_col = starts_pair("col")
    left = jnp.where(first_col, other_ref[...], pair_ref[...])
    right = jnp.where(first_col, pair_ref[...], other_ref[...])
    place = lax.broadcasted_iota(jnp.int32, (traces, samples), 0)
    ext = rows + 2

    def trace(side, c, i):
        e = c * (ext + rows) + i
        return side[e % rows : e % rows + 1, e // rows * samples : (e // rows + 1) * samples]

    def note(side, r, i):
        at = contrasts * (ext + rows) // rows * samples + i
        return side[r : r + 1, at : at + 1]

    def beside(c, i):
        west, east = trace(left, c, i), trace(right, c, i)
        return jnp.where(place == 0, west, jnp.where(place == traces - 1, east, 0.0))

    def spread(values):
        total = values[-1]
        for t in range(traces - 2, -1, -1):
            total = jnp.where(place[:, : values[0].shape[1]] == t, values[t], total)
        return total

    bands = [(ahead_ref[a], back_ref[a]) for a in range(angles)]
    masks = []
    for a in range(angles):
        own = [
            [valid_ref[a, r : r + 1, t : t + 1].astype(F32) for r in range(rows)]
            for t in (0, traces - 1)
        ]
        west, east = ([note(side, r, a) for r in range(rows)] for side in (left, right))
        masks.append(spread([*own[0], *west, *east[::-1], *own[1][::-1]]))
    tile = []
    for c in range(contrasts):
        strength = strength_ref[:, c : c + 1]
        west, east = ([trace(side, c, r + 1) for r in range(rows)] for side in (left, right))
        less = [-strength * line for line in west], [-strength * line for line in east]
        whole = spread([*less[0], *west, *east[::-1], *less[1][::-1]])
        tile.append([whole[:, k * LANES : (k + 1) * LANES] for k in range(n)])
    edge = [jnp.concatenate(line, axis=1) for line in normal(tile, masks, avo_ref, bands)]

    weights = [column(prior_ref[r : r + 1, :]) + 4.0 for r in range(rows)]
    sums = [jnp.zeros((traces, LANES), F32) for _ in range(4)]
    for c in range(contrasts):
        strength = strength_ref[:, c : c + 1]
        beyond = row_pair(far_ref, far_next_ref, c, n)
        over, under = (halo_ref[i, c] - strength * beyond[i] for i in (0, 1))
        lines = [over, *[v_ref[c, r] for r in range(rows)], under]
        lines = [line - strength * beside(c, i) for i, line in enumerate(lines)]
        for r in range(rows):
            here, b = lines[r + 1], b_ref[c, r]
            beyond = []
            for side, has, t, u in (
                (left, has_left, 0, rows + r),
                (right, has_right, traces - 1, traces - rows - 1 - r),
            ):
                weight = note(side, r, angles) + 4.0
                around = trace(side, c, r) + trace(side, c, r + 2) + trace(side, c, ext + r)
                around = around + has * b[t : t + 1]
                prior = strength * (weight * trace(side, c, r + 1) - around)
                beyond.append(edge[c][u : u + 1] + prior)
            around = lateral(here, lines[r], lines[r + 2], *beyond)
            first, last = edge[c][r : r + 1], edge[c][traces - 1 - r : traces - r]
            mend = jnp.where(place == 0, first, jnp.where(place == traces - 1, last, 0.0))
            two = data_ref[c, r] + mend + strength * (weights[r] * here - around)
            one_ref[c, r] = here
            two_ref[c, r] = two
            for q, product in enumerate((b * b, b * here, here * here, here * two)):
                tiles = [product[:, k : k + LANES] for k in range(0, samples, LANES)]
                sums[q] = sums[q] + functools.reduce(jnp.add, tiles)
    lane = lax.broadcasted_iota(jnp.int32, (1, LANES), 1)
    packed = jnp.zeros((1, LANES), F32)
    for q, total in enumerate(sums):
        total = jnp.sum(jnp.sum(total, axis=0, keepdims=True), axis=1, keepdims=True)
        packed = jnp.where(lane == q, total, packed)
    gram_ref[...] = jnp.broadcast_to(packed[None], gram_ref.shape)


def finish_kernel(gram_ref, b_ref, one_ref, two_ref, solution_ref, residual_ref):
    sums = jnp.sum(gram_ref[...], axis=0)
    g00, g01, g11, g12 = (sums[:, q : q + 1] for q in range(4))
    first = g00 / g01
    ratio = first * g11 / g01
    second = (ratio - 1.0) * g01 / (first * g12 - ratio * g11)
    near = first + second * ratio
    far = first * second
    for c in range(b_ref.shape[0]):
        for r in range(b_ref.shape[1]):
            b, one, two = b_ref[c, r], one_ref[c, r], two_ref[c, r]
            solution_ref[c, r] = near * b - far * one
            residual_ref[c, r] = b - near * one + far * two


VMEM = pl.BlockSpec(memory_space=pltpu.VMEM)
HBM = pl.BlockSpec(memory_space=pltpu.HBM)


def call(kernel, outs, ins, flops, scratch=(), places=None):
    moved = sum(x.size * x.dtype.itemsize for x in (*ins, *outs))
    return pl.pallas_call(
        kernel,
        out_shape=outs,
        in_specs=[VMEM] * len(ins) if places is None else places,
        out_specs=jax.tree.map(lambda _: VMEM, outs),
        scratch_shapes=list(scratch),
        compiler_params=pltpu.CompilerParams(vmem_limit_bytes=24 * 1024 * 1024),
        cost_estimate=pl.CostEstimate(flops=flops, bytes_accessed=moved, transcendentals=0),
        name=kernel.__name__,
    )(*ins)


def swap(axis, value, first):
    starts = range(first, lax.axis_size(axis) - 1, 2)
    return lax.ppermute(value, axis, [(i + d, i + 1 - d) for i in starts for d in (0, 1)])


def hand_on(axis, value):
    size = lax.axis_size(axis)
    steps = [(i, i + 2 - 4 * (i % 2)) for i in range(size)]
    return lax.ppermute(value, axis, [(i, j) for i, j in steps if 0 <= j < size])


def shards(seismic, validity, prior_weight, lateral_strength, avo_coeffs, wavelets):
    angles, rows, traces, samples = seismic.shape
    contrasts = avo_coeffs.shape[1]
    avo_coeffs = jnp.swapaxes(avo_coeffs, 0, 1)
    shape = lambda *dims: jax.ShapeDtypeStruct(dims, F32)
    field = shape(contrasts, rows, traces, samples)
    side = shape(rows, contrasts * (2 * rows + 2) // rows * samples + LANES)
    lines = shape(8, 2 * LANES)
    work = 2 * angles * rows * traces * samples * 256 * 4

    given = (seismic, validity, avo_coeffs, wavelets, prior_weight, lateral_strength.reshape(1, -1))
    kept = [given[i] for i in (1, 2, 4, 5)]
    edge = shape(contrasts * samples // LANES + 1, traces, LANES)
    b, near, far, padded, turned, *kept = call(
        start_kernel,
        (
            field, edge, edge, lines, lines,
            *[jax.ShapeDtypeStruct(x.shape, x.dtype) for x in kept],
        ),
        [pltpu.with_memory_space_constraint(x, pltpu.HBM) for x in given],
        work,
        [
            pltpu.VMEM(seismic.shape, seismic.dtype),
            pltpu.VMEM(wavelets.shape, F32),
            pltpu.SemaphoreType.DMA((6,)),
        ],
        [HBM] * 6,
    )
    near = swap("inline", near, 0)
    near_next = swap("inline", far, 1)
    far_next = hand_on("inline", near)
    far = swap("inline", far, 0)
    col_pair, col_other = call(
        column_kernel, (side, side), (b, near, near_next, kept[0], kept[2]), 2 * field.size
    )
    col_other = swap("col", col_other, 1)
    col_pair = swap("col", col_pair, 0)
    bands = jax.ShapeDtypeStruct((angles, 2 * LANES, 2 * LANES), BF16)
    image, data, halo, ahead, back = call(
        inner_kernel,
        (field, field, shape(2, contrasts, traces, samples), bands, bands),
        (b, near, near_next, padded, turned, *kept),
        6 * work,
    )
    axes = ("inline", "col")
    one, two, gram = call(
        image_kernel,
        (field, field, shape(lax.axis_size(axes), 1, LANES)),
        (
            b, image, data, halo, far_next, far, col_other, col_pair,
            *kept, ahead, back,
        ),
        work,
    )
    gram = lax.all_to_all(gram, axes, 0, 0)
    return tuple(call(finish_kernel, (field, field), (gram, b, one, two), 8 * field.size))


def solution(mesh):
    placed = (
        P(None, "inline", "col", None),
        P(None, "inline", "col"),
        P("inline", "col"),
        P(),
        P(),
        P(),
    )
    return jax.shard_map(
        shards,
        mesh=mesh,
        in_specs=placed,
        out_specs=(P(None, "inline", "col", None), P(None, "inline", "col", None)),
        check_vma=False,
    )
```

```python
import functools

import jax
import jax.numpy as jnp
from jax import lax
from jax.experimental import pallas as pl
from jax.experimental.pallas import tpu as pltpu
from jax.sharding import PartitionSpec as P

LANES = 128
F32 = jnp.float32
BF16 = jnp.bfloat16


def split(value):
    high = value.astype(BF16)
    return high, (value - high.astype(F32)).astype(BF16)


def pad_taps(taps_ref, padded_ref):
    padded_ref[...] = jnp.zeros_like(padded_ref)
    padded_ref[0 : taps_ref.shape[0], 0 : taps_ref.shape[1]] = taps_ref[...]


def turn(lines, count):
    n, size = lines.shape
    parts = []
    for _ in range(3):
        parts.append(lines.astype(BF16).astype(F32))
        lines = lines - parts[-1]
    rows = lax.broadcasted_iota(jnp.int32, (size, size), 0)
    cols = lax.broadcasted_iota(jnp.int32, (size, size), 1)
    flip = jnp.where(rows + cols == count - 1, 1.0, 0.0).astype(BF16)
    whole = jnp.concatenate(parts, axis=0).astype(BF16)
    turned = jnp.dot(whole, flip, preferred_element_type=F32)
    return turned[:n] + turned[n : 2 * n] + turned[2 * n :]


def band(line):
    lines = jnp.broadcast_to(line, (LANES, line.shape[1]))
    return jnp.concatenate(split(pltpu.roll(lines, 0, 1, stride=1, stride_axis=0)), axis=0)


def convolve(rows, bands):
    out = lax.dot_general(rows, bands, (((1,), (1,)), ((), ())), preferred_element_type=F32)
    return out[:, :LANES] + out[:, LANES:]


def column(row):
    n = row.shape[1]
    same = lax.broadcasted_iota(jnp.int32, (n, n), 0) == lax.broadcasted_iota(jnp.int32, (n, n), 1)
    return jnp.sum(jnp.where(same, jnp.broadcast_to(row, (n, n)), 0.0), axis=1, keepdims=True)


def trace_columns(ref, *lead):
    rows = ref[lead].astype(F32)
    return jnp.concatenate([column(rows[r : r + 1, :]) for r in range(rows.shape[0])], axis=0)


def windows(tiles):
    pairs = [jnp.concatenate(pair, axis=1) for pair in zip(tiles[:-1], tiles[1:])]
    return jnp.concatenate(pairs, axis=0)


def forward(tiles, bands):
    zero = jnp.zeros_like(tiles[0]).astype(BF16)
    highs, lows = zip(*[split(t) for t in tiles])
    n, size = len(tiles) + 1, tiles[0].shape[0]
    rows = [windows([zero, *part, zero]) for part in (highs, lows)]
    out = convolve(jnp.concatenate(rows, axis=0), bands)
    out = out[: n * size] + out[n * size :]
    return [out[k * size : (k + 1) * size] for k in range(n)]


def backward(parts, bands):
    n, size = len(parts[0]) - 1, parts[0][0].shape[0]
    rows = jnp.concatenate([windows(part) for part in parts], axis=0)
    out = convolve(rows, bands)
    total = out[: n * size]
    for p in range(1, len(parts)):
        total = total + out[p * n * size : (p + 1) * n * size]
    return [total[k * size : (k + 1) * size] for k in range(n)]


def coeff(avo_ref, angle, contrast, k):
    return avo_ref[contrast, angle : angle + 1, pl.ds(k * LANES, LANES)]


def add_terms(total, avo_ref, angle, result):
    for c, line in enumerate(total):
        for k, tile in enumerate(result):
            term = coeff(avo_ref, angle, c, k) * tile
            line[k] = term if angle == 0 else line[k] + term


def store_tiles(out_ref, tiles):
    size = out_ref.shape[2]
    for c in range(out_ref.shape[0]):
        for k, tile in enumerate(tiles[c]):
            for r in range(out_ref.shape[1]):
                out_ref[c, r, :, pl.ds(k * LANES, LANES)] = tile[r * size : (r + 1) * size]


def right_side(seis_ref, masks, avo_ref, padded_ref):
    angles, rows, _, samples = seis_ref.shape
    n = samples // LANES
    total = [[None] * n for _ in range(avo_ref.shape[0])]
    for a in range(angles):
        data = jnp.concatenate([seis_ref[a, r].astype(F32) for r in range(rows)], axis=0)
        data = data * masks[a]
        turned = [
            pltpu.roll(data[:, k * LANES : (k + 1) * LANES], LANES // 2, 1) for k in range(n)
        ]
        zero = jnp.zeros_like(turned[0])
        left_half = lax.broadcasted_iota(jnp.int32, zero.shape, 1) < LANES // 2
        shifted = [
            jnp.where(left_half, before, here).astype(BF16)
            for before, here in zip([zero, *turned], [*turned, zero])
        ]
        add_terms(total, avo_ref, a, backward([shifted], band(padded_ref[a : a + 1, :])))
    return total


def normal(field, masks, avo_ref, bands):
    contrasts, n = len(field), len(field[0])
    total = [[None] * n for _ in range(contrasts)]
    for a, (ahead, back) in enumerate(bands):
        mixed = []
        for k in range(n):
            parts = [coeff(avo_ref, a, c, k) * field[c][k] for c in range(contrasts)]
            mixed.append(functools.reduce(jnp.add, parts))
        synth = [tile * masks[a] for tile in forward(mixed, ahead)]
        left_half = lax.broadcasted_iota(jnp.int32, synth[0].shape, 1) < LANES // 2
        synth[0] = jnp.where(left_half, 0.0, synth[0])
        synth[n] = jnp.where(left_half, synth[n], 0.0)
        result = backward(list(zip(*[split(t) for t in synth])), back)
        add_terms(total, avo_ref, a, result)
    return total


def lateral(here, north, south, west, east):
    traces = here.shape[0]
    place = lax.broadcasted_iota(jnp.int32, here.shape, 0)
    from_west = jnp.where(place == 0, 0.0 if west is None else west, pltpu.roll(here, 1, 0))
    from_east = jnp.where(
        place == traces - 1, 0.0 if east is None else east, pltpu.roll(here, traces - 1, 0)
    )
    around = from_west + from_east
    for other in (north, south):
        around = around if other is None else around + other
    return around


def copy_in(pairs, sems):
    copies = [pltpu.make_async_copy(a, b, sems.at[i]) for i, (a, b) in enumerate(pairs)]
    for copy in copies:
        copy.start()
    return copies


def start_kernel(
    seis_hbm, valid_hbm, avo_hbm, taps_hbm, prior_hbm, strength_hbm,
    b_ref, near_ref, far_ref, padded_ref, valid_ref, avo_ref, prior_ref, strength_ref,
    seis_ref, taps_ref, sems,
):
    copies = copy_in(
        (
            (taps_hbm, taps_ref),
            (valid_hbm, valid_ref),
            (avo_hbm, avo_ref),
            (seis_hbm, seis_ref),
            (prior_hbm, prior_ref),
            (strength_hbm, strength_ref),
        ),
        sems,
    )
    for copy in copies[:2]:
        copy.wait()
    pad_taps(taps_ref, padded_ref)
    angles = avo_ref.shape[1]
    masks = [trace_columns(valid_ref, a) for a in range(angles)]
    for copy in copies[2:]:
        copy.wait()
    store_tiles(b_ref, right_side(seis_ref, masks, avo_ref, padded_ref))
    contrasts, rows, traces, samples = b_ref.shape
    n = samples // LANES
    first = starts_pair("inline")
    lane = lax.broadcasted_iota(jnp.int32, (traces, LANES), 1)
    notes = []
    for r in (0, rows - 1):
        note = jnp.where(lane == angles, column(prior_ref[r : r + 1, :]), 0.0)
        for a in range(angles):
            note = jnp.where(lane == a, masks[a][r * traces : (r + 1) * traces], note)
        notes.append(note)
    edges = [
        [*[b_ref[c, r, :, pl.ds(k * LANES, LANES)] for c in range(contrasts) for k in range(n)], note]
        for r, note in zip((0, rows - 1), notes)
    ]
    for e, (top, bottom) in enumerate(zip(*edges)):
        near_ref[e] = jnp.where(first, bottom, top)
        far_ref[e] = jnp.where(first, top, bottom)


def either_side(pair_ref, next_ref, *where):
    first = starts_pair("inline")
    pair, other = pair_ref[where], next_ref[where]
    return jnp.where(first, other, pair), jnp.where(first, pair, other)


def stack_tiles(ref):
    contrasts, rows, _, samples = ref.shape
    return [
        [
            jnp.concatenate([ref[c, r, :, pl.ds(k, LANES)] for r in range(rows)], axis=0)
            for k in range(0, samples, LANES)
        ]
        for c in range(contrasts)
    ]


def inside(axis):
    place = lax.axis_index(axis)
    last = lax.axis_size(axis) - 1
    return (place > 0).astype(F32), (place < last).astype(F32)


def starts_pair(axis):
    return lax.axis_index(axis) % 2 == 0


def row_pair(near_ref, next_ref, c, n):
    tiles = [either_side(near_ref, next_ref, c * n + k) for k in range(n)]
    return [jnp.concatenate(side, axis=1) for side in zip(*tiles)]


def column_kernel(b_ref, near_ref, near_next_ref, valid_ref, prior_ref, pair_ref, other_ref):
    contrasts, rows, traces, samples = b_ref.shape
    angles = valid_ref.shape[0]
    first_col = starts_pair("col")
    lines = []
    for c in range(contrasts):
        above, below = row_pair(near_ref, near_next_ref, c, samples // LANES)
        own = [b_ref[c, r] for r in range(rows)]
        lines += [(line[0:1], line[traces - 1 :]) for line in (above, *own, below)]
        lines += [(line[1:2], line[traces - 2 : traces - 1]) for line in own]
    for e, (left, right) in enumerate(lines):
        place = (slice(e % rows, e % rows + 1), pl.ds(e // rows * samples, samples))
        pair_ref[place] = jnp.where(first_col, right, left)
        other_ref[place] = jnp.where(first_col, left, right)
    lane = lax.broadcasted_iota(jnp.int32, (1, LANES), 1)
    for r in range(rows):
        notes = []
        for t in (0, traces - 1):
            note = jnp.where(lane == angles, prior_ref[r : r + 1, t : t + 1], 0.0)
            for a in range(angles):
                note = jnp.where(lane == a, valid_ref[a, r : r + 1, t : t + 1].astype(F32), note)
            notes.append(note)
        left, right = notes
        place = (slice(r, r + 1), pl.ds(len(lines) // rows * samples, LANES))
        pair_ref[place] = jnp.where(first_col, right, left)
        other_ref[place] = jnp.where(first_col, left, right)


def inner_kernel(
    count, b_ref, near_ref, near_next_ref, padded_ref, valid_ref, avo_ref, prior_ref, strength_ref,
    v_ref, data_ref, halo_ref, ahead_ref, back_ref,
):
    contrasts, rows, traces, samples = b_ref.shape
    angles, n = avo_ref.shape[1], samples // LANES
    turned = turn(padded_ref[...], count)
    bands = []
    for a in range(angles):
        bands.append((band(turned[a : a + 1]), band(padded_ref[a : a + 1, :])))
        ahead_ref[a], back_ref[a] = bands[a]
    masks = [trace_columns(valid_ref, a) for a in range(angles)]
    weights = [column(prior_ref[r : r + 1, :]) + 4.0 for r in range(rows)]
    above, below = either_side(near_ref, near_next_ref, contrasts * n)
    wide = [
        jnp.concatenate([above[:, a : a + 1], mask, below[:, a : a + 1]], axis=0)
        for a, mask in enumerate(masks)
    ]
    weights = [above[:, angles : angles + 1] + 4.0, *weights, below[:, angles : angles + 1] + 4.0]
    field = []
    for c, line in enumerate(stack_tiles(b_ref)):
        ends = [either_side(near_ref, near_next_ref, c * n + k) for k in range(n)]
        field.append(
            [jnp.concatenate([up, own, low], axis=0) for (up, low), own in zip(ends, line)]
        )
    total = normal(field, wide, avo_ref, bands)
    has_above, has_below = inside("inline")
    for c in range(contrasts):
        strength = strength_ref[:, c : c + 1]
        whole, data = jnp.concatenate(field[c], axis=1), jnp.concatenate(total[c], axis=1)
        lines = [whole[r * traces : (r + 1) * traces] for r in range(rows + 2)]
        for r, here in enumerate(lines):
            north = lines[r - 1] if r else None
            south = lines[r + 1] if r < rows + 1 else None
            if r == 0:
                south = has_above * south
            if r == rows + 1:
                north = has_below * north
            around = lateral(here, north, south, None, None)
            image = data[r * traces : (r + 1) * traces] + strength * (weights[r] * here - around)
            if 0 < r <= rows:
                v_ref[c, r - 1] = image
            else:
                halo_ref[min(r, 1), c] = image
    store_tiles(data_ref, normal(stack_tiles(v_ref), masks, avo_ref, bands))


def image_kernel(
    b_ref, v_ref, data_ref, halo_ref, far_next_ref, far_ref, other_ref, pair_ref,
    valid_ref, avo_ref, prior_ref, strength_ref, ahead_ref, back_ref,
    one_ref, two_ref, gram_ref,
):
    contrasts, rows, traces, samples = b_ref.shape
    angles, n = avo_ref.shape[1], samples // LANES
    has_left, has_right = inside("col")
    first_col = starts_pair("col")
    left = jnp.where(first_col, other_ref[...], pair_ref[...])
    right = jnp.where(first_col, pair_ref[...], other_ref[...])
    place = lax.broadcasted_iota(jnp.int32, (traces, samples), 0)
    ext = rows + 2

    def trace(side, c, i):
        e = c * (ext + rows) + i
        return side[e % rows : e % rows + 1, e // rows * samples : (e // rows + 1) * samples]

    def note(side, r, i):
        at = contrasts * (ext + rows) // rows * samples + i
        return side[r : r + 1, at : at + 1]

    def beside(c, i):
        west, east = trace(left, c, i), trace(right, c, i)
        return jnp.where(place == 0, west, jnp.where(place == traces - 1, east, 0.0))

    def spread(values):
        total = values[-1]
        for t in range(traces - 2, -1, -1):
            total = jnp.where(place[:, : values[0].shape[1]] == t, values[t], total)
        return total

    bands = [(ahead_ref[a], back_ref[a]) for a in range(angles)]
    masks = []
    for a in range(angles):
        own = [
            [valid_ref[a, r : r + 1, t : t + 1].astype(F32) for r in range(rows)]
            for t in (0, traces - 1)
        ]
        west, east = ([note(side, r, a) for r in range(rows)] for side in (left, right))
        masks.append(spread([*own[0], *west, *east[::-1], *own[1][::-1]]))
    tile = []
    for c in range(contrasts):
        strength = strength_ref[:, c : c + 1]
        west, east = ([trace(side, c, r + 1) for r in range(rows)] for side in (left, right))
        less = [-strength * line for line in west], [-strength * line for line in east]
        whole = spread([*less[0], *west, *east[::-1], *less[1][::-1]])
        tile.append([whole[:, k * LANES : (k + 1) * LANES] for k in range(n)])
    edge = [jnp.concatenate(line, axis=1) for line in normal(tile, masks, avo_ref, bands)]

    weights = [column(prior_ref[r : r + 1, :]) + 4.0 for r in range(rows)]
    sums = [jnp.zeros((traces, LANES), F32) for _ in range(4)]
    for c in range(contrasts):
        strength = strength_ref[:, c : c + 1]
        beyond = row_pair(far_ref, far_next_ref, c, n)
        over, under = (halo_ref[i, c] - strength * beyond[i] for i in (0, 1))
        lines = [over, *[v_ref[c, r] for r in range(rows)], under]
        lines = [line - strength * beside(c, i) for i, line in enumerate(lines)]
        for r in range(rows):
            here, b = lines[r + 1], b_ref[c, r]
            beyond = []
            for side, has, t, u in (
                (left, has_left, 0, rows + r),
                (right, has_right, traces - 1, traces - rows - 1 - r),
            ):
                weight = note(side, r, angles) + 4.0
                around = trace(side, c, r) + trace(side, c, r + 2) + trace(side, c, ext + r)
                around = around + has * b[t : t + 1]
                prior = strength * (weight * trace(side, c, r + 1) - around)
                beyond.append(edge[c][u : u + 1] + prior)
            around = lateral(here, lines[r], lines[r + 2], *beyond)
            first, last = edge[c][r : r + 1], edge[c][traces - 1 - r : traces - r]
            mend = jnp.where(place == 0, first, jnp.where(place == traces - 1, last, 0.0))
            two = data_ref[c, r] + mend + strength * (weights[r] * here - around)
            one_ref[c, r] = here
            two_ref[c, r] = two
            for q, product in enumerate((b * b, b * here, here * here, here * two)):
                tiles = [product[:, k : k + LANES] for k in range(0, samples, LANES)]
                sums[q] = sums[q] + functools.reduce(jnp.add, tiles)
    lane = lax.broadcasted_iota(jnp.int32, (1, LANES), 1)
    packed = jnp.zeros((1, LANES), F32)
    for q, total in enumerate(sums):
        total = jnp.sum(jnp.sum(total, axis=0, keepdims=True), axis=1, keepdims=True)
        packed = jnp.where(lane == q, total, packed)
    gram_ref[...] = jnp.broadcast_to(packed[None], gram_ref.shape)


def finish_kernel(gram_ref, b_ref, one_ref, two_ref, solution_ref, residual_ref):
    sums = jnp.sum(gram_ref[...], axis=0)
    g00, g01, g11, g12 = (sums[:, q : q + 1] for q in range(4))
    first = g00 / g01
    ratio = first * g11 / g01
    second = (ratio - 1.0) * g01 / (first * g12 - ratio * g11)
    near = first + second * ratio
    far = first * second
    for c in range(b_ref.shape[0]):
        for r in range(b_ref.shape[1]):
            b, one, two = b_ref[c, r], one_ref[c, r], two_ref[c, r]
            solution_ref[c, r] = near * b - far * one
            residual_ref[c, r] = b - near * one + far * two


VMEM = pl.BlockSpec(memory_space=pltpu.VMEM)
HBM = pl.BlockSpec(memory_space=pltpu.HBM)


def call(kernel, outs, ins, flops, scratch=(), places=None):
    moved = sum(x.size * x.dtype.itemsize for x in (*ins, *outs))
    return pl.pallas_call(
        kernel,
        out_shape=outs,
        in_specs=[VMEM] * len(ins) if places is None else places,
        out_specs=jax.tree.map(lambda _: VMEM, outs),
        scratch_shapes=list(scratch),
        compiler_params=pltpu.CompilerParams(vmem_limit_bytes=24 * 1024 * 1024),
        cost_estimate=pl.CostEstimate(flops=flops, bytes_accessed=moved, transcendentals=0),
        name=getattr(kernel, "func", kernel).__name__,
    )(*ins)


def swap(axis, value, first):
    starts = range(first, lax.axis_size(axis) - 1, 2)
    return lax.ppermute(value, axis, [(i + d, i + 1 - d) for i in starts for d in (0, 1)])


def hand_on(axis, value):
    size = lax.axis_size(axis)
    steps = [(i, i + 2 - 4 * (i % 2)) for i in range(size)]
    return lax.ppermute(value, axis, [(i, j) for i, j in steps if 0 <= j < size])


def shards(seismic, validity, prior_weight, lateral_strength, avo_coeffs, wavelets):
    angles, rows, traces, samples = seismic.shape
    contrasts = avo_coeffs.shape[1]
    avo_coeffs = jnp.swapaxes(avo_coeffs, 0, 1)
    shape = lambda *dims: jax.ShapeDtypeStruct(dims, F32)
    field = shape(contrasts, rows, traces, samples)
    side = shape(rows, contrasts * (2 * rows + 2) // rows * samples + LANES)
    lines = shape(8, 2 * LANES)
    work = 2 * angles * rows * traces * samples * 256 * 4

    given = (seismic, validity, avo_coeffs, wavelets, prior_weight, lateral_strength.reshape(1, -1))
    kept = [given[i] for i in (1, 2, 4, 5)]
    edge = shape(contrasts * samples // LANES + 1, traces, LANES)
    b, near, far, padded, *kept = call(
        start_kernel,
        (
            field, edge, edge, lines,
            *[jax.ShapeDtypeStruct(x.shape, x.dtype) for x in kept],
        ),
        [pltpu.with_memory_space_constraint(x, pltpu.HBM) for x in given],
        work,
        [
            pltpu.VMEM(seismic.shape, seismic.dtype),
            pltpu.VMEM(wavelets.shape, F32),
            pltpu.SemaphoreType.DMA((6,)),
        ],
        [HBM] * 6,
    )
    near = swap("inline", near, 0)
    near_next = swap("inline", far, 1)
    far_next = hand_on("inline", near)
    far = swap("inline", far, 0)
    col_pair, col_other = call(
        column_kernel, (side, side), (b, near, near_next, kept[0], kept[2]), 2 * field.size
    )
    col_other = swap("col", col_other, 1)
    col_pair = swap("col", col_pair, 0)
    bands = jax.ShapeDtypeStruct((angles, 2 * LANES, 2 * LANES), BF16)
    image, data, halo, ahead, back = call(
        functools.partial(inner_kernel, wavelets.shape[1]),
        (field, field, shape(2, contrasts, traces, samples), bands, bands),
        (b, near, near_next, padded, *kept),
        6 * work,
    )
    axes = ("inline", "col")
    one, two, gram = call(
        image_kernel,
        (field, field, shape(lax.axis_size(axes), 1, LANES)),
        (
            b, image, data, halo, far_next, far, col_other, col_pair,
            *kept, ahead, back,
        ),
        work,
    )
    gram = lax.all_to_all(gram, axes, 0, 0)
    return tuple(call(finish_kernel, (field, field), (gram, b, one, two), 8 * field.size))


def solution(mesh):
    placed = (
        P(None, "inline", "col", None),
        P(None, "inline", "col"),
        P("inline", "col"),
        P(),
        P(),
        P(),
    )
    return jax.shard_map(
        shards,
        mesh=mesh,
        in_specs=placed,
        out_specs=(P(None, "inline", "col", None), P(None, "inline", "col", None)),
        check_vma=False,
    )
```

```python
import functools

import jax
import jax.numpy as jnp
from jax import lax
from jax.experimental import pallas as pl
from jax.experimental.pallas import tpu as pltpu
from jax.sharding import PartitionSpec as P

LANES = 128
F32 = jnp.float32
BF16 = jnp.bfloat16


def split(value):
    high = value.astype(BF16)
    return high, (value - high.astype(F32)).astype(BF16)


def pad_taps(taps_ref, padded_ref):
    padded_ref[...] = jnp.zeros_like(padded_ref)
    padded_ref[0 : taps_ref.shape[0], 0 : taps_ref.shape[1]] = taps_ref[...]


def turn(lines, count):
    n, size = lines.shape
    parts = []
    for _ in range(3):
        parts.append(lines.astype(BF16).astype(F32))
        lines = lines - parts[-1]
    rows = lax.broadcasted_iota(jnp.int32, (size, size), 0)
    cols = lax.broadcasted_iota(jnp.int32, (size, size), 1)
    flip = jnp.where(rows + cols == count - 1, 1.0, 0.0).astype(BF16)
    whole = jnp.concatenate(parts, axis=0).astype(BF16)
    turned = jnp.dot(whole, flip, preferred_element_type=F32)
    return turned[:n] + turned[n : 2 * n] + turned[2 * n :]


def band(line):
    lines = jnp.broadcast_to(line, (LANES, line.shape[1]))
    return jnp.concatenate(split(pltpu.roll(lines, 0, 1, stride=1, stride_axis=0)), axis=0)


def convolve(rows, bands):
    out = lax.dot_general(rows, bands, (((1,), (1,)), ((), ())), preferred_element_type=F32)
    return out[:, :LANES] + out[:, LANES:]


def column(row):
    n = row.shape[1]
    same = lax.broadcasted_iota(jnp.int32, (n, n), 0) == lax.broadcasted_iota(jnp.int32, (n, n), 1)
    return jnp.sum(jnp.where(same, jnp.broadcast_to(row, (n, n)), 0.0), axis=1, keepdims=True)


def trace_columns(ref, *lead):
    rows = ref[lead].astype(F32)
    return jnp.concatenate([column(rows[r : r + 1, :]) for r in range(rows.shape[0])], axis=0)


def windows(tiles):
    pairs = [jnp.concatenate(pair, axis=1) for pair in zip(tiles[:-1], tiles[1:])]
    return jnp.concatenate(pairs, axis=0)


def forward(tiles, bands):
    zero = jnp.zeros_like(tiles[0]).astype(BF16)
    highs, lows = zip(*[split(t) for t in tiles])
    n, size = len(tiles) + 1, tiles[0].shape[0]
    rows = [windows([zero, *part, zero]) for part in (highs, lows)]
    out = convolve(jnp.concatenate(rows, axis=0), bands)
    out = out[: n * size] + out[n * size :]
    return [out[k * size : (k + 1) * size] for k in range(n)]


def backward(parts, bands):
    n, size = len(parts[0]) - 1, parts[0][0].shape[0]
    rows = jnp.concatenate([windows(part) for part in parts], axis=0)
    out = convolve(rows, bands)
    total = out[: n * size]
    for p in range(1, len(parts)):
        total = total + out[p * n * size : (p + 1) * n * size]
    return [total[k * size : (k + 1) * size] for k in range(n)]


def coeff(avo_ref, angle, contrast, k):
    return avo_ref[contrast, angle : angle + 1, pl.ds(k * LANES, LANES)]


def add_terms(total, avo_ref, angle, result):
    for c, line in enumerate(total):
        for k, tile in enumerate(result):
            term = coeff(avo_ref, angle, c, k) * tile
            line[k] = term if angle == 0 else line[k] + term


def store_tiles(out_ref, tiles):
    size = out_ref.shape[2]
    for c in range(out_ref.shape[0]):
        for k, tile in enumerate(tiles[c]):
            for r in range(out_ref.shape[1]):
                out_ref[c, r, :, pl.ds(k * LANES, LANES)] = tile[r * size : (r + 1) * size]


def right_side(seis_ref, masks, avo_ref, bands):
    angles, rows, _, samples = seis_ref.shape
    n = samples // LANES
    total = [[None] * n for _ in range(avo_ref.shape[0])]
    for a in range(angles):
        data = jnp.concatenate([seis_ref[a, r].astype(F32) for r in range(rows)], axis=0)
        data = data * masks[a]
        turned = [
            pltpu.roll(data[:, k * LANES : (k + 1) * LANES], LANES // 2, 1) for k in range(n)
        ]
        zero = jnp.zeros_like(turned[0])
        left_half = lax.broadcasted_iota(jnp.int32, zero.shape, 1) < LANES // 2
        shifted = [
            jnp.where(left_half, before, here).astype(BF16)
            for before, here in zip([zero, *turned], [*turned, zero])
        ]
        add_terms(total, avo_ref, a, backward([shifted], bands[a]))
    return total


def normal(field, masks, avo_ref, bands):
    contrasts, n = len(field), len(field[0])
    total = [[None] * n for _ in range(contrasts)]
    for a, (ahead, back) in enumerate(bands):
        mixed = []
        for k in range(n):
            parts = [coeff(avo_ref, a, c, k) * field[c][k] for c in range(contrasts)]
            mixed.append(functools.reduce(jnp.add, parts))
        synth = [tile * masks[a] for tile in forward(mixed, ahead)]
        left_half = lax.broadcasted_iota(jnp.int32, synth[0].shape, 1) < LANES // 2
        synth[0] = jnp.where(left_half, 0.0, synth[0])
        synth[n] = jnp.where(left_half, synth[n], 0.0)
        result = backward(list(zip(*[split(t) for t in synth])), back)
        add_terms(total, avo_ref, a, result)
    return total


def lateral(here, north, south, west, east):
    traces = here.shape[0]
    place = lax.broadcasted_iota(jnp.int32, here.shape, 0)
    from_west = jnp.where(place == 0, 0.0 if west is None else west, pltpu.roll(here, 1, 0))
    from_east = jnp.where(
        place == traces - 1, 0.0 if east is None else east, pltpu.roll(here, traces - 1, 0)
    )
    around = from_west + from_east
    for other in (north, south):
        around = around if other is None else around + other
    return around


def copy_in(pairs, sems):
    copies = [pltpu.make_async_copy(a, b, sems.at[i]) for i, (a, b) in enumerate(pairs)]
    for copy in copies:
        copy.start()
    return copies


def start_kernel(
    seis_hbm, valid_hbm, avo_hbm, taps_hbm, prior_hbm, strength_hbm,
    b_ref, near_ref, far_ref, padded_ref, valid_ref, avo_ref, prior_ref, strength_ref,
    seis_ref, taps_ref, sems,
):
    copies = copy_in(
        (
            (taps_hbm, taps_ref),
            (valid_hbm, valid_ref),
            (avo_hbm, avo_ref),
            (seis_hbm, seis_ref),
            (prior_hbm, prior_ref),
            (strength_hbm, strength_ref),
        ),
        sems,
    )
    for copy in copies[:2]:
        copy.wait()
    pad_taps(taps_ref, padded_ref)
    angles = avo_ref.shape[1]
    bands = [band(padded_ref[a : a + 1, :]) for a in range(angles)]
    masks = [trace_columns(valid_ref, a) for a in range(angles)]
    for copy in copies[2:]:
        copy.wait()
    store_tiles(b_ref, right_side(seis_ref, masks, avo_ref, bands))
    contrasts, rows, traces, samples = b_ref.shape
    n = samples // LANES
    first = starts_pair("inline")
    lane = lax.broadcasted_iota(jnp.int32, (traces, LANES), 1)
    notes = []
    for r in (0, rows - 1):
        note = jnp.where(lane == angles, column(prior_ref[r : r + 1, :]), 0.0)
        for a in range(angles):
            note = jnp.where(lane == a, masks[a][r * traces : (r + 1) * traces], note)
        notes.append(note)
    edges = [
        [*[b_ref[c, r, :, pl.ds(k * LANES, LANES)] for c in range(contrasts) for k in range(n)], note]
        for r, note in zip((0, rows - 1), notes)
    ]
    for e, (top, bottom) in enumerate(zip(*edges)):
        near_ref[e] = jnp.where(first, bottom, top)
        far_ref[e] = jnp.where(first, top, bottom)


def either_side(pair_ref, next_ref, *where):
    first = starts_pair("inline")
    pair, other = pair_ref[where], next_ref[where]
    return jnp.where(first, other, pair), jnp.where(first, pair, other)


def stack_tiles(ref):
    contrasts, rows, _, samples = ref.shape
    return [
        [
            jnp.concatenate([ref[c, r, :, pl.ds(k, LANES)] for r in range(rows)], axis=0)
            for k in range(0, samples, LANES)
        ]
        for c in range(contrasts)
    ]


def inside(axis):
    place = lax.axis_index(axis)
    last = lax.axis_size(axis) - 1
    return (place > 0).astype(F32), (place < last).astype(F32)


def starts_pair(axis):
    return lax.axis_index(axis) % 2 == 0


def row_pair(near_ref, next_ref, c, n):
    tiles = [either_side(near_ref, next_ref, c * n + k) for k in range(n)]
    return [jnp.concatenate(side, axis=1) for side in zip(*tiles)]


def column_kernel(
    b_ref, near_ref, near_next_ref, valid_ref, prior_ref,
    pair_ref, other_ref, own_ref, note_ref, second_ref,
):
    contrasts, rows, traces, samples = b_ref.shape
    angles = valid_ref.shape[0]
    first_col = starts_pair("col")
    half = rows + 2
    second_ref[...] = jnp.zeros_like(second_ref)
    note_ref[...] = jnp.zeros_like(note_ref)
    for c in range(contrasts):
        own = [b_ref[c, r] for r in range(rows)]
        for i, line in enumerate([*own, *row_pair(near_ref, near_next_ref, c, samples // LANES)]):
            own_ref[c, i : i + 1, :] = line[0:1]
            own_ref[c, half + i : half + i + 1, :] = line[traces - 1 :]
        for r, line in enumerate(own):
            at = c * rows + r
            second_ref[0, at : at + 1, :] = line[1:2]
            second_ref[1, at : at + 1, :] = line[traces - 2 : traces - 1]
    lane = lax.broadcasted_iota(jnp.int32, (1, LANES), 1)
    for r in range(rows):
        for side, t in enumerate((0, traces - 1)):
            note = jnp.where(lane == angles, prior_ref[r : r + 1, t : t + 1], 0.0)
            for a in range(angles):
                note = jnp.where(lane == a, valid_ref[a, r : r + 1, t : t + 1].astype(F32), note)
            at = contrasts * rows + r
            second_ref[side, at : at + 1, 0:LANES] = note
            at = r + side * (traces - rows)
            note_ref[at : at + 1, :] = note
    for c in range(contrasts):
        left, right = own_ref[c, 0:half], own_ref[c, half:]
        pair_ref[c] = jnp.where(first_col, right, left)
        other_ref[c] = jnp.where(first_col, left, right)
    for i in range(2):
        left, right = (second_ref[side, i * half : (i + 1) * half] for side in (0, 1))
        pair_ref[contrasts + i] = jnp.where(first_col, right, left)
        other_ref[contrasts + i] = jnp.where(first_col, left, right)


def bands_kernel(count, padded_ref, near_ref, ahead_ref, back_ref):
    turned = turn(padded_ref[...], count)
    for a in range(ahead_ref.shape[0]):
        ahead_ref[a] = band(turned[a : a + 1])
        back_ref[a] = band(padded_ref[a : a + 1, :])


def inner_kernel(
    b_ref, near_ref, near_next_ref, valid_ref, avo_ref, prior_ref, strength_ref, ahead_ref, back_ref,
    v_ref, data_ref, halo_ref,
):
    contrasts, rows, traces, samples = b_ref.shape
    angles, n = avo_ref.shape[1], samples // LANES
    bands = [(ahead_ref[a], back_ref[a]) for a in range(angles)]
    masks = [trace_columns(valid_ref, a) for a in range(angles)]
    weights = [column(prior_ref[r : r + 1, :]) + 4.0 for r in range(rows)]
    above, below = either_side(near_ref, near_next_ref, contrasts * n)
    wide = [
        jnp.concatenate([above[:, a : a + 1], mask, below[:, a : a + 1]], axis=0)
        for a, mask in enumerate(masks)
    ]
    weights = [above[:, angles : angles + 1] + 4.0, *weights, below[:, angles : angles + 1] + 4.0]
    field = []
    for c, line in enumerate(stack_tiles(b_ref)):
        ends = [either_side(near_ref, near_next_ref, c * n + k) for k in range(n)]
        field.append(
            [jnp.concatenate([up, own, low], axis=0) for (up, low), own in zip(ends, line)]
        )
    total = normal(field, wide, avo_ref, bands)
    has_above, has_below = inside("inline")
    for c in range(contrasts):
        strength = strength_ref[:, c : c + 1]
        whole, data = jnp.concatenate(field[c], axis=1), jnp.concatenate(total[c], axis=1)
        lines = [whole[r * traces : (r + 1) * traces] for r in range(rows + 2)]
        for r, here in enumerate(lines):
            north = lines[r - 1] if r else None
            south = lines[r + 1] if r < rows + 1 else None
            if r == 0:
                south = has_above * south
            if r == rows + 1:
                north = has_below * north
            around = lateral(here, north, south, None, None)
            image = data[r * traces : (r + 1) * traces] + strength * (weights[r] * here - around)
            if 0 < r <= rows:
                v_ref[c, r - 1] = image
            else:
                halo_ref[min(r, 1), c] = image
    store_tiles(data_ref, normal(stack_tiles(v_ref), masks, avo_ref, bands))


def image_kernel(
    b_ref, v_ref, data_ref, halo_ref, own_ref, note_ref, far_next_ref, far_ref, other_ref, pair_ref,
    avo_ref, prior_ref, strength_ref, ahead_ref, back_ref,
    one_ref, two_ref, gram_ref,
):
    contrasts, rows, traces, samples = b_ref.shape
    angles, n = avo_ref.shape[1], samples // LANES
    has_left, has_right = inside("col")
    first_col = starts_pair("col")
    place = lax.broadcasted_iota(jnp.int32, (traces, samples), 0)
    west, east = place == 0, place == traces - 1
    half = traces // 2

    def turned(value, k):
        return pltpu.roll(value, k % traces, 0) if k % traces else value

    def sides(i):
        pair, other = pair_ref[i], other_ref[i]
        left, right = jnp.where(first_col, other, pair), jnp.where(first_col, pair, other)
        return jnp.concatenate([left, right], axis=0)

    def at_ends(value, left, right, inner):
        return jnp.where(west, turned(value, left), jnp.where(east, turned(value, right), inner))

    beside = [sides(c) for c in range(contrasts)]
    seconds = [sides(contrasts), sides(contrasts + 1)]
    notes = seconds[1][:, :LANES]
    line = place[:, :LANES]
    theirs = turned(notes, -rows)
    mixed = jnp.where((line == 2) | (line == 3), notes, note_ref[...])
    mixed = jnp.where((line == 4) | (line == 5), theirs, mixed)
    masks = [mixed[:, a : a + 1] for a in range(angles)]
    mine = (place[:, :1] < 2) | (place[:, :1] >= traces - 2)
    tile = []
    for c in range(contrasts):
        scale = jnp.where(mine, -strength_ref[:, c : c + 1], 1.0)
        whole = jnp.where(place % half < rows, beside[c], turned(beside[c], rows)) * scale
        tile.append([whole[:, k * LANES : (k + 1) * LANES] for k in range(n)])
    bands = [(ahead_ref[a], back_ref[a]) for a in range(angles)]
    edge = [jnp.concatenate(tiles, axis=1) for tiles in normal(tile, masks, avo_ref, bands)]

    has = jnp.where(place[:, :1] < half, has_left, has_right)
    far_weight = theirs[:, angles : angles + 1] + 4.0
    weights = [column(prior_ref[r : r + 1, :]) + 4.0 for r in range(rows)]
    sums = [jnp.zeros((traces, LANES), F32) for _ in range(4)]
    for c in range(contrasts):
        strength = strength_ref[:, c : c + 1]
        theirs = beside[c]
        around = turned(seconds[c // 2], -rows * (c % 2)) + turned(theirs, -rows)
        around = around + jnp.where(place % 2 == 1, turned(theirs, 1), turned(theirs, -1))
        prior = far_weight * theirs - (around + has * own_ref[c])
        beyond = jnp.where(place < half, turned(edge[c], -rows), edge[c]) + strength * prior

        far_rows = row_pair(far_ref, far_next_ref, c, n)
        over, under = (halo_ref[i, c] - strength * far_rows[i] for i in (0, 1))
        lines = [over, *[v_ref[c, r] for r in range(rows)], under]
        lines = [
            here - strength * at_ends(theirs, -k, half - 1 - k, 0.0)
            for here, k in zip(lines, (rows, *range(rows), rows + 1))
        ]
        for r in range(rows):
            here, b = lines[r + 1], b_ref[c, r]
            ends = jnp.where(west, turned(beyond, -r), turned(beyond, half - 1 - r))
            around = jnp.where(west, ends, turned(here, 1)) + jnp.where(east, ends, turned(here, -1))
            around = around + lines[r] + lines[r + 2]
            mend = at_ends(edge[c], -r, 1 - r, 0.0)
            two = data_ref[c, r] + mend + strength * (weights[r] * here - around)
            one_ref[c, r] = here
            two_ref[c, r] = two
            for q, product in enumerate((b * b, b * here, here * here, here * two)):
                tiles = [product[:, k : k + LANES] for k in range(0, samples, LANES)]
                sums[q] = sums[q] + functools.reduce(jnp.add, tiles)
    lane = lax.broadcasted_iota(jnp.int32, (1, LANES), 1)
    packed = jnp.zeros((1, LANES), F32)
    for q, total in enumerate(sums):
        total = jnp.sum(jnp.sum(total, axis=0, keepdims=True), axis=1, keepdims=True)
        packed = jnp.where(lane == q, total, packed)
    gram_ref[...] = jnp.broadcast_to(packed[None], gram_ref.shape)


def finish_kernel(gram_ref, b_ref, one_ref, two_ref, solution_ref, residual_ref):
    sums = jnp.sum(gram_ref[...], axis=0)
    g00, g01, g11, g12 = (sums[:, q : q + 1] for q in range(4))
    first = g00 / g01
    ratio = first * g11 / g01
    second = (ratio - 1.0) * g01 / (first * g12 - ratio * g11)
    near = first + second * ratio
    far = first * second
    for c in range(b_ref.shape[0]):
        for r in range(b_ref.shape[1]):
            b, one, two = b_ref[c, r], one_ref[c, r], two_ref[c, r]
            solution_ref[c, r] = near * b - far * one
            residual_ref[c, r] = b - near * one + far * two


VMEM = pl.BlockSpec(memory_space=pltpu.VMEM)
HBM = pl.BlockSpec(memory_space=pltpu.HBM)


def call(kernel, outs, ins, flops, scratch=(), places=None):
    moved = sum(x.size * x.dtype.itemsize for x in (*ins, *outs))
    return pl.pallas_call(
        kernel,
        out_shape=outs,
        in_specs=[VMEM] * len(ins) if places is None else places,
        out_specs=jax.tree.map(lambda _: VMEM, outs),
        scratch_shapes=list(scratch),
        compiler_params=pltpu.CompilerParams(vmem_limit_bytes=24 * 1024 * 1024),
        cost_estimate=pl.CostEstimate(flops=flops, bytes_accessed=moved, transcendentals=0),
        name=getattr(kernel, "func", kernel).__name__,
    )(*ins)


def swap(axis, value, first):
    starts = range(first, lax.axis_size(axis) - 1, 2)
    return lax.ppermute(value, axis, [(i + d, i + 1 - d) for i in starts for d in (0, 1)])


def hand_on(axis, value):
    size = lax.axis_size(axis)
    steps = [(i, i + 2 - 4 * (i % 2)) for i in range(size)]
    return lax.ppermute(value, axis, [(i, j) for i, j in steps if 0 <= j < size])


def shards(seismic, validity, prior_weight, lateral_strength, avo_coeffs, wavelets):
    angles, rows, traces, samples = seismic.shape
    contrasts = avo_coeffs.shape[1]
    avo_coeffs = jnp.swapaxes(avo_coeffs, 0, 1)
    shape = lambda *dims: jax.ShapeDtypeStruct(dims, F32)
    field = shape(contrasts, rows, traces, samples)
    side = shape(contrasts + 2, rows + 2, samples)
    lines = shape(8, 2 * LANES)
    work = 2 * angles * rows * traces * samples * 256 * 4

    given = (seismic, validity, avo_coeffs, wavelets, prior_weight, lateral_strength.reshape(1, -1))
    kept = [given[i] for i in (1, 2, 4, 5)]
    edge = shape(contrasts * samples // LANES + 1, traces, LANES)
    b, near, far, padded, *kept = call(
        start_kernel,
        (
            field, edge, edge, lines,
            *[jax.ShapeDtypeStruct(x.shape, x.dtype) for x in kept],
        ),
        [pltpu.with_memory_space_constraint(x, pltpu.HBM) for x in given],
        work,
        [
            pltpu.VMEM(seismic.shape, seismic.dtype),
            pltpu.VMEM(wavelets.shape, F32),
            pltpu.SemaphoreType.DMA((6,)),
        ],
        [HBM] * 6,
    )
    near = swap("inline", near, 0)
    near_next = swap("inline", far, 1)
    far_next = hand_on("inline", near)
    far = swap("inline", far, 0)
    bands = jax.ShapeDtypeStruct((angles, 2 * LANES, 2 * LANES), BF16)
    ahead, back = call(
        functools.partial(bands_kernel, wavelets.shape[1]), (bands, bands), (padded, near), work // 8
    )
    col_pair, col_other, own, note = call(
        column_kernel,
        (side, side, shape(contrasts, 2 * rows + 4, samples), shape(traces, LANES)),
        (b, near, near_next, kept[0], kept[2]),
        2 * field.size,
        [pltpu.VMEM((2, 2 * rows + 4, samples), F32)],
    )
    col_other = swap("col", col_other, 1)
    col_pair = swap("col", col_pair, 0)
    image, data, halo = call(
        inner_kernel,
        (field, field, shape(2, contrasts, traces, samples)),
        (b, near, near_next, *kept, ahead, back),
        6 * work,
    )
    axes = ("inline", "col")
    one, two, gram = call(
        image_kernel,
        (field, field, shape(lax.axis_size(axes), 1, LANES)),
        (
            b, image, data, halo, own, note, far_next, far, col_other, col_pair,
            *kept[1:], ahead, back,
        ),
        work,
    )
    gram = lax.all_to_all(gram, axes, 0, 0)
    return tuple(call(finish_kernel, (field, field), (gram, b, one, two), 8 * field.size))


def solution(mesh):
    placed = (
        P(None, "inline", "col", None),
        P(None, "inline", "col"),
        P("inline", "col"),
        P(),
        P(),
        P(),
    )
    return jax.shard_map(
        shards,
        mesh=mesh,
        in_specs=placed,
        out_specs=(P(None, "inline", "col", None), P(None, "inline", "col", None)),
        check_vma=False,
    )
```

```python
import functools

import jax
import jax.numpy as jnp
from jax import lax
from jax.experimental import pallas as pl
from jax.experimental.pallas import tpu as pltpu
from jax.sharding import PartitionSpec as P

LANES = 128
F32 = jnp.float32
BF16 = jnp.bfloat16


def split(value):
    high = value.astype(BF16)
    return high, (value - high.astype(F32)).astype(BF16)


def pad_taps(taps_ref, padded_ref):
    padded_ref[...] = jnp.zeros_like(padded_ref)
    padded_ref[0 : taps_ref.shape[0], 0 : taps_ref.shape[1]] = taps_ref[...]


def turn(lines, count):
    n, size = lines.shape
    parts = []
    for _ in range(3):
        parts.append(lines.astype(BF16).astype(F32))
        lines = lines - parts[-1]
    rows = lax.broadcasted_iota(jnp.int32, (size, size), 0)
    cols = lax.broadcasted_iota(jnp.int32, (size, size), 1)
    flip = jnp.where(rows + cols == count - 1, 1.0, 0.0).astype(BF16)
    whole = jnp.concatenate(parts, axis=0).astype(BF16)
    turned = jnp.dot(whole, flip, preferred_element_type=F32)
    return turned[:n] + turned[n : 2 * n] + turned[2 * n :]


def band(line):
    lines = jnp.broadcast_to(line, (LANES, line.shape[1]))
    return pltpu.roll(lines, 0, 1, stride=1, stride_axis=0)


def convolve(rows, line_band):
    halves = jnp.concatenate(split(line_band), axis=0)
    out = lax.dot_general(rows, halves, (((1,), (1,)), ((), ())), preferred_element_type=F32)
    return out[:, :LANES] + out[:, LANES:]


def column(row):
    n = row.shape[1]
    same = lax.broadcasted_iota(jnp.int32, (n, n), 0) == lax.broadcasted_iota(jnp.int32, (n, n), 1)
    return jnp.sum(jnp.where(same, jnp.broadcast_to(row, (n, n)), 0.0), axis=1, keepdims=True)


def trace_columns(ref, *lead):
    rows = ref[lead].astype(F32)
    return jnp.concatenate([column(rows[r : r + 1, :]) for r in range(rows.shape[0])], axis=0)


def windows(tiles):
    pairs = [jnp.concatenate(pair, axis=1) for pair in zip(tiles[:-1], tiles[1:])]
    return jnp.concatenate(pairs, axis=0)


def forward(tiles, bands):
    zero = jnp.zeros_like(tiles[0]).astype(BF16)
    highs, lows = zip(*[split(t) for t in tiles])
    n, size = len(tiles) + 1, tiles[0].shape[0]
    rows = [windows([zero, *part, zero]) for part in (highs, lows)]
    out = convolve(jnp.concatenate(rows, axis=0), bands)
    out = out[: n * size] + out[n * size :]
    return [out[k * size : (k + 1) * size] for k in range(n)]


def backward(parts, bands):
    n, size = len(parts[0]) - 1, parts[0][0].shape[0]
    rows = jnp.concatenate([windows(part) for part in parts], axis=0)
    out = convolve(rows, bands)
    total = out[: n * size]
    for p in range(1, len(parts)):
        total = total + out[p * n * size : (p + 1) * n * size]
    return [total[k * size : (k + 1) * size] for k in range(n)]


def coeff(avo_ref, angle, contrast, k):
    return avo_ref[contrast, angle : angle + 1, pl.ds(k * LANES, LANES)]


def add_terms(total, avo_ref, angle, result):
    for c, line in enumerate(total):
        for k, tile in enumerate(result):
            term = coeff(avo_ref, angle, c, k) * tile
            line[k] = term if angle == 0 else line[k] + term


def store_tiles(out_ref, tiles):
    size = out_ref.shape[2]
    for c in range(out_ref.shape[0]):
        for k, tile in enumerate(tiles[c]):
            for r in range(out_ref.shape[1]):
                out_ref[c, r, :, pl.ds(k * LANES, LANES)] = tile[r * size : (r + 1) * size]


def right_side(seis_ref, masks, avo_ref, bands):
    angles, rows, _, samples = seis_ref.shape
    n = samples // LANES
    total = [[None] * n for _ in range(avo_ref.shape[0])]
    for a in range(angles):
        data = jnp.concatenate([seis_ref[a, r].astype(F32) for r in range(rows)], axis=0)
        data = data * masks[a]
        turned = [
            pltpu.roll(data[:, k * LANES : (k + 1) * LANES], LANES // 2, 1) for k in range(n)
        ]
        zero = jnp.zeros_like(turned[0])
        left_half = lax.broadcasted_iota(jnp.int32, zero.shape, 1) < LANES // 2
        shifted = [
            jnp.where(left_half, before, here).astype(BF16)
            for before, here in zip([zero, *turned], [*turned, zero])
        ]
        add_terms(total, avo_ref, a, backward([shifted], bands[a]))
    return total


def normal(field, masks, avo_ref, bands):
    contrasts, n = len(field), len(field[0])
    total = [[None] * n for _ in range(contrasts)]
    for a, (ahead, back) in enumerate(bands):
        mixed = []
        for k in range(n):
            parts = [coeff(avo_ref, a, c, k) * field[c][k] for c in range(contrasts)]
            mixed.append(functools.reduce(jnp.add, parts))
        synth = [tile * masks[a] for tile in forward(mixed, ahead)]
        left_half = lax.broadcasted_iota(jnp.int32, synth[0].shape, 1) < LANES // 2
        synth[0] = jnp.where(left_half, 0.0, synth[0])
        synth[n] = jnp.where(left_half, synth[n], 0.0)
        result = backward(list(zip(*[split(t) for t in synth])), back)
        add_terms(total, avo_ref, a, result)
    return total


def lateral(here, north, south, west, east):
    traces = here.shape[0]
    place = lax.broadcasted_iota(jnp.int32, here.shape, 0)
    from_west = jnp.where(place == 0, 0.0 if west is None else west, pltpu.roll(here, 1, 0))
    from_east = jnp.where(
        place == traces - 1, 0.0 if east is None else east, pltpu.roll(here, traces - 1, 0)
    )
    around = from_west + from_east
    for other in (north, south):
        around = around if other is None else around + other
    return around


def copy_in(pairs, sems):
    copies = [pltpu.make_async_copy(a, b, sems.at[i]) for i, (a, b) in enumerate(pairs)]
    for copy in copies:
        copy.start()
    return copies


def start_kernel(
    seis_hbm, valid_hbm, avo_hbm, taps_hbm, prior_hbm, strength_hbm,
    b_ref, near_ref, far_ref, padded_ref, valid_ref, avo_ref, prior_ref, strength_ref,
    seis_ref, taps_ref, sems,
):
    copies = copy_in(
        (
            (taps_hbm, taps_ref),
            (valid_hbm, valid_ref),
            (avo_hbm, avo_ref),
            (seis_hbm, seis_ref),
            (prior_hbm, prior_ref),
            (strength_hbm, strength_ref),
        ),
        sems,
    )
    for copy in copies[:2]:
        copy.wait()
    pad_taps(taps_ref, padded_ref)
    angles = avo_ref.shape[1]
    bands = [band(padded_ref[a : a + 1, :]) for a in range(angles)]
    masks = [trace_columns(valid_ref, a) for a in range(angles)]
    for copy in copies[2:]:
        copy.wait()
    store_tiles(b_ref, right_side(seis_ref, masks, avo_ref, bands))
    contrasts, rows, traces, samples = b_ref.shape
    n = samples // LANES
    first = starts_pair("inline")
    lane = lax.broadcasted_iota(jnp.int32, (traces, LANES), 1)
    notes = []
    for r in (0, rows - 1):
        note = jnp.where(lane == angles, column(prior_ref[r : r + 1, :]), 0.0)
        for a in range(angles):
            note = jnp.where(lane == a, masks[a][r * traces : (r + 1) * traces], note)
        notes.append(note)
    edges = [
        [*[b_ref[c, r, :, pl.ds(k * LANES, LANES)] for c in range(contrasts) for k in range(n)], note]
        for r, note in zip((0, rows - 1), notes)
    ]
    for e, (top, bottom) in enumerate(zip(*edges)):
        near_ref[e] = jnp.where(first, bottom, top)
        far_ref[e] = jnp.where(first, top, bottom)


def either_side(pair_ref, next_ref, *where):
    first = starts_pair("inline")
    pair, other = pair_ref[where], next_ref[where]
    return jnp.where(first, other, pair), jnp.where(first, pair, other)


def stack_tiles(ref):
    contrasts, rows, _, samples = ref.shape
    return [
        [
            jnp.concatenate([ref[c, r, :, pl.ds(k, LANES)] for r in range(rows)], axis=0)
            for k in range(0, samples, LANES)
        ]
        for c in range(contrasts)
    ]


def inside(axis):
    place = lax.axis_index(axis)
    last = lax.axis_size(axis) - 1
    return (place > 0).astype(F32), (place < last).astype(F32)


def starts_pair(axis):
    return lax.axis_index(axis) % 2 == 0


def row_pair(near_ref, next_ref, c, n):
    tiles = [either_side(near_ref, next_ref, c * n + k) for k in range(n)]
    return [jnp.concatenate(side, axis=1) for side in zip(*tiles)]


def column_kernel(
    b_ref, near_ref, near_next_ref, valid_ref, prior_ref,
    pair_ref, other_ref, own_ref, note_ref, second_ref,
):
    contrasts, rows, traces, samples = b_ref.shape
    angles = valid_ref.shape[0]
    first_col = starts_pair("col")
    half = rows + 2
    second_ref[...] = jnp.zeros_like(second_ref)
    note_ref[...] = jnp.zeros_like(note_ref)
    for c in range(contrasts):
        own = [b_ref[c, r] for r in range(rows)]
        for i, line in enumerate([*own, *row_pair(near_ref, near_next_ref, c, samples // LANES)]):
            own_ref[c, i : i + 1, :] = line[0:1]
            own_ref[c, half + i : half + i + 1, :] = line[traces - 1 :]
        for r, line in enumerate(own):
            at = c * rows + r
            second_ref[0, at : at + 1, :] = line[1:2]
            second_ref[1, at : at + 1, :] = line[traces - 2 : traces - 1]
    lane = lax.broadcasted_iota(jnp.int32, (1, LANES), 1)
    for r in range(rows):
        for side, t in enumerate((0, traces - 1)):
            note = jnp.where(lane == angles, prior_ref[r : r + 1, t : t + 1], 0.0)
            for a in range(angles):
                note = jnp.where(lane == a, valid_ref[a, r : r + 1, t : t + 1].astype(F32), note)
            at = contrasts * rows + r
            second_ref[side, at : at + 1, 0:LANES] = note
            at = r + side * (traces - rows)
            note_ref[at : at + 1, :] = note
    for c in range(contrasts):
        left, right = own_ref[c, 0:half], own_ref[c, half:]
        pair_ref[c] = jnp.where(first_col, right, left)
        other_ref[c] = jnp.where(first_col, left, right)
    for i in range(2):
        left, right = (second_ref[side, i * half : (i + 1) * half] for side in (0, 1))
        pair_ref[contrasts + i] = jnp.where(first_col, right, left)
        other_ref[contrasts + i] = jnp.where(first_col, left, right)


def bands_kernel(count, padded_ref, near_ref, ahead_ref, back_ref):
    turned = turn(padded_ref[...], count)
    for a in range(ahead_ref.shape[0]):
        ahead_ref[a] = band(turned[a : a + 1])
        back_ref[a] = band(padded_ref[a : a + 1, :])


def inner_kernel(
    b_ref, near_ref, near_next_ref, valid_ref, avo_ref, prior_ref, strength_ref, ahead_ref, back_ref,
    v_ref, data_ref, halo_ref,
):
    contrasts, rows, traces, samples = b_ref.shape
    angles, n = avo_ref.shape[1], samples // LANES
    bands = [(ahead_ref[a], back_ref[a]) for a in range(angles)]
    masks = [trace_columns(valid_ref, a) for a in range(angles)]
    weights = [column(prior_ref[r : r + 1, :]) + 4.0 for r in range(rows)]
    above, below = either_side(near_ref, near_next_ref, contrasts * n)
    wide = [
        jnp.concatenate([above[:, a : a + 1], mask, below[:, a : a + 1]], axis=0)
        for a, mask in enumerate(masks)
    ]
    weights = [above[:, angles : angles + 1] + 4.0, *weights, below[:, angles : angles + 1] + 4.0]
    field = []
    for c, line in enumerate(stack_tiles(b_ref)):
        ends = [either_side(near_ref, near_next_ref, c * n + k) for k in range(n)]
        field.append(
            [jnp.concatenate([up, own, low], axis=0) for (up, low), own in zip(ends, line)]
        )
    total = normal(field, wide, avo_ref, bands)
    has_above, has_below = inside("inline")
    for c in range(contrasts):
        strength = strength_ref[:, c : c + 1]
        whole, data = jnp.concatenate(field[c], axis=1), jnp.concatenate(total[c], axis=1)
        lines = [whole[r * traces : (r + 1) * traces] for r in range(rows + 2)]
        for r, here in enumerate(lines):
            north = lines[r - 1] if r else None
            south = lines[r + 1] if r < rows + 1 else None
            if r == 0:
                south = has_above * south
            if r == rows + 1:
                north = has_below * north
            around = lateral(here, north, south, None, None)
            image = data[r * traces : (r + 1) * traces] + strength * (weights[r] * here - around)
            if 0 < r <= rows:
                v_ref[c, r - 1] = image
            else:
                halo_ref[min(r, 1), c] = image
    store_tiles(data_ref, normal(stack_tiles(v_ref), masks, avo_ref, bands))


def image_kernel(
    b_ref, v_ref, data_ref, halo_ref, own_ref, note_ref, far_next_ref, far_ref, other_ref, pair_ref,
    avo_ref, prior_ref, strength_ref, ahead_ref, back_ref,
    one_ref, two_ref, gram_ref,
):
    contrasts, rows, traces, samples = b_ref.shape
    angles, n = avo_ref.shape[1], samples // LANES
    has_left, has_right = inside("col")
    first_col = starts_pair("col")
    place = lax.broadcasted_iota(jnp.int32, (traces, samples), 0)
    west, east = place == 0, place == traces - 1
    half = traces // 2

    def turned(value, k):
        return pltpu.roll(value, k % traces, 0) if k % traces else value

    def sides(i):
        pair, other = pair_ref[i], other_ref[i]
        left, right = jnp.where(first_col, other, pair), jnp.where(first_col, pair, other)
        return jnp.concatenate([left, right], axis=0)

    def at_ends(value, left, right, inner):
        return jnp.where(west, turned(value, left), jnp.where(east, turned(value, right), inner))

    beside = [sides(c) for c in range(contrasts)]
    seconds = [sides(contrasts), sides(contrasts + 1)]
    notes = seconds[1][:, :LANES]
    line = place[:, :LANES]
    theirs = turned(notes, -rows)
    mixed = jnp.where((line == 2) | (line == 3), notes, note_ref[...])
    mixed = jnp.where((line == 4) | (line == 5), theirs, mixed)
    masks = [mixed[:, a : a + 1] for a in range(angles)]
    mine = (place[:, :1] < 2) | (place[:, :1] >= traces - 2)
    tile = []
    for c in range(contrasts):
        scale = jnp.where(mine, -strength_ref[:, c : c + 1], 1.0)
        whole = jnp.where(place % half < rows, beside[c], turned(beside[c], rows)) * scale
        tile.append([whole[:, k * LANES : (k + 1) * LANES] for k in range(n)])
    bands = [(ahead_ref[a], back_ref[a]) for a in range(angles)]
    edge = [jnp.concatenate(tiles, axis=1) for tiles in normal(tile, masks, avo_ref, bands)]

    has = jnp.where(place[:, :1] < half, has_left, has_right)
    far_weight = theirs[:, angles : angles + 1] + 4.0
    weights = [column(prior_ref[r : r + 1, :]) + 4.0 for r in range(rows)]
    sums = [jnp.zeros((traces, LANES), F32) for _ in range(4)]
    for c in range(contrasts):
        strength = strength_ref[:, c : c + 1]
        theirs = beside[c]
        around = turned(seconds[c // 2], -rows * (c % 2)) + turned(theirs, -rows)
        around = around + jnp.where(place % 2 == 1, turned(theirs, 1), turned(theirs, -1))
        prior = far_weight * theirs - (around + has * own_ref[c])
        beyond = jnp.where(place < half, turned(edge[c], -rows), edge[c]) + strength * prior

        far_rows = row_pair(far_ref, far_next_ref, c, n)
        over, under = (halo_ref[i, c] - strength * far_rows[i] for i in (0, 1))
        lines = [over, *[v_ref[c, r] for r in range(rows)], under]
        lines = [
            here - strength * at_ends(theirs, -k, half - 1 - k, 0.0)
            for here, k in zip(lines, (rows, *range(rows), rows + 1))
        ]
        for r in range(rows):
            here, b = lines[r + 1], b_ref[c, r]
            ends = jnp.where(west, turned(beyond, -r), turned(beyond, half - 1 - r))
            around = jnp.where(west, ends, turned(here, 1)) + jnp.where(east, ends, turned(here, -1))
            around = around + lines[r] + lines[r + 2]
            mend = at_ends(edge[c], -r, 1 - r, 0.0)
            two = data_ref[c, r] + mend + strength * (weights[r] * here - around)
            one_ref[c, r] = here
            two_ref[c, r] = two
            for q, product in enumerate((b * b, b * here, here * here, here * two)):
                tiles = [product[:, k : k + LANES] for k in range(0, samples, LANES)]
                sums[q] = sums[q] + functools.reduce(jnp.add, tiles)
    lane = lax.broadcasted_iota(jnp.int32, (1, LANES), 1)
    packed = jnp.zeros((1, LANES), F32)
    for q, total in enumerate(sums):
        total = jnp.sum(jnp.sum(total, axis=0, keepdims=True), axis=1, keepdims=True)
        packed = jnp.where(lane == q, total, packed)
    gram_ref[...] = jnp.broadcast_to(packed[None], gram_ref.shape)


def finish_kernel(gram_ref, b_ref, one_ref, two_ref, solution_ref, residual_ref):
    sums = jnp.sum(gram_ref[...], axis=0)
    g00, g01, g11, g12 = (sums[:, q : q + 1] for q in range(4))
    first = g00 / g01
    ratio = first * g11 / g01
    second = (ratio - 1.0) * g01 / (first * g12 - ratio * g11)
    near = first + second * ratio
    far = first * second
    for c in range(b_ref.shape[0]):
        for r in range(b_ref.shape[1]):
            b, one, two = b_ref[c, r], one_ref[c, r], two_ref[c, r]
            solution_ref[c, r] = near * b - far * one
            residual_ref[c, r] = b - near * one + far * two


VMEM = pl.BlockSpec(memory_space=pltpu.VMEM)
HBM = pl.BlockSpec(memory_space=pltpu.HBM)


def call(kernel, outs, ins, flops, scratch=(), places=None):
    moved = sum(x.size * x.dtype.itemsize for x in (*ins, *outs))
    return pl.pallas_call(
        kernel,
        out_shape=outs,
        in_specs=[VMEM] * len(ins) if places is None else places,
        out_specs=jax.tree.map(lambda _: VMEM, outs),
        scratch_shapes=list(scratch),
        compiler_params=pltpu.CompilerParams(vmem_limit_bytes=24 * 1024 * 1024),
        cost_estimate=pl.CostEstimate(flops=flops, bytes_accessed=moved, transcendentals=0),
        name=getattr(kernel, "func", kernel).__name__,
    )(*ins)


def swap(axis, value, first):
    starts = range(first, lax.axis_size(axis) - 1, 2)
    return lax.ppermute(value, axis, [(i + d, i + 1 - d) for i in starts for d in (0, 1)])


def hand_on(axis, value):
    size = lax.axis_size(axis)
    steps = [(i, i + 2 - 4 * (i % 2)) for i in range(size)]
    return lax.ppermute(value, axis, [(i, j) for i, j in steps if 0 <= j < size])


def shards(seismic, validity, prior_weight, lateral_strength, avo_coeffs, wavelets):
    angles, rows, traces, samples = seismic.shape
    contrasts = avo_coeffs.shape[1]
    avo_coeffs = jnp.swapaxes(avo_coeffs, 0, 1)
    shape = lambda *dims: jax.ShapeDtypeStruct(dims, F32)
    field = shape(contrasts, rows, traces, samples)
    side = shape(contrasts + 2, rows + 2, samples)
    lines = shape(8, 2 * LANES)
    work = 2 * angles * rows * traces * samples * 256 * 4

    given = (seismic, validity, avo_coeffs, wavelets, prior_weight, lateral_strength.reshape(1, -1))
    kept = [given[i] for i in (1, 2, 4, 5)]
    edge = shape(contrasts * samples // LANES + 1, traces, LANES)
    b, near, far, padded, *kept = call(
        start_kernel,
        (
            field, edge, edge, lines,
            *[jax.ShapeDtypeStruct(x.shape, x.dtype) for x in kept],
        ),
        [pltpu.with_memory_space_constraint(x, pltpu.HBM) for x in given],
        work,
        [
            pltpu.VMEM(seismic.shape, seismic.dtype),
            pltpu.VMEM(wavelets.shape, F32),
            pltpu.SemaphoreType.DMA((6,)),
        ],
        [HBM] * 6,
    )
    near = swap("inline", near, 0)
    near_next = swap("inline", far, 1)
    far_next = hand_on("inline", near)
    far = swap("inline", far, 0)
    bands = shape(angles, LANES, 2 * LANES)
    ahead, back = call(
        functools.partial(bands_kernel, wavelets.shape[1]), (bands, bands), (padded, near), work // 8
    )
    col_pair, col_other, own, note = call(
        column_kernel,
        (side, side, shape(contrasts, 2 * rows + 4, samples), shape(traces, LANES)),
        (b, near, near_next, kept[0], kept[2]),
        2 * field.size,
        [pltpu.VMEM((2, 2 * rows + 4, samples), F32)],
    )
    col_other = swap("col", col_other, 1)
    col_pair = swap("col", col_pair, 0)
    image, data, halo = call(
        inner_kernel,
        (field, field, shape(2, contrasts, traces, samples)),
        (b, near, near_next, *kept, ahead, back),
        6 * work,
    )
    axes = ("inline", "col")
    one, two, gram = call(
        image_kernel,
        (field, field, shape(lax.axis_size(axes), 1, LANES)),
        (
            b, image, data, halo, own, note, far_next, far, col_other, col_pair,
            *kept[1:], ahead, back,
        ),
        work,
    )
    gram = lax.all_to_all(gram, axes, 0, 0)
    return tuple(call(finish_kernel, (field, field), (gram, b, one, two), 8 * field.size))


def solution(mesh):
    placed = (
        P(None, "inline", "col", None),
        P(None, "inline", "col"),
        P("inline", "col"),
        P(),
        P(),
        P(),
    )
    return jax.shard_map(
        shards,
        mesh=mesh,
        in_specs=placed,
        out_specs=(P(None, "inline", "col", None), P(None, "inline", "col", None)),
        check_vma=False,
    )
```

```python
import functools

import jax
import jax.numpy as jnp
from jax import lax
from jax.experimental import pallas as pl
from jax.experimental.pallas import tpu as pltpu
from jax.sharding import PartitionSpec as P

LANES = 128
F32 = jnp.float32
BF16 = jnp.bfloat16


def split(value):
    high = value.astype(BF16)
    return high, (value - high.astype(F32)).astype(BF16)


def pad_taps(taps_ref, padded_ref):
    padded_ref[...] = jnp.zeros_like(padded_ref)
    padded_ref[0 : taps_ref.shape[0], 0 : taps_ref.shape[1]] = taps_ref[...]


def turn(lines, count):
    n, size = lines.shape
    parts = []
    for _ in range(3):
        parts.append(lines.astype(BF16).astype(F32))
        lines = lines - parts[-1]
    rows = lax.broadcasted_iota(jnp.int32, (size, size), 0)
    cols = lax.broadcasted_iota(jnp.int32, (size, size), 1)
    flip = jnp.where(rows + cols == count - 1, 1.0, 0.0).astype(BF16)
    whole = jnp.concatenate(parts, axis=0).astype(BF16)
    turned = jnp.dot(whole, flip, preferred_element_type=F32)
    return turned[:n] + turned[n : 2 * n] + turned[2 * n :]


def band(line):
    lines = jnp.broadcast_to(line, (LANES, line.shape[1]))
    return jnp.concatenate(split(pltpu.roll(lines, 0, 1, stride=1, stride_axis=0)), axis=0)


def convolve(rows, bands):
    out = lax.dot_general(rows, bands, (((1,), (1,)), ((), ())), preferred_element_type=F32)
    return out[:, :LANES] + out[:, LANES:]


def column(row):
    n = row.shape[1]
    same = lax.broadcasted_iota(jnp.int32, (n, n), 0) == lax.broadcasted_iota(jnp.int32, (n, n), 1)
    return jnp.sum(jnp.where(same, jnp.broadcast_to(row, (n, n)), 0.0), axis=1, keepdims=True)


def trace_columns(ref, *lead):
    rows = ref[lead].astype(F32)
    return jnp.concatenate([column(rows[r : r + 1, :]) for r in range(rows.shape[0])], axis=0)


def windows(tiles):
    pairs = [jnp.concatenate(pair, axis=1) for pair in zip(tiles[:-1], tiles[1:])]
    return jnp.concatenate(pairs, axis=0)


def forward(tiles, bands):
    zero = jnp.zeros_like(tiles[0]).astype(BF16)
    highs, lows = zip(*[split(t) for t in tiles])
    n, size = len(tiles) + 1, tiles[0].shape[0]
    rows = [windows([zero, *part, zero]) for part in (highs, lows)]
    out = convolve(jnp.concatenate(rows, axis=0), bands)
    out = out[: n * size] + out[n * size :]
    return [out[k * size : (k + 1) * size] for k in range(n)]


def backward(parts, bands):
    n, size = len(parts[0]) - 1, parts[0][0].shape[0]
    rows = jnp.concatenate([windows(part) for part in parts], axis=0)
    out = convolve(rows, bands)
    total = out[: n * size]
    for p in range(1, len(parts)):
        total = total + out[p * n * size : (p + 1) * n * size]
    return [total[k * size : (k + 1) * size] for k in range(n)]


def coeff(avo_ref, angle, contrast, k):
    return avo_ref[contrast, angle : angle + 1, pl.ds(k * LANES, LANES)]


def add_terms(total, avo_ref, angle, result):
    for c, line in enumerate(total):
        for k, tile in enumerate(result):
            term = coeff(avo_ref, angle, c, k) * tile
            line[k] = term if angle == 0 else line[k] + term


def store_tiles(out_ref, tiles):
    size = out_ref.shape[2]
    for c in range(out_ref.shape[0]):
        for k, tile in enumerate(tiles[c]):
            for r in range(out_ref.shape[1]):
                out_ref[c, r, :, pl.ds(k * LANES, LANES)] = tile[r * size : (r + 1) * size]


def right_side(seis_ref, masks, avo_ref, bands):
    angles, rows, _, samples = seis_ref.shape
    n = samples // LANES
    total = [[None] * n for _ in range(avo_ref.shape[0])]
    for a in range(angles):
        data = jnp.concatenate([seis_ref[a, r].astype(F32) for r in range(rows)], axis=0)
        data = data * masks[a]
        turned = [
            pltpu.roll(data[:, k * LANES : (k + 1) * LANES], LANES // 2, 1) for k in range(n)
        ]
        zero = jnp.zeros_like(turned[0])
        left_half = lax.broadcasted_iota(jnp.int32, zero.shape, 1) < LANES // 2
        shifted = [
            jnp.where(left_half, before, here).astype(BF16)
            for before, here in zip([zero, *turned], [*turned, zero])
        ]
        add_terms(total, avo_ref, a, backward([shifted], bands[a]))
    return total


def normal(field, masks, avo_ref, bands):
    contrasts, n = len(field), len(field[0])
    total = [[None] * n for _ in range(contrasts)]
    for a, (ahead, back) in enumerate(bands):
        mixed = []
        for k in range(n):
            parts = [coeff(avo_ref, a, c, k) * field[c][k] for c in range(contrasts)]
            mixed.append(functools.reduce(jnp.add, parts))
        synth = [tile * masks[a] for tile in forward(mixed, ahead)]
        left_half = lax.broadcasted_iota(jnp.int32, synth[0].shape, 1) < LANES // 2
        synth[0] = jnp.where(left_half, 0.0, synth[0])
        synth[n] = jnp.where(left_half, synth[n], 0.0)
        result = backward(list(zip(*[split(t) for t in synth])), back)
        add_terms(total, avo_ref, a, result)
    return total


def lateral(here, north, south, west, east):
    traces = here.shape[0]
    place = lax.broadcasted_iota(jnp.int32, here.shape, 0)
    from_west = jnp.where(place == 0, 0.0 if west is None else west, pltpu.roll(here, 1, 0))
    from_east = jnp.where(
        place == traces - 1, 0.0 if east is None else east, pltpu.roll(here, traces - 1, 0)
    )
    around = from_west + from_east
    for other in (north, south):
        around = around if other is None else around + other
    return around


def copy_in(pairs, sems):
    copies = [pltpu.make_async_copy(a, b, sems.at[i]) for i, (a, b) in enumerate(pairs)]
    for copy in copies:
        copy.start()
    return copies


def start_kernel(
    seis_hbm, valid_hbm, avo_hbm, taps_hbm, prior_hbm, strength_hbm,
    b_ref, near_ref, far_ref, padded_ref, valid_ref, avo_ref, prior_ref, strength_ref,
    seis_ref, taps_ref, sems,
):
    copies = copy_in(
        (
            (taps_hbm, taps_ref),
            (valid_hbm, valid_ref),
            (avo_hbm, avo_ref),
            (seis_hbm, seis_ref),
            (prior_hbm, prior_ref),
            (strength_hbm, strength_ref),
        ),
        sems,
    )
    for copy in copies[:2]:
        copy.wait()
    pad_taps(taps_ref, padded_ref)
    angles = avo_ref.shape[1]
    bands = [band(padded_ref[a : a + 1, :]) for a in range(angles)]
    masks = [trace_columns(valid_ref, a) for a in range(angles)]
    for copy in copies[2:]:
        copy.wait()
    store_tiles(b_ref, right_side(seis_ref, masks, avo_ref, bands))
    contrasts, rows, traces, samples = b_ref.shape
    n = samples // LANES
    first = starts_pair("inline")
    lane = lax.broadcasted_iota(jnp.int32, (traces, LANES), 1)
    notes = []
    for r in (0, rows - 1):
        note = jnp.where(lane == angles, column(prior_ref[r : r + 1, :]), 0.0)
        for a in range(angles):
            note = jnp.where(lane == a, masks[a][r * traces : (r + 1) * traces], note)
        notes.append(note)
    edges = [
        [*[b_ref[c, r, :, pl.ds(k * LANES, LANES)] for c in range(contrasts) for k in range(n)], note]
        for r, note in zip((0, rows - 1), notes)
    ]
    for e, (top, bottom) in enumerate(zip(*edges)):
        near_ref[e] = jnp.where(first, bottom, top)
        far_ref[e] = jnp.where(first, top, bottom)


def either_side(pair_ref, next_ref, *where):
    first = starts_pair("inline")
    pair, other = pair_ref[where], next_ref[where]
    return jnp.where(first, other, pair), jnp.where(first, pair, other)


def stack_tiles(ref):
    contrasts, rows, _, samples = ref.shape
    return [
        [
            jnp.concatenate([ref[c, r, :, pl.ds(k, LANES)] for r in range(rows)], axis=0)
            for k in range(0, samples, LANES)
        ]
        for c in range(contrasts)
    ]


def inside(axis):
    place = lax.axis_index(axis)
    last = lax.axis_size(axis) - 1
    return (place > 0).astype(F32), (place < last).astype(F32)


def starts_pair(axis):
    return lax.axis_index(axis) % 2 == 0


def row_pair(near_ref, next_ref, c, n):
    tiles = [either_side(near_ref, next_ref, c * n + k) for k in range(n)]
    return [jnp.concatenate(side, axis=1) for side in zip(*tiles)]


def column_kernel(
    b_ref, near_ref, near_next_ref, valid_ref, prior_ref,
    pair_ref, other_ref, own_ref, note_ref, second_ref,
):
    contrasts, rows, traces, samples = b_ref.shape
    angles = valid_ref.shape[0]
    first_col = starts_pair("col")
    half = rows + 2
    second_ref[...] = jnp.zeros_like(second_ref)
    note_ref[...] = jnp.zeros_like(note_ref)
    for c in range(contrasts):
        own = [b_ref[c, r] for r in range(rows)]
        for i, line in enumerate([*own, *row_pair(near_ref, near_next_ref, c, samples // LANES)]):
            own_ref[c, i : i + 1, :] = line[0:1]
            own_ref[c, half + i : half + i + 1, :] = line[traces - 1 :]
        for r, line in enumerate(own):
            at = c * rows + r
            second_ref[0, at : at + 1, :] = line[1:2]
            second_ref[1, at : at + 1, :] = line[traces - 2 : traces - 1]
    lane = lax.broadcasted_iota(jnp.int32, (1, LANES), 1)
    for r in range(rows):
        for side, t in enumerate((0, traces - 1)):
            note = jnp.where(lane == angles, prior_ref[r : r + 1, t : t + 1], 0.0)
            for a in range(angles):
                note = jnp.where(lane == a, valid_ref[a, r : r + 1, t : t + 1].astype(F32), note)
            at = contrasts * rows + r
            second_ref[side, at : at + 1, 0:LANES] = note
            at = r + side * (traces - rows)
            note_ref[at : at + 1, :] = note
    for c in range(contrasts):
        left, right = own_ref[c, 0:half], own_ref[c, half:]
        pair_ref[c] = jnp.where(first_col, right, left)
        other_ref[c] = jnp.where(first_col, left, right)
    for i in range(2):
        left, right = (second_ref[side, i * half : (i + 1) * half] for side in (0, 1))
        pair_ref[contrasts + i] = jnp.where(first_col, right, left)
        other_ref[contrasts + i] = jnp.where(first_col, left, right)


def inner_kernel(
    count, b_ref, near_ref, near_next_ref, padded_ref, valid_ref, avo_ref, prior_ref, strength_ref,
    v_ref, data_ref, halo_ref, ahead_ref, back_ref,
):
    contrasts, rows, traces, samples = b_ref.shape
    angles, n = avo_ref.shape[1], samples // LANES
    turned = turn(padded_ref[...], count)
    bands = []
    for a in range(angles):
        bands.append((band(turned[a : a + 1]), band(padded_ref[a : a + 1, :])))
        ahead_ref[a], back_ref[a] = (half.astype(F32) for half in bands[a])
    masks = [trace_columns(valid_ref, a) for a in range(angles)]
    weights = [column(prior_ref[r : r + 1, :]) + 4.0 for r in range(rows)]
    above, below = either_side(near_ref, near_next_ref, contrasts * n)
    wide = [
        jnp.concatenate([above[:, a : a + 1], mask, below[:, a : a + 1]], axis=0)
        for a, mask in enumerate(masks)
    ]
    weights = [above[:, angles : angles + 1] + 4.0, *weights, below[:, angles : angles + 1] + 4.0]
    field = []
    for c, line in enumerate(stack_tiles(b_ref)):
        ends = [either_side(near_ref, near_next_ref, c * n + k) for k in range(n)]
        field.append(
            [jnp.concatenate([up, own, low], axis=0) for (up, low), own in zip(ends, line)]
        )
    total = normal(field, wide, avo_ref, bands)
    has_above, has_below = inside("inline")
    for c in range(contrasts):
        strength = strength_ref[:, c : c + 1]
        whole, data = jnp.concatenate(field[c], axis=1), jnp.concatenate(total[c], axis=1)
        lines = [whole[r * traces : (r + 1) * traces] for r in range(rows + 2)]
        for r, here in enumerate(lines):
            north = lines[r - 1] if r else None
            south = lines[r + 1] if r < rows + 1 else None
            if r == 0:
                south = has_above * south
            if r == rows + 1:
                north = has_below * north
            around = lateral(here, north, south, None, None)
            image = data[r * traces : (r + 1) * traces] + strength * (weights[r] * here - around)
            if 0 < r <= rows:
                v_ref[c, r - 1] = image
            else:
                halo_ref[min(r, 1), c] = image
    store_tiles(data_ref, normal(stack_tiles(v_ref), masks, avo_ref, bands))


def image_kernel(
    b_ref, v_ref, data_ref, halo_ref, own_ref, note_ref, far_next_ref, far_ref, other_ref, pair_ref,
    avo_ref, prior_ref, strength_ref, ahead_ref, back_ref,
    one_ref, two_ref, gram_ref,
):
    contrasts, rows, traces, samples = b_ref.shape
    angles, n = avo_ref.shape[1], samples // LANES
    has_left, has_right = inside("col")
    first_col = starts_pair("col")
    place = lax.broadcasted_iota(jnp.int32, (traces, samples), 0)
    west, east = place == 0, place == traces - 1
    half = traces // 2

    def turned(value, k):
        return pltpu.roll(value, k % traces, 0) if k % traces else value

    def sides(i):
        pair, other = pair_ref[i], other_ref[i]
        left, right = jnp.where(first_col, other, pair), jnp.where(first_col, pair, other)
        return jnp.concatenate([left, right], axis=0)

    def at_ends(value, left, right, inner):
        return jnp.where(west, turned(value, left), jnp.where(east, turned(value, right), inner))

    beside = [sides(c) for c in range(contrasts)]
    seconds = [sides(contrasts), sides(contrasts + 1)]
    notes = seconds[1][:, :LANES]
    line = place[:, :LANES]
    theirs = turned(notes, -rows)
    mixed = jnp.where((line == 2) | (line == 3), notes, note_ref[...])
    mixed = jnp.where((line == 4) | (line == 5), theirs, mixed)
    masks = [mixed[:, a : a + 1] for a in range(angles)]
    mine = (place[:, :1] < 2) | (place[:, :1] >= traces - 2)
    tile = []
    for c in range(contrasts):
        scale = jnp.where(mine, -strength_ref[:, c : c + 1], 1.0)
        whole = jnp.where(place % half < rows, beside[c], turned(beside[c], rows)) * scale
        tile.append([whole[:, k * LANES : (k + 1) * LANES] for k in range(n)])
    bands = [(ahead_ref[a].astype(BF16), back_ref[a].astype(BF16)) for a in range(angles)]
    edge = [jnp.concatenate(tiles, axis=1) for tiles in normal(tile, masks, avo_ref, bands)]

    has = jnp.where(place[:, :1] < half, has_left, has_right)
    far_weight = theirs[:, angles : angles + 1] + 4.0
    weights = [column(prior_ref[r : r + 1, :]) + 4.0 for r in range(rows)]
    sums = [jnp.zeros((traces, LANES), F32) for _ in range(4)]
    for c in range(contrasts):
        strength = strength_ref[:, c : c + 1]
        theirs = beside[c]
        around = turned(seconds[c // 2], -rows * (c % 2)) + turned(theirs, -rows)
        around = around + jnp.where(place % 2 == 1, turned(theirs, 1), turned(theirs, -1))
        prior = far_weight * theirs - (around + has * own_ref[c])
        beyond = jnp.where(place < half, turned(edge[c], -rows), edge[c]) + strength * prior

        far_rows = row_pair(far_ref, far_next_ref, c, n)
        over, under = (halo_ref[i, c] - strength * far_rows[i] for i in (0, 1))
        lines = [over, *[v_ref[c, r] for r in range(rows)], under]
        lines = [
            here - strength * at_ends(theirs, -k, half - 1 - k, 0.0)
            for here, k in zip(lines, (rows, *range(rows), rows + 1))
        ]
        for r in range(rows):
            here, b = lines[r + 1], b_ref[c, r]
            ends = jnp.where(west, turned(beyond, -r), turned(beyond, half - 1 - r))
            around = jnp.where(west, ends, turned(here, 1)) + jnp.where(east, ends, turned(here, -1))
            around = around + lines[r] + lines[r + 2]
            mend = at_ends(edge[c], -r, 1 - r, 0.0)
            two = data_ref[c, r] + mend + strength * (weights[r] * here - around)
            one_ref[c, r] = here
            two_ref[c, r] = two
            for q, product in enumerate((b * b, b * here, here * here, here * two)):
                tiles = [product[:, k : k + LANES] for k in range(0, samples, LANES)]
                sums[q] = sums[q] + functools.reduce(jnp.add, tiles)
    lane = lax.broadcasted_iota(jnp.int32, (1, LANES), 1)
    packed = jnp.zeros((1, LANES), F32)
    for q, total in enumerate(sums):
        total = jnp.sum(jnp.sum(total, axis=0, keepdims=True), axis=1, keepdims=True)
        packed = jnp.where(lane == q, total, packed)
    gram_ref[...] = jnp.broadcast_to(packed[None], gram_ref.shape)


def finish_kernel(gram_ref, b_ref, one_ref, two_ref, solution_ref, residual_ref):
    sums = jnp.sum(gram_ref[...], axis=0)
    g00, g01, g11, g12 = (sums[:, q : q + 1] for q in range(4))
    first = g00 / g01
    ratio = first * g11 / g01
    second = (ratio - 1.0) * g01 / (first * g12 - ratio * g11)
    near = first + second * ratio
    far = first * second
    for c in range(b_ref.shape[0]):
        for r in range(b_ref.shape[1]):
            b, one, two = b_ref[c, r], one_ref[c, r], two_ref[c, r]
            solution_ref[c, r] = near * b - far * one
            residual_ref[c, r] = b - near * one + far * two


VMEM = pl.BlockSpec(memory_space=pltpu.VMEM)
HBM = pl.BlockSpec(memory_space=pltpu.HBM)


def call(kernel, outs, ins, flops, scratch=(), places=None):
    moved = sum(x.size * x.dtype.itemsize for x in (*ins, *outs))
    return pl.pallas_call(
        kernel,
        out_shape=outs,
        in_specs=[VMEM] * len(ins) if places is None else places,
        out_specs=jax.tree.map(lambda _: VMEM, outs),
        scratch_shapes=list(scratch),
        compiler_params=pltpu.CompilerParams(vmem_limit_bytes=24 * 1024 * 1024),
        cost_estimate=pl.CostEstimate(flops=flops, bytes_accessed=moved, transcendentals=0),
        name=getattr(kernel, "func", kernel).__name__,
    )(*ins)


def swap(axis, value, first):
    starts = range(first, lax.axis_size(axis) - 1, 2)
    return lax.ppermute(value, axis, [(i + d, i + 1 - d) for i in starts for d in (0, 1)])


def hand_on(axis, value):
    size = lax.axis_size(axis)
    steps = [(i, i + 2 - 4 * (i % 2)) for i in range(size)]
    return lax.ppermute(value, axis, [(i, j) for i, j in steps if 0 <= j < size])


def shards(seismic, validity, prior_weight, lateral_strength, avo_coeffs, wavelets):
    angles, rows, traces, samples = seismic.shape
    contrasts = avo_coeffs.shape[1]
    avo_coeffs = jnp.swapaxes(avo_coeffs, 0, 1)
    shape = lambda *dims: jax.ShapeDtypeStruct(dims, F32)
    field = shape(contrasts, rows, traces, samples)
    side = shape(contrasts + 2, rows + 2, samples)
    lines = shape(8, 2 * LANES)
    work = 2 * angles * rows * traces * samples * 256 * 4

    given = (seismic, validity, avo_coeffs, wavelets, prior_weight, lateral_strength.reshape(1, -1))
    kept = [given[i] for i in (1, 2, 4, 5)]
    edge = shape(contrasts * samples // LANES + 1, traces, LANES)
    b, near, far, padded, *kept = call(
        start_kernel,
        (
            field, edge, edge, lines,
            *[jax.ShapeDtypeStruct(x.shape, x.dtype) for x in kept],
        ),
        [pltpu.with_memory_space_constraint(x, pltpu.HBM) for x in given],
        work,
        [
            pltpu.VMEM(seismic.shape, seismic.dtype),
            pltpu.VMEM(wavelets.shape, F32),
            pltpu.SemaphoreType.DMA((6,)),
        ],
        [HBM] * 6,
    )
    near = swap("inline", near, 0)
    near_next = swap("inline", far, 1)
    far_next = hand_on("inline", near)
    far = swap("inline", far, 0)
    col_pair, col_other, own, note = call(
        column_kernel,
        (side, side, shape(contrasts, 2 * rows + 4, samples), shape(traces, LANES)),
        (b, near, near_next, kept[0], kept[2]),
        2 * field.size,
        [pltpu.VMEM((2, 2 * rows + 4, samples), F32)],
    )
    col_other = swap("col", col_other, 1)
    col_pair = swap("col", col_pair, 0)
    bands = shape(angles, 2 * LANES, 2 * LANES)
    image, data, halo, ahead, back = call(
        functools.partial(inner_kernel, wavelets.shape[1]),
        (field, field, shape(2, contrasts, traces, samples), bands, bands),
        (b, near, near_next, padded, *kept),
        6 * work,
    )
    axes = ("inline", "col")
    one, two, gram = call(
        image_kernel,
        (field, field, shape(lax.axis_size(axes), 1, LANES)),
        (
            b, image, data, halo, own, note, far_next, far, col_other, col_pair,
            *kept[1:], ahead, back,
        ),
        work,
    )
    gram = lax.all_to_all(gram, axes, 0, 0)
    return tuple(call(finish_kernel, (field, field), (gram, b, one, two), 8 * field.size))


def solution(mesh):
    placed = (
        P(None, "inline", "col", None),
        P(None, "inline", "col"),
        P("inline", "col"),
        P(),
        P(),
        P(),
    )
    return jax.shard_map(
        shards,
        mesh=mesh,
        in_specs=placed,
        out_specs=(P(None, "inline", "col", None), P(None, "inline", "col", None)),
        check_vma=False,
    )
```

```python
import functools

import jax
import jax.numpy as jnp
from jax import lax
from jax.experimental import pallas as pl
from jax.experimental.pallas import tpu as pltpu
from jax.sharding import PartitionSpec as P

LANES = 128
F32 = jnp.float32
BF16 = jnp.bfloat16


def split(value):
    high = value.astype(BF16)
    return high, (value - high.astype(F32)).astype(BF16)


def pad_taps(taps_ref, padded_ref):
    padded_ref[...] = jnp.zeros_like(padded_ref)
    padded_ref[0 : taps_ref.shape[0], 0 : taps_ref.shape[1]] = taps_ref[...]


def turn(lines, count):
    n, size = lines.shape
    parts = []
    for _ in range(3):
        parts.append(lines.astype(BF16).astype(F32))
        lines = lines - parts[-1]
    rows = lax.broadcasted_iota(jnp.int32, (size, size), 0)
    cols = lax.broadcasted_iota(jnp.int32, (size, size), 1)
    flip = jnp.where(rows + cols == count - 1, 1.0, 0.0).astype(BF16)
    whole = jnp.concatenate(parts, axis=0).astype(BF16)
    turned = jnp.dot(whole, flip, preferred_element_type=F32)
    return turned[:n] + turned[n : 2 * n] + turned[2 * n :]


def band(line):
    lines = jnp.broadcast_to(line, (LANES, line.shape[1]))
    return jnp.concatenate(split(pltpu.roll(lines, 0, 1, stride=1, stride_axis=0)), axis=0)


def convolve(rows, bands):
    out = lax.dot_general(rows, bands, (((1,), (1,)), ((), ())), preferred_element_type=F32)
    return out[:, :LANES] + out[:, LANES:]


def column(row):
    n = row.shape[1]
    same = lax.broadcasted_iota(jnp.int32, (n, n), 0) == lax.broadcasted_iota(jnp.int32, (n, n), 1)
    return jnp.sum(jnp.where(same, jnp.broadcast_to(row, (n, n)), 0.0), axis=1, keepdims=True)


def trace_columns(ref, *lead):
    rows = ref[lead].astype(F32)
    return jnp.concatenate([column(rows[r : r + 1, :]) for r in range(rows.shape[0])], axis=0)


def windows(tiles):
    pairs = [jnp.concatenate(pair, axis=1) for pair in zip(tiles[:-1], tiles[1:])]
    return jnp.concatenate(pairs, axis=0)


def forward(tiles, bands):
    zero = jnp.zeros_like(tiles[0]).astype(BF16)
    highs, lows = zip(*[split(t) for t in tiles])
    n, size = len(tiles) + 1, tiles[0].shape[0]
    rows = [windows([zero, *part, zero]) for part in (highs, lows)]
    out = convolve(jnp.concatenate(rows, axis=0), bands)
    out = out[: n * size] + out[n * size :]
    return [out[k * size : (k + 1) * size] for k in range(n)]


def backward(parts, bands):
    n, size = len(parts[0]) - 1, parts[0][0].shape[0]
    rows = jnp.concatenate([windows(part) for part in parts], axis=0)
    out = convolve(rows, bands)
    total = out[: n * size]
    for p in range(1, len(parts)):
        total = total + out[p * n * size : (p + 1) * n * size]
    return [total[k * size : (k + 1) * size] for k in range(n)]


def coeff(avo_ref, angle, contrast, k):
    return avo_ref[contrast, angle : angle + 1, pl.ds(k * LANES, LANES)]


def add_terms(total, avo_ref, angle, result):
    for c, line in enumerate(total):
        for k, tile in enumerate(result):
            term = coeff(avo_ref, angle, c, k) * tile
            line[k] = term if angle == 0 else line[k] + term


def store_tiles(out_ref, tiles):
    size = out_ref.shape[2]
    for c in range(out_ref.shape[0]):
        for k, tile in enumerate(tiles[c]):
            for r in range(out_ref.shape[1]):
                out_ref[c, r, :, pl.ds(k * LANES, LANES)] = tile[r * size : (r + 1) * size]


def right_side(seis_ref, masks, avo_ref, bands):
    angles, rows, _, samples = seis_ref.shape
    n = samples // LANES
    total = [[None] * n for _ in range(avo_ref.shape[0])]
    for a in range(angles):
        data = jnp.concatenate([seis_ref[a, r].astype(F32) for r in range(rows)], axis=0)
        data = data * masks[a]
        turned = [
            pltpu.roll(data[:, k * LANES : (k + 1) * LANES], LANES // 2, 1) for k in range(n)
        ]
        zero = jnp.zeros_like(turned[0])
        left_half = lax.broadcasted_iota(jnp.int32, zero.shape, 1) < LANES // 2
        shifted = [
            jnp.where(left_half, before, here).astype(BF16)
            for before, here in zip([zero, *turned], [*turned, zero])
        ]
        add_terms(total, avo_ref, a, backward([shifted], bands[a]))
    return total


def normal(field, masks, avo_ref, bands):
    contrasts, n = len(field), len(field[0])
    total = [[None] * n for _ in range(contrasts)]
    for a, (ahead, back) in enumerate(bands):
        mixed = []
        for k in range(n):
            parts = [coeff(avo_ref, a, c, k) * field[c][k] for c in range(contrasts)]
            mixed.append(functools.reduce(jnp.add, parts))
        synth = [tile * masks[a] for tile in forward(mixed, ahead)]
        left_half = lax.broadcasted_iota(jnp.int32, synth[0].shape, 1) < LANES // 2
        synth[0] = jnp.where(left_half, 0.0, synth[0])
        synth[n] = jnp.where(left_half, synth[n], 0.0)
        result = backward(list(zip(*[split(t) for t in synth])), back)
        add_terms(total, avo_ref, a, result)
    return total


def lateral(here, north, south, west, east):
    traces = here.shape[0]
    place = lax.broadcasted_iota(jnp.int32, here.shape, 0)
    from_west = jnp.where(place == 0, 0.0 if west is None else west, pltpu.roll(here, 1, 0))
    from_east = jnp.where(
        place == traces - 1, 0.0 if east is None else east, pltpu.roll(here, traces - 1, 0)
    )
    around = from_west + from_east
    for other in (north, south):
        around = around if other is None else around + other
    return around


def copy_in(pairs, sems):
    copies = [pltpu.make_async_copy(a, b, sems.at[i]) for i, (a, b) in enumerate(pairs)]
    for copy in copies:
        copy.start()
    return copies


def start_kernel(
    seis_hbm, valid_hbm, avo_hbm, taps_hbm, prior_hbm, strength_hbm,
    b_ref, near_ref, far_ref, padded_ref, valid_ref, avo_ref, prior_ref, strength_ref,
    seis_ref, taps_ref, sems,
):
    taps, seis, valid, avo, prior, strength = copy_in(
        (
            (taps_hbm, taps_ref),
            (seis_hbm, seis_ref),
            (valid_hbm, valid_ref),
            (avo_hbm, avo_ref),
            (prior_hbm, prior_ref),
            (strength_hbm, strength_ref),
        ),
        sems,
    )
    taps.wait()
    pad_taps(taps_ref, padded_ref)
    angles = avo_ref.shape[1]
    bands = [band(padded_ref[a : a + 1, :]) for a in range(angles)]
    valid.wait()
    masks = [trace_columns(valid_ref, a) for a in range(angles)]
    for copy in (seis, avo, prior, strength):
        copy.wait()
    store_tiles(b_ref, right_side(seis_ref, masks, avo_ref, bands))
    contrasts, rows, traces, samples = b_ref.shape
    n = samples // LANES
    first = starts_pair("inline")
    lane = lax.broadcasted_iota(jnp.int32, (traces, LANES), 1)
    notes = []
    for r in (0, rows - 1):
        note = jnp.where(lane == angles, column(prior_ref[r : r + 1, :]), 0.0)
        for a in range(angles):
            note = jnp.where(lane == a, masks[a][r * traces : (r + 1) * traces], note)
        notes.append(note)
    edges = [
        [*[b_ref[c, r, :, pl.ds(k * LANES, LANES)] for c in range(contrasts) for k in range(n)], note]
        for r, note in zip((0, rows - 1), notes)
    ]
    for e, (top, bottom) in enumerate(zip(*edges)):
        near_ref[e] = jnp.where(first, bottom, top)
        far_ref[e] = jnp.where(first, top, bottom)


def either_side(pair_ref, next_ref, *where):
    first = starts_pair("inline")
    pair, other = pair_ref[where], next_ref[where]
    return jnp.where(first, other, pair), jnp.where(first, pair, other)


def stack_tiles(ref):
    contrasts, rows, _, samples = ref.shape
    return [
        [
            jnp.concatenate([ref[c, r, :, pl.ds(k, LANES)] for r in range(rows)], axis=0)
            for k in range(0, samples, LANES)
        ]
        for c in range(contrasts)
    ]


def inside(axis):
    place = lax.axis_index(axis)
    last = lax.axis_size(axis) - 1
    return (place > 0).astype(F32), (place < last).astype(F32)


def starts_pair(axis):
    return lax.axis_index(axis) % 2 == 0


def row_pair(near_ref, next_ref, c, n):
    tiles = [either_side(near_ref, next_ref, c * n + k) for k in range(n)]
    return [jnp.concatenate(side, axis=1) for side in zip(*tiles)]


def column_kernel(
    b_ref, near_ref, near_next_ref, valid_ref, prior_ref,
    pair_ref, other_ref, own_ref, note_ref, second_ref,
):
    contrasts, rows, traces, samples = b_ref.shape
    angles = valid_ref.shape[0]
    first_col = starts_pair("col")
    half = rows + 2
    second_ref[...] = jnp.zeros_like(second_ref)
    note_ref[...] = jnp.zeros_like(note_ref)
    for c in range(contrasts):
        own = [b_ref[c, r] for r in range(rows)]
        for i, line in enumerate([*own, *row_pair(near_ref, near_next_ref, c, samples // LANES)]):
            own_ref[c, i : i + 1, :] = line[0:1]
            own_ref[c, half + i : half + i + 1, :] = line[traces - 1 :]
        for r, line in enumerate(own):
            at = c * rows + r
            second_ref[0, at : at + 1, :] = line[1:2]
            second_ref[1, at : at + 1, :] = line[traces - 2 : traces - 1]
    lane = lax.broadcasted_iota(jnp.int32, (1, LANES), 1)
    for r in range(rows):
        for side, t in enumerate((0, traces - 1)):
            note = jnp.where(lane == angles, prior_ref[r : r + 1, t : t + 1], 0.0)
            for a in range(angles):
                note = jnp.where(lane == a, valid_ref[a, r : r + 1, t : t + 1].astype(F32), note)
            at = contrasts * rows + r
            second_ref[side, at : at + 1, 0:LANES] = note
            at = r + side * (traces - rows)
            note_ref[at : at + 1, :] = note
    for c in range(contrasts):
        left, right = own_ref[c, 0:half], own_ref[c, half:]
        pair_ref[c] = jnp.where(first_col, right, left)
        other_ref[c] = jnp.where(first_col, left, right)
    for i in range(2):
        left, right = (second_ref[side, i * half : (i + 1) * half] for side in (0, 1))
        pair_ref[contrasts + i] = jnp.where(first_col, right, left)
        other_ref[contrasts + i] = jnp.where(first_col, left, right)


def inner_kernel(
    count, b_ref, near_ref, near_next_ref, padded_ref, valid_ref, avo_ref, prior_ref, strength_ref,
    v_ref, data_ref, halo_ref, ahead_ref, back_ref, norm_ref,
):
    contrasts, rows, traces, samples = b_ref.shape
    angles, n = avo_ref.shape[1], samples // LANES
    turned = turn(padded_ref[...], count)
    bands = []
    for a in range(angles):
        bands.append((band(turned[a : a + 1]), band(padded_ref[a : a + 1, :])))
        ahead_ref[a], back_ref[a] = (half.astype(F32) for half in bands[a])
    masks = [trace_columns(valid_ref, a) for a in range(angles)]
    weights = [column(prior_ref[r : r + 1, :]) + 4.0 for r in range(rows)]
    above, below = either_side(near_ref, near_next_ref, contrasts * n)
    wide = [
        jnp.concatenate([above[:, a : a + 1], mask, below[:, a : a + 1]], axis=0)
        for a, mask in enumerate(masks)
    ]
    weights = [above[:, angles : angles + 1] + 4.0, *weights, below[:, angles : angles + 1] + 4.0]
    field = []
    for c, line in enumerate(stack_tiles(b_ref)):
        ends = [either_side(near_ref, near_next_ref, c * n + k) for k in range(n)]
        field.append(
            [jnp.concatenate([up, own, low], axis=0) for (up, low), own in zip(ends, line)]
        )
    total = normal(field, wide, avo_ref, bands)
    has_above, has_below = inside("inline")
    for c in range(contrasts):
        strength = strength_ref[:, c : c + 1]
        whole, data = jnp.concatenate(field[c], axis=1), jnp.concatenate(total[c], axis=1)
        lines = [whole[r * traces : (r + 1) * traces] for r in range(rows + 2)]
        for r, here in enumerate(lines):
            north = lines[r - 1] if r else None
            south = lines[r + 1] if r < rows + 1 else None
            if r == 0:
                south = has_above * south
            if r == rows + 1:
                north = has_below * north
            around = lateral(here, north, south, None, None)
            image = data[r * traces : (r + 1) * traces] + strength * (weights[r] * here - around)
            if 0 < r <= rows:
                v_ref[c, r - 1] = image
            else:
                halo_ref[min(r, 1), c] = image
    store_tiles(data_ref, normal(stack_tiles(v_ref), masks, avo_ref, bands))
    norm_ref[...] = functools.reduce(
        jnp.add, [lane_tiles(b_ref[c, r] * b_ref[c, r]) for c in range(contrasts) for r in range(rows)]
    )


def lane_tiles(product):
    tiles = [product[:, k : k + LANES] for k in range(0, product.shape[1], LANES)]
    return functools.reduce(jnp.add, tiles)


def halo_kernel(halo_ref, far_next_ref, far_ref, strength_ref, out_ref):
    contrasts, samples = halo_ref.shape[1], halo_ref.shape[3]
    for c in range(contrasts):
        for i, line in enumerate(row_pair(far_ref, far_next_ref, c, samples // LANES)):
            out_ref[i, c] = halo_ref[i, c] - strength_ref[:, c : c + 1] * line


def image_kernel(
    b_ref, v_ref, data_ref, halo_ref, norm_ref, own_ref, note_ref, other_ref, pair_ref,
    avo_ref, prior_ref, strength_ref, ahead_ref, back_ref,
    one_ref, two_ref, gram_ref,
):
    contrasts, rows, traces, samples = b_ref.shape
    angles, n = avo_ref.shape[1], samples // LANES
    has_left, has_right = inside("col")
    first_col = starts_pair("col")
    place = lax.broadcasted_iota(jnp.int32, (traces, samples), 0)
    west, east = place == 0, place == traces - 1
    half = traces // 2

    def turned(value, k):
        return pltpu.roll(value, k % traces, 0) if k % traces else value

    def sides(i):
        pair, other = pair_ref[i], other_ref[i]
        left, right = jnp.where(first_col, other, pair), jnp.where(first_col, pair, other)
        return jnp.concatenate([left, right], axis=0)

    def at_ends(value, left, right, inner):
        return jnp.where(west, turned(value, left), jnp.where(east, turned(value, right), inner))

    beside = [sides(c) for c in range(contrasts)]
    seconds = [sides(contrasts), sides(contrasts + 1)]
    notes = seconds[1][:, :LANES]
    line = place[:, :LANES]
    theirs = turned(notes, -rows)
    mixed = jnp.where((line == 2) | (line == 3), notes, note_ref[...])
    mixed = jnp.where((line == 4) | (line == 5), theirs, mixed)
    masks = [mixed[:, a : a + 1] for a in range(angles)]
    mine = (place[:, :1] < 2) | (place[:, :1] >= traces - 2)
    tile = []
    for c in range(contrasts):
        scale = jnp.where(mine, -strength_ref[:, c : c + 1], 1.0)
        whole = jnp.where(place % half < rows, beside[c], turned(beside[c], rows)) * scale
        tile.append([whole[:, k * LANES : (k + 1) * LANES] for k in range(n)])
    bands = [(ahead_ref[a].astype(BF16), back_ref[a].astype(BF16)) for a in range(angles)]
    edge = [jnp.concatenate(tiles, axis=1) for tiles in normal(tile, masks, avo_ref, bands)]

    has = jnp.where(place[:, :1] < half, has_left, has_right)
    far_weight = theirs[:, angles : angles + 1] + 4.0
    weights = [column(prior_ref[r : r + 1, :]) + 4.0 for r in range(rows)]
    sums = [norm_ref[...], *[jnp.zeros((traces, LANES), F32) for _ in range(3)]]
    for c in range(contrasts):
        strength = strength_ref[:, c : c + 1]
        theirs = beside[c]
        around = turned(seconds[c // 2], -rows * (c % 2)) + turned(theirs, -rows)
        around = around + jnp.where(place % 2 == 1, turned(theirs, 1), turned(theirs, -1))
        prior = far_weight * theirs - (around + has * own_ref[c])
        beyond = jnp.where(place < half, turned(edge[c], -rows), edge[c]) + strength * prior

        lines = [halo_ref[0, c], *[v_ref[c, r] for r in range(rows)], halo_ref[1, c]]
        lines = [
            here - strength * at_ends(theirs, -k, half - 1 - k, 0.0)
            for here, k in zip(lines, (rows, *range(rows), rows + 1))
        ]
        for r in range(rows):
            here, b = lines[r + 1], b_ref[c, r]
            ends = jnp.where(west, turned(beyond, -r), turned(beyond, half - 1 - r))
            around = jnp.where(west, ends, turned(here, 1)) + jnp.where(east, ends, turned(here, -1))
            around = around + lines[r] + lines[r + 2]
            mend = at_ends(edge[c], -r, 1 - r, 0.0)
            two = data_ref[c, r] + mend + strength * (weights[r] * here - around)
            one_ref[c, r] = here
            two_ref[c, r] = two
            for q, product in enumerate((b * here, here * here, here * two), 1):
                sums[q] = sums[q] + lane_tiles(product)
    lane = lax.broadcasted_iota(jnp.int32, (1, LANES), 1)
    packed = jnp.zeros((1, LANES), F32)
    for q, total in enumerate(sums):
        total = jnp.sum(jnp.sum(total, axis=0, keepdims=True), axis=1, keepdims=True)
        packed = jnp.where(lane == q, total, packed)
    gram_ref[...] = jnp.broadcast_to(packed[None], gram_ref.shape)


def finish_kernel(gram_ref, b_ref, one_ref, two_ref, solution_ref, residual_ref):
    sums = jnp.sum(gram_ref[...], axis=0, keepdims=True)
    g00, g01, g11, g12 = (sums[:, q : q + 1] for q in range(4))
    inverse = 1.0 / g01
    first = g00 * inverse
    quotient = g11 * inverse
    ratio = first * quotient
    second = (ratio - 1.0) * g01 / (first * (g12 - quotient * g11))
    near = first + second * ratio
    far = first * second
    for c in range(b_ref.shape[0]):
        for r in range(b_ref.shape[1]):
            b, one, two = b_ref[c, r], one_ref[c, r], two_ref[c, r]
            solution_ref[c, r] = near * b - far * one
            residual_ref[c, r] = b - near * one + far * two


VMEM = pl.BlockSpec(memory_space=pltpu.VMEM)
HBM = pl.BlockSpec(memory_space=pltpu.HBM)


def call(kernel, outs, ins, flops, scratch=(), places=None):
    moved = sum(x.size * x.dtype.itemsize for x in (*ins, *outs))
    return pl.pallas_call(
        kernel,
        out_shape=outs,
        in_specs=[VMEM] * len(ins) if places is None else places,
        out_specs=jax.tree.map(lambda _: VMEM, outs),
        scratch_shapes=list(scratch),
        compiler_params=pltpu.CompilerParams(vmem_limit_bytes=24 * 1024 * 1024),
        cost_estimate=pl.CostEstimate(flops=flops, bytes_accessed=moved, transcendentals=0),
        name=getattr(kernel, "func", kernel).__name__,
    )(*ins)


def swap(axis, value, first):
    starts = range(first, lax.axis_size(axis) - 1, 2)
    return lax.ppermute(value, axis, [(i + d, i + 1 - d) for i in starts for d in (0, 1)])


def hand_on(axis, value):
    size = lax.axis_size(axis)
    steps = [(i, i + 2 - 4 * (i % 2)) for i in range(size)]
    return lax.ppermute(value, axis, [(i, j) for i, j in steps if 0 <= j < size])


def shards(seismic, validity, prior_weight, lateral_strength, avo_coeffs, wavelets):
    angles, rows, traces, samples = seismic.shape
    contrasts = avo_coeffs.shape[1]
    avo_coeffs = jnp.swapaxes(avo_coeffs, 0, 1)
    shape = lambda *dims: jax.ShapeDtypeStruct(dims, F32)
    field = shape(contrasts, rows, traces, samples)
    side = shape(contrasts + 2, rows + 2, samples)
    lines = shape(8, 2 * LANES)
    work = 2 * angles * rows * traces * samples * 256 * 4

    given = (seismic, validity, avo_coeffs, wavelets, prior_weight, lateral_strength.reshape(1, -1))
    kept = [given[i] for i in (1, 2, 4, 5)]
    edge = shape(contrasts * samples // LANES + 1, traces, LANES)
    b, near, far, padded, *kept = call(
        start_kernel,
        (
            field, edge, edge, lines,
            *[jax.ShapeDtypeStruct(x.shape, x.dtype) for x in kept],
        ),
        [pltpu.with_memory_space_constraint(x, pltpu.HBM) for x in given],
        work,
        [
            pltpu.VMEM(seismic.shape, seismic.dtype),
            pltpu.VMEM(wavelets.shape, F32),
            pltpu.SemaphoreType.DMA((6,)),
        ],
        [HBM] * 6,
    )
    near = swap("inline", near, 0)
    near_next = swap("inline", far, 1)
    far_next = hand_on("inline", near)
    far = swap("inline", far, 0)
    col_pair, col_other, own, note = call(
        column_kernel,
        (side, side, shape(contrasts, 2 * rows + 4, samples), shape(traces, LANES)),
        (b, near, near_next, kept[0], kept[2]),
        2 * field.size,
        [pltpu.VMEM((2, 2 * rows + 4, samples), F32)],
    )
    col_other = swap("col", col_other, 1)
    col_pair = swap("col", col_pair, 0)
    bands = shape(angles, 2 * LANES, 2 * LANES)
    halo = shape(2, contrasts, traces, samples)
    image, data, part, ahead, back, norm = call(
        functools.partial(inner_kernel, wavelets.shape[1]),
        (field, field, halo, bands, bands, shape(traces, LANES)),
        (b, near, near_next, padded, *kept),
        6 * work,
    )
    (halo,) = call(halo_kernel, (halo,), (part, far_next, far, kept[-1]), field.size)
    axes = ("inline", "col")
    one, two, gram = call(
        image_kernel,
        (field, field, shape(lax.axis_size(axes), 1, LANES)),
        (
            b, image, data, halo, norm, own, note, col_other, col_pair,
            *kept[1:], ahead, back,
        ),
        work,
    )
    gram = lax.all_to_all(gram, axes, 0, 0).reshape(-1, LANES)
    return tuple(call(finish_kernel, (field, field), (gram, b, one, two), 8 * field.size))


def solution(mesh):
    placed = (
        P(None, "inline", "col", None),
        P(None, "inline", "col"),
        P("inline", "col"),
        P(),
        P(),
        P(),
    )
    return jax.shard_map(
        shards,
        mesh=mesh,
        in_specs=placed,
        out_specs=(P(None, "inline", "col", None), P(None, "inline", "col", None)),
        check_vma=False,
    )
```

```python
import functools

import jax
import jax.numpy as jnp
from jax import lax
from jax.experimental import pallas as pl
from jax.experimental.pallas import tpu as pltpu
from jax.sharding import PartitionSpec as P

LANES = 128
F32 = jnp.float32
BF16 = jnp.bfloat16


def split(value):
    high = value.astype(BF16)
    return high, (value - high.astype(F32)).astype(BF16)


def pad_taps(taps_ref, padded_ref):
    padded_ref[...] = jnp.zeros_like(padded_ref)
    padded_ref[0 : taps_ref.shape[0], 0 : taps_ref.shape[1]] = taps_ref[...]


def turn(lines, count):
    n, size = lines.shape
    parts = []
    for _ in range(3):
        parts.append(lines.astype(BF16).astype(F32))
        lines = lines - parts[-1]
    rows = lax.broadcasted_iota(jnp.int32, (size, size), 0)
    cols = lax.broadcasted_iota(jnp.int32, (size, size), 1)
    flip = jnp.where(rows + cols == count - 1, 1.0, 0.0).astype(BF16)
    whole = jnp.concatenate(parts, axis=0).astype(BF16)
    turned = jnp.dot(whole, flip, preferred_element_type=F32)
    return turned[:n] + turned[n : 2 * n] + turned[2 * n :]


def band(line):
    lines = jnp.broadcast_to(line, (LANES, line.shape[1]))
    return jnp.concatenate(split(pltpu.roll(lines, 0, 1, stride=1, stride_axis=0)), axis=0)


def convolve(rows, bands):
    out = lax.dot_general(rows, bands, (((1,), (1,)), ((), ())), preferred_element_type=F32)
    return out[:, :LANES] + out[:, LANES:]


def column(row):
    n = row.shape[1]
    same = lax.broadcasted_iota(jnp.int32, (n, n), 0) == lax.broadcasted_iota(jnp.int32, (n, n), 1)
    return jnp.sum(jnp.where(same, jnp.broadcast_to(row, (n, n)), 0.0), axis=1, keepdims=True)


def trace_columns(ref, *lead):
    rows = ref[lead].astype(F32)
    return jnp.concatenate([column(rows[r : r + 1, :]) for r in range(rows.shape[0])], axis=0)


def windows(tiles):
    pairs = [jnp.concatenate(pair, axis=1) for pair in zip(tiles[:-1], tiles[1:])]
    return jnp.concatenate(pairs, axis=0)


def forward(tiles, bands):
    zero = jnp.zeros_like(tiles[0]).astype(BF16)
    highs, lows = zip(*[split(t) for t in tiles])
    n, size = len(tiles) + 1, tiles[0].shape[0]
    rows = [windows([zero, *part, zero]) for part in (highs, lows)]
    out = convolve(jnp.concatenate(rows, axis=0), bands)
    out = out[: n * size] + out[n * size :]
    return [out[k * size : (k + 1) * size] for k in range(n)]


def backward(parts, bands):
    n, size = len(parts[0]) - 1, parts[0][0].shape[0]
    rows = jnp.concatenate([windows(part) for part in parts], axis=0)
    out = convolve(rows, bands)
    total = out[: n * size]
    for p in range(1, len(parts)):
        total = total + out[p * n * size : (p + 1) * n * size]
    return [total[k * size : (k + 1) * size] for k in range(n)]


def coeff(avo_ref, angle, contrast, k):
    return avo_ref[contrast, angle : angle + 1, pl.ds(k * LANES, LANES)]


def add_terms(total, avo_ref, angle, result):
    for c, line in enumerate(total):
        for k, tile in enumerate(result):
            term = coeff(avo_ref, angle, c, k) * tile
            line[k] = term if angle == 0 else line[k] + term


def store_tiles(out_ref, tiles):
    size = out_ref.shape[2]
    for c in range(out_ref.shape[0]):
        for k, tile in enumerate(tiles[c]):
            for r in range(out_ref.shape[1]):
                out_ref[c, r, :, pl.ds(k * LANES, LANES)] = tile[r * size : (r + 1) * size]


def right_side(seis_ref, masks, avo_ref, bands, copies):
    angles, rows, _, samples = seis_ref.shape
    n = samples // LANES
    total = [[None] * n for _ in range(avo_ref.shape[0])]
    for a in range(angles):
        copies[a].wait()
        data = jnp.concatenate([seis_ref[a, r].astype(F32) for r in range(rows)], axis=0)
        data = data * masks[a]
        turned = [
            pltpu.roll(data[:, k * LANES : (k + 1) * LANES], LANES // 2, 1) for k in range(n)
        ]
        zero = jnp.zeros_like(turned[0])
        left_half = lax.broadcasted_iota(jnp.int32, zero.shape, 1) < LANES // 2
        shifted = [
            jnp.where(left_half, before, here).astype(BF16)
            for before, here in zip([zero, *turned], [*turned, zero])
        ]
        add_terms(total, avo_ref, a, backward([shifted], bands[a]))
    return total


def normal(field, masks, avo_ref, bands):
    contrasts, n = len(field), len(field[0])
    total = [[None] * n for _ in range(contrasts)]
    for a, (ahead, back) in enumerate(bands):
        mixed = []
        for k in range(n):
            parts = [coeff(avo_ref, a, c, k) * field[c][k] for c in range(contrasts)]
            mixed.append(functools.reduce(jnp.add, parts))
        synth = [tile * masks[a] for tile in forward(mixed, ahead)]
        left_half = lax.broadcasted_iota(jnp.int32, synth[0].shape, 1) < LANES // 2
        synth[0] = jnp.where(left_half, 0.0, synth[0])
        synth[n] = jnp.where(left_half, synth[n], 0.0)
        result = backward(list(zip(*[split(t) for t in synth])), back)
        add_terms(total, avo_ref, a, result)
    return total


def lateral(here, north, south, west, east):
    traces = here.shape[0]
    place = lax.broadcasted_iota(jnp.int32, here.shape, 0)
    from_west = jnp.where(place == 0, 0.0 if west is None else west, pltpu.roll(here, 1, 0))
    from_east = jnp.where(
        place == traces - 1, 0.0 if east is None else east, pltpu.roll(here, traces - 1, 0)
    )
    around = from_west + from_east
    for other in (north, south):
        around = around if other is None else around + other
    return around


def copy_in(pairs, sems):
    copies = [pltpu.make_async_copy(a, b, sems.at[i]) for i, (a, b) in enumerate(pairs)]
    for copy in copies:
        copy.start()
    return copies


def start_kernel(
    seis_hbm, valid_hbm, avo_hbm, taps_hbm, prior_hbm, strength_hbm,
    b_ref, near_ref, far_ref, padded_ref, valid_ref, avo_ref, prior_ref, strength_ref,
    seis_ref, taps_ref, sems,
):
    contrasts, angles, _ = avo_ref.shape
    taps, *rest = copy_in(
        (
            (taps_hbm, taps_ref),
            *((seis_hbm.at[a], seis_ref.at[a]) for a in range(angles)),
            *((avo_hbm.at[c], avo_ref.at[c]) for c in range(contrasts)),
            (valid_hbm, valid_ref),
            (prior_hbm, prior_ref),
            (strength_hbm, strength_ref),
        ),
        sems,
    )
    taps.wait()
    pad_taps(taps_ref, padded_ref)
    bands = [band(padded_ref[a : a + 1, :]) for a in range(angles)]
    for copy in rest[angles:]:
        copy.wait()
    masks = [trace_columns(valid_ref, a) for a in range(angles)]
    store_tiles(b_ref, right_side(seis_ref, masks, avo_ref, bands, rest[:angles]))
    _, rows, traces, samples = b_ref.shape
    n = samples // LANES
    first = starts_pair("inline")
    lane = lax.broadcasted_iota(jnp.int32, (traces, LANES), 1)
    notes = []
    for r in (0, rows - 1):
        note = jnp.where(lane == angles, column(prior_ref[r : r + 1, :]), 0.0)
        for a in range(angles):
            note = jnp.where(lane == a, masks[a][r * traces : (r + 1) * traces], note)
        notes.append(note)
    edges = [
        [*[b_ref[c, r, :, pl.ds(k * LANES, LANES)] for c in range(contrasts) for k in range(n)], note]
        for r, note in zip((0, rows - 1), notes)
    ]
    for e, (top, bottom) in enumerate(zip(*edges)):
        near_ref[e] = jnp.where(first, bottom, top)
        far_ref[e] = jnp.where(first, top, bottom)


def either_side(pair_ref, next_ref, *where):
    first = starts_pair("inline")
    pair, other = pair_ref[where], next_ref[where]
    return jnp.where(first, other, pair), jnp.where(first, pair, other)


def stack_tiles(ref):
    contrasts, rows, _, samples = ref.shape
    return [
        [
            jnp.concatenate([ref[c, r, :, pl.ds(k, LANES)] for r in range(rows)], axis=0)
            for k in range(0, samples, LANES)
        ]
        for c in range(contrasts)
    ]


def inside(axis):
    place = lax.axis_index(axis)
    last = lax.axis_size(axis) - 1
    return (place > 0).astype(F32), (place < last).astype(F32)


def starts_pair(axis):
    return lax.axis_index(axis) % 2 == 0


def row_pair(near_ref, next_ref, c, n):
    tiles = [either_side(near_ref, next_ref, c * n + k) for k in range(n)]
    return [jnp.concatenate(side, axis=1) for side in zip(*tiles)]


def column_kernel(
    b_ref, near_ref, near_next_ref, valid_ref, prior_ref,
    pair_ref, other_ref, own_ref, note_ref, second_ref,
):
    contrasts, rows, traces, samples = b_ref.shape
    angles = valid_ref.shape[0]
    first_col = starts_pair("col")
    half = rows + 2
    second_ref[...] = jnp.zeros_like(second_ref)
    note_ref[...] = jnp.zeros_like(note_ref)
    for c in range(contrasts):
        own = [b_ref[c, r] for r in range(rows)]
        for i, line in enumerate([*own, *row_pair(near_ref, near_next_ref, c, samples // LANES)]):
            own_ref[c, i : i + 1, :] = line[0:1]
            own_ref[c, half + i : half + i + 1, :] = line[traces - 1 :]
        for r, line in enumerate(own):
            at = c * rows + r
            second_ref[0, at : at + 1, :] = line[1:2]
            second_ref[1, at : at + 1, :] = line[traces - 2 : traces - 1]
    lane = lax.broadcasted_iota(jnp.int32, (1, LANES), 1)
    for r in range(rows):
        for side, t in enumerate((0, traces - 1)):
            note = jnp.where(lane == angles, prior_ref[r : r + 1, t : t + 1], 0.0)
            for a in range(angles):
                note = jnp.where(lane == a, valid_ref[a, r : r + 1, t : t + 1].astype(F32), note)
            at = contrasts * rows + r
            second_ref[side, at : at + 1, 0:LANES] = note
            at = r + side * (traces - rows)
            note_ref[at : at + 1, :] = note
    for c in range(contrasts):
        left, right = own_ref[c, 0:half], own_ref[c, half:]
        pair_ref[c] = jnp.where(first_col, right, left)
        other_ref[c] = jnp.where(first_col, left, right)
    for i in range(2):
        left, right = (second_ref[side, i * half : (i + 1) * half] for side in (0, 1))
        pair_ref[contrasts + i] = jnp.where(first_col, right, left)
        other_ref[contrasts + i] = jnp.where(first_col, left, right)


def inner_kernel(
    count, b_ref, near_ref, near_next_ref, padded_ref, valid_ref, avo_ref, prior_ref, strength_ref,
    v_ref, data_ref, halo_ref, ahead_ref, back_ref, norm_ref,
):
    contrasts, rows, traces, samples = b_ref.shape
    angles, n = avo_ref.shape[1], samples // LANES
    turned = turn(padded_ref[...], count)
    bands = []
    for a in range(angles):
        bands.append((band(turned[a : a + 1]), band(padded_ref[a : a + 1, :])))
        ahead_ref[a], back_ref[a] = (half.astype(F32) for half in bands[a])
    masks = [trace_columns(valid_ref, a) for a in range(angles)]
    weights = [column(prior_ref[r : r + 1, :]) + 4.0 for r in range(rows)]
    above, below = either_side(near_ref, near_next_ref, contrasts * n)
    wide = [
        jnp.concatenate([above[:, a : a + 1], mask, below[:, a : a + 1]], axis=0)
        for a, mask in enumerate(masks)
    ]
    weights = [above[:, angles : angles + 1] + 4.0, *weights, below[:, angles : angles + 1] + 4.0]
    field = []
    for c, line in enumerate(stack_tiles(b_ref)):
        ends = [either_side(near_ref, near_next_ref, c * n + k) for k in range(n)]
        field.append(
            [jnp.concatenate([up, own, low], axis=0) for (up, low), own in zip(ends, line)]
        )
    total = normal(field, wide, avo_ref, bands)
    has_above, has_below = inside("inline")
    for c in range(contrasts):
        strength = strength_ref[:, c : c + 1]
        whole, data = jnp.concatenate(field[c], axis=1), jnp.concatenate(total[c], axis=1)
        lines = [whole[r * traces : (r + 1) * traces] for r in range(rows + 2)]
        for r, here in enumerate(lines):
            north = lines[r - 1] if r else None
            south = lines[r + 1] if r < rows + 1 else None
            if r == 0:
                south = has_above * south
            if r == rows + 1:
                north = has_below * north
            around = lateral(here, north, south, None, None)
            image = data[r * traces : (r + 1) * traces] + strength * (weights[r] * here - around)
            if 0 < r <= rows:
                v_ref[c, r - 1] = image
            else:
                halo_ref[min(r, 1), c] = image
    store_tiles(data_ref, normal(stack_tiles(v_ref), masks, avo_ref, bands))
    norm_ref[...] = functools.reduce(
        jnp.add, [lane_tiles(b_ref[c, r] * b_ref[c, r]) for c in range(contrasts) for r in range(rows)]
    )


def lane_tiles(product):
    tiles = [product[:, k : k + LANES] for k in range(0, product.shape[1], LANES)]
    return functools.reduce(jnp.add, tiles)


def halo_kernel(halo_ref, far_next_ref, far_ref, strength_ref, out_ref):
    contrasts, samples = halo_ref.shape[1], halo_ref.shape[3]
    for c in range(contrasts):
        for i, line in enumerate(row_pair(far_ref, far_next_ref, c, samples // LANES)):
            out_ref[i, c] = halo_ref[i, c] - strength_ref[:, c : c + 1] * line


def image_kernel(
    b_ref, v_ref, data_ref, halo_ref, norm_ref, own_ref, note_ref, other_ref, pair_ref,
    avo_ref, prior_ref, strength_ref, ahead_ref, back_ref,
    one_ref, two_ref, gram_ref,
):
    contrasts, rows, traces, samples = b_ref.shape
    angles, n = avo_ref.shape[1], samples // LANES
    has_left, has_right = inside("col")
    first_col = starts_pair("col")
    place = lax.broadcasted_iota(jnp.int32, (traces, samples), 0)
    west, east = place == 0, place == traces - 1
    half = traces // 2

    def turned(value, k):
        return pltpu.roll(value, k % traces, 0) if k % traces else value

    def sides(i):
        pair, other = pair_ref[i], other_ref[i]
        left, right = jnp.where(first_col, other, pair), jnp.where(first_col, pair, other)
        return jnp.concatenate([left, right], axis=0)

    def at_ends(value, left, right, inner):
        return jnp.where(west, turned(value, left), jnp.where(east, turned(value, right), inner))

    beside = [sides(c) for c in range(contrasts)]
    seconds = [sides(contrasts), sides(contrasts + 1)]
    notes = seconds[1][:, :LANES]
    line = place[:, :LANES]
    theirs = turned(notes, -rows)
    mixed = jnp.where((line == 2) | (line == 3), notes, note_ref[...])
    mixed = jnp.where((line == 4) | (line == 5), theirs, mixed)
    masks = [mixed[:, a : a + 1] for a in range(angles)]
    mine = (place[:, :1] < 2) | (place[:, :1] >= traces - 2)
    tile = []
    for c in range(contrasts):
        scale = jnp.where(mine, -strength_ref[:, c : c + 1], 1.0)
        whole = jnp.where(place % half < rows, beside[c], turned(beside[c], rows)) * scale
        tile.append([whole[:, k * LANES : (k + 1) * LANES] for k in range(n)])
    bands = [(ahead_ref[a].astype(BF16), back_ref[a].astype(BF16)) for a in range(angles)]
    edge = [jnp.concatenate(tiles, axis=1) for tiles in normal(tile, masks, avo_ref, bands)]

    has = jnp.where(place[:, :1] < half, has_left, has_right)
    far_weight = theirs[:, angles : angles + 1] + 4.0
    weights = [column(prior_ref[r : r + 1, :]) + 4.0 for r in range(rows)]
    sums = [norm_ref[...], *[jnp.zeros((traces, LANES), F32) for _ in range(3)]]
    for c in range(contrasts):
        strength = strength_ref[:, c : c + 1]
        theirs = beside[c]
        around = turned(seconds[c // 2], -rows * (c % 2)) + turned(theirs, -rows)
        around = around + jnp.where(place % 2 == 1, turned(theirs, 1), turned(theirs, -1))
        prior = far_weight * theirs - (around + has * own_ref[c])
        beyond = jnp.where(place < half, turned(edge[c], -rows), edge[c]) + strength * prior

        lines = [halo_ref[0, c], *[v_ref[c, r] for r in range(rows)], halo_ref[1, c]]
        lines = [
            here - strength * at_ends(theirs, -k, half - 1 - k, 0.0)
            for here, k in zip(lines, (rows, *range(rows), rows + 1))
        ]
        for r in range(rows):
            here, b = lines[r + 1], b_ref[c, r]
            ends = jnp.where(west, turned(beyond, -r), turned(beyond, half - 1 - r))
            around = jnp.where(west, ends, turned(here, 1)) + jnp.where(east, ends, turned(here, -1))
            around = around + lines[r] + lines[r + 2]
            mend = at_ends(edge[c], -r, 1 - r, 0.0)
            two = data_ref[c, r] + mend + strength * (weights[r] * here - around)
            one_ref[c, r] = here
            two_ref[c, r] = two
            for q, product in enumerate((b * here, here * here, here * two), 1):
                sums[q] = sums[q] + lane_tiles(product)
    lane = lax.broadcasted_iota(jnp.int32, (1, LANES), 1)
    packed = jnp.zeros((1, LANES), F32)
    for q, total in enumerate(sums):
        total = jnp.sum(jnp.sum(total, axis=0, keepdims=True), axis=1, keepdims=True)
        packed = jnp.where(lane == q, total, packed)
    gram_ref[...] = jnp.broadcast_to(packed[None], gram_ref.shape)


def finish_kernel(gram_ref, b_ref, one_ref, two_ref, solution_ref, residual_ref):
    sums = jnp.sum(gram_ref[...], axis=0)
    g00, g01, g11, g12 = (sums[:, q : q + 1] for q in range(4))
    inverse = 1.0 / g01
    first = g00 * inverse
    quotient = g11 * inverse
    ratio = first * quotient
    second = (ratio - 1.0) * g01 / (first * (g12 - quotient * g11))
    near = first + second * ratio
    far = first * second
    for c in range(b_ref.shape[0]):
        for r in range(b_ref.shape[1]):
            b, one, two = b_ref[c, r], one_ref[c, r], two_ref[c, r]
            solution_ref[c, r] = near * b - far * one
            residual_ref[c, r] = b - near * one + far * two


VMEM = pl.BlockSpec(memory_space=pltpu.VMEM)
HBM = pl.BlockSpec(memory_space=pltpu.HBM)


def call(kernel, outs, ins, flops, scratch=(), places=None):
    moved = sum(x.size * x.dtype.itemsize for x in (*ins, *outs))
    return pl.pallas_call(
        kernel,
        out_shape=outs,
        in_specs=[VMEM] * len(ins) if places is None else places,
        out_specs=jax.tree.map(lambda _: VMEM, outs),
        scratch_shapes=list(scratch),
        compiler_params=pltpu.CompilerParams(vmem_limit_bytes=24 * 1024 * 1024),
        cost_estimate=pl.CostEstimate(flops=flops, bytes_accessed=moved, transcendentals=0),
        name=getattr(kernel, "func", kernel).__name__,
    )(*ins)


def swap(axis, value, first):
    starts = range(first, lax.axis_size(axis) - 1, 2)
    return lax.ppermute(value, axis, [(i + d, i + 1 - d) for i in starts for d in (0, 1)])


def hand_on(axis, value):
    size = lax.axis_size(axis)
    steps = [(i, i + 2 - 4 * (i % 2)) for i in range(size)]
    return lax.ppermute(value, axis, [(i, j) for i, j in steps if 0 <= j < size])


def shards(seismic, validity, prior_weight, lateral_strength, avo_coeffs, wavelets):
    angles, rows, traces, samples = seismic.shape
    contrasts = avo_coeffs.shape[1]
    avo_coeffs = jnp.swapaxes(avo_coeffs, 0, 1)
    shape = lambda *dims: jax.ShapeDtypeStruct(dims, F32)
    field = shape(contrasts, rows, traces, samples)
    side = shape(contrasts + 2, rows + 2, samples)
    lines = shape(8, 2 * LANES)
    work = 2 * angles * rows * traces * samples * 256 * 4

    given = (seismic, validity, avo_coeffs, wavelets, prior_weight, lateral_strength.reshape(1, -1))
    kept = [given[i] for i in (1, 2, 4, 5)]
    edge = shape(contrasts * samples // LANES + 1, traces, LANES)
    b, near, far, padded, *kept = call(
        start_kernel,
        (
            field, edge, edge, lines,
            *[jax.ShapeDtypeStruct(x.shape, x.dtype) for x in kept],
        ),
        [pltpu.with_memory_space_constraint(x, pltpu.HBM) for x in given],
        work,
        [
            pltpu.VMEM(seismic.shape, seismic.dtype),
            pltpu.VMEM(wavelets.shape, F32),
            pltpu.SemaphoreType.DMA((angles + contrasts + 4,)),
        ],
        [HBM] * 6,
    )
    near = swap("inline", near, 0)
    near_next = swap("inline", far, 1)
    far_next = hand_on("inline", near)
    far = swap("inline", far, 0)
    col_pair, col_other, own, note = call(
        column_kernel,
        (side, side, shape(contrasts, 2 * rows + 4, samples), shape(traces, LANES)),
        (b, near, near_next, kept[0], kept[2]),
        2 * field.size,
        [pltpu.VMEM((2, 2 * rows + 4, samples), F32)],
    )
    col_other = swap("col", col_other, 1)
    col_pair = swap("col", col_pair, 0)
    bands = shape(angles, 2 * LANES, 2 * LANES)
    halo = shape(2, contrasts, traces, samples)
    image, data, part, ahead, back, norm = call(
        functools.partial(inner_kernel, wavelets.shape[1]),
        (field, field, halo, bands, bands, shape(traces, LANES)),
        (b, near, near_next, padded, *kept),
        6 * work,
    )
    (halo,) = call(halo_kernel, (halo,), (part, far_next, far, kept[-1]), field.size)
    axes = ("inline", "col")
    one, two, gram = call(
        image_kernel,
        (field, field, shape(lax.axis_size(axes), 1, LANES)),
        (
            b, image, data, halo, norm, own, note, col_other, col_pair,
            *kept[1:], ahead, back,
        ),
        work,
    )
    gram = lax.all_to_all(gram, axes, 0, 0)
    return tuple(call(finish_kernel, (field, field), (gram, b, one, two), 8 * field.size))


def solution(mesh):
    placed = (
        P(None, "inline", "col", None),
        P(None, "inline", "col"),
        P("inline", "col"),
        P(),
        P(),
        P(),
    )
    return jax.shard_map(
        shards,
        mesh=mesh,
        in_specs=placed,
        out_specs=(P(None, "inline", "col", None), P(None, "inline", "col", None)),
        check_vma=False,
    )
```

```python
import functools

import jax
import jax.numpy as jnp
from jax import lax
from jax.experimental import pallas as pl
from jax.experimental.pallas import tpu as pltpu
from jax.sharding import PartitionSpec as P

LANES = 128
F32 = jnp.float32
BF16 = jnp.bfloat16


def split(value):
    high = value.astype(BF16)
    return high, (value - high.astype(F32)).astype(BF16)


def pad_taps(taps_ref, padded_ref):
    padded_ref[...] = jnp.zeros_like(padded_ref)
    padded_ref[0 : taps_ref.shape[0], 0 : taps_ref.shape[1]] = taps_ref[...]


def turn(lines, count):
    n, size = lines.shape
    parts = []
    for _ in range(3):
        parts.append(lines.astype(BF16).astype(F32))
        lines = lines - parts[-1]
    rows = lax.broadcasted_iota(jnp.int32, (size, size), 0)
    cols = lax.broadcasted_iota(jnp.int32, (size, size), 1)
    flip = jnp.where(rows + cols == count - 1, 1.0, 0.0).astype(BF16)
    whole = jnp.concatenate(parts, axis=0).astype(BF16)
    turned = jnp.dot(whole, flip, preferred_element_type=F32)
    return turned[:n] + turned[n : 2 * n] + turned[2 * n :]


def band(line):
    lines = jnp.broadcast_to(line, (LANES, line.shape[1]))
    return jnp.concatenate(split(pltpu.roll(lines, 0, 1, stride=1, stride_axis=0)), axis=0)


def convolve(rows, bands):
    out = lax.dot_general(rows, bands, (((1,), (1,)), ((), ())), preferred_element_type=F32)
    return out[:, :LANES] + out[:, LANES:]


def column(row):
    n = row.shape[1]
    same = lax.broadcasted_iota(jnp.int32, (n, n), 0) == lax.broadcasted_iota(jnp.int32, (n, n), 1)
    return jnp.sum(jnp.where(same, jnp.broadcast_to(row, (n, n)), 0.0), axis=1, keepdims=True)


def trace_columns(ref, *lead):
    rows = ref[lead].astype(F32)
    return jnp.concatenate([column(rows[r : r + 1, :]) for r in range(rows.shape[0])], axis=0)


def windows(tiles):
    pairs = [jnp.concatenate(pair, axis=1) for pair in zip(tiles[:-1], tiles[1:])]
    return jnp.concatenate(pairs, axis=0)


def forward(tiles, bands):
    zero = jnp.zeros_like(tiles[0]).astype(BF16)
    highs, lows = zip(*[split(t) for t in tiles])
    n, size = len(tiles) + 1, tiles[0].shape[0]
    rows = [windows([zero, *part, zero]) for part in (highs, lows)]
    out = convolve(jnp.concatenate(rows, axis=0), bands)
    out = out[: n * size] + out[n * size :]
    return [out[k * size : (k + 1) * size] for k in range(n)]


def backward(parts, bands):
    n, size = len(parts[0]) - 1, parts[0][0].shape[0]
    rows = jnp.concatenate([windows(part) for part in parts], axis=0)
    out = convolve(rows, bands)
    total = out[: n * size]
    for p in range(1, len(parts)):
        total = total + out[p * n * size : (p + 1) * n * size]
    return [total[k * size : (k + 1) * size] for k in range(n)]


def coeff(avo_ref, angle, contrast, k):
    return avo_ref[contrast, angle : angle + 1, pl.ds(k * LANES, LANES)]


def add_terms(total, avo_ref, angle, result):
    for c, line in enumerate(total):
        for k, tile in enumerate(result):
            term = coeff(avo_ref, angle, c, k) * tile
            line[k] = term if angle == 0 else line[k] + term


def store_tiles(out_ref, tiles):
    size = out_ref.shape[2]
    for c in range(out_ref.shape[0]):
        for k, tile in enumerate(tiles[c]):
            for r in range(out_ref.shape[1]):
                out_ref[c, r, :, pl.ds(k * LANES, LANES)] = tile[r * size : (r + 1) * size]


def right_side(seis_ref, masks, avo_ref, bands):
    angles, rows, _, samples = seis_ref.shape
    n = samples // LANES
    total = [[None] * n for _ in range(avo_ref.shape[0])]
    for a in range(angles):
        data = jnp.concatenate([seis_ref[a, r].astype(F32) for r in range(rows)], axis=0)
        data = data * masks[a]
        turned = [
            pltpu.roll(data[:, k * LANES : (k + 1) * LANES], LANES // 2, 1) for k in range(n)
        ]
        zero = jnp.zeros_like(turned[0])
        left_half = lax.broadcasted_iota(jnp.int32, zero.shape, 1) < LANES // 2
        shifted = [
            jnp.where(left_half, before, here).astype(BF16)
            for before, here in zip([zero, *turned], [*turned, zero])
        ]
        add_terms(total, avo_ref, a, backward([shifted], bands[a]))
    return total


def normal(field, masks, avo_ref, bands):
    contrasts, n = len(field), len(field[0])
    total = [[None] * n for _ in range(contrasts)]
    for a, (ahead, back) in enumerate(bands):
        mixed = []
        for k in range(n):
            parts = [coeff(avo_ref, a, c, k) * field[c][k] for c in range(contrasts)]
            mixed.append(functools.reduce(jnp.add, parts))
        synth = [tile * masks[a] for tile in forward(mixed, ahead)]
        left_half = lax.broadcasted_iota(jnp.int32, synth[0].shape, 1) < LANES // 2
        synth[0] = jnp.where(left_half, 0.0, synth[0])
        synth[n] = jnp.where(left_half, synth[n], 0.0)
        result = backward(list(zip(*[split(t) for t in synth])), back)
        add_terms(total, avo_ref, a, result)
    return total


def lateral(here, north, south, west, east):
    traces = here.shape[0]
    place = lax.broadcasted_iota(jnp.int32, here.shape, 0)
    from_west = jnp.where(place == 0, 0.0 if west is None else west, pltpu.roll(here, 1, 0))
    from_east = jnp.where(
        place == traces - 1, 0.0 if east is None else east, pltpu.roll(here, traces - 1, 0)
    )
    around = from_west + from_east
    for other in (north, south):
        around = around if other is None else around + other
    return around


def copy_in(pairs, sems):
    copies = [pltpu.make_async_copy(a, b, sems.at[i]) for i, (a, b) in enumerate(pairs)]
    for copy in copies:
        copy.start()
    return copies


def start_kernel(
    seis_hbm, valid_hbm, avo_hbm, taps_hbm, prior_hbm,
    b_ref, near_ref, far_ref, padded_ref, valid_ref, avo_ref, prior_ref,
    seis_ref, taps_ref, sems,
):
    taps, seis, valid, avo, prior = copy_in(
        (
            (taps_hbm, taps_ref),
            (seis_hbm, seis_ref),
            (valid_hbm, valid_ref),
            (avo_hbm, avo_ref),
            (prior_hbm, prior_ref),
        ),
        sems,
    )
    taps.wait()
    pad_taps(taps_ref, padded_ref)
    angles = avo_ref.shape[1]
    bands = [band(padded_ref[a : a + 1, :]) for a in range(angles)]
    valid.wait()
    masks = [trace_columns(valid_ref, a) for a in range(angles)]
    for copy in (seis, avo, prior):
        copy.wait()
    store_tiles(b_ref, right_side(seis_ref, masks, avo_ref, bands))
    contrasts, rows, traces, samples = b_ref.shape
    n = samples // LANES
    first = starts_pair("inline")
    lane = lax.broadcasted_iota(jnp.int32, (traces, LANES), 1)
    notes = []
    for r in (0, rows - 1):
        note = jnp.where(lane == angles, column(prior_ref[r : r + 1, :]), 0.0)
        for a in range(angles):
            note = jnp.where(lane == a, masks[a][r * traces : (r + 1) * traces], note)
        notes.append(note)
    edges = [
        [*[b_ref[c, r, :, pl.ds(k * LANES, LANES)] for c in range(contrasts) for k in range(n)], note]
        for r, note in zip((0, rows - 1), notes)
    ]
    for e, (top, bottom) in enumerate(zip(*edges)):
        near_ref[e] = jnp.where(first, bottom, top)
        far_ref[e] = jnp.where(first, top, bottom)


def either_side(pair_ref, next_ref, *where):
    first = starts_pair("inline")
    pair, other = pair_ref[where], next_ref[where]
    return jnp.where(first, other, pair), jnp.where(first, pair, other)


def stack_tiles(ref):
    contrasts, rows, _, samples = ref.shape
    return [
        [
            jnp.concatenate([ref[c, r, :, pl.ds(k, LANES)] for r in range(rows)], axis=0)
            for k in range(0, samples, LANES)
        ]
        for c in range(contrasts)
    ]


def inside(axis):
    place = lax.axis_index(axis)
    last = lax.axis_size(axis) - 1
    return (place > 0).astype(F32), (place < last).astype(F32)


def starts_pair(axis):
    return lax.axis_index(axis) % 2 == 0


def row_pair(near_ref, next_ref, c, n):
    tiles = [either_side(near_ref, next_ref, c * n + k) for k in range(n)]
    return [jnp.concatenate(side, axis=1) for side in zip(*tiles)]


def column_kernel(
    b_ref, near_ref, near_next_ref, valid_ref, prior_ref,
    pair_ref, other_ref, own_ref, note_ref, second_ref,
):
    contrasts, rows, traces, samples = b_ref.shape
    angles = valid_ref.shape[0]
    first_col = starts_pair("col")
    half = rows + 2
    second_ref[...] = jnp.zeros_like(second_ref)
    note_ref[...] = jnp.zeros_like(note_ref)
    for c in range(contrasts):
        own = [b_ref[c, r] for r in range(rows)]
        for i, line in enumerate([*own, *row_pair(near_ref, near_next_ref, c, samples // LANES)]):
            own_ref[c, i : i + 1, :] = line[0:1]
            own_ref[c, half + i : half + i + 1, :] = line[traces - 1 :]
        for r, line in enumerate(own):
            at = c * rows + r
            second_ref[0, at : at + 1, :] = line[1:2]
            second_ref[1, at : at + 1, :] = line[traces - 2 : traces - 1]
    lane = lax.broadcasted_iota(jnp.int32, (1, LANES), 1)
    for r in range(rows):
        for side, t in enumerate((0, traces - 1)):
            note = jnp.where(lane == angles, prior_ref[r : r + 1, t : t + 1], 0.0)
            for a in range(angles):
                note = jnp.where(lane == a, valid_ref[a, r : r + 1, t : t + 1].astype(F32), note)
            at = contrasts * rows + r
            second_ref[side, at : at + 1, 0:LANES] = note
            at = r + side * (traces - rows)
            note_ref[at : at + 1, :] = note
    for c in range(contrasts):
        left, right = own_ref[c, 0:half], own_ref[c, half:]
        pair_ref[c] = jnp.where(first_col, right, left)
        other_ref[c] = jnp.where(first_col, left, right)
    for i in range(2):
        left, right = (second_ref[side, i * half : (i + 1) * half] for side in (0, 1))
        pair_ref[contrasts + i] = jnp.where(first_col, right, left)
        other_ref[contrasts + i] = jnp.where(first_col, left, right)


def inner_kernel(
    count, strength_hbm, b_ref, near_ref, near_next_ref, padded_ref, valid_ref, avo_ref, prior_ref,
    v_ref, data_ref, halo_ref, ahead_ref, back_ref, norm_ref, strength_ref, sem,
):
    contrasts, rows, traces, samples = b_ref.shape
    angles, n = avo_ref.shape[1], samples // LANES
    (copy,) = copy_in(((strength_hbm, strength_ref),), sem)
    turned = turn(padded_ref[...], count)
    bands = []
    for a in range(angles):
        bands.append((band(turned[a : a + 1]), band(padded_ref[a : a + 1, :])))
        ahead_ref[a], back_ref[a] = (half.astype(F32) for half in bands[a])
    masks = [trace_columns(valid_ref, a) for a in range(angles)]
    weights = [column(prior_ref[r : r + 1, :]) + 4.0 for r in range(rows)]
    above, below = either_side(near_ref, near_next_ref, contrasts * n)
    wide = [
        jnp.concatenate([above[:, a : a + 1], mask, below[:, a : a + 1]], axis=0)
        for a, mask in enumerate(masks)
    ]
    weights = [above[:, angles : angles + 1] + 4.0, *weights, below[:, angles : angles + 1] + 4.0]
    field = []
    for c, line in enumerate(stack_tiles(b_ref)):
        ends = [either_side(near_ref, near_next_ref, c * n + k) for k in range(n)]
        field.append(
            [jnp.concatenate([up, own, low], axis=0) for (up, low), own in zip(ends, line)]
        )
    total = normal(field, wide, avo_ref, bands)
    copy.wait()
    has_above, has_below = inside("inline")
    for c in range(contrasts):
        strength = strength_ref[:, c : c + 1]
        whole, data = jnp.concatenate(field[c], axis=1), jnp.concatenate(total[c], axis=1)
        lines = [whole[r * traces : (r + 1) * traces] for r in range(rows + 2)]
        for r, here in enumerate(lines):
            north = lines[r - 1] if r else None
            south = lines[r + 1] if r < rows + 1 else None
            if r == 0:
                south = has_above * south
            if r == rows + 1:
                north = has_below * north
            around = lateral(here, north, south, None, None)
            image = data[r * traces : (r + 1) * traces] + strength * (weights[r] * here - around)
            if 0 < r <= rows:
                v_ref[c, r - 1] = image
            else:
                halo_ref[min(r, 1), c] = image
    store_tiles(data_ref, normal(stack_tiles(v_ref), masks, avo_ref, bands))
    norm_ref[...] = functools.reduce(
        jnp.add, [lane_tiles(b_ref[c, r] * b_ref[c, r]) for c in range(contrasts) for r in range(rows)]
    )


def lane_tiles(product):
    tiles = [product[:, k : k + LANES] for k in range(0, product.shape[1], LANES)]
    return functools.reduce(jnp.add, tiles)


def halo_kernel(halo_ref, far_next_ref, far_ref, strength_ref, out_ref):
    contrasts, samples = halo_ref.shape[1], halo_ref.shape[3]
    for c in range(contrasts):
        for i, line in enumerate(row_pair(far_ref, far_next_ref, c, samples // LANES)):
            out_ref[i, c] = halo_ref[i, c] - strength_ref[:, c : c + 1] * line


def image_kernel(
    b_ref, v_ref, data_ref, halo_ref, norm_ref, own_ref, note_ref, other_ref, pair_ref,
    avo_ref, prior_ref, strength_ref, ahead_ref, back_ref,
    one_ref, two_ref, gram_ref,
):
    contrasts, rows, traces, samples = b_ref.shape
    angles, n = avo_ref.shape[1], samples // LANES
    has_left, has_right = inside("col")
    first_col = starts_pair("col")
    place = lax.broadcasted_iota(jnp.int32, (traces, samples), 0)
    west, east = place == 0, place == traces - 1
    half = traces // 2

    def turned(value, k):
        return pltpu.roll(value, k % traces, 0) if k % traces else value

    def sides(i):
        pair, other = pair_ref[i], other_ref[i]
        left, right = jnp.where(first_col, other, pair), jnp.where(first_col, pair, other)
        return jnp.concatenate([left, right], axis=0)

    def at_ends(value, left, right, inner):
        return jnp.where(west, turned(value, left), jnp.where(east, turned(value, right), inner))

    beside = [sides(c) for c in range(contrasts)]
    seconds = [sides(contrasts), sides(contrasts + 1)]
    notes = seconds[1][:, :LANES]
    line = place[:, :LANES]
    theirs = turned(notes, -rows)
    mixed = jnp.where((line == 2) | (line == 3), notes, note_ref[...])
    mixed = jnp.where((line == 4) | (line == 5), theirs, mixed)
    masks = [mixed[:, a : a + 1] for a in range(angles)]
    mine = (place[:, :1] < 2) | (place[:, :1] >= traces - 2)
    tile = []
    for c in range(contrasts):
        scale = jnp.where(mine, -strength_ref[:, c : c + 1], 1.0)
        whole = jnp.where(place % half < rows, beside[c], turned(beside[c], rows)) * scale
        tile.append([whole[:, k * LANES : (k + 1) * LANES] for k in range(n)])
    bands = [(ahead_ref[a].astype(BF16), back_ref[a].astype(BF16)) for a in range(angles)]
    edge = [jnp.concatenate(tiles, axis=1) for tiles in normal(tile, masks, avo_ref, bands)]

    has = jnp.where(place[:, :1] < half, has_left, has_right)
    far_weight = theirs[:, angles : angles + 1] + 4.0
    weights = [column(prior_ref[r : r + 1, :]) + 4.0 for r in range(rows)]
    sums = [norm_ref[...], *[jnp.zeros((traces, LANES), F32) for _ in range(3)]]
    for c in range(contrasts):
        strength = strength_ref[:, c : c + 1]
        theirs = beside[c]
        around = turned(seconds[c // 2], -rows * (c % 2)) + turned(theirs, -rows)
        around = around + jnp.where(place % 2 == 1, turned(theirs, 1), turned(theirs, -1))
        prior = far_weight * theirs - (around + has * own_ref[c])
        beyond = jnp.where(place < half, turned(edge[c], -rows), edge[c]) + strength * prior

        lines = [halo_ref[0, c], *[v_ref[c, r] for r in range(rows)], halo_ref[1, c]]
        lines = [
            here - strength * at_ends(theirs, -k, half - 1 - k, 0.0)
            for here, k in zip(lines, (rows, *range(rows), rows + 1))
        ]
        for r in range(rows):
            here, b = lines[r + 1], b_ref[c, r]
            ends = jnp.where(west, turned(beyond, -r), turned(beyond, half - 1 - r))
            around = jnp.where(west, ends, turned(here, 1)) + jnp.where(east, ends, turned(here, -1))
            around = around + lines[r] + lines[r + 2]
            mend = at_ends(edge[c], -r, 1 - r, 0.0)
            two = data_ref[c, r] + mend + strength * (weights[r] * here - around)
            one_ref[c, r] = here
            two_ref[c, r] = two
            for q, product in enumerate((b * here, here * here, here * two), 1):
                sums[q] = sums[q] + lane_tiles(product)
    lane = lax.broadcasted_iota(jnp.int32, (1, LANES), 1)
    packed = jnp.zeros((1, LANES), F32)
    for q, total in enumerate(sums):
        total = jnp.sum(jnp.sum(total, axis=0, keepdims=True), axis=1, keepdims=True)
        packed = jnp.where(lane == q, total, packed)
    gram_ref[...] = jnp.broadcast_to(packed[None], gram_ref.shape)


def finish_kernel(gram_ref, b_ref, one_ref, two_ref, solution_ref, residual_ref):
    sums = jnp.sum(gram_ref[...], axis=0)
    shares = sums / sums[:, 1:2]
    first, middle, last = (shares[:, q : q + 1] for q in (0, 2, 3))
    ratio = first * middle
    second = (ratio - 1.0) / (first * last - ratio * middle)
    near = first + second * ratio
    far = first * second
    for c in range(b_ref.shape[0]):
        for r in range(b_ref.shape[1]):
            b, one, two = b_ref[c, r], one_ref[c, r], two_ref[c, r]
            solution_ref[c, r] = near * b - far * one
            residual_ref[c, r] = b - near * one + far * two


VMEM = pl.BlockSpec(memory_space=pltpu.VMEM)
HBM = pl.BlockSpec(memory_space=pltpu.HBM)


def call(kernel, outs, ins, flops, scratch=(), places=None):
    moved = sum(x.size * x.dtype.itemsize for x in (*ins, *outs))
    return pl.pallas_call(
        kernel,
        out_shape=outs,
        in_specs=[VMEM] * len(ins) if places is None else places,
        out_specs=jax.tree.map(lambda _: VMEM, outs),
        scratch_shapes=list(scratch),
        compiler_params=pltpu.CompilerParams(vmem_limit_bytes=24 * 1024 * 1024),
        cost_estimate=pl.CostEstimate(flops=flops, bytes_accessed=moved, transcendentals=0),
        name=getattr(kernel, "func", kernel).__name__,
    )(*ins)


def swap(axis, value, first):
    starts = range(first, lax.axis_size(axis) - 1, 2)
    return lax.ppermute(value, axis, [(i + d, i + 1 - d) for i in starts for d in (0, 1)])


def hand_on(axis, value):
    size = lax.axis_size(axis)
    steps = [(i, i + 2 - 4 * (i % 2)) for i in range(size)]
    return lax.ppermute(value, axis, [(i, j) for i, j in steps if 0 <= j < size])


def shards(seismic, validity, prior_weight, lateral_strength, avo_coeffs, wavelets):
    angles, rows, traces, samples = seismic.shape
    contrasts = avo_coeffs.shape[1]
    avo_coeffs = jnp.swapaxes(avo_coeffs, 0, 1)
    shape = lambda *dims: jax.ShapeDtypeStruct(dims, F32)
    field = shape(contrasts, rows, traces, samples)
    side = shape(contrasts + 2, rows + 2, samples)
    lines = shape(8, 2 * LANES)
    work = 2 * angles * rows * traces * samples * 256 * 4

    given = (seismic, validity, avo_coeffs, wavelets, prior_weight)
    kept = [given[i] for i in (1, 2, 4)]
    edge = shape(contrasts * samples // LANES + 1, traces, LANES)
    b, near, far, padded, *kept = call(
        start_kernel,
        (
            field, edge, edge, lines,
            *[jax.ShapeDtypeStruct(x.shape, x.dtype) for x in kept],
        ),
        [pltpu.with_memory_space_constraint(x, pltpu.HBM) for x in given],
        work,
        [
            pltpu.VMEM(seismic.shape, seismic.dtype),
            pltpu.VMEM(wavelets.shape, F32),
            pltpu.SemaphoreType.DMA((5,)),
        ],
        [HBM] * 5,
    )
    near = swap("inline", near, 0)
    near_next = swap("inline", far, 1)
    far_next = hand_on("inline", near)
    far = swap("inline", far, 0)
    col_pair, col_other, own, note = call(
        column_kernel,
        (side, side, shape(contrasts, 2 * rows + 4, samples), shape(traces, LANES)),
        (b, near, near_next, kept[0], kept[2]),
        2 * field.size,
        [pltpu.VMEM((2, 2 * rows + 4, samples), F32)],
    )
    col_other = swap("col", col_other, 1)
    col_pair = swap("col", col_pair, 0)
    bands = shape(angles, 2 * LANES, 2 * LANES)
    halo = shape(2, contrasts, traces, samples)
    strength = lateral_strength.reshape(1, -1)
    image, data, part, ahead, back, norm, strength = call(
        functools.partial(inner_kernel, wavelets.shape[1]),
        (field, field, halo, bands, bands, shape(traces, LANES), shape(*strength.shape)),
        (
            pltpu.with_memory_space_constraint(strength, pltpu.HBM),
            b, near, near_next, padded, *kept,
        ),
        6 * work,
        [pltpu.SemaphoreType.DMA((1,))],
        [HBM] + [VMEM] * 7,
    )
    (halo,) = call(halo_kernel, (halo,), (part, far_next, far, strength), field.size)
    axes = ("inline", "col")
    one, two, gram = call(
        image_kernel,
        (field, field, shape(lax.axis_size(axes), 1, LANES)),
        (
            b, image, data, halo, norm, own, note, col_other, col_pair,
            *kept[1:], strength, ahead, back,
        ),
        work,
    )
    gram = lax.all_to_all(gram, axes, 0, 0)
    return tuple(call(finish_kernel, (field, field), (gram, b, one, two), 8 * field.size))


def solution(mesh):
    placed = (
        P(None, "inline", "col", None),
        P(None, "inline", "col"),
        P("inline", "col"),
        P(),
        P(),
        P(),
    )
    return jax.shard_map(
        shards,
        mesh=mesh,
        in_specs=placed,
        out_specs=(P(None, "inline", "col", None), P(None, "inline", "col", None)),
        check_vma=False,
    )
```

```python
import functools

import jax
import jax.numpy as jnp
from jax import lax
from jax.experimental import pallas as pl
from jax.experimental.pallas import tpu as pltpu
from jax.sharding import PartitionSpec as P

LANES = 128
F32 = jnp.float32
BF16 = jnp.bfloat16


def split(value):
    high = value.astype(BF16)
    return high, (value - high.astype(F32)).astype(BF16)


def pad_taps(taps_ref, padded_ref):
    padded_ref[...] = jnp.zeros_like(padded_ref)
    padded_ref[0 : taps_ref.shape[0], 0 : taps_ref.shape[1]] = taps_ref[...]


def turn(lines, count):
    n, size = lines.shape
    parts = []
    for _ in range(3):
        parts.append(lines.astype(BF16).astype(F32))
        lines = lines - parts[-1]
    rows = lax.broadcasted_iota(jnp.int32, (size, size), 0)
    cols = lax.broadcasted_iota(jnp.int32, (size, size), 1)
    flip = jnp.where(rows + cols == count - 1, 1.0, 0.0).astype(BF16)
    whole = jnp.concatenate(parts, axis=0).astype(BF16)
    turned = jnp.dot(whole, flip, preferred_element_type=F32)
    return turned[:n] + turned[n : 2 * n] + turned[2 * n :]


def band(line):
    lines = jnp.broadcast_to(line, (LANES, line.shape[1]))
    return jnp.concatenate(split(pltpu.roll(lines, 0, 1, stride=1, stride_axis=0)), axis=0)


def convolve(rows, bands):
    out = lax.dot_general(rows, bands, (((1,), (1,)), ((), ())), preferred_element_type=F32)
    return out[:, :LANES] + out[:, LANES:]


def column(row):
    n = row.shape[1]
    same = lax.broadcasted_iota(jnp.int32, (n, n), 0) == lax.broadcasted_iota(jnp.int32, (n, n), 1)
    return jnp.sum(jnp.where(same, jnp.broadcast_to(row, (n, n)), 0.0), axis=1, keepdims=True)


def trace_columns(ref, *lead):
    rows = ref[lead].astype(F32)
    return jnp.concatenate([column(rows[r : r + 1, :]) for r in range(rows.shape[0])], axis=0)


def windows(tiles):
    pairs = [jnp.concatenate(pair, axis=1) for pair in zip(tiles[:-1], tiles[1:])]
    return jnp.concatenate(pairs, axis=0)


def forward(tiles, bands):
    zero = jnp.zeros_like(tiles[0]).astype(BF16)
    highs, lows = zip(*[split(t) for t in tiles])
    n, size = len(tiles) + 1, tiles[0].shape[0]
    rows = [windows([zero, *part, zero]) for part in (highs, lows)]
    out = convolve(jnp.concatenate(rows, axis=0), bands)
    out = out[: n * size] + out[n * size :]
    return [out[k * size : (k + 1) * size] for k in range(n)]


def backward(parts, bands):
    n, size = len(parts[0]) - 1, parts[0][0].shape[0]
    rows = jnp.concatenate([windows(part) for part in parts], axis=0)
    out = convolve(rows, bands)
    total = out[: n * size]
    for p in range(1, len(parts)):
        total = total + out[p * n * size : (p + 1) * n * size]
    return [total[k * size : (k + 1) * size] for k in range(n)]


def coeff(avo_ref, angle, contrast, k):
    return avo_ref[contrast, angle : angle + 1, pl.ds(k * LANES, LANES)]


def add_terms(total, avo_ref, angle, result):
    for c, line in enumerate(total):
        for k, tile in enumerate(result):
            term = coeff(avo_ref, angle, c, k) * tile
            line[k] = term if angle == 0 else line[k] + term


def store_tiles(out_ref, tiles):
    size = out_ref.shape[2]
    for c in range(out_ref.shape[0]):
        for k, tile in enumerate(tiles[c]):
            for r in range(out_ref.shape[1]):
                out_ref[c, r, :, pl.ds(k * LANES, LANES)] = tile[r * size : (r + 1) * size]


def right_side(seis_ref, masks, avo_ref, bands):
    angles, rows, _, samples = seis_ref.shape
    n = samples // LANES
    total = [[None] * n for _ in range(avo_ref.shape[0])]
    for a in range(angles):
        data = jnp.concatenate([seis_ref[a, r].astype(F32) for r in range(rows)], axis=0)
        data = data * masks[a]
        turned = [
            pltpu.roll(data[:, k * LANES : (k + 1) * LANES], LANES // 2, 1) for k in range(n)
        ]
        zero = jnp.zeros_like(turned[0])
        left_half = lax.broadcasted_iota(jnp.int32, zero.shape, 1) < LANES // 2
        shifted = [
            jnp.where(left_half, before, here).astype(BF16)
            for before, here in zip([zero, *turned], [*turned, zero])
        ]
        add_terms(total, avo_ref, a, backward([shifted], bands[a]))
    return total


def normal(field, masks, avo_ref, bands):
    contrasts, n = len(field), len(field[0])
    total = [[None] * n for _ in range(contrasts)]
    for a, (ahead, back) in enumerate(bands):
        mixed = []
        for k in range(n):
            parts = [coeff(avo_ref, a, c, k) * field[c][k] for c in range(contrasts)]
            mixed.append(functools.reduce(jnp.add, parts))
        synth = [tile * masks[a] for tile in forward(mixed, ahead)]
        left_half = lax.broadcasted_iota(jnp.int32, synth[0].shape, 1) < LANES // 2
        synth[0] = jnp.where(left_half, 0.0, synth[0])
        synth[n] = jnp.where(left_half, synth[n], 0.0)
        result = backward(list(zip(*[split(t) for t in synth])), back)
        add_terms(total, avo_ref, a, result)
    return total


def lateral(here, north, south, west, east):
    traces = here.shape[0]
    place = lax.broadcasted_iota(jnp.int32, here.shape, 0)
    from_west = jnp.where(place == 0, 0.0 if west is None else west, pltpu.roll(here, 1, 0))
    from_east = jnp.where(
        place == traces - 1, 0.0 if east is None else east, pltpu.roll(here, traces - 1, 0)
    )
    around = from_west + from_east
    for other in (north, south):
        around = around if other is None else around + other
    return around


def copy_in(pairs, sems):
    copies = [pltpu.make_async_copy(a, b, sems.at[i]) for i, (a, b) in enumerate(pairs)]
    for copy in copies:
        copy.start()
    return copies


def start_kernel(
    seis_hbm, valid_hbm, avo_hbm, taps_hbm, prior_hbm,
    b_ref, near_ref, far_ref, padded_ref, valid_ref, avo_ref, prior_ref,
    seis_ref, taps_ref, sems,
):
    angles = avo_ref.shape[1]
    taps, valid, *rest = copy_in(
        (
            (taps_hbm, taps_ref),
            (valid_hbm, valid_ref),
            *((seis_hbm.at[a], seis_ref.at[a]) for a in range(angles)),
            (avo_hbm, avo_ref),
            (prior_hbm, prior_ref),
        ),
        sems,
    )
    taps.wait()
    pad_taps(taps_ref, padded_ref)
    bands = [band(padded_ref[a : a + 1, :]) for a in range(angles)]
    valid.wait()
    masks = [trace_columns(valid_ref, a) for a in range(angles)]
    for copy in rest:
        copy.wait()
    store_tiles(b_ref, right_side(seis_ref, masks, avo_ref, bands))
    contrasts, rows, traces, samples = b_ref.shape
    n = samples // LANES
    first = starts_pair("inline")
    lane = lax.broadcasted_iota(jnp.int32, (traces, LANES), 1)
    notes = []
    for r in (0, rows - 1):
        note = jnp.where(lane == angles, column(prior_ref[r : r + 1, :]), 0.0)
        for a in range(angles):
            note = jnp.where(lane == a, masks[a][r * traces : (r + 1) * traces], note)
        notes.append(note)
    edges = [
        [*[b_ref[c, r, :, pl.ds(k * LANES, LANES)] for c in range(contrasts) for k in range(n)], note]
        for r, note in zip((0, rows - 1), notes)
    ]
    for e, (top, bottom) in enumerate(zip(*edges)):
        near_ref[e] = jnp.where(first, bottom, top)
        far_ref[e] = jnp.where(first, top, bottom)


def either_side(pair_ref, next_ref, *where):
    first = starts_pair("inline")
    pair, other = pair_ref[where], next_ref[where]
    return jnp.where(first, other, pair), jnp.where(first, pair, other)


def stack_tiles(ref):
    contrasts, rows, _, samples = ref.shape
    return [
        [
            jnp.concatenate([ref[c, r, :, pl.ds(k, LANES)] for r in range(rows)], axis=0)
            for k in range(0, samples, LANES)
        ]
        for c in range(contrasts)
    ]


def inside(axis):
    place = lax.axis_index(axis)
    last = lax.axis_size(axis) - 1
    return (place > 0).astype(F32), (place < last).astype(F32)


def starts_pair(axis):
    return lax.axis_index(axis) % 2 == 0


def row_pair(near_ref, next_ref, c, n):
    tiles = [either_side(near_ref, next_ref, c * n + k) for k in range(n)]
    return [jnp.concatenate(side, axis=1) for side in zip(*tiles)]


def column_kernel(
    b_ref, near_ref, near_next_ref, valid_ref, prior_ref,
    pair_ref, other_ref, own_ref, note_ref, second_ref,
):
    contrasts, rows, traces, samples = b_ref.shape
    angles = valid_ref.shape[0]
    first_col = starts_pair("col")
    half = rows + 2
    second_ref[...] = jnp.zeros_like(second_ref)
    note_ref[...] = jnp.zeros_like(note_ref)
    for c in range(contrasts):
        own = [b_ref[c, r] for r in range(rows)]
        for i, line in enumerate([*own, *row_pair(near_ref, near_next_ref, c, samples // LANES)]):
            own_ref[c, i : i + 1, :] = line[0:1]
            own_ref[c, half + i : half + i + 1, :] = line[traces - 1 :]
        for r, line in enumerate(own):
            at = c * rows + r
            second_ref[0, at : at + 1, :] = line[1:2]
            second_ref[1, at : at + 1, :] = line[traces - 2 : traces - 1]
    lane = lax.broadcasted_iota(jnp.int32, (1, LANES), 1)
    for r in range(rows):
        for side, t in enumerate((0, traces - 1)):
            note = jnp.where(lane == angles, prior_ref[r : r + 1, t : t + 1], 0.0)
            for a in range(angles):
                note = jnp.where(lane == a, valid_ref[a, r : r + 1, t : t + 1].astype(F32), note)
            at = contrasts * rows + r
            second_ref[side, at : at + 1, 0:LANES] = note
            at = r + side * (traces - rows)
            note_ref[at : at + 1, :] = note
    for c in range(contrasts):
        left, right = own_ref[c, 0:half], own_ref[c, half:]
        pair_ref[c] = jnp.where(first_col, right, left)
        other_ref[c] = jnp.where(first_col, left, right)
    for i in range(2):
        left, right = (second_ref[side, i * half : (i + 1) * half] for side in (0, 1))
        pair_ref[contrasts + i] = jnp.where(first_col, right, left)
        other_ref[contrasts + i] = jnp.where(first_col, left, right)


def inner_kernel(
    count, strength_hbm, b_ref, near_ref, near_next_ref, padded_ref, valid_ref, avo_ref, prior_ref,
    v_ref, data_ref, halo_ref, ahead_ref, back_ref, norm_ref, strength_ref, sem,
):
    contrasts, rows, traces, samples = b_ref.shape
    angles, n = avo_ref.shape[1], samples // LANES
    (copy,) = copy_in(((strength_hbm, strength_ref),), sem)
    turned = turn(padded_ref[...], count)
    bands = []
    for a in range(angles):
        bands.append((band(turned[a : a + 1]), band(padded_ref[a : a + 1, :])))
        ahead_ref[a], back_ref[a] = (half.astype(F32) for half in bands[a])
    masks = [trace_columns(valid_ref, a) for a in range(angles)]
    weights = [column(prior_ref[r : r + 1, :]) + 4.0 for r in range(rows)]
    above, below = either_side(near_ref, near_next_ref, contrasts * n)
    wide = [
        jnp.concatenate([above[:, a : a + 1], mask, below[:, a : a + 1]], axis=0)
        for a, mask in enumerate(masks)
    ]
    weights = [above[:, angles : angles + 1] + 4.0, *weights, below[:, angles : angles + 1] + 4.0]
    field = []
    for c, line in enumerate(stack_tiles(b_ref)):
        ends = [either_side(near_ref, near_next_ref, c * n + k) for k in range(n)]
        field.append(
            [jnp.concatenate([up, own, low], axis=0) for (up, low), own in zip(ends, line)]
        )
    total = normal(field, wide, avo_ref, bands)
    copy.wait()
    has_above, has_below = inside("inline")
    for c in range(contrasts):
        strength = strength_ref[:, c : c + 1]
        whole, data = jnp.concatenate(field[c], axis=1), jnp.concatenate(total[c], axis=1)
        lines = [whole[r * traces : (r + 1) * traces] for r in range(rows + 2)]
        for r, here in enumerate(lines):
            north = lines[r - 1] if r else None
            south = lines[r + 1] if r < rows + 1 else None
            if r == 0:
                south = has_above * south
            if r == rows + 1:
                north = has_below * north
            around = lateral(here, north, south, None, None)
            image = data[r * traces : (r + 1) * traces] + strength * (weights[r] * here - around)
            if 0 < r <= rows:
                v_ref[c, r - 1] = image
            else:
                halo_ref[min(r, 1), c] = image
    store_tiles(data_ref, normal(stack_tiles(v_ref), masks, avo_ref, bands))
    norm_ref[...] = functools.reduce(
        jnp.add, [lane_tiles(b_ref[c, r] * b_ref[c, r]) for c in range(contrasts) for r in range(rows)]
    )


def lane_tiles(product):
    tiles = [product[:, k : k + LANES] for k in range(0, product.shape[1], LANES)]
    return functools.reduce(jnp.add, tiles)


def halo_kernel(halo_ref, far_next_ref, far_ref, strength_ref, out_ref):
    contrasts, samples = halo_ref.shape[1], halo_ref.shape[3]
    for c in range(contrasts):
        for i, line in enumerate(row_pair(far_ref, far_next_ref, c, samples // LANES)):
            out_ref[i, c] = halo_ref[i, c] - strength_ref[:, c : c + 1] * line


def image_kernel(
    b_ref, v_ref, data_ref, halo_ref, norm_ref, own_ref, note_ref, other_ref, pair_ref,
    avo_ref, prior_ref, strength_ref, ahead_ref, back_ref,
    one_ref, two_ref, gram_ref,
):
    contrasts, rows, traces, samples = b_ref.shape
    angles, n = avo_ref.shape[1], samples // LANES
    has_left, has_right = inside("col")
    first_col = starts_pair("col")
    place = lax.broadcasted_iota(jnp.int32, (traces, samples), 0)
    west, east = place == 0, place == traces - 1
    half = traces // 2

    def turned(value, k):
        return pltpu.roll(value, k % traces, 0) if k % traces else value

    def sides(i):
        pair, other = pair_ref[i], other_ref[i]
        left, right = jnp.where(first_col, other, pair), jnp.where(first_col, pair, other)
        return jnp.concatenate([left, right], axis=0)

    def at_ends(value, left, right, inner):
        return jnp.where(west, turned(value, left), jnp.where(east, turned(value, right), inner))

    beside = [sides(c) for c in range(contrasts)]
    seconds = [sides(contrasts), sides(contrasts + 1)]
    notes = seconds[1][:, :LANES]
    line = place[:, :LANES]
    theirs = turned(notes, -rows)
    mixed = jnp.where((line == 2) | (line == 3), notes, note_ref[...])
    mixed = jnp.where((line == 4) | (line == 5), theirs, mixed)
    masks = [mixed[:, a : a + 1] for a in range(angles)]
    mine = (place[:, :1] < 2) | (place[:, :1] >= traces - 2)
    tile = []
    for c in range(contrasts):
        scale = jnp.where(mine, -strength_ref[:, c : c + 1], 1.0)
        whole = jnp.where(place % half < rows, beside[c], turned(beside[c], rows)) * scale
        tile.append([whole[:, k * LANES : (k + 1) * LANES] for k in range(n)])
    bands = [(ahead_ref[a].astype(BF16), back_ref[a].astype(BF16)) for a in range(angles)]
    edge = [jnp.concatenate(tiles, axis=1) for tiles in normal(tile, masks, avo_ref, bands)]

    has = jnp.where(place[:, :1] < half, has_left, has_right)
    far_weight = theirs[:, angles : angles + 1] + 4.0
    weights = [column(prior_ref[r : r + 1, :]) + 4.0 for r in range(rows)]
    sums = [norm_ref[...], *[jnp.zeros((traces, LANES), F32) for _ in range(3)]]
    for c in range(contrasts):
        strength = strength_ref[:, c : c + 1]
        theirs = beside[c]
        around = turned(seconds[c // 2], -rows * (c % 2)) + turned(theirs, -rows)
        around = around + jnp.where(place % 2 == 1, turned(theirs, 1), turned(theirs, -1))
        prior = far_weight * theirs - (around + has * own_ref[c])
        beyond = jnp.where(place < half, turned(edge[c], -rows), edge[c]) + strength * prior

        lines = [halo_ref[0, c], *[v_ref[c, r] for r in range(rows)], halo_ref[1, c]]
        lines = [
            here - strength * at_ends(theirs, -k, half - 1 - k, 0.0)
            for here, k in zip(lines, (rows, *range(rows), rows + 1))
        ]
        for r in range(rows):
            here, b = lines[r + 1], b_ref[c, r]
            ends = jnp.where(west, turned(beyond, -r), turned(beyond, half - 1 - r))
            around = jnp.where(west, ends, turned(here, 1)) + jnp.where(east, ends, turned(here, -1))
            around = around + lines[r] + lines[r + 2]
            mend = at_ends(edge[c], -r, 1 - r, 0.0)
            two = data_ref[c, r] + mend + strength * (weights[r] * here - around)
            one_ref[c, r] = here
            two_ref[c, r] = two
            for q, product in enumerate((b * here, here * here, here * two), 1):
                sums[q] = sums[q] + lane_tiles(product)
    lane = lax.broadcasted_iota(jnp.int32, (1, LANES), 1)
    packed = jnp.zeros((1, LANES), F32)
    for q, total in enumerate(sums):
        total = jnp.sum(jnp.sum(total, axis=0, keepdims=True), axis=1, keepdims=True)
        packed = jnp.where(lane == q, total, packed)
    gram_ref[...] = jnp.broadcast_to(packed[None], gram_ref.shape)


def finish_kernel(
    gram_ref, b_ref, one_ref, two_ref, solution_hbm, residual_hbm, solution_ref, residual_ref, sems
):
    sums = jnp.sum(gram_ref[...], axis=0)
    g00, g01, g11, g12 = (sums[:, q : q + 1] for q in range(4))
    first = g00 / g01
    ratio = first * g11 / g01
    second = (ratio - 1.0) * g01 / (first * g12 - ratio * g11)
    near = first + second * ratio
    far = first * second
    blocks = [(c, r) for c in range(b_ref.shape[0]) for r in range(b_ref.shape[1])]
    for block in blocks:
        solution_ref[block] = near * b_ref[block] - far * one_ref[block]
    done = pltpu.make_async_copy(solution_ref, solution_hbm, sems.at[0])
    done.start()
    for block in blocks:
        residual_ref[block] = b_ref[block] - near * one_ref[block] + far * two_ref[block]
    last = pltpu.make_async_copy(residual_ref, residual_hbm, sems.at[1])
    last.start()
    done.wait()
    last.wait()


VMEM = pl.BlockSpec(memory_space=pltpu.VMEM)
HBM = pl.BlockSpec(memory_space=pltpu.HBM)


def call(kernel, outs, ins, flops, scratch=(), places=None, to=VMEM):
    moved = sum(x.size * x.dtype.itemsize for x in (*ins, *outs))
    return pl.pallas_call(
        kernel,
        out_shape=outs,
        in_specs=[VMEM] * len(ins) if places is None else places,
        out_specs=jax.tree.map(lambda _: to, outs),
        scratch_shapes=list(scratch),
        compiler_params=pltpu.CompilerParams(vmem_limit_bytes=24 * 1024 * 1024),
        cost_estimate=pl.CostEstimate(flops=flops, bytes_accessed=moved, transcendentals=0),
        name=getattr(kernel, "func", kernel).__name__,
    )(*ins)


def swap(axis, value, first):
    starts = range(first, lax.axis_size(axis) - 1, 2)
    return lax.ppermute(value, axis, [(i + d, i + 1 - d) for i in starts for d in (0, 1)])


def hand_on(axis, value):
    size = lax.axis_size(axis)
    steps = [(i, i + 2 - 4 * (i % 2)) for i in range(size)]
    return lax.ppermute(value, axis, [(i, j) for i, j in steps if 0 <= j < size])


def shards(seismic, validity, prior_weight, lateral_strength, avo_coeffs, wavelets):
    angles, rows, traces, samples = seismic.shape
    contrasts = avo_coeffs.shape[1]
    avo_coeffs = jnp.swapaxes(avo_coeffs, 0, 1)
    shape = lambda *dims: jax.ShapeDtypeStruct(dims, F32)
    field = shape(contrasts, rows, traces, samples)
    side = shape(contrasts + 2, rows + 2, samples)
    lines = shape(8, 2 * LANES)
    work = 2 * angles * rows * traces * samples * 256 * 4

    given = (seismic, validity, avo_coeffs, wavelets, prior_weight)
    kept = [given[i] for i in (1, 2, 4)]
    edge = shape(contrasts * samples // LANES + 1, traces, LANES)
    b, near, far, padded, *kept = call(
        start_kernel,
        (
            field, edge, edge, lines,
            *[jax.ShapeDtypeStruct(x.shape, x.dtype) for x in kept],
        ),
        [pltpu.with_memory_space_constraint(x, pltpu.HBM) for x in given],
        work,
        [
            pltpu.VMEM(seismic.shape, seismic.dtype),
            pltpu.VMEM(wavelets.shape, F32),
            pltpu.SemaphoreType.DMA((angles + 4,)),
        ],
        [HBM] * 5,
    )
    near = swap("inline", near, 0)
    near_next = swap("inline", far, 1)
    far_next = hand_on("inline", near)
    far = swap("inline", far, 0)
    col_pair, col_other, own, note = call(
        column_kernel,
        (side, side, shape(contrasts, 2 * rows + 4, samples), shape(traces, LANES)),
        (b, near, near_next, kept[0], kept[2]),
        2 * field.size,
        [pltpu.VMEM((2, 2 * rows + 4, samples), F32)],
    )
    col_other = swap("col", col_other, 1)
    col_pair = swap("col", col_pair, 0)
    bands = shape(angles, 2 * LANES, 2 * LANES)
    halo = shape(2, contrasts, traces, samples)
    strength = lateral_strength.reshape(1, -1)
    image, data, part, ahead, back, norm, strength = call(
        functools.partial(inner_kernel, wavelets.shape[1]),
        (field, field, halo, bands, bands, shape(traces, LANES), shape(*strength.shape)),
        (
            pltpu.with_memory_space_constraint(strength, pltpu.HBM),
            b, near, near_next, padded, *kept,
        ),
        6 * work,
        [pltpu.SemaphoreType.DMA((1,))],
        [HBM] + [VMEM] * 7,
    )
    (halo,) = call(halo_kernel, (halo,), (part, far_next, far, strength), field.size)
    axes = ("inline", "col")
    one, two, gram = call(
        image_kernel,
        (field, field, shape(lax.axis_size(axes), 1, LANES)),
        (
            b, image, data, halo, norm, own, note, col_other, col_pair,
            *kept[1:], strength, ahead, back,
        ),
        work,
    )
    gram = lax.all_to_all(gram, axes, 0, 0)
    work = 8 * field.size
    room = [pltpu.VMEM(field.shape, F32)] * 2 + [pltpu.SemaphoreType.DMA((2,))]
    return tuple(
        call(finish_kernel, (field, field), (gram, b, one, two), work, room, to=HBM)
    )


def solution(mesh):
    placed = (
        P(None, "inline", "col", None),
        P(None, "inline", "col"),
        P("inline", "col"),
        P(),
        P(),
        P(),
    )
    return jax.shard_map(
        shards,
        mesh=mesh,
        in_specs=placed,
        out_specs=(P(None, "inline", "col", None), P(None, "inline", "col", None)),
        check_vma=False,
    )
```

```python
import functools

import jax
import jax.numpy as jnp
from jax import lax
from jax.experimental import pallas as pl
from jax.experimental.pallas import tpu as pltpu
from jax.sharding import PartitionSpec as P

LANES = 128
F32 = jnp.float32
BF16 = jnp.bfloat16


def split(value):
    high = value.astype(BF16)
    return high, (value - high.astype(F32)).astype(BF16)


def pad_taps(taps_ref, padded_ref):
    padded_ref[...] = jnp.zeros_like(padded_ref)
    padded_ref[0 : taps_ref.shape[0], 0 : taps_ref.shape[1]] = taps_ref[...]


def turn(lines, count):
    n, size = lines.shape
    parts = []
    for _ in range(3):
        parts.append(lines.astype(BF16).astype(F32))
        lines = lines - parts[-1]
    rows = lax.broadcasted_iota(jnp.int32, (size, size), 0)
    cols = lax.broadcasted_iota(jnp.int32, (size, size), 1)
    flip = jnp.where(rows + cols == count - 1, 1.0, 0.0).astype(BF16)
    whole = jnp.concatenate(parts, axis=0).astype(BF16)
    turned = jnp.dot(whole, flip, preferred_element_type=F32)
    return turned[:n] + turned[n : 2 * n] + turned[2 * n :]


def band(line):
    lines = jnp.broadcast_to(line, (LANES, line.shape[1]))
    return jnp.concatenate(split(pltpu.roll(lines, 0, 1, stride=1, stride_axis=0)), axis=0)


def convolve(rows, bands):
    rows = rows.astype(BF16)
    out = lax.dot_general(rows, bands, (((1,), (1,)), ((), ())), preferred_element_type=F32)
    return out[:, :LANES] + out[:, LANES:]


def column(row):
    n = row.shape[1]
    same = lax.broadcasted_iota(jnp.int32, (n, n), 0) == lax.broadcasted_iota(jnp.int32, (n, n), 1)
    return jnp.sum(jnp.where(same, jnp.broadcast_to(row, (n, n)), 0.0), axis=1, keepdims=True)


def trace_columns(ref, *lead):
    rows = ref[lead].astype(F32)
    return jnp.concatenate([column(rows[r : r + 1, :]) for r in range(rows.shape[0])], axis=0)


def halves(value):
    if value.shape[0] % 16 == 0:
        return split(value)
    high = value.astype(BF16).astype(F32)
    return high, value - high


def windows(tiles):
    pairs = [jnp.concatenate(pair, axis=1) for pair in zip(tiles[:-1], tiles[1:])]
    return jnp.concatenate(pairs, axis=0)


def forward(tiles, bands):
    highs, lows = zip(*[halves(t) for t in tiles])
    zero = jnp.zeros_like(highs[0])
    n, size = len(tiles) + 1, tiles[0].shape[0]
    rows = [windows([zero, *part, zero]) for part in (highs, lows)]
    out = convolve(jnp.concatenate(rows, axis=0), bands)
    out = out[: n * size] + out[n * size :]
    return [out[k * size : (k + 1) * size] for k in range(n)]


def backward(parts, bands):
    n, size = len(parts[0]) - 1, parts[0][0].shape[0]
    rows = jnp.concatenate([windows(part) for part in parts], axis=0)
    out = convolve(rows, bands)
    total = out[: n * size]
    for p in range(1, len(parts)):
        total = total + out[p * n * size : (p + 1) * n * size]
    return [total[k * size : (k + 1) * size] for k in range(n)]


def coeff(avo_ref, angle, contrast, k):
    return avo_ref[contrast, angle : angle + 1, pl.ds(k * LANES, LANES)]


def add_terms(total, avo_ref, angle, result):
    for c, line in enumerate(total):
        for k, tile in enumerate(result):
            term = coeff(avo_ref, angle, c, k) * tile
            line[k] = term if angle == 0 else line[k] + term


def store_tiles(out_ref, tiles):
    size = out_ref.shape[2]
    for c in range(out_ref.shape[0]):
        for k, tile in enumerate(tiles[c]):
            for r in range(out_ref.shape[1]):
                out_ref[c, r, :, pl.ds(k * LANES, LANES)] = tile[r * size : (r + 1) * size]


def right_side(seis_ref, masks, avo_ref, bands):
    angles, rows, _, samples = seis_ref.shape
    n = samples // LANES
    total = [[None] * n for _ in range(avo_ref.shape[0])]
    for a in range(angles):
        data = jnp.concatenate([seis_ref[a, r].astype(F32) for r in range(rows)], axis=0)
        data = data * masks[a]
        turned = [
            pltpu.roll(data[:, k * LANES : (k + 1) * LANES], LANES // 2, 1) for k in range(n)
        ]
        zero = jnp.zeros_like(turned[0])
        left_half = lax.broadcasted_iota(jnp.int32, zero.shape, 1) < LANES // 2
        shifted = [
            jnp.where(left_half, before, here).astype(BF16)
            for before, here in zip([zero, *turned], [*turned, zero])
        ]
        add_terms(total, avo_ref, a, backward([shifted], bands[a]))
    return total


def normal(field, masks, avo_ref, bands):
    contrasts, n = len(field), len(field[0])
    total = [[None] * n for _ in range(contrasts)]
    for a, (ahead, back) in enumerate(bands):
        mixed = []
        for k in range(n):
            parts = [coeff(avo_ref, a, c, k) * field[c][k] for c in range(contrasts)]
            mixed.append(functools.reduce(jnp.add, parts))
        synth = [tile * masks[a] for tile in forward(mixed, ahead)]
        left_half = lax.broadcasted_iota(jnp.int32, synth[0].shape, 1) < LANES // 2
        synth[0] = jnp.where(left_half, 0.0, synth[0])
        synth[n] = jnp.where(left_half, synth[n], 0.0)
        result = backward(list(zip(*[halves(t) for t in synth])), back)
        add_terms(total, avo_ref, a, result)
    return total


def lateral(here, north, south, west, east):
    traces = here.shape[0]
    place = lax.broadcasted_iota(jnp.int32, here.shape, 0)
    from_west = jnp.where(place == 0, 0.0 if west is None else west, pltpu.roll(here, 1, 0))
    from_east = jnp.where(
        place == traces - 1, 0.0 if east is None else east, pltpu.roll(here, traces - 1, 0)
    )
    around = from_west + from_east
    for other in (north, south):
        around = around if other is None else around + other
    return around


def copy_in(pairs, sems):
    copies = [pltpu.make_async_copy(a, b, sems.at[i]) for i, (a, b) in enumerate(pairs)]
    for copy in copies:
        copy.start()
    return copies


def start_kernel(
    seis_hbm, valid_hbm, avo_hbm, taps_hbm, prior_hbm,
    b_ref, near_ref, far_ref, padded_ref, valid_ref, avo_ref, prior_ref,
    seis_ref, taps_ref, sems,
):
    angles = avo_ref.shape[1]
    taps, valid, *rest = copy_in(
        (
            (taps_hbm, taps_ref),
            (valid_hbm, valid_ref),
            *((seis_hbm.at[a], seis_ref.at[a]) for a in range(angles)),
            (avo_hbm, avo_ref),
            (prior_hbm, prior_ref),
        ),
        sems,
    )
    taps.wait()
    pad_taps(taps_ref, padded_ref)
    bands = [band(padded_ref[a : a + 1, :]) for a in range(angles)]
    valid.wait()
    masks = [trace_columns(valid_ref, a) for a in range(angles)]
    for copy in rest:
        copy.wait()
    store_tiles(b_ref, right_side(seis_ref, masks, avo_ref, bands))
    contrasts, rows, traces, samples = b_ref.shape
    n = samples // LANES
    first = starts_pair("inline")
    lane = lax.broadcasted_iota(jnp.int32, (traces, LANES), 1)
    notes = []
    for r in (0, rows - 1):
        note = jnp.where(lane == angles, column(prior_ref[r : r + 1, :]), 0.0)
        for a in range(angles):
            note = jnp.where(lane == a, masks[a][r * traces : (r + 1) * traces], note)
        notes.append(note)
    edges = [
        [*[b_ref[c, r, :, pl.ds(k * LANES, LANES)] for c in range(contrasts) for k in range(n)], note]
        for r, note in zip((0, rows - 1), notes)
    ]
    for e, (top, bottom) in enumerate(zip(*edges)):
        near_ref[e] = jnp.where(first, bottom, top)
        far_ref[e] = jnp.where(first, top, bottom)


def either_side(pair_ref, next_ref, *where):
    first = starts_pair("inline")
    pair, other = pair_ref[where], next_ref[where]
    return jnp.where(first, other, pair), jnp.where(first, pair, other)


def stack_tiles(ref):
    contrasts, rows, _, samples = ref.shape
    return [
        [
            jnp.concatenate([ref[c, r, :, pl.ds(k, LANES)] for r in range(rows)], axis=0)
            for k in range(0, samples, LANES)
        ]
        for c in range(contrasts)
    ]


def inside(axis):
    place = lax.axis_index(axis)
    last = lax.axis_size(axis) - 1
    return (place > 0).astype(F32), (place < last).astype(F32)


def starts_pair(axis):
    return lax.axis_index(axis) % 2 == 0


def row_pair(near_ref, next_ref, c, n):
    tiles = [either_side(near_ref, next_ref, c * n + k) for k in range(n)]
    return [jnp.concatenate(side, axis=1) for side in zip(*tiles)]


def column_kernel(
    b_ref, near_ref, near_next_ref, valid_ref, prior_ref,
    pair_ref, other_ref, own_ref, note_ref, second_ref,
):
    contrasts, rows, traces, samples = b_ref.shape
    angles = valid_ref.shape[0]
    first_col = starts_pair("col")
    half = rows + 2
    second_ref[...] = jnp.zeros_like(second_ref)
    note_ref[...] = jnp.zeros_like(note_ref)
    for c in range(contrasts):
        own = [b_ref[c, r] for r in range(rows)]
        for i, line in enumerate([*own, *row_pair(near_ref, near_next_ref, c, samples // LANES)]):
            own_ref[c, i : i + 1, :] = line[0:1]
            own_ref[c, half + i : half + i + 1, :] = line[traces - 1 :]
        for r, line in enumerate(own):
            at = c * rows + r
            second_ref[0, at : at + 1, :] = line[1:2]
            second_ref[1, at : at + 1, :] = line[traces - 2 : traces - 1]
    lane = lax.broadcasted_iota(jnp.int32, (1, LANES), 1)
    for r in range(rows):
        for side, t in enumerate((0, traces - 1)):
            note = jnp.where(lane == angles, prior_ref[r : r + 1, t : t + 1], 0.0)
            for a in range(angles):
                note = jnp.where(lane == a, valid_ref[a, r : r + 1, t : t + 1].astype(F32), note)
            at = contrasts * rows + r
            second_ref[side, at : at + 1, 0:LANES] = note
            at = r + side * (traces - rows)
            note_ref[at : at + 1, :] = note
    for c in range(contrasts):
        left, right = own_ref[c, 0:half], own_ref[c, half:]
        pair_ref[c] = jnp.where(first_col, right, left)
        other_ref[c] = jnp.where(first_col, left, right)
    for i in range(2):
        left, right = (second_ref[side, i * half : (i + 1) * half] for side in (0, 1))
        pair_ref[contrasts + i] = jnp.where(first_col, right, left)
        other_ref[contrasts + i] = jnp.where(first_col, left, right)


def inner_kernel(
    count, strength_hbm, b_ref, near_ref, near_next_ref, padded_ref, valid_ref, avo_ref, prior_ref,
    v_ref, data_ref, halo_ref, ahead_ref, back_ref, norm_ref, strength_ref, sem,
):
    contrasts, rows, traces, samples = b_ref.shape
    angles, n = avo_ref.shape[1], samples // LANES
    (copy,) = copy_in(((strength_hbm, strength_ref),), sem)
    turned = turn(padded_ref[...], count)
    bands = []
    for a in range(angles):
        bands.append((band(turned[a : a + 1]), band(padded_ref[a : a + 1, :])))
        ahead_ref[a], back_ref[a] = (half.astype(F32) for half in bands[a])
    masks = [trace_columns(valid_ref, a) for a in range(angles)]
    weights = [column(prior_ref[r : r + 1, :]) + 4.0 for r in range(rows)]
    above, below = either_side(near_ref, near_next_ref, contrasts * n)
    wide = [
        jnp.concatenate([above[:, a : a + 1], mask, below[:, a : a + 1]], axis=0)
        for a, mask in enumerate(masks)
    ]
    weights = [above[:, angles : angles + 1] + 4.0, *weights, below[:, angles : angles + 1] + 4.0]
    field = []
    for c, line in enumerate(stack_tiles(b_ref)):
        ends = [either_side(near_ref, near_next_ref, c * n + k) for k in range(n)]
        field.append(
            [jnp.concatenate([up, own, low], axis=0) for (up, low), own in zip(ends, line)]
        )
    total = normal(field, wide, avo_ref, bands)
    copy.wait()
    has_above, has_below = inside("inline")
    for c in range(contrasts):
        strength = strength_ref[:, c : c + 1]
        whole, data = jnp.concatenate(field[c], axis=1), jnp.concatenate(total[c], axis=1)
        lines = [whole[r * traces : (r + 1) * traces] for r in range(rows + 2)]
        for r, here in enumerate(lines):
            north = lines[r - 1] if r else None
            south = lines[r + 1] if r < rows + 1 else None
            if r == 0:
                south = has_above * south
            if r == rows + 1:
                north = has_below * north
            around = lateral(here, north, south, None, None)
            image = data[r * traces : (r + 1) * traces] + strength * (weights[r] * here - around)
            if 0 < r <= rows:
                v_ref[c, r - 1] = image
            else:
                halo_ref[min(r, 1), c] = image
    store_tiles(data_ref, normal(stack_tiles(v_ref), masks, avo_ref, bands))
    norm_ref[...] = functools.reduce(
        jnp.add, [lane_tiles(b_ref[c, r] * b_ref[c, r]) for c in range(contrasts) for r in range(rows)]
    )


def lane_tiles(product):
    tiles = [product[:, k : k + LANES] for k in range(0, product.shape[1], LANES)]
    return functools.reduce(jnp.add, tiles)


def halo_kernel(halo_ref, far_next_ref, far_ref, strength_ref, out_ref):
    contrasts, samples = halo_ref.shape[1], halo_ref.shape[3]
    for c in range(contrasts):
        for i, line in enumerate(row_pair(far_ref, far_next_ref, c, samples // LANES)):
            out_ref[i, c] = halo_ref[i, c] - strength_ref[:, c : c + 1] * line


def image_kernel(
    b_ref, v_ref, data_ref, halo_ref, norm_ref, own_ref, note_ref, other_ref, pair_ref,
    avo_ref, prior_ref, strength_ref, ahead_ref, back_ref,
    one_ref, two_ref, gram_ref,
):
    contrasts, rows, traces, samples = b_ref.shape
    angles, n = avo_ref.shape[1], samples // LANES
    has_left, has_right = inside("col")
    first_col = starts_pair("col")
    place = lax.broadcasted_iota(jnp.int32, (traces, samples), 0)
    west, east = place == 0, place == traces - 1
    half = traces // 2

    def turned(value, k):
        return pltpu.roll(value, k % traces, 0) if k % traces else value

    def sides(i):
        pair, other = pair_ref[i], other_ref[i]
        left, right = jnp.where(first_col, other, pair), jnp.where(first_col, pair, other)
        return jnp.concatenate([left, right], axis=0)

    def at_ends(value, left, right, inner):
        return jnp.where(west, turned(value, left), jnp.where(east, turned(value, right), inner))

    beside = [sides(c) for c in range(contrasts)]
    seconds = [sides(contrasts), sides(contrasts + 1)]
    notes = seconds[1][:, :LANES]
    line = place[:, :LANES]
    theirs = turned(notes, -rows)
    mixed = jnp.where((line == 2) | (line == 3), notes, note_ref[...])
    mixed = jnp.where((line == 4) | (line == 5), theirs, mixed)
    masks = [mixed[:, a : a + 1] for a in range(angles)]
    mine = (place[:, :1] < 2) | (place[:, :1] >= traces - 2)
    tile = []
    for c in range(contrasts):
        scale = jnp.where(mine, -strength_ref[:, c : c + 1], 1.0)
        whole = jnp.where(place % half < rows, beside[c], turned(beside[c], rows)) * scale
        tile.append([whole[:, k * LANES : (k + 1) * LANES] for k in range(n)])
    bands = [(ahead_ref[a].astype(BF16), back_ref[a].astype(BF16)) for a in range(angles)]
    edge = [jnp.concatenate(tiles, axis=1) for tiles in normal(tile, masks, avo_ref, bands)]

    has = jnp.where(place[:, :1] < half, has_left, has_right)
    far_weight = theirs[:, angles : angles + 1] + 4.0
    weights = [column(prior_ref[r : r + 1, :]) + 4.0 for r in range(rows)]
    sums = [norm_ref[...], *[jnp.zeros((traces, LANES), F32) for _ in range(3)]]
    for c in range(contrasts):
        strength = strength_ref[:, c : c + 1]
        theirs = beside[c]
        around = turned(seconds[c // 2], -rows * (c % 2)) + turned(theirs, -rows)
        around = around + jnp.where(place % 2 == 1, turned(theirs, 1), turned(theirs, -1))
        prior = far_weight * theirs - (around + has * own_ref[c])
        beyond = jnp.where(place < half, turned(edge[c], -rows), edge[c]) + strength * prior

        lines = [halo_ref[0, c], *[v_ref[c, r] for r in range(rows)], halo_ref[1, c]]
        lines = [
            here - strength * at_ends(theirs, -k, half - 1 - k, 0.0)
            for here, k in zip(lines, (rows, *range(rows), rows + 1))
        ]
        for r in range(rows):
            here, b = lines[r + 1], b_ref[c, r]
            ends = jnp.where(west, turned(beyond, -r), turned(beyond, half - 1 - r))
            around = jnp.where(west, ends, turned(here, 1)) + jnp.where(east, ends, turned(here, -1))
            around = around + lines[r] + lines[r + 2]
            mend = at_ends(edge[c], -r, 1 - r, 0.0)
            two = data_ref[c, r] + mend + strength * (weights[r] * here - around)
            one_ref[c, r] = here
            two_ref[c, r] = two
            for q, product in enumerate((b * here, here * here, here * two), 1):
                sums[q] = sums[q] + lane_tiles(product)
    lane = lax.broadcasted_iota(jnp.int32, (1, LANES), 1)
    packed = jnp.zeros((1, LANES), F32)
    for q, total in enumerate(sums):
        total = jnp.sum(jnp.sum(total, axis=0, keepdims=True), axis=1, keepdims=True)
        packed = jnp.where(lane == q, total, packed)
    gram_ref[...] = jnp.broadcast_to(packed[None], gram_ref.shape)


def finish_kernel(
    gram_ref, b_ref, one_ref, two_ref, solution_hbm, residual_hbm, solution_ref, residual_ref, sems
):
    sums = jnp.sum(gram_ref[...], axis=0)
    g00, g01, g11, g12 = (sums[:, q : q + 1] for q in range(4))
    first = g00 / g01
    ratio = first * g11 / g01
    second = (ratio - 1.0) * g01 / (first * g12 - ratio * g11)
    near = first + second * ratio
    far = first * second
    blocks = [(c, r) for c in range(b_ref.shape[0]) for r in range(b_ref.shape[1])]
    for block in blocks:
        solution_ref[block] = near * b_ref[block] - far * one_ref[block]
    done = pltpu.make_async_copy(solution_ref, solution_hbm, sems.at[0])
    done.start()
    for block in blocks:
        residual_ref[block] = b_ref[block] - near * one_ref[block] + far * two_ref[block]
    last = pltpu.make_async_copy(residual_ref, residual_hbm, sems.at[1])
    last.start()
    done.wait()
    last.wait()


VMEM = pl.BlockSpec(memory_space=pltpu.VMEM)
HBM = pl.BlockSpec(memory_space=pltpu.HBM)


def call(kernel, outs, ins, flops, scratch=(), places=None, to=VMEM):
    moved = sum(x.size * x.dtype.itemsize for x in (*ins, *outs))
    return pl.pallas_call(
        kernel,
        out_shape=outs,
        in_specs=[VMEM] * len(ins) if places is None else places,
        out_specs=jax.tree.map(lambda _: to, outs),
        scratch_shapes=list(scratch),
        compiler_params=pltpu.CompilerParams(vmem_limit_bytes=24 * 1024 * 1024),
        cost_estimate=pl.CostEstimate(flops=flops, bytes_accessed=moved, transcendentals=0),
        name=getattr(kernel, "func", kernel).__name__,
    )(*ins)


def swap(axis, value, first):
    starts = range(first, lax.axis_size(axis) - 1, 2)
    return lax.ppermute(value, axis, [(i + d, i + 1 - d) for i in starts for d in (0, 1)])


def hand_on(axis, value):
    size = lax.axis_size(axis)
    steps = [(i, i + 2 - 4 * (i % 2)) for i in range(size)]
    return lax.ppermute(value, axis, [(i, j) for i, j in steps if 0 <= j < size])


def shards(seismic, validity, prior_weight, lateral_strength, avo_coeffs, wavelets):
    angles, rows, traces, samples = seismic.shape
    contrasts = avo_coeffs.shape[1]
    avo_coeffs = jnp.swapaxes(avo_coeffs, 0, 1)
    shape = lambda *dims: jax.ShapeDtypeStruct(dims, F32)
    field = shape(contrasts, rows, traces, samples)
    side = shape(contrasts + 2, rows + 2, samples)
    lines = shape(8, 2 * LANES)
    work = 2 * angles * rows * traces * samples * 256 * 4

    given = (seismic, validity, avo_coeffs, wavelets, prior_weight)
    kept = [given[i] for i in (1, 2, 4)]
    edge = shape(contrasts * samples // LANES + 1, traces, LANES)
    b, near, far, padded, *kept = call(
        start_kernel,
        (
            field, edge, edge, lines,
            *[jax.ShapeDtypeStruct(x.shape, x.dtype) for x in kept],
        ),
        [pltpu.with_memory_space_constraint(x, pltpu.HBM) for x in given],
        work,
        [
            pltpu.VMEM(seismic.shape, seismic.dtype),
            pltpu.VMEM(wavelets.shape, F32),
            pltpu.SemaphoreType.DMA((angles + 4,)),
        ],
        [HBM] * 5,
    )
    near = swap("inline", near, 0)
    near_next = swap("inline", far, 1)
    far_next = hand_on("inline", near)
    far = swap("inline", far, 0)
    col_pair, col_other, own, note = call(
        column_kernel,
        (side, side, shape(contrasts, 2 * rows + 4, samples), shape(traces, LANES)),
        (b, near, near_next, kept[0], kept[2]),
        2 * field.size,
        [pltpu.VMEM((2, 2 * rows + 4, samples), F32)],
    )
    col_other = swap("col", col_other, 1)
    col_pair = swap("col", col_pair, 0)
    bands = shape(angles, 2 * LANES, 2 * LANES)
    halo = shape(2, contrasts, traces, samples)
    strength = lateral_strength.reshape(1, -1)
    image, data, part, ahead, back, norm, strength = call(
        functools.partial(inner_kernel, wavelets.shape[1]),
        (field, field, halo, bands, bands, shape(traces, LANES), shape(*strength.shape)),
        (
            pltpu.with_memory_space_constraint(strength, pltpu.HBM),
            b, near, near_next, padded, *kept,
        ),
        6 * work,
        [pltpu.SemaphoreType.DMA((1,))],
        [HBM] + [VMEM] * 7,
    )
    (halo,) = call(halo_kernel, (halo,), (part, far_next, far, strength), field.size)
    axes = ("inline", "col")
    one, two, gram = call(
        image_kernel,
        (field, field, shape(lax.axis_size(axes), 1, LANES)),
        (
            b, image, data, halo, norm, own, note, col_other, col_pair,
            *kept[1:], strength, ahead, back,
        ),
        work,
    )
    gram = lax.all_to_all(gram, axes, 0, 0)
    work = 8 * field.size
    room = [pltpu.VMEM(field.shape, F32)] * 2 + [pltpu.SemaphoreType.DMA((2,))]
    return tuple(
        call(finish_kernel, (field, field), (gram, b, one, two), work, room, to=HBM)
    )


def solution(mesh):
    placed = (
        P(None, "inline", "col", None),
        P(None, "inline", "col"),
        P("inline", "col"),
        P(),
        P(),
        P(),
    )
    return jax.shard_map(
        shards,
        mesh=mesh,
        in_specs=placed,
        out_specs=(P(None, "inline", "col", None), P(None, "inline", "col", None)),
        check_vma=False,
    )
```

```python
import functools

import jax
import jax.numpy as jnp
from jax import lax
from jax.experimental import pallas as pl
from jax.experimental.pallas import tpu as pltpu
from jax.sharding import PartitionSpec as P

LANES = 128
F32 = jnp.float32
BF16 = jnp.bfloat16


def split(value):
    high = value.astype(BF16)
    return high, (value - high.astype(F32)).astype(BF16)


def pad_taps(taps_ref, padded_ref):
    padded_ref[...] = jnp.zeros_like(padded_ref)
    padded_ref[0 : taps_ref.shape[0], 0 : taps_ref.shape[1]] = taps_ref[...]


def turn(lines, count):
    n, size = lines.shape
    parts = []
    for _ in range(3):
        parts.append(lines.astype(BF16).astype(F32))
        lines = lines - parts[-1]
    rows = lax.broadcasted_iota(jnp.int32, (size, size), 0)
    cols = lax.broadcasted_iota(jnp.int32, (size, size), 1)
    flip = jnp.where(rows + cols == count - 1, 1.0, 0.0).astype(BF16)
    whole = jnp.concatenate(parts, axis=0).astype(BF16)
    turned = jnp.dot(whole, flip, preferred_element_type=F32)
    return turned[:n] + turned[n : 2 * n] + turned[2 * n :]


def band(line):
    lines = jnp.broadcast_to(line, (LANES, line.shape[1]))
    return jnp.concatenate(split(pltpu.roll(lines, 0, 1, stride=1, stride_axis=0)), axis=0)


def convolve(rows, bands):
    rows = rows.astype(BF16)
    out = lax.dot_general(rows, bands, (((1,), (1,)), ((), ())), preferred_element_type=F32)
    return out[:, :LANES] + out[:, LANES:]


def column(row):
    n = row.shape[1]
    same = lax.broadcasted_iota(jnp.int32, (n, n), 0) == lax.broadcasted_iota(jnp.int32, (n, n), 1)
    return jnp.sum(jnp.where(same, jnp.broadcast_to(row, (n, n)), 0.0), axis=1, keepdims=True)


def trace_columns(ref, *lead):
    rows = ref[lead].astype(F32)
    return jnp.concatenate([column(rows[r : r + 1, :]) for r in range(rows.shape[0])], axis=0)


def halves(value):
    if value.shape[0] % 16 == 0:
        return split(value)
    high = value.astype(BF16).astype(F32)
    return high, value - high


def windows(tiles):
    pairs = [jnp.concatenate(pair, axis=1) for pair in zip(tiles[:-1], tiles[1:])]
    return jnp.concatenate(pairs, axis=0)


def forward(tiles, bands):
    highs, lows = zip(*[halves(t) for t in tiles])
    zero = jnp.zeros_like(highs[0])
    n, size = len(tiles) + 1, tiles[0].shape[0]
    rows = [windows([zero, *part, zero]) for part in (highs, lows)]
    out = convolve(jnp.concatenate(rows, axis=0), bands)
    out = out[: n * size] + out[n * size :]
    return [out[k * size : (k + 1) * size] for k in range(n)]


def backward(parts, bands):
    n, size = len(parts[0]) - 1, parts[0][0].shape[0]
    rows = jnp.concatenate([windows(part) for part in parts], axis=0)
    out = convolve(rows, bands)
    total = out[: n * size]
    for p in range(1, len(parts)):
        total = total + out[p * n * size : (p + 1) * n * size]
    return [total[k * size : (k + 1) * size] for k in range(n)]


def coeff(avo_ref, angle, contrast, k):
    return avo_ref[contrast, angle : angle + 1, pl.ds(k * LANES, LANES)]


def add_terms(total, avo_ref, angle, result):
    for c, line in enumerate(total):
        for k, tile in enumerate(result):
            term = coeff(avo_ref, angle, c, k) * tile
            line[k] = term if angle == 0 else line[k] + term


def store_tiles(out_ref, tiles):
    size = out_ref.shape[2]
    for c in range(out_ref.shape[0]):
        for k, tile in enumerate(tiles[c]):
            for r in range(out_ref.shape[1]):
                out_ref[c, r, :, pl.ds(k * LANES, LANES)] = tile[r * size : (r + 1) * size]


def right_side(seis_ref, masks, avo_ref, bands):
    angles, rows, _, samples = seis_ref.shape
    n = samples // LANES
    total = [[None] * n for _ in range(avo_ref.shape[0])]
    for a in range(angles):
        data = jnp.concatenate([seis_ref[a, r].astype(F32) for r in range(rows)], axis=0)
        data = data * masks[a]
        turned = [
            pltpu.roll(data[:, k * LANES : (k + 1) * LANES], LANES // 2, 1) for k in range(n)
        ]
        zero = jnp.zeros_like(turned[0])
        left_half = lax.broadcasted_iota(jnp.int32, zero.shape, 1) < LANES // 2
        shifted = [
            jnp.where(left_half, before, here).astype(BF16)
            for before, here in zip([zero, *turned], [*turned, zero])
        ]
        add_terms(total, avo_ref, a, backward([shifted], bands[a]))
    return total


def normal(field, masks, avo_ref, bands):
    contrasts, n = len(field), len(field[0])
    total = [[None] * n for _ in range(contrasts)]
    for a, (ahead, back) in enumerate(bands):
        mixed = []
        for k in range(n):
            parts = [coeff(avo_ref, a, c, k) * field[c][k] for c in range(contrasts)]
            mixed.append(functools.reduce(jnp.add, parts))
        synth = [tile * masks[a] for tile in forward(mixed, ahead)]
        left_half = lax.broadcasted_iota(jnp.int32, synth[0].shape, 1) < LANES // 2
        synth[0] = jnp.where(left_half, 0.0, synth[0])
        synth[n] = jnp.where(left_half, synth[n], 0.0)
        result = backward(list(zip(*[halves(t) for t in synth])), back)
        add_terms(total, avo_ref, a, result)
    return total


def lateral(here, north, south, west, east):
    traces = here.shape[0]
    place = lax.broadcasted_iota(jnp.int32, here.shape, 0)
    from_west = jnp.where(place == 0, 0.0 if west is None else west, pltpu.roll(here, 1, 0))
    from_east = jnp.where(
        place == traces - 1, 0.0 if east is None else east, pltpu.roll(here, traces - 1, 0)
    )
    around = from_west + from_east
    for other in (north, south):
        around = around if other is None else around + other
    return around


def copy_in(pairs, sems):
    copies = [pltpu.make_async_copy(a, b, sems.at[i]) for i, (a, b) in enumerate(pairs)]
    for copy in copies:
        copy.start()
    return copies


def start_kernel(
    seis_hbm, valid_hbm, avo_hbm, taps_hbm, prior_hbm,
    b_ref, near_ref, far_ref, padded_ref, valid_ref, avo_ref, prior_ref,
    seis_ref, taps_ref, sems,
):
    angles = avo_ref.shape[1]
    taps, valid, *rest = copy_in(
        (
            (taps_hbm, taps_ref),
            (valid_hbm, valid_ref),
            *((seis_hbm.at[a], seis_ref.at[a]) for a in range(angles)),
            (avo_hbm, avo_ref),
            (prior_hbm, prior_ref),
        ),
        sems,
    )
    taps.wait()
    pad_taps(taps_ref, padded_ref)
    bands = [band(padded_ref[a : a + 1, :]) for a in range(angles)]
    valid.wait()
    masks = [trace_columns(valid_ref, a) for a in range(angles)]
    for copy in rest:
        copy.wait()
    store_tiles(b_ref, right_side(seis_ref, masks, avo_ref, bands))
    contrasts, rows, traces, samples = b_ref.shape
    n = samples // LANES
    first = starts_pair("inline")
    lane = lax.broadcasted_iota(jnp.int32, (traces, LANES), 1)
    notes = []
    for r in (0, rows - 1):
        note = jnp.where(lane == angles, column(prior_ref[r : r + 1, :]), 0.0)
        for a in range(angles):
            note = jnp.where(lane == a, masks[a][r * traces : (r + 1) * traces], note)
        notes.append(note)

    @pl.loop(0, contrasts)
    def _(c):
        for k in range(n):
            top, bottom = (b_ref[c, r, :, pl.ds(k * LANES, LANES)] for r in (0, rows - 1))
            near_ref[c * n + k] = jnp.where(first, bottom, top)
            far_ref[c * n + k] = jnp.where(first, top, bottom)

    near_ref[contrasts * n] = jnp.where(first, notes[1], notes[0])
    far_ref[contrasts * n] = jnp.where(first, notes[0], notes[1])


def either_side(pair_ref, next_ref, *where):
    first = starts_pair("inline")
    pair, other = pair_ref[where], next_ref[where]
    return jnp.where(first, other, pair), jnp.where(first, pair, other)


def stack_tiles(ref):
    contrasts, rows, _, samples = ref.shape
    return [
        [
            jnp.concatenate([ref[c, r, :, pl.ds(k, LANES)] for r in range(rows)], axis=0)
            for k in range(0, samples, LANES)
        ]
        for c in range(contrasts)
    ]


def inside(axis):
    place = lax.axis_index(axis)
    last = lax.axis_size(axis) - 1
    return (place > 0).astype(F32), (place < last).astype(F32)


def starts_pair(axis):
    return lax.axis_index(axis) % 2 == 0


def row_pair(near_ref, next_ref, c, n):
    tiles = [either_side(near_ref, next_ref, c * n + k) for k in range(n)]
    return [jnp.concatenate(side, axis=1) for side in zip(*tiles)]


def column_kernel(
    b_ref, near_ref, near_next_ref, valid_ref, prior_ref,
    pair_ref, other_ref, own_ref, note_ref, second_ref,
):
    contrasts, rows, traces, samples = b_ref.shape
    angles = valid_ref.shape[0]
    first_col = starts_pair("col")
    half = rows + 2
    second_ref[...] = jnp.zeros_like(second_ref)
    note_ref[...] = jnp.zeros_like(note_ref)
    for c in range(contrasts):
        own = [b_ref[c, r] for r in range(rows)]
        for i, line in enumerate([*own, *row_pair(near_ref, near_next_ref, c, samples // LANES)]):
            own_ref[c, i : i + 1, :] = line[0:1]
            own_ref[c, half + i : half + i + 1, :] = line[traces - 1 :]
        for r, line in enumerate(own):
            at = c * rows + r
            second_ref[0, at : at + 1, :] = line[1:2]
            second_ref[1, at : at + 1, :] = line[traces - 2 : traces - 1]
    lane = lax.broadcasted_iota(jnp.int32, (1, LANES), 1)
    for r in range(rows):
        for side, t in enumerate((0, traces - 1)):
            note = jnp.where(lane == angles, prior_ref[r : r + 1, t : t + 1], 0.0)
            for a in range(angles):
                note = jnp.where(lane == a, valid_ref[a, r : r + 1, t : t + 1].astype(F32), note)
            at = contrasts * rows + r
            second_ref[side, at : at + 1, 0:LANES] = note
            at = r + side * (traces - rows)
            note_ref[at : at + 1, :] = note
    for c in range(contrasts):
        left, right = own_ref[c, 0:half], own_ref[c, half:]
        pair_ref[c] = jnp.where(first_col, right, left)
        other_ref[c] = jnp.where(first_col, left, right)
    for i in range(2):
        left, right = (second_ref[side, i * half : (i + 1) * half] for side in (0, 1))
        pair_ref[contrasts + i] = jnp.where(first_col, right, left)
        other_ref[contrasts + i] = jnp.where(first_col, left, right)


def inner_kernel(
    count, strength_hbm, b_ref, near_ref, near_next_ref, padded_ref, valid_ref, avo_ref, prior_ref,
    v_ref, data_ref, halo_ref, ahead_ref, back_ref, norm_ref, strength_ref, sem,
):
    contrasts, rows, traces, samples = b_ref.shape
    angles, n = avo_ref.shape[1], samples // LANES
    (copy,) = copy_in(((strength_hbm, strength_ref),), sem)
    turned = turn(padded_ref[...], count)
    bands = []
    for a in range(angles):
        bands.append((band(turned[a : a + 1]), band(padded_ref[a : a + 1, :])))
        ahead_ref[a], back_ref[a] = (half.astype(F32) for half in bands[a])
    masks = [trace_columns(valid_ref, a) for a in range(angles)]
    weights = [column(prior_ref[r : r + 1, :]) + 4.0 for r in range(rows)]
    above, below = either_side(near_ref, near_next_ref, contrasts * n)
    wide = [
        jnp.concatenate([above[:, a : a + 1], mask, below[:, a : a + 1]], axis=0)
        for a, mask in enumerate(masks)
    ]
    weights = [above[:, angles : angles + 1] + 4.0, *weights, below[:, angles : angles + 1] + 4.0]
    field = []
    for c, line in enumerate(stack_tiles(b_ref)):
        ends = [either_side(near_ref, near_next_ref, c * n + k) for k in range(n)]
        field.append(
            [jnp.concatenate([up, own, low], axis=0) for (up, low), own in zip(ends, line)]
        )
    total = normal(field, wide, avo_ref, bands)
    copy.wait()
    has_above, has_below = inside("inline")
    for c in range(contrasts):
        strength = strength_ref[:, c : c + 1]
        whole, data = jnp.concatenate(field[c], axis=1), jnp.concatenate(total[c], axis=1)
        lines = [whole[r * traces : (r + 1) * traces] for r in range(rows + 2)]
        for r, here in enumerate(lines):
            north = lines[r - 1] if r else None
            south = lines[r + 1] if r < rows + 1 else None
            if r == 0:
                south = has_above * south
            if r == rows + 1:
                north = has_below * north
            around = lateral(here, north, south, None, None)
            image = data[r * traces : (r + 1) * traces] + strength * (weights[r] * here - around)
            if 0 < r <= rows:
                v_ref[c, r - 1] = image
            else:
                halo_ref[min(r, 1), c] = image
    store_tiles(data_ref, normal(stack_tiles(v_ref), masks, avo_ref, bands))
    norm_ref[...] = functools.reduce(
        jnp.add, [lane_tiles(b_ref[c, r] * b_ref[c, r]) for c in range(contrasts) for r in range(rows)]
    )


def lane_tiles(product):
    tiles = [product[:, k : k + LANES] for k in range(0, product.shape[1], LANES)]
    return functools.reduce(jnp.add, tiles)


def halo_kernel(halo_ref, far_next_ref, far_ref, strength_ref, out_ref):
    contrasts, samples = halo_ref.shape[1], halo_ref.shape[3]
    for c in range(contrasts):
        for i, line in enumerate(row_pair(far_ref, far_next_ref, c, samples // LANES)):
            out_ref[i, c] = halo_ref[i, c] - strength_ref[:, c : c + 1] * line


def image_kernel(
    b_ref, v_ref, data_ref, halo_ref, norm_ref, own_ref, note_ref, other_ref, pair_ref,
    avo_ref, prior_ref, strength_ref, ahead_ref, back_ref,
    one_ref, two_ref, gram_ref,
):
    contrasts, rows, traces, samples = b_ref.shape
    angles, n = avo_ref.shape[1], samples // LANES
    has_left, has_right = inside("col")
    first_col = starts_pair("col")
    place = lax.broadcasted_iota(jnp.int32, (traces, samples), 0)
    west, east = place == 0, place == traces - 1
    half = traces // 2

    def turned(value, k):
        return pltpu.roll(value, k % traces, 0) if k % traces else value

    def sides(i):
        pair, other = pair_ref[i], other_ref[i]
        left, right = jnp.where(first_col, other, pair), jnp.where(first_col, pair, other)
        return jnp.concatenate([left, right], axis=0)

    def at_ends(value, left, right, inner):
        return jnp.where(west, turned(value, left), jnp.where(east, turned(value, right), inner))

    beside = [sides(c) for c in range(contrasts)]
    seconds = [sides(contrasts), sides(contrasts + 1)]
    notes = seconds[1][:, :LANES]
    line = place[:, :LANES]
    theirs = turned(notes, -rows)
    mixed = jnp.where((line == 2) | (line == 3), notes, note_ref[...])
    mixed = jnp.where((line == 4) | (line == 5), theirs, mixed)
    masks = [mixed[:, a : a + 1] for a in range(angles)]
    mine = (place[:, :1] < 2) | (place[:, :1] >= traces - 2)
    tile = []
    for c in range(contrasts):
        scale = jnp.where(mine, -strength_ref[:, c : c + 1], 1.0)
        whole = jnp.where(place % half < rows, beside[c], turned(beside[c], rows)) * scale
        tile.append([whole[:, k * LANES : (k + 1) * LANES] for k in range(n)])
    bands = [(ahead_ref[a].astype(BF16), back_ref[a].astype(BF16)) for a in range(angles)]
    edge = [jnp.concatenate(tiles, axis=1) for tiles in normal(tile, masks, avo_ref, bands)]

    has = jnp.where(place[:, :1] < half, has_left, has_right)
    far_weight = theirs[:, angles : angles + 1] + 4.0
    weights = [column(prior_ref[r : r + 1, :]) + 4.0 for r in range(rows)]
    sums = [norm_ref[...], *[jnp.zeros((traces, LANES), F32) for _ in range(3)]]
    for c in range(contrasts):
        strength = strength_ref[:, c : c + 1]
        theirs = beside[c]
        around = turned(seconds[c // 2], -rows * (c % 2)) + turned(theirs, -rows)
        around = around + jnp.where(place % 2 == 1, turned(theirs, 1), turned(theirs, -1))
        prior = far_weight * theirs - (around + has * own_ref[c])
        beyond = jnp.where(place < half, turned(edge[c], -rows), edge[c]) + strength * prior

        lines = [halo_ref[0, c], *[v_ref[c, r] for r in range(rows)], halo_ref[1, c]]
        lines = [
            here - strength * at_ends(theirs, -k, half - 1 - k, 0.0)
            for here, k in zip(lines, (rows, *range(rows), rows + 1))
        ]
        for r in range(rows):
            here, b = lines[r + 1], b_ref[c, r]
            ends = jnp.where(west, turned(beyond, -r), turned(beyond, half - 1 - r))
            around = jnp.where(west, ends, turned(here, 1)) + jnp.where(east, ends, turned(here, -1))
            around = around + lines[r] + lines[r + 2]
            mend = at_ends(edge[c], -r, 1 - r, 0.0)
            two = data_ref[c, r] + mend + strength * (weights[r] * here - around)
            one_ref[c, r] = here
            two_ref[c, r] = two
            for q, product in enumerate((b * here, here * here, here * two), 1):
                sums[q] = sums[q] + lane_tiles(product)
    lane = lax.broadcasted_iota(jnp.int32, (1, LANES), 1)
    packed = jnp.zeros((1, LANES), F32)
    for q, total in enumerate(sums):
        total = jnp.sum(jnp.sum(total, axis=0, keepdims=True), axis=1, keepdims=True)
        packed = jnp.where(lane == q, total, packed)
    gram_ref[...] = jnp.broadcast_to(packed[None], gram_ref.shape)


def finish_kernel(gram_ref, b_ref, one_ref, two_ref, solution_ref, residual_ref):
    sums = jnp.sum(gram_ref[...], axis=0)
    g00, g01, g11, g12 = (sums[:, q : q + 1] for q in range(4))
    first = g00 / g01
    ratio = first * g11 / g01
    second = (ratio - 1.0) * g01 / (first * g12 - ratio * g11)
    near = first + second * ratio
    far = first * second
    rows = b_ref.shape[1]

    @pl.loop(0, b_ref.shape[0] * rows)
    def _(i):
        block = (i // rows, i % rows)
        b, one, two = b_ref[block], one_ref[block], two_ref[block]
        solution_ref[block] = near * b - far * one
        residual_ref[block] = b - near * one + far * two


VMEM = pl.BlockSpec(memory_space=pltpu.VMEM)
HBM = pl.BlockSpec(memory_space=pltpu.HBM)


def call(kernel, outs, ins, flops, scratch=(), places=None):
    moved = sum(x.size * x.dtype.itemsize for x in (*ins, *outs))
    return pl.pallas_call(
        kernel,
        out_shape=outs,
        in_specs=[VMEM] * len(ins) if places is None else places,
        out_specs=jax.tree.map(lambda _: VMEM, outs),
        scratch_shapes=list(scratch),
        compiler_params=pltpu.CompilerParams(vmem_limit_bytes=24 * 1024 * 1024),
        cost_estimate=pl.CostEstimate(flops=flops, bytes_accessed=moved, transcendentals=0),
        name=getattr(kernel, "func", kernel).__name__,
    )(*ins)


def swap(axis, value, first):
    starts = range(first, lax.axis_size(axis) - 1, 2)
    return lax.ppermute(value, axis, [(i + d, i + 1 - d) for i in starts for d in (0, 1)])


def hand_on(axis, value):
    size = lax.axis_size(axis)
    steps = [(i, i + 2 - 4 * (i % 2)) for i in range(size)]
    return lax.ppermute(value, axis, [(i, j) for i, j in steps if 0 <= j < size])


def shards(seismic, validity, prior_weight, lateral_strength, avo_coeffs, wavelets):
    angles, rows, traces, samples = seismic.shape
    contrasts = avo_coeffs.shape[1]
    avo_coeffs = jnp.swapaxes(avo_coeffs, 0, 1)
    shape = lambda *dims: jax.ShapeDtypeStruct(dims, F32)
    field = shape(contrasts, rows, traces, samples)
    side = shape(contrasts + 2, rows + 2, samples)
    lines = shape(8, 2 * LANES)
    work = 2 * angles * rows * traces * samples * 256 * 4

    given = (seismic, validity, avo_coeffs, wavelets, prior_weight)
    kept = [given[i] for i in (1, 2, 4)]
    edge = shape(contrasts * samples // LANES + 1, traces, LANES)
    b, near, far, padded, *kept = call(
        start_kernel,
        (
            field, edge, edge, lines,
            *[jax.ShapeDtypeStruct(x.shape, x.dtype) for x in kept],
        ),
        [pltpu.with_memory_space_constraint(x, pltpu.HBM) for x in given],
        work,
        [
            pltpu.VMEM(seismic.shape, seismic.dtype),
            pltpu.VMEM(wavelets.shape, F32),
            pltpu.SemaphoreType.DMA((angles + 4,)),
        ],
        [HBM] * 5,
    )
    near = swap("inline", near, 0)
    near_next = swap("inline", far, 1)
    far_next = hand_on("inline", near)
    far = swap("inline", far, 0)
    col_pair, col_other, own, note = call(
        column_kernel,
        (side, side, shape(contrasts, 2 * rows + 4, samples), shape(traces, LANES)),
        (b, near, near_next, kept[0], kept[2]),
        2 * field.size,
        [pltpu.VMEM((2, 2 * rows + 4, samples), F32)],
    )
    col_other = swap("col", col_other, 1)
    col_pair = swap("col", col_pair, 0)
    bands = shape(angles, 2 * LANES, 2 * LANES)
    halo = shape(2, contrasts, traces, samples)
    strength = lateral_strength.reshape(1, -1)
    image, data, part, ahead, back, norm, strength = call(
        functools.partial(inner_kernel, wavelets.shape[1]),
        (field, field, halo, bands, bands, shape(traces, LANES), shape(*strength.shape)),
        (
            pltpu.with_memory_space_constraint(strength, pltpu.HBM),
            b, near, near_next, padded, *kept,
        ),
        6 * work,
        [pltpu.SemaphoreType.DMA((1,))],
        [HBM] + [VMEM] * 7,
    )
    (halo,) = call(halo_kernel, (halo,), (part, far_next, far, strength), field.size)
    axes = ("inline", "col")
    one, two, gram = call(
        image_kernel,
        (field, field, shape(lax.axis_size(axes), 1, LANES)),
        (
            b, image, data, halo, norm, own, note, col_other, col_pair,
            *kept[1:], strength, ahead, back,
        ),
        work,
    )
    gram = lax.all_to_all(gram, axes, 0, 0)
    return tuple(call(finish_kernel, (field, field), (gram, b, one, two), 8 * field.size))


def solution(mesh):
    placed = (
        P(None, "inline", "col", None),
        P(None, "inline", "col"),
        P("inline", "col"),
        P(),
        P(),
        P(),
    )
    return jax.shard_map(
        shards,
        mesh=mesh,
        in_specs=placed,
        out_specs=(P(None, "inline", "col", None), P(None, "inline", "col", None)),
        check_vma=False,
    )
```

```python
import functools

import jax
import jax.numpy as jnp
from jax import lax
from jax.experimental import pallas as pl
from jax.experimental.pallas import tpu as pltpu
from jax.sharding import PartitionSpec as P

LANES = 128
F32 = jnp.float32
BF16 = jnp.bfloat16


def split(value):
    high = value.astype(BF16)
    return high, (value - high.astype(F32)).astype(BF16)


def pad_taps(taps_ref, padded_ref):
    padded_ref[...] = jnp.zeros_like(padded_ref)
    padded_ref[0 : taps_ref.shape[0], 0 : taps_ref.shape[1]] = taps_ref[...]


def turn(lines, count):
    n, size = lines.shape
    parts = []
    for _ in range(3):
        parts.append(lines.astype(BF16).astype(F32))
        lines = lines - parts[-1]
    rows = lax.broadcasted_iota(jnp.int32, (size, size), 0)
    cols = lax.broadcasted_iota(jnp.int32, (size, size), 1)
    flip = jnp.where(rows + cols == count - 1, 1.0, 0.0).astype(BF16)
    whole = jnp.concatenate(parts, axis=0).astype(BF16)
    turned = jnp.dot(whole, flip, preferred_element_type=F32)
    return turned[:n] + turned[n : 2 * n] + turned[2 * n :]


def band(line):
    lines = jnp.broadcast_to(line, (LANES, line.shape[1]))
    return jnp.concatenate(split(pltpu.roll(lines, 0, 1, stride=1, stride_axis=0)), axis=0)


def convolve(rows, bands):
    rows = rows.astype(BF16)
    out = lax.dot_general(rows, bands, (((1,), (1,)), ((), ())), preferred_element_type=F32)
    return out[:, :LANES] + out[:, LANES:]


def column(row):
    n = row.shape[1]
    same = lax.broadcasted_iota(jnp.int32, (n, n), 0) == lax.broadcasted_iota(jnp.int32, (n, n), 1)
    return jnp.sum(jnp.where(same, jnp.broadcast_to(row, (n, n)), 0.0), axis=1, keepdims=True)


def trace_columns(ref, *lead):
    rows = ref[lead].astype(F32)
    return jnp.concatenate([column(rows[r : r + 1, :]) for r in range(rows.shape[0])], axis=0)


def thirds(value):
    kind = BF16 if value.shape[0] % 16 == 0 else F32
    parts = []
    for _ in range(3):
        high = value.astype(BF16)
        parts.append(high.astype(kind))
        value = value - high.astype(F32)
    return parts


def windows(tiles):
    pairs = [jnp.concatenate(pair, axis=1) for pair in zip(tiles[:-1], tiles[1:])]
    return jnp.concatenate(pairs, axis=0)


def forward(tiles, bands):
    parts = list(zip(*[thirds(t) for t in tiles]))
    zero = jnp.zeros_like(parts[0][0])
    n, size = len(tiles) + 1, tiles[0].shape[0]
    rows = [windows([zero, *part, zero]) for part in parts]
    out = convolve(jnp.concatenate(rows, axis=0), bands)
    out = out[: n * size] + (out[n * size : 2 * n * size] + out[2 * n * size :])
    return [out[k * size : (k + 1) * size] for k in range(n)]


def backward(parts, bands):
    n, size = len(parts[0]) - 1, parts[0][0].shape[0]
    rows = jnp.concatenate([windows(part) for part in parts], axis=0)
    out = convolve(rows, bands)
    total = out[: n * size]
    for p in range(1, len(parts)):
        total = total + out[p * n * size : (p + 1) * n * size]
    return [total[k * size : (k + 1) * size] for k in range(n)]


def coeff(avo_ref, angle, contrast, k):
    return avo_ref[contrast, angle : angle + 1, pl.ds(k * LANES, LANES)]


def add_terms(total, avo_ref, angle, result):
    for c, line in enumerate(total):
        for k, tile in enumerate(result):
            term = coeff(avo_ref, angle, c, k) * tile
            line[k] = term if angle == 0 else line[k] + term


def store_tiles(out_ref, tiles):
    size = out_ref.shape[2]
    for c in range(out_ref.shape[0]):
        for k, tile in enumerate(tiles[c]):
            for r in range(out_ref.shape[1]):
                out_ref[c, r, :, pl.ds(k * LANES, LANES)] = tile[r * size : (r + 1) * size]


def right_side(seis_ref, masks, avo_ref, bands):
    angles, rows, _, samples = seis_ref.shape
    n = samples // LANES
    total = [[None] * n for _ in range(avo_ref.shape[0])]
    for a in range(angles):
        data = jnp.concatenate([seis_ref[a, r].astype(F32) for r in range(rows)], axis=0)
        data = data * masks[a]
        turned = [
            pltpu.roll(data[:, k * LANES : (k + 1) * LANES], LANES // 2, 1) for k in range(n)
        ]
        zero = jnp.zeros_like(turned[0])
        left_half = lax.broadcasted_iota(jnp.int32, zero.shape, 1) < LANES // 2
        shifted = [
            jnp.where(left_half, before, here).astype(BF16)
            for before, here in zip([zero, *turned], [*turned, zero])
        ]
        add_terms(total, avo_ref, a, backward([shifted], bands[a]))
    return total


def normal(field, masks, avo_ref, bands):
    contrasts, n = len(field), len(field[0])
    total = [[None] * n for _ in range(contrasts)]
    for a, (ahead, back) in enumerate(bands):
        mixed = []
        for k in range(n):
            parts = [coeff(avo_ref, a, c, k) * field[c][k] for c in range(contrasts)]
            mixed.append(functools.reduce(jnp.add, parts))
        synth = [tile * masks[a] for tile in forward(mixed, ahead)]
        left_half = lax.broadcasted_iota(jnp.int32, synth[0].shape, 1) < LANES // 2
        synth[0] = jnp.where(left_half, 0.0, synth[0])
        synth[n] = jnp.where(left_half, synth[n], 0.0)
        result = backward(list(zip(*[thirds(t) for t in synth])), back)
        add_terms(total, avo_ref, a, result)
    return total


def lateral(here, north, south, west, east):
    traces = here.shape[0]
    place = lax.broadcasted_iota(jnp.int32, here.shape, 0)
    from_west = jnp.where(place == 0, 0.0 if west is None else west, pltpu.roll(here, 1, 0))
    from_east = jnp.where(
        place == traces - 1, 0.0 if east is None else east, pltpu.roll(here, traces - 1, 0)
    )
    around = from_west + from_east
    for other in (north, south):
        around = around if other is None else around + other
    return around


def copy_in(pairs, sems):
    copies = [pltpu.make_async_copy(a, b, sems.at[i]) for i, (a, b) in enumerate(pairs)]
    for copy in copies:
        copy.start()
    return copies


def start_kernel(
    seis_hbm, valid_hbm, avo_hbm, taps_hbm, prior_hbm,
    b_ref, near_ref, far_ref, padded_ref, valid_ref, avo_ref, prior_ref,
    seis_ref, taps_ref, sems,
):
    angles = avo_ref.shape[1]
    taps, valid, *rest = copy_in(
        (
            (taps_hbm, taps_ref),
            (valid_hbm, valid_ref),
            *((seis_hbm.at[a], seis_ref.at[a]) for a in range(angles)),
            (avo_hbm, avo_ref),
            (prior_hbm, prior_ref),
        ),
        sems,
    )
    taps.wait()
    pad_taps(taps_ref, padded_ref)
    bands = [band(padded_ref[a : a + 1, :]) for a in range(angles)]
    valid.wait()
    masks = [trace_columns(valid_ref, a) for a in range(angles)]
    for copy in rest:
        copy.wait()
    store_tiles(b_ref, right_side(seis_ref, masks, avo_ref, bands))
    contrasts, rows, traces, samples = b_ref.shape
    n = samples // LANES
    first = starts_pair("inline")
    lane = lax.broadcasted_iota(jnp.int32, (traces, LANES), 1)
    notes = []
    for r in (0, rows - 1):
        note = jnp.where(lane == angles, column(prior_ref[r : r + 1, :]), 0.0)
        for a in range(angles):
            note = jnp.where(lane == a, masks[a][r * traces : (r + 1) * traces], note)
        notes.append(note)
    edges = [
        [*[b_ref[c, r, :, pl.ds(k * LANES, LANES)] for c in range(contrasts) for k in range(n)], note]
        for r, note in zip((0, rows - 1), notes)
    ]
    for e, (top, bottom) in enumerate(zip(*edges)):
        near_ref[e] = jnp.where(first, bottom, top)
        far_ref[e] = jnp.where(first, top, bottom)


def either_side(pair_ref, next_ref, *where):
    first = starts_pair("inline")
    pair, other = pair_ref[where], next_ref[where]
    return jnp.where(first, other, pair), jnp.where(first, pair, other)


def stack_tiles(ref):
    contrasts, rows, _, samples = ref.shape
    return [
        [
            jnp.concatenate([ref[c, r, :, pl.ds(k, LANES)] for r in range(rows)], axis=0)
            for k in range(0, samples, LANES)
        ]
        for c in range(contrasts)
    ]


def inside(axis):
    place = lax.axis_index(axis)
    last = lax.axis_size(axis) - 1
    return (place > 0).astype(F32), (place < last).astype(F32)


def starts_pair(axis):
    return lax.axis_index(axis) % 2 == 0


def row_pair(near_ref, next_ref, c, n):
    tiles = [either_side(near_ref, next_ref, c * n + k) for k in range(n)]
    return [jnp.concatenate(side, axis=1) for side in zip(*tiles)]


def column_kernel(
    b_ref, near_ref, near_next_ref, valid_ref, prior_ref,
    pair_ref, other_ref, own_ref, note_ref, second_ref,
):
    contrasts, rows, traces, samples = b_ref.shape
    angles = valid_ref.shape[0]
    first_col = starts_pair("col")
    half = rows + 2
    second_ref[...] = jnp.zeros_like(second_ref)
    note_ref[...] = jnp.zeros_like(note_ref)
    for c in range(contrasts):
        own = [b_ref[c, r] for r in range(rows)]
        for i, line in enumerate([*own, *row_pair(near_ref, near_next_ref, c, samples // LANES)]):
            own_ref[c, i : i + 1, :] = line[0:1]
            own_ref[c, half + i : half + i + 1, :] = line[traces - 1 :]
        for r, line in enumerate(own):
            at = c * rows + r
            second_ref[0, at : at + 1, :] = line[1:2]
            second_ref[1, at : at + 1, :] = line[traces - 2 : traces - 1]
    lane = lax.broadcasted_iota(jnp.int32, (1, LANES), 1)
    for r in range(rows):
        for side, t in enumerate((0, traces - 1)):
            note = jnp.where(lane == angles, prior_ref[r : r + 1, t : t + 1], 0.0)
            for a in range(angles):
                note = jnp.where(lane == a, valid_ref[a, r : r + 1, t : t + 1].astype(F32), note)
            at = contrasts * rows + r
            second_ref[side, at : at + 1, 0:LANES] = note
            at = r + side * (traces - rows)
            note_ref[at : at + 1, :] = note
    for c in range(contrasts):
        left, right = own_ref[c, 0:half], own_ref[c, half:]
        pair_ref[c] = jnp.where(first_col, right, left)
        other_ref[c] = jnp.where(first_col, left, right)
    for i in range(2):
        left, right = (second_ref[side, i * half : (i + 1) * half] for side in (0, 1))
        pair_ref[contrasts + i] = jnp.where(first_col, right, left)
        other_ref[contrasts + i] = jnp.where(first_col, left, right)


def inner_kernel(
    count, strength_hbm, b_ref, near_ref, near_next_ref, padded_ref, valid_ref, avo_ref, prior_ref,
    v_ref, data_ref, halo_ref, ahead_ref, back_ref, norm_ref, strength_ref, sem,
):
    contrasts, rows, traces, samples = b_ref.shape
    angles, n = avo_ref.shape[1], samples // LANES
    (copy,) = copy_in(((strength_hbm, strength_ref),), sem)
    turned = turn(padded_ref[...], count)
    bands = []
    for a in range(angles):
        bands.append((band(turned[a : a + 1]), band(padded_ref[a : a + 1, :])))
        ahead_ref[a], back_ref[a] = (half.astype(F32) for half in bands[a])
    masks = [trace_columns(valid_ref, a) for a in range(angles)]
    weights = [column(prior_ref[r : r + 1, :]) + 4.0 for r in range(rows)]
    above, below = either_side(near_ref, near_next_ref, contrasts * n)
    wide = [
        jnp.concatenate([above[:, a : a + 1], mask, below[:, a : a + 1]], axis=0)
        for a, mask in enumerate(masks)
    ]
    weights = [above[:, angles : angles + 1] + 4.0, *weights, below[:, angles : angles + 1] + 4.0]
    field = []
    for c, line in enumerate(stack_tiles(b_ref)):
        ends = [either_side(near_ref, near_next_ref, c * n + k) for k in range(n)]
        field.append(
            [jnp.concatenate([up, own, low], axis=0) for (up, low), own in zip(ends, line)]
        )
    total = normal(field, wide, avo_ref, bands)
    copy.wait()
    has_above, has_below = inside("inline")
    for c in range(contrasts):
        strength = strength_ref[:, c : c + 1]
        whole, data = jnp.concatenate(field[c], axis=1), jnp.concatenate(total[c], axis=1)
        lines = [whole[r * traces : (r + 1) * traces] for r in range(rows + 2)]
        for r, here in enumerate(lines):
            north = lines[r - 1] if r else None
            south = lines[r + 1] if r < rows + 1 else None
            if r == 0:
                south = has_above * south
            if r == rows + 1:
                north = has_below * north
            around = lateral(here, north, south, None, None)
            image = data[r * traces : (r + 1) * traces] + strength * (weights[r] * here - around)
            if 0 < r <= rows:
                v_ref[c, r - 1] = image
            else:
                halo_ref[min(r, 1), c] = image
    store_tiles(data_ref, normal(stack_tiles(v_ref), masks, avo_ref, bands))
    norm_ref[...] = functools.reduce(
        jnp.add, [lane_tiles(b_ref[c, r] * b_ref[c, r]) for c in range(contrasts) for r in range(rows)]
    )


def lane_tiles(product):
    tiles = [product[:, k : k + LANES] for k in range(0, product.shape[1], LANES)]
    return functools.reduce(jnp.add, tiles)


def halo_kernel(halo_ref, far_next_ref, far_ref, strength_ref, out_ref):
    contrasts, samples = halo_ref.shape[1], halo_ref.shape[3]
    for c in range(contrasts):
        for i, line in enumerate(row_pair(far_ref, far_next_ref, c, samples // LANES)):
            out_ref[i, c] = halo_ref[i, c] - strength_ref[:, c : c + 1] * line


def image_kernel(
    b_ref, v_ref, data_ref, halo_ref, norm_ref, own_ref, note_ref, other_ref, pair_ref,
    avo_ref, prior_ref, strength_ref, ahead_ref, back_ref,
    one_ref, two_ref, gram_ref,
):
    contrasts, rows, traces, samples = b_ref.shape
    angles, n = avo_ref.shape[1], samples // LANES
    has_left, has_right = inside("col")
    first_col = starts_pair("col")
    place = lax.broadcasted_iota(jnp.int32, (traces, samples), 0)
    west, east = place == 0, place == traces - 1
    half = traces // 2

    def turned(value, k):
        return pltpu.roll(value, k % traces, 0) if k % traces else value

    def sides(i):
        pair, other = pair_ref[i], other_ref[i]
        left, right = jnp.where(first_col, other, pair), jnp.where(first_col, pair, other)
        return jnp.concatenate([left, right], axis=0)

    def at_ends(value, left, right, inner):
        return jnp.where(west, turned(value, left), jnp.where(east, turned(value, right), inner))

    beside = [sides(c) for c in range(contrasts)]
    seconds = [sides(contrasts), sides(contrasts + 1)]
    notes = seconds[1][:, :LANES]
    line = place[:, :LANES]
    theirs = turned(notes, -rows)
    mixed = jnp.where((line == 2) | (line == 3), notes, note_ref[...])
    mixed = jnp.where((line == 4) | (line == 5), theirs, mixed)
    masks = [mixed[:, a : a + 1] for a in range(angles)]
    mine = (place[:, :1] < 2) | (place[:, :1] >= traces - 2)
    tile = []
    for c in range(contrasts):
        scale = jnp.where(mine, -strength_ref[:, c : c + 1], 1.0)
        whole = jnp.where(place % half < rows, beside[c], turned(beside[c], rows)) * scale
        tile.append([whole[:, k * LANES : (k + 1) * LANES] for k in range(n)])
    bands = [(ahead_ref[a].astype(BF16), back_ref[a].astype(BF16)) for a in range(angles)]
    edge = [jnp.concatenate(tiles, axis=1) for tiles in normal(tile, masks, avo_ref, bands)]

    has = jnp.where(place[:, :1] < half, has_left, has_right)
    far_weight = theirs[:, angles : angles + 1] + 4.0
    weights = [column(prior_ref[r : r + 1, :]) + 4.0 for r in range(rows)]
    sums = [norm_ref[...], *[jnp.zeros((traces, LANES), F32) for _ in range(3)]]
    for c in range(contrasts):
        strength = strength_ref[:, c : c + 1]
        theirs = beside[c]
        around = turned(seconds[c // 2], -rows * (c % 2)) + turned(theirs, -rows)
        around = around + jnp.where(place % 2 == 1, turned(theirs, 1), turned(theirs, -1))
        prior = far_weight * theirs - (around + has * own_ref[c])
        beyond = jnp.where(place < half, turned(edge[c], -rows), edge[c]) + strength * prior

        lines = [halo_ref[0, c], *[v_ref[c, r] for r in range(rows)], halo_ref[1, c]]
        lines = [
            here - strength * at_ends(theirs, -k, half - 1 - k, 0.0)
            for here, k in zip(lines, (rows, *range(rows), rows + 1))
        ]
        for r in range(rows):
            here, b = lines[r + 1], b_ref[c, r]
            ends = jnp.where(west, turned(beyond, -r), turned(beyond, half - 1 - r))
            around = jnp.where(west, ends, turned(here, 1)) + jnp.where(east, ends, turned(here, -1))
            around = around + lines[r] + lines[r + 2]
            mend = at_ends(edge[c], -r, 1 - r, 0.0)
            two = data_ref[c, r] + mend + strength * (weights[r] * here - around)
            one_ref[c, r] = here
            two_ref[c, r] = two
            for q, product in enumerate((b * here, here * here, here * two), 1):
                sums[q] = sums[q] + lane_tiles(product)
    lane = lax.broadcasted_iota(jnp.int32, (1, LANES), 1)
    packed = jnp.zeros((1, LANES), F32)
    for q, total in enumerate(sums):
        total = jnp.sum(jnp.sum(total, axis=0, keepdims=True), axis=1, keepdims=True)
        packed = jnp.where(lane == q, total, packed)
    gram_ref[...] = jnp.broadcast_to(packed[None], gram_ref.shape)


def finish_kernel(
    gram_ref, b_ref, one_ref, two_ref, solution_hbm, residual_hbm, solution_ref, residual_ref, sems
):
    sums = jnp.sum(gram_ref[...], axis=0)
    g00, g01, g11, g12 = (sums[:, q : q + 1] for q in range(4))
    first = g00 / g01
    ratio = first * g11 / g01
    second = (ratio - 1.0) * g01 / (first * g12 - ratio * g11)
    near = first + second * ratio
    far = first * second
    blocks = [(c, r) for c in range(b_ref.shape[0]) for r in range(b_ref.shape[1])]
    for block in blocks:
        solution_ref[block] = near * b_ref[block] - far * one_ref[block]
    done = pltpu.make_async_copy(solution_ref, solution_hbm, sems.at[0])
    done.start()
    for block in blocks:
        residual_ref[block] = b_ref[block] - near * one_ref[block] + far * two_ref[block]
    last = pltpu.make_async_copy(residual_ref, residual_hbm, sems.at[1])
    last.start()
    done.wait()
    last.wait()


VMEM = pl.BlockSpec(memory_space=pltpu.VMEM)
HBM = pl.BlockSpec(memory_space=pltpu.HBM)


def call(kernel, outs, ins, flops, scratch=(), places=None, to=VMEM):
    moved = sum(x.size * x.dtype.itemsize for x in (*ins, *outs))
    return pl.pallas_call(
        kernel,
        out_shape=outs,
        in_specs=[VMEM] * len(ins) if places is None else places,
        out_specs=jax.tree.map(lambda _: to, outs),
        scratch_shapes=list(scratch),
        compiler_params=pltpu.CompilerParams(vmem_limit_bytes=24 * 1024 * 1024),
        cost_estimate=pl.CostEstimate(flops=flops, bytes_accessed=moved, transcendentals=0),
        name=getattr(kernel, "func", kernel).__name__,
    )(*ins)


def swap(axis, value, first):
    starts = range(first, lax.axis_size(axis) - 1, 2)
    return lax.ppermute(value, axis, [(i + d, i + 1 - d) for i in starts for d in (0, 1)])


def hand_on(axis, value):
    size = lax.axis_size(axis)
    steps = [(i, i + 2 - 4 * (i % 2)) for i in range(size)]
    return lax.ppermute(value, axis, [(i, j) for i, j in steps if 0 <= j < size])


def shards(seismic, validity, prior_weight, lateral_strength, avo_coeffs, wavelets):
    angles, rows, traces, samples = seismic.shape
    contrasts = avo_coeffs.shape[1]
    avo_coeffs = jnp.swapaxes(avo_coeffs, 0, 1)
    shape = lambda *dims: jax.ShapeDtypeStruct(dims, F32)
    field = shape(contrasts, rows, traces, samples)
    side = shape(contrasts + 2, rows + 2, samples)
    lines = shape(8, 2 * LANES)
    work = 2 * angles * rows * traces * samples * 256 * 4

    given = (seismic, validity, avo_coeffs, wavelets, prior_weight)
    kept = [given[i] for i in (1, 2, 4)]
    edge = shape(contrasts * samples // LANES + 1, traces, LANES)
    b, near, far, padded, *kept = call(
        start_kernel,
        (
            field, edge, edge, lines,
            *[jax.ShapeDtypeStruct(x.shape, x.dtype) for x in kept],
        ),
        [pltpu.with_memory_space_constraint(x, pltpu.HBM) for x in given],
        work,
        [
            pltpu.VMEM(seismic.shape, seismic.dtype),
            pltpu.VMEM(wavelets.shape, F32),
            pltpu.SemaphoreType.DMA((angles + 4,)),
        ],
        [HBM] * 5,
    )
    near = swap("inline", near, 0)
    near_next = swap("inline", far, 1)
    far_next = hand_on("inline", near)
    far = swap("inline", far, 0)
    col_pair, col_other, own, note = call(
        column_kernel,
        (side, side, shape(contrasts, 2 * rows + 4, samples), shape(traces, LANES)),
        (b, near, near_next, kept[0], kept[2]),
        2 * field.size,
        [pltpu.VMEM((2, 2 * rows + 4, samples), F32)],
    )
    col_other = swap("col", col_other, 1)
    col_pair = swap("col", col_pair, 0)
    bands = shape(angles, 2 * LANES, 2 * LANES)
    halo = shape(2, contrasts, traces, samples)
    strength = lateral_strength.reshape(1, -1)
    image, data, part, ahead, back, norm, strength = call(
        functools.partial(inner_kernel, wavelets.shape[1]),
        (field, field, halo, bands, bands, shape(traces, LANES), shape(*strength.shape)),
        (
            pltpu.with_memory_space_constraint(strength, pltpu.HBM),
            b, near, near_next, padded, *kept,
        ),
        6 * work,
        [pltpu.SemaphoreType.DMA((1,))],
        [HBM] + [VMEM] * 7,
    )
    (halo,) = call(halo_kernel, (halo,), (part, far_next, far, strength), field.size)
    axes = ("inline", "col")
    one, two, gram = call(
        image_kernel,
        (field, field, shape(lax.axis_size(axes), 1, LANES)),
        (
            b, image, data, halo, norm, own, note, col_other, col_pair,
            *kept[1:], strength, ahead, back,
        ),
        work,
    )
    gram = lax.all_to_all(gram, axes, 0, 0)
    work = 8 * field.size
    room = [pltpu.VMEM(field.shape, F32)] * 2 + [pltpu.SemaphoreType.DMA((2,))]
    return tuple(
        call(finish_kernel, (field, field), (gram, b, one, two), work, room, to=HBM)
    )


def solution(mesh):
    placed = (
        P(None, "inline", "col", None),
        P(None, "inline", "col"),
        P("inline", "col"),
        P(),
        P(),
        P(),
    )
    return jax.shard_map(
        shards,
        mesh=mesh,
        in_specs=placed,
        out_specs=(P(None, "inline", "col", None), P(None, "inline", "col", None)),
        check_vma=False,
    )
```

```python
import functools

import jax
import jax.numpy as jnp
from jax import lax
from jax.experimental import pallas as pl
from jax.experimental.pallas import tpu as pltpu
from jax.sharding import PartitionSpec as P

LANES = 128
F32 = jnp.float32
BF16 = jnp.bfloat16


def split(value):
    high = value.astype(BF16)
    return high, (value - high.astype(F32)).astype(BF16)


def pad_taps(taps_ref, padded_ref):
    padded_ref[...] = jnp.zeros_like(padded_ref)
    padded_ref[0 : taps_ref.shape[0], 0 : taps_ref.shape[1]] = taps_ref[...]


def turn(lines, count):
    n, size = lines.shape
    parts = []
    for _ in range(3):
        parts.append(lines.astype(BF16).astype(F32))
        lines = lines - parts[-1]
    rows = lax.broadcasted_iota(jnp.int32, (size, size), 0)
    cols = lax.broadcasted_iota(jnp.int32, (size, size), 1)
    flip = jnp.where(rows + cols == count - 1, 1.0, 0.0).astype(BF16)
    whole = jnp.concatenate(parts, axis=0).astype(BF16)
    turned = jnp.dot(whole, flip, preferred_element_type=F32)
    return turned[:n] + turned[n : 2 * n] + turned[2 * n :]


def band(line):
    lines = jnp.broadcast_to(line, (LANES, line.shape[1]))
    return jnp.concatenate(split(pltpu.roll(lines, 0, 1, stride=1, stride_axis=0)), axis=0)


def convolve(rows, bands):
    rows = rows.astype(BF16)
    out = lax.dot_general(rows, bands, (((1,), (1,)), ((), ())), preferred_element_type=F32)
    return out[:, :LANES] + out[:, LANES:]


def column(row):
    n = row.shape[1]
    same = lax.broadcasted_iota(jnp.int32, (n, n), 0) == lax.broadcasted_iota(jnp.int32, (n, n), 1)
    return jnp.sum(jnp.where(same, jnp.broadcast_to(row, (n, n)), 0.0), axis=1, keepdims=True)


def trace_columns(ref, *lead):
    rows = ref[lead].astype(F32)
    return jnp.concatenate([column(rows[r : r + 1, :]) for r in range(rows.shape[0])], axis=0)


def thirds(value):
    kind = BF16 if value.shape[0] % 16 == 0 else F32
    parts = []
    for _ in range(3):
        high = value.astype(BF16)
        parts.append(high.astype(kind))
        value = value - high.astype(F32)
    return parts


def windows(tiles):
    pairs = [jnp.concatenate(pair, axis=1) for pair in zip(tiles[:-1], tiles[1:])]
    return jnp.concatenate(pairs, axis=0)


def forward(tiles, bands):
    parts = list(zip(*[thirds(t) for t in tiles]))
    zero = jnp.zeros_like(parts[0][0])
    n, size = len(tiles) + 1, tiles[0].shape[0]
    rows = [windows([zero, *part, zero]) for part in parts]
    out = convolve(jnp.concatenate(rows, axis=0), bands)
    out = out[: n * size] + (out[n * size : 2 * n * size] + out[2 * n * size :])
    return [out[k * size : (k + 1) * size] for k in range(n)]


def backward(parts, bands):
    n, size = len(parts[0]) - 1, parts[0][0].shape[0]
    rows = jnp.concatenate([windows(part) for part in parts], axis=0)
    out = convolve(rows, bands)
    total = out[: n * size]
    for p in range(1, len(parts)):
        total = total + out[p * n * size : (p + 1) * n * size]
    return [total[k * size : (k + 1) * size] for k in range(n)]


def coeff(avo_ref, angle, contrast, k):
    return avo_ref[contrast, angle : angle + 1, pl.ds(k * LANES, LANES)]


def add_terms(total, avo_ref, angle, result):
    for c, line in enumerate(total):
        for k, tile in enumerate(result):
            term = coeff(avo_ref, angle, c, k) * tile
            line[k] = term if angle == 0 else line[k] + term


def store_tiles(out_ref, tiles):
    size = out_ref.shape[2]
    for c in range(out_ref.shape[0]):
        for k, tile in enumerate(tiles[c]):
            for r in range(out_ref.shape[1]):
                out_ref[c, r, :, pl.ds(k * LANES, LANES)] = tile[r * size : (r + 1) * size]


def right_side(seis_ref, masks, avo_ref, bands):
    angles, rows, _, samples = seis_ref.shape
    n = samples // LANES
    total = [[None] * n for _ in range(avo_ref.shape[0])]
    for a in range(angles):
        data = jnp.concatenate([seis_ref[a, r].astype(F32) for r in range(rows)], axis=0)
        data = data * masks[a]
        turned = [
            pltpu.roll(data[:, k * LANES : (k + 1) * LANES], LANES // 2, 1) for k in range(n)
        ]
        zero = jnp.zeros_like(turned[0])
        left_half = lax.broadcasted_iota(jnp.int32, zero.shape, 1) < LANES // 2
        shifted = [
            jnp.where(left_half, before, here).astype(BF16)
            for before, here in zip([zero, *turned], [*turned, zero])
        ]
        add_terms(total, avo_ref, a, backward([shifted], bands[a]))
    return total


def normal(field, masks, avo_ref, bands):
    contrasts, n = len(field), len(field[0])
    total = [[None] * n for _ in range(contrasts)]
    for a, (ahead, back) in enumerate(bands):
        mixed = []
        for k in range(n):
            parts = [coeff(avo_ref, a, c, k) * field[c][k] for c in range(contrasts)]
            mixed.append(functools.reduce(jnp.add, parts))
        synth = [tile * masks[a] for tile in forward(mixed, ahead)]
        left_half = lax.broadcasted_iota(jnp.int32, synth[0].shape, 1) < LANES // 2
        synth[0] = jnp.where(left_half, 0.0, synth[0])
        synth[n] = jnp.where(left_half, synth[n], 0.0)
        result = backward(list(zip(*[thirds(t) for t in synth])), back)
        add_terms(total, avo_ref, a, result)
    return total


def lateral(here, north, south, west, east):
    traces = here.shape[0]
    place = lax.broadcasted_iota(jnp.int32, here.shape, 0)
    from_west = jnp.where(place == 0, 0.0 if west is None else west, pltpu.roll(here, 1, 0))
    from_east = jnp.where(
        place == traces - 1, 0.0 if east is None else east, pltpu.roll(here, traces - 1, 0)
    )
    around = from_west + from_east
    for other in (north, south):
        around = around if other is None else around + other
    return around


def copy_in(pairs, sems):
    copies = [pltpu.make_async_copy(a, b, sems.at[i]) for i, (a, b) in enumerate(pairs)]
    for copy in copies:
        copy.start()
    return copies


def start_kernel(
    seis_hbm, valid_hbm, avo_hbm, taps_hbm, prior_hbm,
    b_ref, near_ref, far_ref, padded_ref, valid_ref, avo_ref, prior_ref,
    seis_ref, taps_ref, sems,
):
    angles = avo_ref.shape[1]
    taps, valid, *rest = copy_in(
        (
            (taps_hbm, taps_ref),
            (valid_hbm, valid_ref),
            *((seis_hbm.at[a], seis_ref.at[a]) for a in range(angles)),
            (avo_hbm, avo_ref),
            (prior_hbm, prior_ref),
        ),
        sems,
    )
    taps.wait()
    pad_taps(taps_ref, padded_ref)
    bands = [band(padded_ref[a : a + 1, :]) for a in range(angles)]
    valid.wait()
    masks = [trace_columns(valid_ref, a) for a in range(angles)]
    for copy in rest:
        copy.wait()
    store_tiles(b_ref, right_side(seis_ref, masks, avo_ref, bands))
    contrasts, rows, traces, samples = b_ref.shape
    n = samples // LANES
    first = starts_pair("inline")
    lane = lax.broadcasted_iota(jnp.int32, (traces, LANES), 1)
    notes = []
    for r in (0, rows - 1):
        note = jnp.where(lane == angles, column(prior_ref[r : r + 1, :]), 0.0)
        for a in range(angles):
            note = jnp.where(lane == a, masks[a][r * traces : (r + 1) * traces], note)
        notes.append(note)
    edges = [
        [*[b_ref[c, r, :, pl.ds(k * LANES, LANES)] for c in range(contrasts) for k in range(n)], note]
        for r, note in zip((0, rows - 1), notes)
    ]
    for e, (top, bottom) in enumerate(zip(*edges)):
        near_ref[e] = jnp.where(first, bottom, top)
        far_ref[e] = jnp.where(first, top, bottom)


def either_side(pair_ref, next_ref, *where):
    first = starts_pair("inline")
    pair, other = pair_ref[where], next_ref[where]
    return jnp.where(first, other, pair), jnp.where(first, pair, other)


def stack_tiles(ref):
    contrasts, rows, _, samples = ref.shape
    return [
        [
            jnp.concatenate([ref[c, r, :, pl.ds(k, LANES)] for r in range(rows)], axis=0)
            for k in range(0, samples, LANES)
        ]
        for c in range(contrasts)
    ]


def inside(axis):
    place = lax.axis_index(axis)
    last = lax.axis_size(axis) - 1
    return (place > 0).astype(F32), (place < last).astype(F32)


def starts_pair(axis):
    return lax.axis_index(axis) % 2 == 0


def row_pair(near_ref, next_ref, c, n):
    tiles = [either_side(near_ref, next_ref, c * n + k) for k in range(n)]
    return [jnp.concatenate(side, axis=1) for side in zip(*tiles)]


def column_kernel(
    b_ref, near_ref, near_next_ref, valid_ref, prior_ref, _,
    pair_ref, other_ref, own_ref, note_ref, second_ref,
):
    contrasts, rows, traces, samples = b_ref.shape
    angles = valid_ref.shape[0]
    first_col = starts_pair("col")
    half = rows + 2
    second_ref[...] = jnp.zeros_like(second_ref)
    note_ref[...] = jnp.zeros_like(note_ref)
    for c in range(contrasts):
        own = [b_ref[c, r] for r in range(rows)]
        for i, line in enumerate([*own, *row_pair(near_ref, near_next_ref, c, samples // LANES)]):
            own_ref[c, i : i + 1, :] = line[0:1]
            own_ref[c, half + i : half + i + 1, :] = line[traces - 1 :]
        for r, line in enumerate(own):
            at = c * rows + r
            second_ref[0, at : at + 1, :] = line[1:2]
            second_ref[1, at : at + 1, :] = line[traces - 2 : traces - 1]
    lane = lax.broadcasted_iota(jnp.int32, (1, LANES), 1)
    for r in range(rows):
        for side, t in enumerate((0, traces - 1)):
            note = jnp.where(lane == angles, prior_ref[r : r + 1, t : t + 1], 0.0)
            for a in range(angles):
                note = jnp.where(lane == a, valid_ref[a, r : r + 1, t : t + 1].astype(F32), note)
            at = contrasts * rows + r
            second_ref[side, at : at + 1, 0:LANES] = note
            at = r + side * (traces - rows)
            note_ref[at : at + 1, :] = note
    for c in range(contrasts):
        left, right = own_ref[c, 0:half], own_ref[c, half:]
        pair_ref[c] = jnp.where(first_col, right, left)
        other_ref[c] = jnp.where(first_col, left, right)
    for i in range(2):
        left, right = (second_ref[side, i * half : (i + 1) * half] for side in (0, 1))
        pair_ref[contrasts + i] = jnp.where(first_col, right, left)
        other_ref[contrasts + i] = jnp.where(first_col, left, right)


def data_kernel(
    count, strength_hbm, b_ref, padded_ref, valid_ref, avo_ref,
    data_ref, ahead_ref, back_ref, norm_ref, strength_ref, sem,
):
    contrasts, rows = b_ref.shape[:2]
    angles = avo_ref.shape[1]
    (copy,) = copy_in(((strength_hbm, strength_ref),), sem)
    turned = turn(padded_ref[...], count)
    bands = []
    for a in range(angles):
        bands.append((band(turned[a : a + 1]), band(padded_ref[a : a + 1, :])))
        ahead_ref[a], back_ref[a] = (half.astype(F32) for half in bands[a])
    masks = [trace_columns(valid_ref, a) for a in range(angles)]
    store_tiles(data_ref, normal(stack_tiles(b_ref), masks, avo_ref, bands))
    norm_ref[...] = functools.reduce(
        jnp.add, [lane_tiles(b_ref[c, r] * b_ref[c, r]) for c in range(contrasts) for r in range(rows)]
    )
    copy.wait()


def inner_kernel(
    b_ref, first_ref, near_ref, near_next_ref, valid_ref, avo_ref, prior_ref, strength_ref,
    ahead_ref, back_ref, v_ref, data_ref, halo_ref,
):
    contrasts, rows, traces, samples = b_ref.shape
    angles, n = avo_ref.shape[1], samples // LANES
    bands = [(ahead_ref[a].astype(BF16), back_ref[a].astype(BF16)) for a in range(angles)]
    above, below = either_side(near_ref, near_next_ref, contrasts * n)
    weights = [column(prior_ref[r : r + 1, :]) + 4.0 for r in range(rows)]
    ends = [row_pair(near_ref, near_next_ref, c, n) for c in range(contrasts)]
    for c in range(contrasts):
        strength = strength_ref[:, c : c + 1]
        lines = [ends[c][0], *[b_ref[c, r] for r in range(rows)], ends[c][1]]
        for r in range(rows):
            around = lateral(lines[r + 1], lines[r], lines[r + 2], None, None)
            v_ref[c, r] = first_ref[c, r] + strength * (weights[r] * lines[r + 1] - around)
    masks = [
        jnp.concatenate([above[:, a : a + 1], trace_columns(valid_ref, a), below[:, a : a + 1]], axis=0)
        for a in range(angles)
    ]
    field = [
        [
            jnp.concatenate([up[:, k : k + LANES], own, low[:, k : k + LANES]], axis=0)
            for k, own in zip(range(0, samples, LANES), line)
        ]
        for (up, low), line in zip(ends, stack_tiles(v_ref))
    ]
    total = normal(field, masks, avo_ref, bands)
    has = inside("inline")
    for c in range(contrasts):
        strength = strength_ref[:, c : c + 1]
        data = jnp.concatenate(total[c], axis=1)
        for r in range(rows):
            data_ref[c, r] = data[(r + 1) * traces : (r + 2) * traces]
        for i, (note, own, at) in enumerate(((above, 0, 0), (below, rows - 1, rows + 1))):
            here = ends[c][i]
            around = lateral(here, None, has[i] * b_ref[c, own], None, None)
            prior = (note[:, angles : angles + 1] + 4.0) * here - around
            halo_ref[i, c] = data[at * traces : (at + 1) * traces] + strength * prior


def lane_tiles(product):
    tiles = [product[:, k : k + LANES] for k in range(0, product.shape[1], LANES)]
    return functools.reduce(jnp.add, tiles)


def halo_kernel(halo_ref, far_next_ref, far_ref, strength_ref, out_ref):
    contrasts, samples = halo_ref.shape[1], halo_ref.shape[3]
    for c in range(contrasts):
        for i, line in enumerate(row_pair(far_ref, far_next_ref, c, samples // LANES)):
            out_ref[i, c] = halo_ref[i, c] - strength_ref[:, c : c + 1] * line


def image_kernel(
    b_ref, v_ref, data_ref, halo_ref, norm_ref, own_ref, note_ref, other_ref, pair_ref,
    avo_ref, prior_ref, strength_ref, ahead_ref, back_ref,
    one_ref, two_ref, gram_ref,
):
    contrasts, rows, traces, samples = b_ref.shape
    angles, n = avo_ref.shape[1], samples // LANES
    has_left, has_right = inside("col")
    first_col = starts_pair("col")
    place = lax.broadcasted_iota(jnp.int32, (traces, samples), 0)
    west, east = place == 0, place == traces - 1
    half = traces // 2

    def turned(value, k):
        return pltpu.roll(value, k % traces, 0) if k % traces else value

    def sides(i):
        pair, other = pair_ref[i], other_ref[i]
        left, right = jnp.where(first_col, other, pair), jnp.where(first_col, pair, other)
        return jnp.concatenate([left, right], axis=0)

    def at_ends(value, left, right, inner):
        return jnp.where(west, turned(value, left), jnp.where(east, turned(value, right), inner))

    beside = [sides(c) for c in range(contrasts)]
    seconds = [sides(contrasts), sides(contrasts + 1)]
    notes = seconds[1][:, :LANES]
    line = place[:, :LANES]
    theirs = turned(notes, -rows)
    mixed = jnp.where((line == 2) | (line == 3), notes, note_ref[...])
    mixed = jnp.where((line == 4) | (line == 5), theirs, mixed)
    masks = [mixed[:, a : a + 1] for a in range(angles)]
    mine = (place[:, :1] < 2) | (place[:, :1] >= traces - 2)
    tile = []
    for c in range(contrasts):
        scale = jnp.where(mine, -strength_ref[:, c : c + 1], 1.0)
        whole = jnp.where(place % half < rows, beside[c], turned(beside[c], rows)) * scale
        tile.append([whole[:, k * LANES : (k + 1) * LANES] for k in range(n)])
    bands = [(ahead_ref[a].astype(BF16), back_ref[a].astype(BF16)) for a in range(angles)]
    edge = [jnp.concatenate(tiles, axis=1) for tiles in normal(tile, masks, avo_ref, bands)]

    has = jnp.where(place[:, :1] < half, has_left, has_right)
    far_weight = theirs[:, angles : angles + 1] + 4.0
    weights = [column(prior_ref[r : r + 1, :]) + 4.0 for r in range(rows)]
    sums = [norm_ref[...], *[jnp.zeros((traces, LANES), F32) for _ in range(3)]]
    for c in range(contrasts):
        strength = strength_ref[:, c : c + 1]
        theirs = beside[c]
        around = turned(seconds[c // 2], -rows * (c % 2)) + turned(theirs, -rows)
        around = around + jnp.where(place % 2 == 1, turned(theirs, 1), turned(theirs, -1))
        prior = far_weight * theirs - (around + has * own_ref[c])
        beyond = jnp.where(place < half, turned(edge[c], -rows), edge[c]) + strength * prior

        lines = [halo_ref[0, c], *[v_ref[c, r] for r in range(rows)], halo_ref[1, c]]
        lines = [
            here - strength * at_ends(theirs, -k, half - 1 - k, 0.0)
            for here, k in zip(lines, (rows, *range(rows), rows + 1))
        ]
        for r in range(rows):
            here, b = lines[r + 1], b_ref[c, r]
            ends = jnp.where(west, turned(beyond, -r), turned(beyond, half - 1 - r))
            around = jnp.where(west, ends, turned(here, 1)) + jnp.where(east, ends, turned(here, -1))
            around = around + lines[r] + lines[r + 2]
            mend = at_ends(edge[c], -r, 1 - r, 0.0)
            two = data_ref[c, r] + mend + strength * (weights[r] * here - around)
            one_ref[c, r] = here
            two_ref[c, r] = two
            for q, product in enumerate((b * here, here * here, here * two), 1):
                sums[q] = sums[q] + lane_tiles(product)
    lane = lax.broadcasted_iota(jnp.int32, (1, LANES), 1)
    packed = jnp.zeros((1, LANES), F32)
    for q, total in enumerate(sums):
        total = jnp.sum(jnp.sum(total, axis=0, keepdims=True), axis=1, keepdims=True)
        packed = jnp.where(lane == q, total, packed)
    gram_ref[...] = jnp.broadcast_to(packed[None], gram_ref.shape)


def finish_kernel(
    gram_ref, b_ref, one_ref, two_ref, solution_hbm, residual_hbm, solution_ref, residual_ref, sems
):
    sums = jnp.sum(gram_ref[...], axis=0)
    g00, g01, g11, g12 = (sums[:, q : q + 1] for q in range(4))
    first = g00 / g01
    ratio = first * g11 / g01
    second = (ratio - 1.0) * g01 / (first * g12 - ratio * g11)
    near = first + second * ratio
    far = first * second
    blocks = [(c, r) for c in range(b_ref.shape[0]) for r in range(b_ref.shape[1])]
    for block in blocks:
        solution_ref[block] = near * b_ref[block] - far * one_ref[block]
    done = pltpu.make_async_copy(solution_ref, solution_hbm, sems.at[0])
    done.start()
    for block in blocks:
        residual_ref[block] = b_ref[block] - near * one_ref[block] + far * two_ref[block]
    last = pltpu.make_async_copy(residual_ref, residual_hbm, sems.at[1])
    last.start()
    done.wait()
    last.wait()


VMEM = pl.BlockSpec(memory_space=pltpu.VMEM)
HBM = pl.BlockSpec(memory_space=pltpu.HBM)


def call(kernel, outs, ins, flops, scratch=(), places=None, to=VMEM):
    moved = sum(x.size * x.dtype.itemsize for x in (*ins, *outs))
    return pl.pallas_call(
        kernel,
        out_shape=outs,
        in_specs=[VMEM] * len(ins) if places is None else places,
        out_specs=jax.tree.map(lambda _: to, outs),
        scratch_shapes=list(scratch),
        compiler_params=pltpu.CompilerParams(vmem_limit_bytes=24 * 1024 * 1024),
        cost_estimate=pl.CostEstimate(flops=flops, bytes_accessed=moved, transcendentals=0),
        name=getattr(kernel, "func", kernel).__name__,
    )(*ins)


def swap(axis, value, first):
    starts = range(first, lax.axis_size(axis) - 1, 2)
    return lax.ppermute(value, axis, [(i + d, i + 1 - d) for i in starts for d in (0, 1)])


def hand_on(axis, value):
    size = lax.axis_size(axis)
    steps = [(i, i + 2 - 4 * (i % 2)) for i in range(size)]
    return lax.ppermute(value, axis, [(i, j) for i, j in steps if 0 <= j < size])


def shards(seismic, validity, prior_weight, lateral_strength, avo_coeffs, wavelets):
    angles, rows, traces, samples = seismic.shape
    contrasts = avo_coeffs.shape[1]
    avo_coeffs = jnp.swapaxes(avo_coeffs, 0, 1)
    shape = lambda *dims: jax.ShapeDtypeStruct(dims, F32)
    field = shape(contrasts, rows, traces, samples)
    side = shape(contrasts + 2, rows + 2, samples)
    lines = shape(8, 2 * LANES)
    work = 2 * angles * rows * traces * samples * 256 * 4

    given = (seismic, validity, avo_coeffs, wavelets, prior_weight)
    kept = [given[i] for i in (1, 2, 4)]
    edge = shape(contrasts * samples // LANES + 1, traces, LANES)
    b, near, far, padded, *kept = call(
        start_kernel,
        (
            field, edge, edge, lines,
            *[jax.ShapeDtypeStruct(x.shape, x.dtype) for x in kept],
        ),
        [pltpu.with_memory_space_constraint(x, pltpu.HBM) for x in given],
        work,
        [
            pltpu.VMEM(seismic.shape, seismic.dtype),
            pltpu.VMEM(wavelets.shape, F32),
            pltpu.SemaphoreType.DMA((angles + 4,)),
        ],
        [HBM] * 5,
    )
    near = swap("inline", near, 0)
    near_next = swap("inline", far, 1)
    far_next = hand_on("inline", near)
    far = swap("inline", far, 0)
    bands = shape(angles, 2 * LANES, 2 * LANES)
    strength = lateral_strength.reshape(1, -1)
    first, ahead, back, norm, strength = call(
        functools.partial(data_kernel, wavelets.shape[1]),
        (field, bands, bands, shape(traces, LANES), shape(*strength.shape)),
        (pltpu.with_memory_space_constraint(strength, pltpu.HBM), b, padded, kept[0], kept[1]),
        2 * work,
        [pltpu.SemaphoreType.DMA((1,))],
        [HBM] + [VMEM] * 4,
    )
    col_pair, col_other, own, note = call(
        column_kernel,
        (side, side, shape(contrasts, 2 * rows + 4, samples), shape(traces, LANES)),
        (b, near, near_next, kept[0], kept[2], first),
        2 * field.size,
        [pltpu.VMEM((2, 2 * rows + 4, samples), F32)],
    )
    col_other = swap("col", col_other, 1)
    col_pair = swap("col", col_pair, 0)
    bands = shape(angles, 2 * LANES, 2 * LANES)
    halo = shape(2, contrasts, traces, samples)
    image, data, part = call(
        inner_kernel,
        (field, field, halo),
        (b, first, near, near_next, *kept, strength, ahead, back),
        4 * work,
    )
    (halo,) = call(halo_kernel, (halo,), (part, far_next, far, strength), field.size)
    axes = ("inline", "col")
    one, two, gram = call(
        image_kernel,
        (field, field, shape(lax.axis_size(axes), 1, LANES)),
        (
            b, image, data, halo, norm, own, note, col_other, col_pair,
            *kept[1:], strength, ahead, back,
        ),
        work,
    )
    gram = lax.all_to_all(gram, axes, 0, 0)
    work = 8 * field.size
    room = [pltpu.VMEM(field.shape, F32)] * 2 + [pltpu.SemaphoreType.DMA((2,))]
    return tuple(
        call(finish_kernel, (field, field), (gram, b, one, two), work, room, to=HBM)
    )


def solution(mesh):
    placed = (
        P(None, "inline", "col", None),
        P(None, "inline", "col"),
        P("inline", "col"),
        P(),
        P(),
        P(),
    )
    return jax.shard_map(
        shards,
        mesh=mesh,
        in_specs=placed,
        out_specs=(P(None, "inline", "col", None), P(None, "inline", "col", None)),
        check_vma=False,
    )
```

```python
import functools

import jax
import jax.numpy as jnp
from jax import lax
from jax.experimental import pallas as pl
from jax.experimental.pallas import tpu as pltpu
from jax.sharding import PartitionSpec as P

LANES = 128
F32 = jnp.float32
BF16 = jnp.bfloat16


def split(value):
    high = value.astype(BF16)
    return high, (value - high.astype(F32)).astype(BF16)


def pad_taps(taps_ref, padded_ref):
    padded_ref[...] = jnp.zeros_like(padded_ref)
    padded_ref[0 : taps_ref.shape[0], 0 : taps_ref.shape[1]] = taps_ref[...]


def turn(lines, count):
    n, size = lines.shape
    parts = []
    for _ in range(3):
        parts.append(lines.astype(BF16).astype(F32))
        lines = lines - parts[-1]
    rows = lax.broadcasted_iota(jnp.int32, (size, size), 0)
    cols = lax.broadcasted_iota(jnp.int32, (size, size), 1)
    flip = jnp.where(rows + cols == count - 1, 1.0, 0.0).astype(BF16)
    whole = jnp.concatenate(parts, axis=0).astype(BF16)
    turned = jnp.dot(whole, flip, preferred_element_type=F32)
    return turned[:n] + turned[n : 2 * n] + turned[2 * n :]


def band(line):
    lines = jnp.broadcast_to(line, (LANES, line.shape[1]))
    return jnp.concatenate(split(pltpu.roll(lines, 0, 1, stride=1, stride_axis=0)), axis=0)


def convolve(rows, bands):
    rows = rows.astype(BF16)
    out = lax.dot_general(rows, bands, (((1,), (1,)), ((), ())), preferred_element_type=F32)
    return out[:, :LANES] + out[:, LANES:]


def column(row):
    n = row.shape[1]
    same = lax.broadcasted_iota(jnp.int32, (n, n), 0) == lax.broadcasted_iota(jnp.int32, (n, n), 1)
    return jnp.sum(jnp.where(same, jnp.broadcast_to(row, (n, n)), 0.0), axis=1, keepdims=True)


def trace_columns(ref, *lead):
    rows = ref[lead].astype(F32)
    return jnp.concatenate([column(rows[r : r + 1, :]) for r in range(rows.shape[0])], axis=0)


def thirds(value):
    kind = BF16 if value.shape[0] % 16 == 0 else F32
    parts = []
    for _ in range(3):
        high = value.astype(BF16)
        parts.append(high.astype(kind))
        value = value - high.astype(F32)
    return parts


def windows(tiles):
    pairs = [jnp.concatenate(pair, axis=1) for pair in zip(tiles[:-1], tiles[1:])]
    return jnp.concatenate(pairs, axis=0)


def forward(tiles, bands):
    parts = list(zip(*[thirds(t) for t in tiles]))
    zero = jnp.zeros_like(parts[0][0])
    n, size = len(tiles) + 1, tiles[0].shape[0]
    rows = [windows([zero, *part, zero]) for part in parts]
    out = convolve(jnp.concatenate(rows, axis=0), bands)
    out = out[: n * size] + (out[n * size : 2 * n * size] + out[2 * n * size :])
    return [out[k * size : (k + 1) * size] for k in range(n)]


def backward(parts, bands):
    n, size = len(parts[0]) - 1, parts[0][0].shape[0]
    rows = jnp.concatenate([windows(part) for part in parts], axis=0)
    out = convolve(rows, bands)
    total = out[: n * size]
    for p in range(1, len(parts)):
        total = total + out[p * n * size : (p + 1) * n * size]
    return [total[k * size : (k + 1) * size] for k in range(n)]


def coeff(avo_ref, angle, contrast, k):
    return avo_ref[contrast, angle : angle + 1, pl.ds(k * LANES, LANES)]


def add_terms(total, avo_ref, angle, result):
    for c, line in enumerate(total):
        for k, tile in enumerate(result):
            term = coeff(avo_ref, angle, c, k) * tile
            line[k] = term if angle == 0 else line[k] + term


def store_tiles(out_ref, tiles):
    size = out_ref.shape[2]
    for c in range(out_ref.shape[0]):
        for k, tile in enumerate(tiles[c]):
            for r in range(out_ref.shape[1]):
                out_ref[c, r, :, pl.ds(k * LANES, LANES)] = tile[r * size : (r + 1) * size]


def right_side(seis_ref, masks, avo_ref, bands):
    angles, rows, _, samples = seis_ref.shape
    n = samples // LANES
    total = [[None] * n for _ in range(avo_ref.shape[0])]
    for a in range(angles):
        data = jnp.concatenate([seis_ref[a, r].astype(F32) for r in range(rows)], axis=0)
        data = data * masks[a]
        turned = [
            pltpu.roll(data[:, k * LANES : (k + 1) * LANES], LANES // 2, 1) for k in range(n)
        ]
        zero = jnp.zeros_like(turned[0])
        left_half = lax.broadcasted_iota(jnp.int32, zero.shape, 1) < LANES // 2
        shifted = [
            jnp.where(left_half, before, here).astype(BF16)
            for before, here in zip([zero, *turned], [*turned, zero])
        ]
        add_terms(total, avo_ref, a, backward([shifted], bands[a]))
    return total


def normal(field, masks, avo_ref, bands):
    contrasts, n = len(field), len(field[0])
    total = [[None] * n for _ in range(contrasts)]
    for a, (ahead, back) in enumerate(bands):
        mixed = []
        for k in range(n):
            parts = [coeff(avo_ref, a, c, k) * field[c][k] for c in range(contrasts)]
            mixed.append(functools.reduce(jnp.add, parts))
        synth = [tile * masks[a] for tile in forward(mixed, ahead)]
        left_half = lax.broadcasted_iota(jnp.int32, synth[0].shape, 1) < LANES // 2
        synth[0] = jnp.where(left_half, 0.0, synth[0])
        synth[n] = jnp.where(left_half, synth[n], 0.0)
        result = backward(list(zip(*[thirds(t) for t in synth])), back)
        add_terms(total, avo_ref, a, result)
    return total


def lateral(here, north, south, west, east):
    traces = here.shape[0]
    place = lax.broadcasted_iota(jnp.int32, here.shape, 0)
    from_west = jnp.where(place == 0, 0.0 if west is None else west, pltpu.roll(here, 1, 0))
    from_east = jnp.where(
        place == traces - 1, 0.0 if east is None else east, pltpu.roll(here, traces - 1, 0)
    )
    around = from_west + from_east
    for other in (north, south):
        around = around if other is None else around + other
    return around


def copy_in(pairs, sems):
    copies = [pltpu.make_async_copy(a, b, sems.at[i]) for i, (a, b) in enumerate(pairs)]
    for copy in copies:
        copy.start()
    return copies


def start_kernel(
    seis_hbm, valid_hbm, avo_hbm, taps_hbm, prior_hbm,
    b_ref, near_ref, far_ref, padded_ref, valid_ref, avo_ref, prior_ref,
    seis_ref, taps_ref, sems,
):
    angles = avo_ref.shape[1]
    taps, valid, *rest = copy_in(
        (
            (taps_hbm, taps_ref),
            (valid_hbm, valid_ref),
            (seis_hbm, seis_ref),
            (avo_hbm, avo_ref),
            (prior_hbm, prior_ref),
        ),
        sems,
    )
    taps.wait()
    pad_taps(taps_ref, padded_ref)
    bands = [band(padded_ref[a : a + 1, :]) for a in range(angles)]
    valid.wait()
    masks = [trace_columns(valid_ref, a) for a in range(angles)]
    for copy in rest:
        copy.wait()
    store_tiles(b_ref, right_side(seis_ref, masks, avo_ref, bands))
    contrasts, rows, traces, samples = b_ref.shape
    n = samples // LANES
    first = starts_pair("inline")
    lane = lax.broadcasted_iota(jnp.int32, (traces, LANES), 1)
    notes = []
    for r in (0, rows - 1):
        note = jnp.where(lane == angles, column(prior_ref[r : r + 1, :]), 0.0)
        for a in range(angles):
            note = jnp.where(lane == a, masks[a][r * traces : (r + 1) * traces], note)
        notes.append(note)
    edges = [
        [*[b_ref[c, r, :, pl.ds(k * LANES, LANES)] for c in range(contrasts) for k in range(n)], note]
        for r, note in zip((0, rows - 1), notes)
    ]
    for e, (top, bottom) in enumerate(zip(*edges)):
        near_ref[e] = jnp.where(first, bottom, top)
        far_ref[e] = jnp.where(first, top, bottom)


def either_side(pair_ref, next_ref, *where):
    first = starts_pair("inline")
    pair, other = pair_ref[where], next_ref[where]
    return jnp.where(first, other, pair), jnp.where(first, pair, other)


def stack_tiles(ref):
    contrasts, rows, _, samples = ref.shape
    return [
        [
            jnp.concatenate([ref[c, r, :, pl.ds(k, LANES)] for r in range(rows)], axis=0)
            for k in range(0, samples, LANES)
        ]
        for c in range(contrasts)
    ]


def inside(axis):
    place = lax.axis_index(axis)
    last = lax.axis_size(axis) - 1
    return (place > 0).astype(F32), (place < last).astype(F32)


def starts_pair(axis):
    return lax.axis_index(axis) % 2 == 0


def row_pair(near_ref, next_ref, c, n):
    tiles = [either_side(near_ref, next_ref, c * n + k) for k in range(n)]
    return [jnp.concatenate(side, axis=1) for side in zip(*tiles)]


def column_kernel(
    b_ref, near_ref, near_next_ref, valid_ref, prior_ref, _,
    pair_ref, other_ref, own_ref, note_ref, second_ref,
):
    contrasts, rows, traces, samples = b_ref.shape
    angles = valid_ref.shape[0]
    first_col = starts_pair("col")
    half = rows + 2
    second_ref[...] = jnp.zeros_like(second_ref)
    note_ref[...] = jnp.zeros_like(note_ref)
    for c in range(contrasts):
        own = [b_ref[c, r] for r in range(rows)]
        for i, line in enumerate([*own, *row_pair(near_ref, near_next_ref, c, samples // LANES)]):
            own_ref[c, i : i + 1, :] = line[0:1]
            own_ref[c, half + i : half + i + 1, :] = line[traces - 1 :]
        for r, line in enumerate(own):
            at = c * rows + r
            second_ref[0, at : at + 1, :] = line[1:2]
            second_ref[1, at : at + 1, :] = line[traces - 2 : traces - 1]
    lane = lax.broadcasted_iota(jnp.int32, (1, LANES), 1)
    for r in range(rows):
        for side, t in enumerate((0, traces - 1)):
            note = jnp.where(lane == angles, prior_ref[r : r + 1, t : t + 1], 0.0)
            for a in range(angles):
                note = jnp.where(lane == a, valid_ref[a, r : r + 1, t : t + 1].astype(F32), note)
            at = contrasts * rows + r
            second_ref[side, at : at + 1, 0:LANES] = note
            at = r + side * (traces - rows)
            note_ref[at : at + 1, :] = note
    for c in range(contrasts):
        left, right = own_ref[c, 0:half], own_ref[c, half:]
        pair_ref[c] = jnp.where(first_col, right, left)
        other_ref[c] = jnp.where(first_col, left, right)
    for i in range(2):
        left, right = (second_ref[side, i * half : (i + 1) * half] for side in (0, 1))
        pair_ref[contrasts + i] = jnp.where(first_col, right, left)
        other_ref[contrasts + i] = jnp.where(first_col, left, right)


def data_kernel(
    count, strength_hbm, b_ref, padded_ref, valid_ref, avo_ref,
    data_ref, ahead_ref, back_ref, norm_ref, strength_ref, sem,
):
    contrasts, rows = b_ref.shape[:2]
    angles = avo_ref.shape[1]
    (copy,) = copy_in(((strength_hbm, strength_ref),), sem)
    turned = turn(padded_ref[...], count)
    bands = []
    for a in range(angles):
        bands.append((band(turned[a : a + 1]), band(padded_ref[a : a + 1, :])))
        ahead_ref[a], back_ref[a] = (half.astype(F32) for half in bands[a])
    masks = [trace_columns(valid_ref, a) for a in range(angles)]
    store_tiles(data_ref, normal(stack_tiles(b_ref), masks, avo_ref, bands))
    norm_ref[...] = functools.reduce(
        jnp.add, [lane_tiles(b_ref[c, r] * b_ref[c, r]) for c in range(contrasts) for r in range(rows)]
    )
    copy.wait()


def inner_kernel(
    b_ref, first_ref, near_ref, near_next_ref, valid_ref, avo_ref, prior_ref, strength_ref,
    ahead_ref, back_ref, v_ref, data_ref, halo_ref,
):
    contrasts, rows, traces, samples = b_ref.shape
    angles, n = avo_ref.shape[1], samples // LANES
    bands = [(ahead_ref[a].astype(BF16), back_ref[a].astype(BF16)) for a in range(angles)]
    above, below = either_side(near_ref, near_next_ref, contrasts * n)
    weights = [column(prior_ref[r : r + 1, :]) + 4.0 for r in range(rows)]
    ends = [row_pair(near_ref, near_next_ref, c, n) for c in range(contrasts)]
    for c in range(contrasts):
        strength = strength_ref[:, c : c + 1]
        lines = [ends[c][0], *[b_ref[c, r] for r in range(rows)], ends[c][1]]
        for r in range(rows):
            around = lateral(lines[r + 1], lines[r], lines[r + 2], None, None)
            v_ref[c, r] = first_ref[c, r] + strength * (weights[r] * lines[r + 1] - around)
    masks = [
        jnp.concatenate([above[:, a : a + 1], trace_columns(valid_ref, a), below[:, a : a + 1]], axis=0)
        for a in range(angles)
    ]
    field = [
        [
            jnp.concatenate([up[:, k : k + LANES], own, low[:, k : k + LANES]], axis=0)
            for k, own in zip(range(0, samples, LANES), line)
        ]
        for (up, low), line in zip(ends, stack_tiles(v_ref))
    ]
    total = normal(field, masks, avo_ref, bands)
    has = inside("inline")
    for c in range(contrasts):
        strength = strength_ref[:, c : c + 1]
        data = jnp.concatenate(total[c], axis=1)
        for r in range(rows):
            data_ref[c, r] = data[(r + 1) * traces : (r + 2) * traces]
        for i, (note, own, at) in enumerate(((above, 0, 0), (below, rows - 1, rows + 1))):
            here = ends[c][i]
            around = lateral(here, None, has[i] * b_ref[c, own], None, None)
            prior = (note[:, angles : angles + 1] + 4.0) * here - around
            halo_ref[i, c] = data[at * traces : (at + 1) * traces] + strength * prior


def lane_tiles(product):
    tiles = [product[:, k : k + LANES] for k in range(0, product.shape[1], LANES)]
    return functools.reduce(jnp.add, tiles)


def halo_kernel(halo_ref, far_next_ref, far_ref, strength_ref, out_ref):
    contrasts, samples = halo_ref.shape[1], halo_ref.shape[3]
    for c in range(contrasts):
        for i, line in enumerate(row_pair(far_ref, far_next_ref, c, samples // LANES)):
            out_ref[i, c] = halo_ref[i, c] - strength_ref[:, c : c + 1] * line


def image_kernel(
    b_ref, v_ref, data_ref, halo_ref, norm_ref, own_ref, note_ref, other_ref, pair_ref,
    avo_ref, prior_ref, strength_ref, ahead_ref, back_ref,
    one_ref, two_ref, gram_ref,
):
    contrasts, rows, traces, samples = b_ref.shape
    angles, n = avo_ref.shape[1], samples // LANES
    has_left, has_right = inside("col")
    first_col = starts_pair("col")
    place = lax.broadcasted_iota(jnp.int32, (traces, samples), 0)
    west, east = place == 0, place == traces - 1
    half = traces // 2

    def turned(value, k):
        return pltpu.roll(value, k % traces, 0) if k % traces else value

    def sides(i):
        pair, other = pair_ref[i], other_ref[i]
        left, right = jnp.where(first_col, other, pair), jnp.where(first_col, pair, other)
        return jnp.concatenate([left, right], axis=0)

    def at_ends(value, left, right, inner):
        return jnp.where(west, turned(value, left), jnp.where(east, turned(value, right), inner))

    beside = [sides(c) for c in range(contrasts)]
    seconds = [sides(contrasts), sides(contrasts + 1)]
    notes = seconds[1][:, :LANES]
    line = place[:, :LANES]
    theirs = turned(notes, -rows)
    mixed = jnp.where((line == 2) | (line == 3), notes, note_ref[...])
    mixed = jnp.where((line == 4) | (line == 5), theirs, mixed)
    masks = [mixed[:, a : a + 1] for a in range(angles)]
    mine = (place[:, :1] < 2) | (place[:, :1] >= traces - 2)
    tile = []
    for c in range(contrasts):
        scale = jnp.where(mine, -strength_ref[:, c : c + 1], 1.0)
        whole = jnp.where(place % half < rows, beside[c], turned(beside[c], rows)) * scale
        tile.append([whole[:, k * LANES : (k + 1) * LANES] for k in range(n)])
    bands = [(ahead_ref[a].astype(BF16), back_ref[a].astype(BF16)) for a in range(angles)]
    edge = [jnp.concatenate(tiles, axis=1) for tiles in normal(tile, masks, avo_ref, bands)]

    has = jnp.where(place[:, :1] < half, has_left, has_right)
    far_weight = theirs[:, angles : angles + 1] + 4.0
    weights = [column(prior_ref[r : r + 1, :]) + 4.0 for r in range(rows)]
    sums = [norm_ref[...], *[jnp.zeros((traces, LANES), F32) for _ in range(3)]]
    for c in range(contrasts):
        strength = strength_ref[:, c : c + 1]
        theirs = beside[c]
        around = turned(seconds[c // 2], -rows * (c % 2)) + turned(theirs, -rows)
        around = around + jnp.where(place % 2 == 1, turned(theirs, 1), turned(theirs, -1))
        prior = far_weight * theirs - (around + has * own_ref[c])
        beyond = jnp.where(place < half, turned(edge[c], -rows), edge[c]) + strength * prior

        lines = [halo_ref[0, c], *[v_ref[c, r] for r in range(rows)], halo_ref[1, c]]
        lines = [
            here - strength * at_ends(theirs, -k, half - 1 - k, 0.0)
            for here, k in zip(lines, (rows, *range(rows), rows + 1))
        ]
        for r in range(rows):
            here, b = lines[r + 1], b_ref[c, r]
            ends = jnp.where(west, turned(beyond, -r), turned(beyond, half - 1 - r))
            around = jnp.where(west, ends, turned(here, 1)) + jnp.where(east, ends, turned(here, -1))
            around = around + lines[r] + lines[r + 2]
            mend = at_ends(edge[c], -r, 1 - r, 0.0)
            two = data_ref[c, r] + mend + strength * (weights[r] * here - around)
            one_ref[c, r] = here
            two_ref[c, r] = two
            for q, product in enumerate((b * here, here * here, here * two), 1):
                sums[q] = sums[q] + lane_tiles(product)
    lane = lax.broadcasted_iota(jnp.int32, (1, LANES), 1)
    packed = jnp.zeros((1, LANES), F32)
    for q, total in enumerate(sums):
        total = jnp.sum(jnp.sum(total, axis=0, keepdims=True), axis=1, keepdims=True)
        packed = jnp.where(lane == q, total, packed)
    gram_ref[...] = jnp.broadcast_to(packed[None], gram_ref.shape)


def finish_kernel(
    gram_ref, b_ref, one_ref, two_ref, solution_hbm, residual_hbm, solution_ref, residual_ref, sems
):
    sums = jnp.sum(gram_ref[...], axis=0)
    g00, g01, g11, g12 = (sums[:, q : q + 1] for q in range(4))
    first = g00 / g01
    ratio = first * g11 / g01
    second = (ratio - 1.0) * g01 / (first * g12 - ratio * g11)
    near = first + second * ratio
    far = first * second
    blocks = [(c, r) for c in range(b_ref.shape[0]) for r in range(b_ref.shape[1])]
    for block in blocks:
        solution_ref[block] = near * b_ref[block] - far * one_ref[block]
    done = pltpu.make_async_copy(solution_ref, solution_hbm, sems.at[0])
    done.start()
    for block in blocks:
        residual_ref[block] = b_ref[block] - near * one_ref[block] + far * two_ref[block]
    last = pltpu.make_async_copy(residual_ref, residual_hbm, sems.at[1])
    last.start()
    done.wait()
    last.wait()


VMEM = pl.BlockSpec(memory_space=pltpu.VMEM)
HBM = pl.BlockSpec(memory_space=pltpu.HBM)


def call(kernel, outs, ins, flops, scratch=(), places=None, to=VMEM):
    moved = sum(x.size * x.dtype.itemsize for x in (*ins, *outs))
    return pl.pallas_call(
        kernel,
        out_shape=outs,
        in_specs=[VMEM] * len(ins) if places is None else places,
        out_specs=jax.tree.map(lambda _: to, outs),
        scratch_shapes=list(scratch),
        compiler_params=pltpu.CompilerParams(vmem_limit_bytes=24 * 1024 * 1024),
        cost_estimate=pl.CostEstimate(flops=flops, bytes_accessed=moved, transcendentals=0),
        name=getattr(kernel, "func", kernel).__name__,
    )(*ins)


def swap(axis, value, first):
    starts = range(first, lax.axis_size(axis) - 1, 2)
    return lax.ppermute(value, axis, [(i + d, i + 1 - d) for i in starts for d in (0, 1)])


def hand_on(axis, value):
    size = lax.axis_size(axis)
    steps = [(i, i + 2 - 4 * (i % 2)) for i in range(size)]
    return lax.ppermute(value, axis, [(i, j) for i, j in steps if 0 <= j < size])


def shards(seismic, validity, prior_weight, lateral_strength, avo_coeffs, wavelets):
    angles, rows, traces, samples = seismic.shape
    contrasts = avo_coeffs.shape[1]
    avo_coeffs = jnp.swapaxes(avo_coeffs, 0, 1)
    shape = lambda *dims: jax.ShapeDtypeStruct(dims, F32)
    field = shape(contrasts, rows, traces, samples)
    side = shape(contrasts + 2, rows + 2, samples)
    lines = shape(8, 2 * LANES)
    work = 2 * angles * rows * traces * samples * 256 * 4

    given = (seismic, validity, avo_coeffs, wavelets, prior_weight)
    kept = [given[i] for i in (1, 2, 4)]
    edge = shape(contrasts * samples // LANES + 1, traces, LANES)
    b, near, far, padded, *kept = call(
        start_kernel,
        (
            field, edge, edge, lines,
            *[jax.ShapeDtypeStruct(x.shape, x.dtype) for x in kept],
        ),
        [pltpu.with_memory_space_constraint(x, pltpu.HBM) for x in given],
        work,
        [
            pltpu.VMEM(seismic.shape, seismic.dtype),
            pltpu.VMEM(wavelets.shape, F32),
            pltpu.SemaphoreType.DMA((5,)),
        ],
        [HBM] * 5,
    )
    near = swap("inline", near, 0)
    near_next = swap("inline", far, 1)
    far_next = hand_on("inline", near)
    far = swap("inline", far, 0)
    bands = shape(angles, 2 * LANES, 2 * LANES)
    strength = lateral_strength.reshape(1, -1)
    first, ahead, back, norm, strength = call(
        functools.partial(data_kernel, wavelets.shape[1]),
        (field, bands, bands, shape(traces, LANES), shape(*strength.shape)),
        (pltpu.with_memory_space_constraint(strength, pltpu.HBM), b, padded, kept[0], kept[1]),
        2 * work,
        [pltpu.SemaphoreType.DMA((1,))],
        [HBM] + [VMEM] * 4,
    )
    col_pair, col_other, own, note = call(
        column_kernel,
        (side, side, shape(contrasts, 2 * rows + 4, samples), shape(traces, LANES)),
        (b, near, near_next, kept[0], kept[2], first),
        2 * field.size,
        [pltpu.VMEM((2, 2 * rows + 4, samples), F32)],
    )
    col_other = swap("col", col_other, 1)
    col_pair = swap("col", col_pair, 0)
    bands = shape(angles, 2 * LANES, 2 * LANES)
    halo = shape(2, contrasts, traces, samples)
    image, data, part = call(
        inner_kernel,
        (field, field, halo),
        (b, first, near, near_next, *kept, strength, ahead, back),
        4 * work,
    )
    (halo,) = call(halo_kernel, (halo,), (part, far_next, far, strength), field.size)
    axes = ("inline", "col")
    one, two, gram = call(
        image_kernel,
        (field, field, shape(lax.axis_size(axes), 1, LANES)),
        (
            b, image, data, halo, norm, own, note, col_other, col_pair,
            *kept[1:], strength, ahead, back,
        ),
        work,
    )
    gram = lax.all_to_all(gram, axes, 0, 0)
    work = 8 * field.size
    room = [pltpu.VMEM(field.shape, F32)] * 2 + [pltpu.SemaphoreType.DMA((2,))]
    return tuple(
        call(finish_kernel, (field, field), (gram, b, one, two), work, room, to=HBM)
    )


def solution(mesh):
    placed = (
        P(None, "inline", "col", None),
        P(None, "inline", "col"),
        P("inline", "col"),
        P(),
        P(),
        P(),
    )
    return jax.shard_map(
        shards,
        mesh=mesh,
        in_specs=placed,
        out_specs=(P(None, "inline", "col", None), P(None, "inline", "col", None)),
        check_vma=False,
    )
```

```python
import functools

import jax
import jax.numpy as jnp
from jax import lax
from jax.experimental import pallas as pl
from jax.experimental.pallas import tpu as pltpu
from jax.sharding import PartitionSpec as P

LANES = 128
F32 = jnp.float32
BF16 = jnp.bfloat16


def split(value):
    high = value.astype(BF16)
    return high, (value - high.astype(F32)).astype(BF16)


def pad_taps(taps_ref, padded_ref):
    padded_ref[...] = jnp.zeros_like(padded_ref)
    padded_ref[0 : taps_ref.shape[0], 0 : taps_ref.shape[1]] = taps_ref[...]


def turn(lines, count):
    n, size = lines.shape
    parts = []
    for _ in range(3):
        parts.append(lines.astype(BF16).astype(F32))
        lines = lines - parts[-1]
    rows = lax.broadcasted_iota(jnp.int32, (size, size), 0)
    cols = lax.broadcasted_iota(jnp.int32, (size, size), 1)
    flip = jnp.where(rows + cols == count - 1, 1.0, 0.0).astype(BF16)
    whole = jnp.concatenate(parts, axis=0).astype(BF16)
    turned = jnp.dot(whole, flip, preferred_element_type=F32)
    return turned[:n] + turned[n : 2 * n] + turned[2 * n :]


def band(line):
    lines = jnp.broadcast_to(line, (LANES, line.shape[1]))
    return jnp.concatenate(split(pltpu.roll(lines, 0, 1, stride=1, stride_axis=0)), axis=0)


def convolve(rows, bands):
    rows = rows.astype(BF16)
    out = lax.dot_general(rows, bands, (((1,), (1,)), ((), ())), preferred_element_type=F32)
    return out[:, :LANES] + out[:, LANES:]


def column(row):
    n = row.shape[1]
    same = lax.broadcasted_iota(jnp.int32, (n, n), 0) == lax.broadcasted_iota(jnp.int32, (n, n), 1)
    return jnp.sum(jnp.where(same, jnp.broadcast_to(row, (n, n)), 0.0), axis=1, keepdims=True)


def trace_columns(ref, *lead):
    rows = ref[lead].astype(F32)
    return jnp.concatenate([column(rows[r : r + 1, :]) for r in range(rows.shape[0])], axis=0)


def thirds(value):
    kind = BF16 if value.shape[0] % 16 == 0 else F32
    parts = []
    for _ in range(3):
        high = value.astype(BF16)
        parts.append(high.astype(kind))
        value = value - high.astype(F32)
    return parts


def windows(tiles):
    pairs = [jnp.concatenate(pair, axis=1) for pair in zip(tiles[:-1], tiles[1:])]
    return jnp.concatenate(pairs, axis=0)


def forward(tiles, bands):
    parts = list(zip(*[thirds(t) for t in tiles]))
    zero = jnp.zeros_like(parts[0][0])
    n, size = len(tiles) + 1, tiles[0].shape[0]
    rows = [windows([zero, *part, zero]) for part in parts]
    out = convolve(jnp.concatenate(rows, axis=0), bands)
    out = out[: n * size] + (out[n * size : 2 * n * size] + out[2 * n * size :])
    return [out[k * size : (k + 1) * size] for k in range(n)]


def backward(parts, bands):
    n, size = len(parts[0]) - 1, parts[0][0].shape[0]
    rows = jnp.concatenate([windows(part) for part in parts], axis=0)
    out = convolve(rows, bands)
    total = out[: n * size]
    for p in range(1, len(parts)):
        total = total + out[p * n * size : (p + 1) * n * size]
    return [total[k * size : (k + 1) * size] for k in range(n)]


def coeff(avo_ref, angle, contrast, k):
    return avo_ref[contrast, angle : angle + 1, pl.ds(k * LANES, LANES)]


def add_terms(total, avo_ref, angle, result):
    for c, line in enumerate(total):
        for k, tile in enumerate(result):
            term = coeff(avo_ref, angle, c, k) * tile
            line[k] = term if angle == 0 else line[k] + term


def store_tiles(out_ref, tiles):
    size = out_ref.shape[2]
    for c in range(out_ref.shape[0]):
        for k, tile in enumerate(tiles[c]):
            for r in range(out_ref.shape[1]):
                out_ref[c, r, :, pl.ds(k * LANES, LANES)] = tile[r * size : (r + 1) * size]


def right_side(seis_ref, masks, avo_ref, bands):
    angles, rows, _, samples = seis_ref.shape
    n = samples // LANES
    total = [[None] * n for _ in range(avo_ref.shape[0])]
    for a in range(angles):
        data = jnp.concatenate([seis_ref[a, r].astype(F32) for r in range(rows)], axis=0)
        data = data * masks[a]
        turned = [
            pltpu.roll(data[:, k * LANES : (k + 1) * LANES], LANES // 2, 1) for k in range(n)
        ]
        zero = jnp.zeros_like(turned[0])
        left_half = lax.broadcasted_iota(jnp.int32, zero.shape, 1) < LANES // 2
        shifted = [
            jnp.where(left_half, before, here).astype(BF16)
            for before, here in zip([zero, *turned], [*turned, zero])
        ]
        add_terms(total, avo_ref, a, backward([shifted], bands[a]))
    return total


def normal(field, masks, avo_ref, bands):
    contrasts, n = len(field), len(field[0])
    total = [[None] * n for _ in range(contrasts)]
    for a, (ahead, back) in enumerate(bands):
        mixed = []
        for k in range(n):
            parts = [coeff(avo_ref, a, c, k) * field[c][k] for c in range(contrasts)]
            mixed.append(functools.reduce(jnp.add, parts))
        synth = [tile * masks[a] for tile in forward(mixed, ahead)]
        left_half = lax.broadcasted_iota(jnp.int32, synth[0].shape, 1) < LANES // 2
        synth[0] = jnp.where(left_half, 0.0, synth[0])
        synth[n] = jnp.where(left_half, synth[n], 0.0)
        result = backward(list(zip(*[thirds(t) for t in synth])), back)
        add_terms(total, avo_ref, a, result)
    return total


def lateral(here, north, south, west, east):
    traces = here.shape[0]
    place = lax.broadcasted_iota(jnp.int32, here.shape, 0)
    from_west = jnp.where(place == 0, 0.0 if west is None else west, pltpu.roll(here, 1, 0))
    from_east = jnp.where(
        place == traces - 1, 0.0 if east is None else east, pltpu.roll(here, traces - 1, 0)
    )
    around = from_west + from_east
    for other in (north, south):
        around = around if other is None else around + other
    return around


def copy_in(pairs, sems):
    copies = [pltpu.make_async_copy(a, b, sems.at[i]) for i, (a, b) in enumerate(pairs)]
    for copy in copies:
        copy.start()
    return copies


def start_kernel(
    seis_hbm, valid_hbm, avo_hbm, taps_hbm, prior_hbm,
    b_ref, near_ref, far_ref, padded_ref, turned_ref, valid_ref, avo_ref, prior_ref,
    seis_ref, taps_ref, sems,
):
    angles = avo_ref.shape[1]
    taps, valid, *rest = copy_in(
        (
            (taps_hbm, taps_ref),
            (valid_hbm, valid_ref),
            (seis_hbm, seis_ref),
            (avo_hbm, avo_ref),
            (prior_hbm, prior_ref),
        ),
        sems,
    )
    taps.wait()
    pad_taps(taps_ref, padded_ref)
    turned_ref[...] = turn(padded_ref[...], taps_ref.shape[1])
    bands = [band(padded_ref[a : a + 1, :]) for a in range(angles)]
    valid.wait()
    masks = [trace_columns(valid_ref, a) for a in range(angles)]
    for copy in rest:
        copy.wait()
    store_tiles(b_ref, right_side(seis_ref, masks, avo_ref, bands))
    contrasts, rows, traces, samples = b_ref.shape
    n = samples // LANES
    first = starts_pair("inline")
    lane = lax.broadcasted_iota(jnp.int32, (traces, LANES), 1)
    notes = []
    for r in (0, rows - 1):
        note = jnp.where(lane == angles, column(prior_ref[r : r + 1, :]), 0.0)
        for a in range(angles):
            note = jnp.where(lane == a, masks[a][r * traces : (r + 1) * traces], note)
        notes.append(note)
    edges = [
        [*[b_ref[c, r, :, pl.ds(k * LANES, LANES)] for c in range(contrasts) for k in range(n)], note]
        for r, note in zip((0, rows - 1), notes)
    ]
    for e, (top, bottom) in enumerate(zip(*edges)):
        near_ref[e] = jnp.where(first, bottom, top)
        far_ref[e] = jnp.where(first, top, bottom)


def either_side(pair_ref, next_ref, *where):
    first = starts_pair("inline")
    pair, other = pair_ref[where], next_ref[where]
    return jnp.where(first, other, pair), jnp.where(first, pair, other)


def stack_tiles(ref):
    contrasts, rows, _, samples = ref.shape
    return [
        [
            jnp.concatenate([ref[c, r, :, pl.ds(k, LANES)] for r in range(rows)], axis=0)
            for k in range(0, samples, LANES)
        ]
        for c in range(contrasts)
    ]


def inside(axis):
    place = lax.axis_index(axis)
    last = lax.axis_size(axis) - 1
    return (place > 0).astype(F32), (place < last).astype(F32)


def starts_pair(axis):
    return lax.axis_index(axis) % 2 == 0


def row_pair(near_ref, next_ref, c, n):
    tiles = [either_side(near_ref, next_ref, c * n + k) for k in range(n)]
    return [jnp.concatenate(side, axis=1) for side in zip(*tiles)]


def column_kernel(
    b_ref, near_ref, near_next_ref, valid_ref, prior_ref, _,
    pair_ref, other_ref, own_ref, note_ref, second_ref,
):
    contrasts, rows, traces, samples = b_ref.shape
    angles = valid_ref.shape[0]
    first_col = starts_pair("col")
    half = rows + 2
    second_ref[...] = jnp.zeros_like(second_ref)
    note_ref[...] = jnp.zeros_like(note_ref)
    for c in range(contrasts):
        own = [b_ref[c, r] for r in range(rows)]
        for i, line in enumerate([*own, *row_pair(near_ref, near_next_ref, c, samples // LANES)]):
            own_ref[c, i : i + 1, :] = line[0:1]
            own_ref[c, half + i : half + i + 1, :] = line[traces - 1 :]
        for r, line in enumerate(own):
            at = c * rows + r
            second_ref[0, at : at + 1, :] = line[1:2]
            second_ref[1, at : at + 1, :] = line[traces - 2 : traces - 1]
    lane = lax.broadcasted_iota(jnp.int32, (1, LANES), 1)
    for r in range(rows):
        for side, t in enumerate((0, traces - 1)):
            note = jnp.where(lane == angles, prior_ref[r : r + 1, t : t + 1], 0.0)
            for a in range(angles):
                note = jnp.where(lane == a, valid_ref[a, r : r + 1, t : t + 1].astype(F32), note)
            at = contrasts * rows + r
            second_ref[side, at : at + 1, 0:LANES] = note
            at = r + side * (traces - rows)
            note_ref[at : at + 1, :] = note
    for c in range(contrasts):
        left, right = own_ref[c, 0:half], own_ref[c, half:]
        pair_ref[c] = jnp.where(first_col, right, left)
        other_ref[c] = jnp.where(first_col, left, right)
    for i in range(2):
        left, right = (second_ref[side, i * half : (i + 1) * half] for side in (0, 1))
        pair_ref[contrasts + i] = jnp.where(first_col, right, left)
        other_ref[contrasts + i] = jnp.where(first_col, left, right)


def data_kernel(
    strength_hbm, b_ref, padded_ref, turned_ref, valid_ref, avo_ref,
    data_ref, ahead_ref, back_ref, strength_ref, sem,
):
    angles = avo_ref.shape[1]
    (copy,) = copy_in(((strength_hbm, strength_ref),), sem)
    bands = []
    for a in range(angles):
        bands.append((band(turned_ref[a : a + 1, :]), band(padded_ref[a : a + 1, :])))
        ahead_ref[a], back_ref[a] = (half.astype(F32) for half in bands[a])
    masks = [trace_columns(valid_ref, a) for a in range(angles)]
    store_tiles(data_ref, normal(stack_tiles(b_ref), masks, avo_ref, bands))
    copy.wait()


def inner_kernel(
    b_ref, first_ref, near_ref, near_next_ref, valid_ref, avo_ref, prior_ref, strength_ref,
    ahead_ref, back_ref, v_ref, data_ref, halo_ref, norm_ref,
):
    contrasts, rows, traces, samples = b_ref.shape
    angles, n = avo_ref.shape[1], samples // LANES
    bands = [(ahead_ref[a].astype(BF16), back_ref[a].astype(BF16)) for a in range(angles)]
    above, below = either_side(near_ref, near_next_ref, contrasts * n)
    weights = [column(prior_ref[r : r + 1, :]) + 4.0 for r in range(rows)]
    ends = [row_pair(near_ref, near_next_ref, c, n) for c in range(contrasts)]
    for c in range(contrasts):
        strength = strength_ref[:, c : c + 1]
        lines = [ends[c][0], *[b_ref[c, r] for r in range(rows)], ends[c][1]]
        for r in range(rows):
            around = lateral(lines[r + 1], lines[r], lines[r + 2], None, None)
            v_ref[c, r] = first_ref[c, r] + strength * (weights[r] * lines[r + 1] - around)
    masks = [
        jnp.concatenate([above[:, a : a + 1], trace_columns(valid_ref, a), below[:, a : a + 1]], axis=0)
        for a in range(angles)
    ]
    field = [
        [
            jnp.concatenate([up[:, k : k + LANES], own, low[:, k : k + LANES]], axis=0)
            for k, own in zip(range(0, samples, LANES), line)
        ]
        for (up, low), line in zip(ends, stack_tiles(v_ref))
    ]
    total = normal(field, masks, avo_ref, bands)
    norm_ref[...] = functools.reduce(
        jnp.add, [lane_tiles(b_ref[c, r] * b_ref[c, r]) for c in range(contrasts) for r in range(rows)]
    )
    has = inside("inline")
    for c in range(contrasts):
        strength = strength_ref[:, c : c + 1]
        data = jnp.concatenate(total[c], axis=1)
        for r in range(rows):
            data_ref[c, r] = data[(r + 1) * traces : (r + 2) * traces]
        for i, (note, own, at) in enumerate(((above, 0, 0), (below, rows - 1, rows + 1))):
            here = ends[c][i]
            around = lateral(here, None, has[i] * b_ref[c, own], None, None)
            prior = (note[:, angles : angles + 1] + 4.0) * here - around
            halo_ref[i, c] = data[at * traces : (at + 1) * traces] + strength * prior


def lane_tiles(product):
    tiles = [product[:, k : k + LANES] for k in range(0, product.shape[1], LANES)]
    return functools.reduce(jnp.add, tiles)


def halo_kernel(halo_ref, far_next_ref, far_ref, strength_ref, out_ref):
    contrasts, samples = halo_ref.shape[1], halo_ref.shape[3]
    for c in range(contrasts):
        for i, line in enumerate(row_pair(far_ref, far_next_ref, c, samples // LANES)):
            out_ref[i, c] = halo_ref[i, c] - strength_ref[:, c : c + 1] * line


def image_kernel(
    b_ref, v_ref, data_ref, halo_ref, norm_ref, own_ref, note_ref, other_ref, pair_ref,
    avo_ref, prior_ref, strength_ref, ahead_ref, back_ref,
    one_ref, two_ref, gram_ref,
):
    contrasts, rows, traces, samples = b_ref.shape
    angles, n = avo_ref.shape[1], samples // LANES
    has_left, has_right = inside("col")
    first_col = starts_pair("col")
    place = lax.broadcasted_iota(jnp.int32, (traces, samples), 0)
    west, east = place == 0, place == traces - 1
    half = traces // 2

    def turned(value, k):
        return pltpu.roll(value, k % traces, 0) if k % traces else value

    def sides(i):
        pair, other = pair_ref[i], other_ref[i]
        left, right = jnp.where(first_col, other, pair), jnp.where(first_col, pair, other)
        return jnp.concatenate([left, right], axis=0)

    def at_ends(value, left, right, inner):
        return jnp.where(west, turned(value, left), jnp.where(east, turned(value, right), inner))

    beside = [sides(c) for c in range(contrasts)]
    seconds = [sides(contrasts), sides(contrasts + 1)]
    notes = seconds[1][:, :LANES]
    line = place[:, :LANES]
    theirs = turned(notes, -rows)
    mixed = jnp.where((line == 2) | (line == 3), notes, note_ref[...])
    mixed = jnp.where((line == 4) | (line == 5), theirs, mixed)
    masks = [mixed[:, a : a + 1] for a in range(angles)]
    mine = (place[:, :1] < 2) | (place[:, :1] >= traces - 2)
    tile = []
    for c in range(contrasts):
        scale = jnp.where(mine, -strength_ref[:, c : c + 1], 1.0)
        whole = jnp.where(place % half < rows, beside[c], turned(beside[c], rows)) * scale
        tile.append([whole[:, k * LANES : (k + 1) * LANES] for k in range(n)])
    bands = [(ahead_ref[a].astype(BF16), back_ref[a].astype(BF16)) for a in range(angles)]
    edge = [jnp.concatenate(tiles, axis=1) for tiles in normal(tile, masks, avo_ref, bands)]

    has = jnp.where(place[:, :1] < half, has_left, has_right)
    far_weight = theirs[:, angles : angles + 1] + 4.0
    weights = [column(prior_ref[r : r + 1, :]) + 4.0 for r in range(rows)]
    sums = [norm_ref[...], *[jnp.zeros((traces, LANES), F32) for _ in range(3)]]
    for c in range(contrasts):
        strength = strength_ref[:, c : c + 1]
        theirs = beside[c]
        around = turned(seconds[c // 2], -rows * (c % 2)) + turned(theirs, -rows)
        around = around + jnp.where(place % 2 == 1, turned(theirs, 1), turned(theirs, -1))
        prior = far_weight * theirs - (around + has * own_ref[c])
        beyond = jnp.where(place < half, turned(edge[c], -rows), edge[c]) + strength * prior

        lines = [halo_ref[0, c], *[v_ref[c, r] for r in range(rows)], halo_ref[1, c]]
        lines = [
            here - strength * at_ends(theirs, -k, half - 1 - k, 0.0)
            for here, k in zip(lines, (rows, *range(rows), rows + 1))
        ]
        for r in range(rows):
            here, b = lines[r + 1], b_ref[c, r]
            ends = jnp.where(west, turned(beyond, -r), turned(beyond, half - 1 - r))
            around = jnp.where(west, ends, turned(here, 1)) + jnp.where(east, ends, turned(here, -1))
            around = around + lines[r] + lines[r + 2]
            mend = at_ends(edge[c], -r, 1 - r, 0.0)
            two = data_ref[c, r] + mend + strength * (weights[r] * here - around)
            one_ref[c, r] = here
            two_ref[c, r] = two
            for q, product in enumerate((b * here, here * here, here * two), 1):
                sums[q] = sums[q] + lane_tiles(product)
    lane = lax.broadcasted_iota(jnp.int32, (1, LANES), 1)
    packed = jnp.zeros((1, LANES), F32)
    for q, total in enumerate(sums):
        total = jnp.sum(jnp.sum(total, axis=0, keepdims=True), axis=1, keepdims=True)
        packed = jnp.where(lane == q, total, packed)
    gram_ref[...] = jnp.broadcast_to(packed[None], gram_ref.shape)


def finish_kernel(
    gram_ref, b_ref, one_ref, two_ref, solution_hbm, residual_hbm, solution_ref, residual_ref, sems
):
    sums = jnp.sum(gram_ref[...], axis=0)
    g00, g01, g11, g12 = (sums[:, q : q + 1] for q in range(4))
    first = g00 / g01
    ratio = first * g11 / g01
    second = (ratio - 1.0) * g01 / (first * g12 - ratio * g11)
    near = first + second * ratio
    far = first * second
    blocks = [(c, r) for c in range(b_ref.shape[0]) for r in range(b_ref.shape[1])]
    for block in blocks:
        solution_ref[block] = near * b_ref[block] - far * one_ref[block]
    done = pltpu.make_async_copy(solution_ref, solution_hbm, sems.at[0])
    done.start()
    for block in blocks:
        residual_ref[block] = b_ref[block] - near * one_ref[block] + far * two_ref[block]
    last = pltpu.make_async_copy(residual_ref, residual_hbm, sems.at[1])
    last.start()
    done.wait()
    last.wait()


VMEM = pl.BlockSpec(memory_space=pltpu.VMEM)
HBM = pl.BlockSpec(memory_space=pltpu.HBM)


def call(kernel, outs, ins, flops, scratch=(), places=None, to=VMEM):
    moved = sum(x.size * x.dtype.itemsize for x in (*ins, *outs))
    return pl.pallas_call(
        kernel,
        out_shape=outs,
        in_specs=[VMEM] * len(ins) if places is None else places,
        out_specs=jax.tree.map(lambda _: to, outs),
        scratch_shapes=list(scratch),
        compiler_params=pltpu.CompilerParams(vmem_limit_bytes=24 * 1024 * 1024),
        cost_estimate=pl.CostEstimate(flops=flops, bytes_accessed=moved, transcendentals=0),
        name=getattr(kernel, "func", kernel).__name__,
    )(*ins)


def swap(axis, value, first):
    starts = range(first, lax.axis_size(axis) - 1, 2)
    return lax.ppermute(value, axis, [(i + d, i + 1 - d) for i in starts for d in (0, 1)])


def hand_on(axis, value):
    size = lax.axis_size(axis)
    steps = [(i, i + 2 - 4 * (i % 2)) for i in range(size)]
    return lax.ppermute(value, axis, [(i, j) for i, j in steps if 0 <= j < size])


def shards(seismic, validity, prior_weight, lateral_strength, avo_coeffs, wavelets):
    angles, rows, traces, samples = seismic.shape
    contrasts = avo_coeffs.shape[1]
    avo_coeffs = jnp.swapaxes(avo_coeffs, 0, 1)
    shape = lambda *dims: jax.ShapeDtypeStruct(dims, F32)
    field = shape(contrasts, rows, traces, samples)
    side = shape(contrasts + 2, rows + 2, samples)
    lines = shape(8, 2 * LANES)
    work = 2 * angles * rows * traces * samples * 256 * 4

    given = (seismic, validity, avo_coeffs, wavelets, prior_weight)
    kept = [given[i] for i in (1, 2, 4)]
    edge = shape(contrasts * samples // LANES + 1, traces, LANES)
    b, near, far, padded, turned, *kept = call(
        start_kernel,
        (
            field, edge, edge, lines, lines,
            *[jax.ShapeDtypeStruct(x.shape, x.dtype) for x in kept],
        ),
        [pltpu.with_memory_space_constraint(x, pltpu.HBM) for x in given],
        work,
        [
            pltpu.VMEM(seismic.shape, seismic.dtype),
            pltpu.VMEM(wavelets.shape, F32),
            pltpu.SemaphoreType.DMA((5,)),
        ],
        [HBM] * 5,
    )
    near = swap("inline", near, 0)
    near_next = swap("inline", far, 1)
    far_next = hand_on("inline", near)
    far = swap("inline", far, 0)
    bands = shape(angles, 2 * LANES, 2 * LANES)
    strength = lateral_strength.reshape(1, -1)
    first, ahead, back, strength = call(
        data_kernel,
        (field, bands, bands, shape(*strength.shape)),
        (pltpu.with_memory_space_constraint(strength, pltpu.HBM), b, padded, turned, *kept[:2]),
        2 * work,
        [pltpu.SemaphoreType.DMA((1,))],
        [HBM] + [VMEM] * 5,
    )
    col_pair, col_other, own, note = call(
        column_kernel,
        (side, side, shape(contrasts, 2 * rows + 4, samples), shape(traces, LANES)),
        (b, near, near_next, kept[0], kept[2], first),
        2 * field.size,
        [pltpu.VMEM((2, 2 * rows + 4, samples), F32)],
    )
    col_other = swap("col", col_other, 1)
    col_pair = swap("col", col_pair, 0)
    bands = shape(angles, 2 * LANES, 2 * LANES)
    halo = shape(2, contrasts, traces, samples)
    image, data, part, norm = call(
        inner_kernel,
        (field, field, halo, shape(traces, LANES)),
        (b, first, near, near_next, *kept, strength, ahead, back),
        4 * work,
    )
    (halo,) = call(halo_kernel, (halo,), (part, far_next, far, strength), field.size)
    axes = ("inline", "col")
    one, two, gram = call(
        image_kernel,
        (field, field, shape(lax.axis_size(axes), 1, LANES)),
        (
            b, image, data, halo, norm, own, note, col_other, col_pair,
            *kept[1:], strength, ahead, back,
        ),
        work,
    )
    gram = lax.all_to_all(gram, axes, 0, 0)
    work = 8 * field.size
    room = [pltpu.VMEM(field.shape, F32)] * 2 + [pltpu.SemaphoreType.DMA((2,))]
    return tuple(
        call(finish_kernel, (field, field), (gram, b, one, two), work, room, to=HBM)
    )


def solution(mesh):
    placed = (
        P(None, "inline", "col", None),
        P(None, "inline", "col"),
        P("inline", "col"),
        P(),
        P(),
        P(),
    )
    return jax.shard_map(
        shards,
        mesh=mesh,
        in_specs=placed,
        out_specs=(P(None, "inline", "col", None), P(None, "inline", "col", None)),
        check_vma=False,
    )
```

```python
import functools

import jax
import jax.numpy as jnp
from jax import lax
from jax.experimental import pallas as pl
from jax.experimental.pallas import tpu as pltpu
from jax.sharding import PartitionSpec as P

LANES = 128
F32 = jnp.float32
BF16 = jnp.bfloat16


def split(value):
    high = value.astype(BF16)
    return high, (value - high.astype(F32)).astype(BF16)


def pad_taps(taps_ref, padded_ref):
    padded_ref[...] = jnp.zeros_like(padded_ref)
    padded_ref[0 : taps_ref.shape[0], 0 : taps_ref.shape[1]] = taps_ref[...]


def turn(lines, count):
    n, size = lines.shape
    parts = []
    for _ in range(3):
        parts.append(lines.astype(BF16).astype(F32))
        lines = lines - parts[-1]
    rows = lax.broadcasted_iota(jnp.int32, (size, size), 0)
    cols = lax.broadcasted_iota(jnp.int32, (size, size), 1)
    flip = jnp.where(rows + cols == count - 1, 1.0, 0.0).astype(BF16)
    whole = jnp.concatenate(parts, axis=0).astype(BF16)
    turned = jnp.dot(whole, flip, preferred_element_type=F32)
    return turned[:n] + turned[n : 2 * n] + turned[2 * n :]


def band(line):
    lines = jnp.broadcast_to(line, (LANES, line.shape[1]))
    return jnp.concatenate(split(pltpu.roll(lines, 0, 1, stride=1, stride_axis=0)), axis=0)


def convolve(rows, bands):
    rows = rows.astype(BF16)
    out = lax.dot_general(rows, bands, (((1,), (1,)), ((), ())), preferred_element_type=F32)
    return out[:, :LANES] + out[:, LANES:]


def column(row):
    n = row.shape[1]
    same = lax.broadcasted_iota(jnp.int32, (n, n), 0) == lax.broadcasted_iota(jnp.int32, (n, n), 1)
    return jnp.sum(jnp.where(same, jnp.broadcast_to(row, (n, n)), 0.0), axis=1, keepdims=True)


def trace_columns(ref, *lead):
    rows = ref[lead].astype(F32)
    return jnp.concatenate([column(rows[r : r + 1, :]) for r in range(rows.shape[0])], axis=0)


def thirds(value):
    kind = BF16
    parts = []
    for _ in range(3):
        high = value.astype(BF16)
        parts.append(high.astype(kind))
        value = value - high.astype(F32)
    return parts


def windows(tiles):
    pairs = [jnp.concatenate(pair, axis=1) for pair in zip(tiles[:-1], tiles[1:])]
    return jnp.concatenate(pairs, axis=0)


def forward(tiles, bands):
    parts = list(zip(*[thirds(t) for t in tiles]))
    zero = jnp.zeros_like(parts[0][0])
    n, size = len(tiles) + 1, tiles[0].shape[0]
    rows = [windows([zero, *part, zero]) for part in parts]
    out = convolve(jnp.concatenate(rows, axis=0), bands)
    out = out[: n * size] + (out[n * size : 2 * n * size] + out[2 * n * size :])
    return [out[k * size : (k + 1) * size] for k in range(n)]


def backward(parts, bands):
    n, size = len(parts[0]) - 1, parts[0][0].shape[0]
    rows = jnp.concatenate([windows(part) for part in parts], axis=0)
    out = convolve(rows, bands)
    total = out[: n * size]
    for p in range(1, len(parts)):
        total = total + out[p * n * size : (p + 1) * n * size]
    return [total[k * size : (k + 1) * size] for k in range(n)]


def coeff(avo_ref, angle, contrast, k):
    return avo_ref[contrast, angle : angle + 1, pl.ds(k * LANES, LANES)]


def add_terms(total, avo_ref, angle, result):
    for c, line in enumerate(total):
        for k, tile in enumerate(result):
            term = coeff(avo_ref, angle, c, k) * tile
            line[k] = term if angle == 0 else line[k] + term


def store_tiles(out_ref, tiles):
    size = out_ref.shape[2]
    for c in range(out_ref.shape[0]):
        for k, tile in enumerate(tiles[c]):
            for r in range(out_ref.shape[1]):
                out_ref[c, r, :, pl.ds(k * LANES, LANES)] = tile[r * size : (r + 1) * size]


def right_side(seis_ref, masks, avo_ref, bands):
    angles, rows, _, samples = seis_ref.shape
    n = samples // LANES
    total = [[None] * n for _ in range(avo_ref.shape[0])]
    for a in range(angles):
        data = jnp.concatenate([seis_ref[a, r].astype(F32) for r in range(rows)], axis=0)
        data = data * masks[a]
        turned = [
            pltpu.roll(data[:, k * LANES : (k + 1) * LANES], LANES // 2, 1) for k in range(n)
        ]
        zero = jnp.zeros_like(turned[0])
        left_half = lax.broadcasted_iota(jnp.int32, zero.shape, 1) < LANES // 2
        shifted = [
            jnp.where(left_half, before, here).astype(BF16)
            for before, here in zip([zero, *turned], [*turned, zero])
        ]
        add_terms(total, avo_ref, a, backward([shifted], bands[a]))
    return total


def normal(field, masks, avo_ref, bands):
    contrasts, n = len(field), len(field[0])
    total = [[None] * n for _ in range(contrasts)]
    for a, (ahead, back) in enumerate(bands):
        mixed = []
        for k in range(n):
            parts = [coeff(avo_ref, a, c, k) * field[c][k] for c in range(contrasts)]
            mixed.append(functools.reduce(jnp.add, parts))
        synth = [tile * masks[a] for tile in forward(mixed, ahead)]
        left_half = lax.broadcasted_iota(jnp.int32, synth[0].shape, 1) < LANES // 2
        synth[0] = jnp.where(left_half, 0.0, synth[0])
        synth[n] = jnp.where(left_half, synth[n], 0.0)
        result = backward(list(zip(*[thirds(t) for t in synth])), back)
        add_terms(total, avo_ref, a, result)
    return total


def lateral(here, north, south, west, east):
    traces = here.shape[0]
    place = lax.broadcasted_iota(jnp.int32, here.shape, 0)
    from_west = jnp.where(place == 0, 0.0 if west is None else west, pltpu.roll(here, 1, 0))
    from_east = jnp.where(
        place == traces - 1, 0.0 if east is None else east, pltpu.roll(here, traces - 1, 0)
    )
    around = from_west + from_east
    for other in (north, south):
        around = around if other is None else around + other
    return around


def copy_in(pairs, sems):
    copies = [pltpu.make_async_copy(a, b, sems.at[i]) for i, (a, b) in enumerate(pairs)]
    for copy in copies:
        copy.start()
    return copies


def start_kernel(
    seis_hbm, valid_hbm, avo_hbm, taps_hbm, prior_hbm,
    b_ref, near_ref, far_ref, padded_ref, valid_ref, avo_ref, prior_ref,
    seis_ref, taps_ref, sems,
):
    angles = avo_ref.shape[1]
    taps, valid, *rest = copy_in(
        (
            (taps_hbm, taps_ref),
            (valid_hbm, valid_ref),
            (seis_hbm, seis_ref),
            (avo_hbm, avo_ref),
            (prior_hbm, prior_ref),
        ),
        sems,
    )
    taps.wait()
    pad_taps(taps_ref, padded_ref)
    bands = [band(padded_ref[a : a + 1, :]) for a in range(angles)]
    valid.wait()
    masks = [trace_columns(valid_ref, a) for a in range(angles)]
    for copy in rest:
        copy.wait()
    store_tiles(b_ref, right_side(seis_ref, masks, avo_ref, bands))
    contrasts, rows, traces, samples = b_ref.shape
    n = samples // LANES
    first = starts_pair("inline")
    lane = lax.broadcasted_iota(jnp.int32, (traces, LANES), 1)
    notes = []
    for r in (0, rows - 1):
        note = jnp.where(lane == angles, column(prior_ref[r : r + 1, :]), 0.0)
        for a in range(angles):
            note = jnp.where(lane == a, masks[a][r * traces : (r + 1) * traces], note)
        notes.append(note)
    edges = [
        [*[b_ref[c, r, :, pl.ds(k * LANES, LANES)] for c in range(contrasts) for k in range(n)], note]
        for r, note in zip((0, rows - 1), notes)
    ]
    for e, (top, bottom) in enumerate(zip(*edges)):
        near_ref[e] = jnp.where(first, bottom, top)
        far_ref[e] = jnp.where(first, top, bottom)


def either_side(pair_ref, next_ref, *where):
    first = starts_pair("inline")
    pair, other = pair_ref[where], next_ref[where]
    return jnp.where(first, other, pair), jnp.where(first, pair, other)


def stack_tiles(ref):
    contrasts, rows, _, samples = ref.shape
    return [
        [
            jnp.concatenate([ref[c, r, :, pl.ds(k, LANES)] for r in range(rows)], axis=0)
            for k in range(0, samples, LANES)
        ]
        for c in range(contrasts)
    ]


def inside(axis):
    place = lax.axis_index(axis)
    last = lax.axis_size(axis) - 1
    return (place > 0).astype(F32), (place < last).astype(F32)


def starts_pair(axis):
    return lax.axis_index(axis) % 2 == 0


def row_pair(near_ref, next_ref, c, n):
    tiles = [either_side(near_ref, next_ref, c * n + k) for k in range(n)]
    return [jnp.concatenate(side, axis=1) for side in zip(*tiles)]


def column_kernel(
    b_ref, near_ref, near_next_ref, valid_ref, prior_ref, _,
    pair_ref, other_ref, own_ref, note_ref, second_ref,
):
    contrasts, rows, traces, samples = b_ref.shape
    angles = valid_ref.shape[0]
    first_col = starts_pair("col")
    half = rows + 2
    second_ref[...] = jnp.zeros_like(second_ref)
    note_ref[...] = jnp.zeros_like(note_ref)
    for c in range(contrasts):
        own = [b_ref[c, r] for r in range(rows)]
        for i, line in enumerate([*own, *row_pair(near_ref, near_next_ref, c, samples // LANES)]):
            own_ref[c, i : i + 1, :] = line[0:1]
            own_ref[c, half + i : half + i + 1, :] = line[traces - 1 :]
        for r, line in enumerate(own):
            at = c * rows + r
            second_ref[0, at : at + 1, :] = line[1:2]
            second_ref[1, at : at + 1, :] = line[traces - 2 : traces - 1]
    lane = lax.broadcasted_iota(jnp.int32, (1, LANES), 1)
    for r in range(rows):
        for side, t in enumerate((0, traces - 1)):
            note = jnp.where(lane == angles, prior_ref[r : r + 1, t : t + 1], 0.0)
            for a in range(angles):
                note = jnp.where(lane == a, valid_ref[a, r : r + 1, t : t + 1].astype(F32), note)
            at = contrasts * rows + r
            second_ref[side, at : at + 1, 0:LANES] = note
            at = r + side * (traces - rows)
            note_ref[at : at + 1, :] = note
    for c in range(contrasts):
        left, right = own_ref[c, 0:half], own_ref[c, half:]
        pair_ref[c] = jnp.where(first_col, right, left)
        other_ref[c] = jnp.where(first_col, left, right)
    for i in range(2):
        left, right = (second_ref[side, i * half : (i + 1) * half] for side in (0, 1))
        pair_ref[contrasts + i] = jnp.where(first_col, right, left)
        other_ref[contrasts + i] = jnp.where(first_col, left, right)


def data_kernel(
    count, strength_hbm, b_ref, padded_ref, valid_ref, avo_ref,
    data_ref, ahead_ref, back_ref, norm_ref, strength_ref, sem,
):
    contrasts, rows = b_ref.shape[:2]
    angles = avo_ref.shape[1]
    (copy,) = copy_in(((strength_hbm, strength_ref),), sem)
    turned = turn(padded_ref[...], count)
    bands = []
    for a in range(angles):
        bands.append((band(turned[a : a + 1]), band(padded_ref[a : a + 1, :])))
        ahead_ref[a], back_ref[a] = (half.astype(F32) for half in bands[a])
    masks = [trace_columns(valid_ref, a) for a in range(angles)]
    store_tiles(data_ref, normal(stack_tiles(b_ref), masks, avo_ref, bands))
    norm_ref[...] = functools.reduce(
        jnp.add, [lane_tiles(b_ref[c, r] * b_ref[c, r]) for c in range(contrasts) for r in range(rows)]
    )
    copy.wait()


def inner_kernel(
    b_ref, first_ref, near_ref, near_next_ref, valid_ref, avo_ref, prior_ref, strength_ref,
    ahead_ref, back_ref, v_ref, data_ref, halo_ref,
):
    contrasts, rows, traces, samples = b_ref.shape
    angles, n = avo_ref.shape[1], samples // LANES
    bands = [(ahead_ref[a].astype(BF16), back_ref[a].astype(BF16)) for a in range(angles)]
    above, below = either_side(near_ref, near_next_ref, contrasts * n)
    weights = [column(prior_ref[r : r + 1, :]) + 4.0 for r in range(rows)]
    ends = [row_pair(near_ref, near_next_ref, c, n) for c in range(contrasts)]
    for c in range(contrasts):
        strength = strength_ref[:, c : c + 1]
        lines = [ends[c][0], *[b_ref[c, r] for r in range(rows)], ends[c][1]]
        for r in range(rows):
            around = lateral(lines[r + 1], lines[r], lines[r + 2], None, None)
            v_ref[c, r] = first_ref[c, r] + strength * (weights[r] * lines[r + 1] - around)
    masks = [
        jnp.concatenate([above[:, a : a + 1], trace_columns(valid_ref, a), below[:, a : a + 1]], axis=0)
        for a in range(angles)
    ]
    field = [
        [
            jnp.concatenate([up[:, k : k + LANES], own, low[:, k : k + LANES]], axis=0)
            for k, own in zip(range(0, samples, LANES), line)
        ]
        for (up, low), line in zip(ends, stack_tiles(v_ref))
    ]
    total = normal(field, masks, avo_ref, bands)
    has = inside("inline")
    for c in range(contrasts):
        strength = strength_ref[:, c : c + 1]
        data = jnp.concatenate(total[c], axis=1)
        for r in range(rows):
            data_ref[c, r] = data[(r + 1) * traces : (r + 2) * traces]
        for i, (note, own, at) in enumerate(((above, 0, 0), (below, rows - 1, rows + 1))):
            here = ends[c][i]
            around = lateral(here, None, has[i] * b_ref[c, own], None, None)
            prior = (note[:, angles : angles + 1] + 4.0) * here - around
            halo_ref[i, c] = data[at * traces : (at + 1) * traces] + strength * prior


def lane_tiles(product):
    tiles = [product[:, k : k + LANES] for k in range(0, product.shape[1], LANES)]
    return functools.reduce(jnp.add, tiles)


def halo_kernel(halo_ref, far_next_ref, far_ref, strength_ref, out_ref):
    contrasts, samples = halo_ref.shape[1], halo_ref.shape[3]
    for c in range(contrasts):
        for i, line in enumerate(row_pair(far_ref, far_next_ref, c, samples // LANES)):
            out_ref[i, c] = halo_ref[i, c] - strength_ref[:, c : c + 1] * line


def image_kernel(
    b_ref, v_ref, data_ref, halo_ref, norm_ref, own_ref, note_ref, other_ref, pair_ref,
    avo_ref, prior_ref, strength_ref, ahead_ref, back_ref,
    one_ref, two_ref, gram_ref,
):
    contrasts, rows, traces, samples = b_ref.shape
    angles, n = avo_ref.shape[1], samples // LANES
    has_left, has_right = inside("col")
    first_col = starts_pair("col")
    place = lax.broadcasted_iota(jnp.int32, (traces, samples), 0)
    west, east = place == 0, place == traces - 1
    half = traces // 2

    def turned(value, k):
        return pltpu.roll(value, k % traces, 0) if k % traces else value

    def sides(i):
        pair, other = pair_ref[i], other_ref[i]
        left, right = jnp.where(first_col, other, pair), jnp.where(first_col, pair, other)
        return jnp.concatenate([left, right], axis=0)

    def at_ends(value, left, right, inner):
        return jnp.where(west, turned(value, left), jnp.where(east, turned(value, right), inner))

    beside = [sides(c) for c in range(contrasts)]
    seconds = [sides(contrasts), sides(contrasts + 1)]
    notes = seconds[1][:, :LANES]
    line = place[:, :LANES]
    theirs = turned(notes, -rows)
    mixed = jnp.where((line == 2) | (line == 3), notes, note_ref[...])
    mixed = jnp.where((line == 4) | (line == 5), theirs, mixed)
    masks = [mixed[:, a : a + 1] for a in range(angles)]
    mine = (place[:, :1] < 2) | (place[:, :1] >= traces - 2)
    tile = []
    for c in range(contrasts):
        scale = jnp.where(mine, -strength_ref[:, c : c + 1], 1.0)
        whole = jnp.where(place % half < rows, beside[c], turned(beside[c], rows)) * scale
        tile.append([whole[:, k * LANES : (k + 1) * LANES] for k in range(n)])
    bands = [(ahead_ref[a].astype(BF16), back_ref[a].astype(BF16)) for a in range(angles)]
    edge = [jnp.concatenate(tiles, axis=1) for tiles in normal(tile, masks, avo_ref, bands)]

    has = jnp.where(place[:, :1] < half, has_left, has_right)
    far_weight = theirs[:, angles : angles + 1] + 4.0
    weights = [column(prior_ref[r : r + 1, :]) + 4.0 for r in range(rows)]
    sums = [norm_ref[...], *[jnp.zeros((traces, LANES), F32) for _ in range(3)]]
    for c in range(contrasts):
        strength = strength_ref[:, c : c + 1]
        theirs = beside[c]
        around = turned(seconds[c // 2], -rows * (c % 2)) + turned(theirs, -rows)
        around = around + jnp.where(place % 2 == 1, turned(theirs, 1), turned(theirs, -1))
        prior = far_weight * theirs - (around + has * own_ref[c])
        beyond = jnp.where(place < half, turned(edge[c], -rows), edge[c]) + strength * prior

        lines = [halo_ref[0, c], *[v_ref[c, r] for r in range(rows)], halo_ref[1, c]]
        lines = [
            here - strength * at_ends(theirs, -k, half - 1 - k, 0.0)
            for here, k in zip(lines, (rows, *range(rows), rows + 1))
        ]
        for r in range(rows):
            here, b = lines[r + 1], b_ref[c, r]
            ends = jnp.where(west, turned(beyond, -r), turned(beyond, half - 1 - r))
            around = jnp.where(west, ends, turned(here, 1)) + jnp.where(east, ends, turned(here, -1))
            around = around + lines[r] + lines[r + 2]
            mend = at_ends(edge[c], -r, 1 - r, 0.0)
            two = data_ref[c, r] + mend + strength * (weights[r] * here - around)
            one_ref[c, r] = here
            two_ref[c, r] = two
            for q, product in enumerate((b * here, here * here, here * two), 1):
                sums[q] = sums[q] + lane_tiles(product)
    lane = lax.broadcasted_iota(jnp.int32, (1, LANES), 1)
    packed = jnp.zeros((1, LANES), F32)
    for q, total in enumerate(sums):
        total = jnp.sum(jnp.sum(total, axis=0, keepdims=True), axis=1, keepdims=True)
        packed = jnp.where(lane == q, total, packed)
    gram_ref[...] = jnp.broadcast_to(packed[None], gram_ref.shape)


def finish_kernel(
    gram_ref, b_ref, one_ref, two_ref, solution_hbm, residual_hbm, solution_ref, residual_ref, sems
):
    sums = jnp.sum(gram_ref[...], axis=0)
    g00, g01, g11, g12 = (sums[:, q : q + 1] for q in range(4))
    first = g00 / g01
    ratio = first * g11 / g01
    second = (ratio - 1.0) * g01 / (first * g12 - ratio * g11)
    near = first + second * ratio
    far = first * second
    blocks = [(c, r) for c in range(b_ref.shape[0]) for r in range(b_ref.shape[1])]
    for block in blocks:
        solution_ref[block] = near * b_ref[block] - far * one_ref[block]
    done = pltpu.make_async_copy(solution_ref, solution_hbm, sems.at[0])
    done.start()
    for block in blocks:
        residual_ref[block] = b_ref[block] - near * one_ref[block] + far * two_ref[block]
    last = pltpu.make_async_copy(residual_ref, residual_hbm, sems.at[1])
    last.start()
    done.wait()
    last.wait()


VMEM = pl.BlockSpec(memory_space=pltpu.VMEM)
HBM = pl.BlockSpec(memory_space=pltpu.HBM)


def call(kernel, outs, ins, flops, scratch=(), places=None, to=VMEM):
    moved = sum(x.size * x.dtype.itemsize for x in (*ins, *outs))
    return pl.pallas_call(
        kernel,
        out_shape=outs,
        in_specs=[VMEM] * len(ins) if places is None else places,
        out_specs=jax.tree.map(lambda _: to, outs),
        scratch_shapes=list(scratch),
        compiler_params=pltpu.CompilerParams(vmem_limit_bytes=24 * 1024 * 1024),
        cost_estimate=pl.CostEstimate(flops=flops, bytes_accessed=moved, transcendentals=0),
        name=getattr(kernel, "func", kernel).__name__,
    )(*ins)


def swap(axis, value, first):
    starts = range(first, lax.axis_size(axis) - 1, 2)
    return lax.ppermute(value, axis, [(i + d, i + 1 - d) for i in starts for d in (0, 1)])


def hand_on(axis, value):
    size = lax.axis_size(axis)
    steps = [(i, i + 2 - 4 * (i % 2)) for i in range(size)]
    return lax.ppermute(value, axis, [(i, j) for i, j in steps if 0 <= j < size])


def shards(seismic, validity, prior_weight, lateral_strength, avo_coeffs, wavelets):
    angles, rows, traces, samples = seismic.shape
    contrasts = avo_coeffs.shape[1]
    avo_coeffs = jnp.swapaxes(avo_coeffs, 0, 1)
    shape = lambda *dims: jax.ShapeDtypeStruct(dims, F32)
    field = shape(contrasts, rows, traces, samples)
    side = shape(contrasts + 2, rows + 2, samples)
    lines = shape(8, 2 * LANES)
    work = 2 * angles * rows * traces * samples * 256 * 4

    given = (seismic, validity, avo_coeffs, wavelets, prior_weight)
    kept = [given[i] for i in (1, 2, 4)]
    edge = shape(contrasts * samples // LANES + 1, traces, LANES)
    b, near, far, padded, *kept = call(
        start_kernel,
        (
            field, edge, edge, lines,
            *[jax.ShapeDtypeStruct(x.shape, x.dtype) for x in kept],
        ),
        [pltpu.with_memory_space_constraint(x, pltpu.HBM) for x in given],
        work,
        [
            pltpu.VMEM(seismic.shape, seismic.dtype),
            pltpu.VMEM(wavelets.shape, F32),
            pltpu.SemaphoreType.DMA((5,)),
        ],
        [HBM] * 5,
    )
    near = swap("inline", near, 0)
    near_next = swap("inline", far, 1)
    far_next = hand_on("inline", near)
    far = swap("inline", far, 0)
    bands = shape(angles, 2 * LANES, 2 * LANES)
    strength = lateral_strength.reshape(1, -1)
    first, ahead, back, norm, strength = call(
        functools.partial(data_kernel, wavelets.shape[1]),
        (field, bands, bands, shape(traces, LANES), shape(*strength.shape)),
        (pltpu.with_memory_space_constraint(strength, pltpu.HBM), b, padded, kept[0], kept[1]),
        2 * work,
        [pltpu.SemaphoreType.DMA((1,))],
        [HBM] + [VMEM] * 4,
    )
    col_pair, col_other, own, note = call(
        column_kernel,
        (side, side, shape(contrasts, 2 * rows + 4, samples), shape(traces, LANES)),
        (b, near, near_next, kept[0], kept[2], first),
        2 * field.size,
        [pltpu.VMEM((2, 2 * rows + 4, samples), F32)],
    )
    col_other = swap("col", col_other, 1)
    col_pair = swap("col", col_pair, 0)
    bands = shape(angles, 2 * LANES, 2 * LANES)
    halo = shape(2, contrasts, traces, samples)
    image, data, part = call(
        inner_kernel,
        (field, field, halo),
        (b, first, near, near_next, *kept, strength, ahead, back),
        4 * work,
    )
    (halo,) = call(halo_kernel, (halo,), (part, far_next, far, strength), field.size)
    axes = ("inline", "col")
    one, two, gram = call(
        image_kernel,
        (field, field, shape(lax.axis_size(axes), 1, LANES)),
        (
            b, image, data, halo, norm, own, note, col_other, col_pair,
            *kept[1:], strength, ahead, back,
        ),
        work,
    )
    gram = lax.all_to_all(gram, axes, 0, 0)
    work = 8 * field.size
    room = [pltpu.VMEM(field.shape, F32)] * 2 + [pltpu.SemaphoreType.DMA((2,))]
    return tuple(
        call(finish_kernel, (field, field), (gram, b, one, two), work, room, to=HBM)
    )


def solution(mesh):
    placed = (
        P(None, "inline", "col", None),
        P(None, "inline", "col"),
        P("inline", "col"),
        P(),
        P(),
        P(),
    )
    return jax.shard_map(
        shards,
        mesh=mesh,
        in_specs=placed,
        out_specs=(P(None, "inline", "col", None), P(None, "inline", "col", None)),
        check_vma=False,
    )
```
